32 devices in a mesh: ctx: 16 (over z, x, core), fsdp: 2 (over y).
Axes of the slice: x: 2, y: 2, z: 4, core: 2. Of those that a mesh axis runs over, the one named last changes fastest.
Arguments:
- inputs: float32 [2, 2048, 1024], P('fsdp', 'ctx'), may hold values from -6 to 6
- qkv_weight: bfloat16 [1024, 3072], P('fsdp'), may hold values from -0.1875 to 0.1875
- gate_weight: bfloat16 [1024, 1024], P('fsdp'), may hold values from -0.1875 to 0.1875
- out_weight: bfloat16 [1024, 1024], P('fsdp'), may hold values from -0.75 to 0.75
- up_weight: bfloat16 [1024, 5632], P('fsdp'), may hold values from -0.1875 to 0.1875
- down_weight: bfloat16 [2816, 1024], P('fsdp'), may hold values from -0.109375 to 0.109375
- conv_taps: bfloat16 [4, 3072], P(None, 'fsdp'), may hold values from -3 to 3
- gain_attn: bfloat16 [1024], P('fsdp'), may hold values from 0.5 to 1.5
- gain_ffn: bfloat16 [1024], P('fsdp'), may hold values from 0.5 to 1.5
- ridge_terms: bfloat16 [1024], P('fsdp'), may hold values from 0.099609375 to 1
- forget: float32 [2, 2048, 8], P('fsdp', 'ctx'), may hold values from 0 to 1, as said below
- cotangent: float32 [2, 2048, 1024], P('fsdp', 'ctx'), may hold values from -6 to 6
Outputs:
- output: float32 [2, 2048, 1024], P('fsdp', 'ctx')
- grad_inputs: float32 [2, 2048, 1024], P('fsdp', 'ctx')
- grad_qkv: float32 [1024, 3072], P(('ctx', 'fsdp'))
- grad_gate: float32 [1024, 1024], P(('ctx', 'fsdp'))
- grad_out: float32 [1024, 1024], P(('ctx', 'fsdp'))
- grad_up: float32 [1024, 5632], P(('ctx', 'fsdp'))
- grad_down: float32 [2816, 1024], P(('ctx', 'fsdp'))
- grad_taps: float32 [4, 3072], P(None, ('ctx', 'fsdp'))
- grad_gain_attn: float32 [1024], P(('ctx', 'fsdp'))
- grad_gain_ffn: float32 [1024], P(('ctx', 'fsdp'))
- grad_ridge: float32 [1024], P(('ctx', 'fsdp'))
The draws below stay inside these ranges and needn't reach their ends.
Inputs may be any that keep to these rules, and one draw needn't show every extreme that they name: forget gates lie strictly between 0 and 1.
All inputs are finite; a program needn't handle non-finite values.
Results may differ from the reference program's by a relative error of at most 0.024.
Values may be sent and summed in bfloat16 or wider, within the bound.
No kernel may reach another device: no remote copies, remote signals or barrier semaphores. Data moves between devices by JAX's collectives and lax.ppermute only.
A program may use at most 576 MiB of HBM per device.

```python
import math
import jax
import jax.numpy as jnp
from jax import lax

D = 1024
HEADS = 8
FF = 2816
KW = 4
ITERS = 8
TOK_DEV = 128
HEAD_DIM = 128
SEQS = 2
SEQUENCE_LENGTH = 2048


def draw_forget(key, part):
    key = jax.random.fold_in(key, 7)
    parallel_flows = jax.random.split(key, 6)
    lattice_shape = (SEQS, SEQUENCE_LENGTH, HEADS)
    strong_share = 0.5
    chosen = jax.random.uniform(parallel_flows[0], (SEQS, 1, HEADS)) < strong_share
    strong = jnp.exp(jax.random.uniform(parallel_flows[1], (SEQS, 1, HEADS), minval=jnp.log(1.0 / 50.0), maxval=jnp.log(1.0 / 30.0)))
    weak = jnp.exp(jax.random.uniform(parallel_flows[2], (SEQS, 1, HEADS), minval=jnp.log(0.1), maxval=jnp.log(0.5))) / SEQUENCE_LENGTH
    baseline_rate = jnp.where(chosen, strong, weak)
    coarse_estimate = jax.random.uniform(parallel_flows[3], lattice_shape, minval=0.5, maxval=2.0)
    sudden_spike = jax.random.uniform(parallel_flows[4], lattice_shape) < 3.0 / SEQUENCE_LENGTH
    discarded_tokens = jax.random.uniform(parallel_flows[5], lattice_shape, minval=0.6, maxval=0.8)
    gate_logarithm = -baseline_rate * coarse_estimate + jnp.where(sudden_spike, jnp.log(discarded_tokens), 0.0)
    return jnp.exp(gate_logarithm).astype(jnp.float32)


def block_scale(key, dims, shards, smallest, top_value):
    def one(dim, parts):
        draws = jax.random.uniform(jax.random.fold_in(jax.random.fold_in(key, 6), dim), (parts,), jnp.float32, smallest / len(shards), top_value / len(shards))
        return jnp.repeat(jnp.exp(draws), dims[dim] // parts).reshape((-1,) + (1,) * (len(dims) - dim - 1))

    factor_of = one(*shards[0])
    for cut in shards[1:]:
        factor_of = factor_of * one(*cut)
    return factor_of


def noise(key, dims, scale, limit, cuts=(), dtype=jnp.bfloat16):
    result = scale * jax.random.normal(key, dims, jnp.float32)
    if cuts:
        result = result * block_scale(key, dims, cuts, -0.22, 0.18)
    return jnp.clip(result, -limit, limit).astype(dtype)


def setup_inputs(seed: int = 0) -> dict:
    splits = jax.random.split(jax.random.key(seed), 13)
    return {
        "inputs": noise(splits[0], (SEQS, SEQUENCE_LENGTH, D), 1.0, 6.0, ((0, 2), (1, 16)), jnp.float32),
        "qkv_weight": noise(splits[1], (D, 3 * D), D ** -0.5, 0.1875, ((0, 2),)),
        "gate_weight": noise(splits[2], (D, D), D ** -0.5, 0.1875, ((0, 2),)),
        "out_weight": noise(splits[3], (D, D), (D // 16) ** -0.5, 0.75, ((0, 2),)),
        "up_weight": noise(splits[4], (D, 2 * FF), D ** -0.5, 0.1875, ((0, 2),)),
        "down_weight": noise(splits[5], (FF, D), FF ** -0.5, 0.109375, ((0, 2),)),
        "conv_taps": noise(splits[6], (KW, 3 * D), 0.5, 3.0, ((1, 2),)),
        "gain_attn": jnp.clip(1.0 + 0.1 * jax.random.normal(splits[7], (D,), jnp.float32), 0.5, 1.5).astype(jnp.bfloat16),
        "gain_ffn": jnp.clip(1.0 + 0.1 * jax.random.normal(splits[8], (D,), jnp.float32), 0.5, 1.5).astype(jnp.bfloat16),
        "ridge_terms": jnp.clip(jnp.exp(math.log(1.0) - 2.306499 * jax.random.uniform(splits[9], (D,), jnp.float32) ** block_scale(splits[9], (D,), ((0, 2),), -0.2, 0.2)), 0.099609375, 1.0).astype(jnp.bfloat16),
        "forget": draw_forget(jax.random.fold_in(splits[12], 71), 0),
        "cotangent": noise(splits[11], (SEQS, SEQUENCE_LENGTH, D), 1.0, 6.0, ((0, 2), (1, 16)), jnp.float32),
    }


@jax.custom_vjp
def low(v):
    return lax.optimization_barrier(v.astype(jnp.bfloat16)).astype(jnp.float32)

@jax.custom_vjp
def low_back(v):
    return v

def low_keep(v):
    return (low(v), None)

def low_pass(kept, grad):
    return (grad,)

def back_keep(v):
    return (v, None)

def back_low(kept, grad):
    return (low(grad),)
low.defvjp(low_keep, low_pass)
low_back.defvjp(back_keep, back_low)
highest = lax.Precision.HIGHEST

def matmul(left, right):
    return jnp.matmul(left, right, precision=highest)

def rms_scale(values, gain):
    return values * lax.rsqrt(lax.optimization_barrier(jnp.mean(values * values, axis=-1, keepdims=True)) + 1e-05) * gain

def unit_rows(values):
    return values * lax.rsqrt(lax.optimization_barrier(jnp.sum(values * values, axis=-1, keepdims=True)) + 1e-06)

def decay_tables(gate_logarithm, strength):
    cumulative = jnp.cumsum(gate_logarithm, axis=-1)
    length_here = gate_logarithm.shape[-1]
    causal = jnp.arange(length_here)[:, None] >= jnp.arange(length_here)[None, :]
    spread = cumulative[..., :, None] - cumulative[..., None, :]
    within = jnp.where(causal, jnp.exp(jnp.where(causal, spread, 0.0)), 0.0) * strength[..., None, :]
    start_decay = jnp.exp(cumulative)
    ending = jnp.exp(cumulative[..., -1:] - cumulative) * strength
    return (within, start_decay, ending, jnp.exp(cumulative[..., -1]))

def block_states(key_rows, value_rows, ending):
    own_key = jnp.einsum('hsi,hsj->hij', key_rows * ending[..., None], key_rows, precision=highest)
    own_value = jnp.einsum('hsi,hsj->hij', value_rows * ending[..., None], key_rows, precision=highest)
    return (own_key, own_value)

def solve_heads(queries, key_rows, value_rows, state_key, state_value, ridge_heads, within, start_decay):

    def operator_apply(direction):
        from_state = start_decay[..., None] * jnp.einsum('htj,hij->hti', direction, state_key, precision=highest)
        scores = jnp.einsum('htd,hsd->hts', direction, key_rows, precision=highest) * within
        local_part = jnp.einsum('hts,hsd->htd', scores, key_rows, precision=highest)
        return from_state + local_part + direction * ridge_heads[:, None, :]
    solution = jnp.zeros_like(queries)
    residual = queries
    direction = queries
    norm_now = lax.optimization_barrier(jnp.sum(residual * residual, axis=-1, keepdims=True))
    for iteration in range(ITERS):
        image_rows = operator_apply(direction)
        step_size = norm_now / lax.optimization_barrier(jnp.sum(direction * image_rows, axis=-1, keepdims=True))
        solution = solution + step_size * direction
        residual = residual - step_size * image_rows
        norm_next = lax.optimization_barrier(jnp.sum(residual * residual, axis=-1, keepdims=True))
        direction = residual + norm_next / norm_now * direction
        norm_now = norm_next
    from_state = start_decay[..., None] * jnp.einsum('htj,hij->hti', solution, state_value, precision=highest)
    scores = jnp.einsum('htd,hsd->hts', solution, key_rows, precision=highest) * within
    return from_state + jnp.einsum('hts,hsd->htd', scores, value_rows, precision=highest)

def forward(inputs, qkv_weight, gate_weight, out_weight, up_weight, down_weight, conv_taps, gain_attn, gain_ffn, ridge_terms, forget):
    normed = low(rms_scale(inputs, gain_attn))
    projected = low_back(matmul(normed, qkv_weight))
    padded = jnp.pad(projected, ((0, 0), (KW - 1, 0), (0, 0)))
    conv_sum = conv_taps[0] * padded[:, 0:SEQUENCE_LENGTH]
    for offset in range(1, KW):
        conv_sum = conv_sum + conv_taps[offset] * padded[:, offset:offset + SEQUENCE_LENGTH]
    activated = jax.nn.silu(conv_sum)
    queries = unit_rows(activated[..., :D].reshape(SEQS, SEQUENCE_LENGTH, HEADS, HEAD_DIM))
    key_rows = unit_rows(activated[..., D:2 * D].reshape(SEQS, SEQUENCE_LENGTH, HEADS, HEAD_DIM))
    value_rows = activated[..., 2 * D:].reshape(SEQS, SEQUENCE_LENGTH, HEADS, HEAD_DIM)
    blocks = SEQUENCE_LENGTH // TOK_DEV

    def to_blocks(array):
        return array.reshape(SEQS, blocks, TOK_DEV, HEADS, HEAD_DIM).transpose(1, 0, 3, 2, 4)
    gate_blocks = jnp.log(forget).reshape(SEQS, blocks, TOK_DEV, HEADS).transpose(1, 0, 3, 2)
    strength_blocks = (1.0 - forget).reshape(SEQS, blocks, TOK_DEV, HEADS).transpose(1, 0, 3, 2)
    ridge_heads = ridge_terms.reshape(HEADS, HEAD_DIM)

    def one_sequence(q_block, k_block, v_block, log_block, strength_block, key_state, value_state):
        within, start_decay, ending, decay_all = decay_tables(log_block, strength_block)
        attended = solve_heads(q_block, k_block, v_block, key_state, value_state, ridge_heads, within, start_decay)
        own_key, own_value = block_states(k_block, v_block, ending)
        next_key = decay_all[:, None, None] * key_state + own_key
        next_value = decay_all[:, None, None] * value_state + own_value
        return (attended, next_key, next_value)

    def group_step(carry, pieces):
        attended, next_key, next_value = jax.vmap(one_sequence)(pieces[0], pieces[1], pieces[2], pieces[3], pieces[4], carry[0], carry[1])
        return ((next_key, next_value), attended)
    initial = (jnp.zeros((SEQS, HEADS, HEAD_DIM, HEAD_DIM), jnp.float32), jnp.zeros((SEQS, HEADS, HEAD_DIM, HEAD_DIM), jnp.float32))
    carried, outputs = lax.scan(jax.checkpoint(group_step), initial, (to_blocks(queries), to_blocks(key_rows), to_blocks(value_rows), gate_blocks, strength_blocks))
    attended = outputs.transpose(1, 0, 3, 2, 4).reshape(SEQS, SEQUENCE_LENGTH, D)
    gate_logit = low_back(matmul(normed, gate_weight))
    gated_mix = low(attended * jax.nn.sigmoid(gate_logit))
    hidden = inputs + low_back(matmul(gated_mix, out_weight))
    normed_ffn = low(rms_scale(hidden, gain_ffn))
    gate_up = low_back(matmul(normed_ffn, up_weight))
    inner = low(jax.nn.silu(gate_up[..., :FF]) * gate_up[..., FF:])
    return hidden + low_back(matmul(inner, down_weight))

def reference(inputs, qkv_weight, gate_weight, out_weight, up_weight, down_weight, conv_taps, gain_attn, gain_ffn, ridge_terms, forget, cotangent):
    params = [array.astype(jnp.float32) for array in (qkv_weight, gate_weight, out_weight, up_weight, down_weight, conv_taps, gain_attn, gain_ffn, ridge_terms)]

    def wrapped(source, *weights):
        return forward(source, *weights, forget)
    output, pullback = jax.vjp(wrapped, inputs, *params)
    gradients = pullback(cotangent)
    return (output, gradients[0], gradients[1], gradients[2], gradients[3], gradients[4], gradients[5], gradients[6], gradients[7], gradients[8], gradients[9])
```

```python
import functools
import jax
import jax.numpy as jnp
from jax import lax
from jax.experimental import pallas as pl
from jax.experimental.pallas import tpu as pltpu
from jax.sharding import PartitionSpec as P

D = 1024
HEADS = 8
FF = 2816
KW = 4
ITERS = 8
HEAD_DIM = 128
GROUP = 4

f32 = jnp.float32
bf16 = jnp.bfloat16
VMEM_LIMIT = 56 * 1024 * 1024


def nn(a, b):
    return lax.dot_general(a, b, (((1,), (0,)), ((), ())), preferred_element_type=f32)


def nt(a, b):
    return lax.dot_general(a, b, (((1,), (1,)), ((), ())), preferred_element_type=f32)


def tn(a, b):
    return lax.dot_general(a, b, (((0,), (0,)), ((), ())), preferred_element_type=f32)


def column(row, like):
    return jnp.broadcast_to(row, like).T


def decay_mask(c, b, tokens):
    shape = (tokens, tokens)
    late = lax.broadcasted_iota(jnp.int32, shape, 1) >= lax.broadcasted_iota(jnp.int32, shape, 0)
    spread = jnp.broadcast_to(c, shape) - column(c, shape)
    return jnp.where(late, jnp.exp(jnp.where(late, spread, 0.0)), 0.0) * column(b, shape)


def conv_parts(proj, halo, taps):
    padded = jnp.concatenate([halo, proj], axis=0)
    rows = proj.shape[0]
    shifted = [padded[8 - KW + 1 + j : 8 - KW + 1 + j + rows] for j in range(KW)]
    total = taps[0:1] * shifted[0]
    for j in range(1, KW):
        total = total + taps[j : j + 1] * shifted[j]
    return total, shifted


def features_kernel(pq, pk, pv, hq, hk, hv, tq, tk, tv, c_ref, b_ref, q_out, k_out, v_out, st_out):
    head = pl.program_id(0)
    tokens = pq.shape[0]
    shape = (tokens, HEAD_DIM)

    def activated(p, h, t):
        total, _ = conv_parts(p[...], h[...], t[...])
        return total * jax.nn.sigmoid(total)

    def unit(a):
        return a * lax.rsqrt(jnp.sum(a * a, axis=-1, keepdims=True) + 1e-06)

    c = c_ref[pl.ds(head, 1), :]
    b = b_ref[pl.ds(head, 1), :]
    ending = column(jnp.exp(c[:, tokens - 1 :] - c) * b, (HEAD_DIM, tokens))
    q = unit(activated(pq, hq, tq))
    k = unit(activated(pk, hk, tk))
    v = activated(pv, hv, tv)
    k_low = k.astype(bf16)
    q_out[0] = q.T
    k_out[0] = k_low
    v_out[0] = v.astype(bf16)
    st_out[0, 0] = tn((k * ending).astype(bf16), k_low).astype(bf16)
    st_out[0, 1] = tn((v * ending).astype(bf16), k_low).astype(bf16)


def thirds(rows):
    return [pl.BlockSpec((rows, HEAD_DIM), lambda h, i=i: (0, i * HEADS + h)) for i in range(3)]


def whole(*shape):
    return pl.BlockSpec(shape, lambda h: (0,) * len(shape))


def per_head(*shape):
    return pl.BlockSpec((1,) + shape, lambda h: (h,) + (0,) * len(shape))


def features(proj, halo, taps, c, b):
    tokens = proj.shape[0]
    square = (HEADS, HEAD_DIM, tokens)
    return pl.pallas_call(
        features_kernel,
        grid=(HEADS,),
        in_specs=thirds(tokens) + thirds(8) + thirds(KW) + [whole(HEADS, tokens)] * 2,
        out_specs=[
            per_head(HEAD_DIM, tokens),
            per_head(tokens, HEAD_DIM),
            per_head(tokens, HEAD_DIM),
            per_head(2, HEAD_DIM, HEAD_DIM),
        ],
        out_shape=[
            jax.ShapeDtypeStruct(square, f32),
            jax.ShapeDtypeStruct((HEADS, tokens, HEAD_DIM), bf16),
            jax.ShapeDtypeStruct((HEADS, tokens, HEAD_DIM), bf16),
            jax.ShapeDtypeStruct((HEADS, 2, HEAD_DIM, HEAD_DIM), bf16),
        ],
        cost_estimate=pl.CostEstimate(flops=70_000_000, bytes_accessed=4_000_000, transcendentals=400_000),
        name="features",
    )(proj, proj, proj, halo, halo, halo, taps, taps, taps, c, b)


def solve_kernel(
    q_ref, k_ref, v_ref, st_ref, c_ref, b_ref, ridge_ref,
    att_ref, x_out, p_out, m_out, scal_out,
    left, kt, mask, decay, ridge, x_s, r_s, p_s,
):
    group = pl.program_id(0)
    tokens = q_ref.shape[2]
    shape = (HEAD_DIM, tokens)
    first = []
    for h in range(GROUP):
        c = c_ref[pl.ds(group * GROUP + h, 1), :]
        b = b_ref[pl.ds(group * GROUP + h, 1), :]
        left[h, :HEAD_DIM] = st_ref[h, 0]
        left[h, HEAD_DIM:] = k_ref[h]
        kt[h] = k_ref[h].T
        mask[h] = decay_mask(c, b, tokens)
        decay[h] = jnp.broadcast_to(jnp.exp(c), (8, tokens))
        ridge[h] = column(ridge_ref[pl.ds(group * GROUP + h, 1), :], (tokens, HEAD_DIM))
        q = q_ref[h]
        x_s[h] = jnp.zeros(shape, f32)
        r_s[h] = q
        p_s[h] = q
        first.append(jnp.sum(q * q, axis=0, keepdims=True))

    def step(i, norms):
        after = []
        for h in range(GROUP):
            p = p_s[h]
            p_low = p.astype(bf16)
            both = nn(left[h], p_low)
            scores = (both[HEAD_DIM:] * mask[h]).astype(bf16)
            image = decay[h, 0:1] * both[:HEAD_DIM] + nn(kt[h], scores) + ridge[h] * p
            dot = jnp.sum(p * image, axis=0, keepdims=True)
            size = norms[h] / dot
            p_out[i, h] = p
            m_out[i, h] = image
            scal_out[h, pl.ds(i, 1)] = norms[h]
            scal_out[h, pl.ds(ITERS + i, 1)] = dot
            x_s[h] = x_s[h] + size * p
            r = r_s[h] - size * image
            r_s[h] = r
            norm = jnp.sum(r * r, axis=0, keepdims=True)
            p_s[h] = r + (norm / norms[h]) * p
            after.append(norm)
        return tuple(after)

    lax.fori_loop(0, ITERS, step, tuple(first))
    for h in range(GROUP):
        x_low = x_s[h].astype(bf16)
        x_out[h] = x_low
        scores = (nn(k_ref[h], x_low) * mask[h]).astype(bf16)
        out = decay[h, 0:1] * nn(st_ref[h, 1], x_low) + tn(v_ref[h], scores)
        att_ref[:, h * HEAD_DIM : (h + 1) * HEAD_DIM] = out.T


def grouped(*shape):
    return pl.BlockSpec((GROUP,) + shape, lambda g: (g,) + (0,) * len(shape))


def solve(q, k, v, states, c, b, ridge):
    tokens = q.shape[2]
    steps = pl.BlockSpec((ITERS, GROUP, HEAD_DIM, tokens), lambda g: (0, g, 0, 0))
    square = pltpu.VMEM((GROUP, HEAD_DIM, tokens), f32)
    return pl.pallas_call(
        solve_kernel,
        grid=(HEADS // GROUP,),
        in_specs=[
            grouped(HEAD_DIM, tokens),
            grouped(tokens, HEAD_DIM),
            grouped(tokens, HEAD_DIM),
            grouped(2, HEAD_DIM, HEAD_DIM),
            whole(HEADS, tokens),
            whole(HEADS, tokens),
            whole(HEADS, HEAD_DIM),
        ],
        out_specs=[
            pl.BlockSpec((tokens, GROUP * HEAD_DIM), lambda g: (0, g)),
            grouped(HEAD_DIM, tokens),
            steps,
            steps,
            grouped(2 * ITERS, tokens),
        ],
        out_shape=[
            jax.ShapeDtypeStruct((tokens, D), f32),
            jax.ShapeDtypeStruct((HEADS, HEAD_DIM, tokens), bf16),
            jax.ShapeDtypeStruct((ITERS, HEADS, HEAD_DIM, tokens), f32),
            jax.ShapeDtypeStruct((ITERS, HEADS, HEAD_DIM, tokens), f32),
            jax.ShapeDtypeStruct((HEADS, 2 * ITERS, tokens), f32),
        ],
        scratch_shapes=[
            pltpu.VMEM((GROUP, HEAD_DIM + tokens, HEAD_DIM), bf16),
            pltpu.VMEM((GROUP, HEAD_DIM, tokens), bf16),
            pltpu.VMEM((GROUP, tokens, tokens), f32),
            pltpu.VMEM((GROUP, 8, tokens), f32),
            square, square, square, square,
        ],
        compiler_params=pltpu.CompilerParams(vmem_limit_bytes=VMEM_LIMIT),
        cost_estimate=pl.CostEstimate(flops=900_000_000, bytes_accessed=12_000_000, transcendentals=200_000),
        name="solve",
    )(q, k, v, states, c, b, ridge)


def adjoint_kernel(
    ga_ref, k_ref, v_ref, st_ref, c_ref, b_ref, ridge_ref, x_ref, p_ref, m_ref, scal_ref,
    dq_ref, dk_ref, dv_ref, dst_ref, dridge_ref,
    left, kt, mask, decay, ridge, gx_s, gr_s, gp_s, acc_s, wide, rows, scaled,
):
    group = pl.program_id(0)
    tokens = k_ref.shape[1]
    steps = ITERS * tokens
    first = []
    for h in range(GROUP):
        c = c_ref[pl.ds(group * GROUP + h, 1), :]
        b = b_ref[pl.ds(group * GROUP + h, 1), :]
        k = k_ref[h]
        left[h, :HEAD_DIM] = st_ref[h, 0]
        left[h, HEAD_DIM:] = k
        kt[h] = k.T
        mask[h] = decay_mask(c, b, tokens)
        decay[h] = jnp.broadcast_to(jnp.exp(c), (8, tokens))
        ridge[h] = column(ridge_ref[pl.ds(group * GROUP + h, 1), :], (tokens, HEAD_DIM))
        e = decay[h, 0:1]
        ga = ga_ref[:, h * HEAD_DIM : (h + 1) * HEAD_DIM].T
        ga_low = ga.astype(bf16)
        x = x_ref[h]
        scores = (nn(k, x) * mask[h]).astype(bf16)
        dscores = (nn(v_ref[h], ga_low) * mask[h]).astype(bf16)
        gx = e * tn(st_ref[h, 1], ga_low) + nn(kt[h], dscores)
        gx_s[h] = gx
        dv_ref[h] = nt(scores, ga_low)
        dst_ref[h, 1] = nt((e * ga).astype(bf16), x).astype(bf16)
        wide[h, :, 2 * steps :] = dscores
        rows[h, :, 2 * steps :] = x
        for i in range(ITERS):
            low = p_ref[i, h].astype(bf16)
            rows[h, :, steps + i * tokens : steps + (i + 1) * tokens] = low
            wide[h, :, i * tokens : (i + 1) * tokens] = (nn(k, low) * mask[h]).astype(bf16)
        i = ITERS - 1
        p, m = p_ref[i, h], m_ref[i, h]
        norm = scal_ref[h, i : i + 1]
        dot = scal_ref[h, ITERS + i : ITERS + i + 1]
        size = norm / dot
        gsize = jnp.sum(gx * p, axis=0, keepdims=True)
        gdot = -gsize * size / dot
        gm = gdot * p
        low = gm.astype(bf16)
        gp_s[h] = size * gx + 2.0 * gdot * m
        gr_s[h] = jnp.zeros_like(gx)
        acc_s[h] = gm * p
        rows[h, :, i * tokens : (i + 1) * tokens] = low
        wide[h, :, steps + i * tokens : steps + (i + 1) * tokens] = (nn(k, low) * mask[h]).astype(bf16)
        scaled[h, :, i * tokens : (i + 1) * tokens] = (e * gm).astype(bf16)
        first.append(gsize / dot)

    def step(back, gnorms):
        i = ITERS - 2 - back
        at = pl.multiple_of(i * tokens, tokens)
        after = []
        for h in range(GROUP):
            e = decay[h, 0:1]
            p, m = p_ref[i, h], m_ref[i, h]
            norm = scal_ref[h, pl.ds(i, 1)]
            norm_next = scal_ref[h, pl.ds(i + 1, 1)]
            dot = scal_ref[h, pl.ds(ITERS + i, 1)]
            size = norm / dot
            ratio = norm_next / norm
            gp = gp_s[h]
            gx = gx_s[h]
            gratio = jnp.sum(gp * p, axis=0, keepdims=True)
            gnext = gnorms[h] + gratio / norm
            residual = p_ref[i + 1, h] - ratio * p
            gr = gr_s[h] + gp + 2.0 * gnext * residual
            gsize = jnp.sum(gx * p - gr * m, axis=0, keepdims=True)
            gdot = -gsize * size / dot
            gm = gdot * p - size * gr
            low = gm.astype(bf16)
            both = nn(left[h], low)
            dscores = (both[HEAD_DIM:] * mask[h]).astype(bf16)
            image = e * both[:HEAD_DIM] + nn(kt[h], dscores) + ridge[h] * gm
            gp_s[h] = ratio * gp + size * gx + gdot * m + image
            gr_s[h] = gr
            acc_s[h] = acc_s[h] + gm * p
            rows[h, :, pl.ds(at, tokens)] = low
            wide[h, :, pl.ds(steps + at, tokens)] = dscores
            scaled[h, :, pl.ds(at, tokens)] = (e * gm).astype(bf16)
            after.append(gsize / dot - gratio * ratio / norm)
        return tuple(after)

    gnorms = lax.fori_loop(0, ITERS - 1, step, tuple(first))
    for h in range(GROUP):
        dq_ref[h] = gr_s[h] + gp_s[h] + 2.0 * gnorms[h] * p_ref[0, h]
        dk_ref[h] = nt(wide[h], rows[h])
        dst_ref[h, 0] = nt(scaled[h], rows[h, :, steps : 2 * steps]).astype(bf16)
        dridge_ref[h] = jnp.sum(acc_s[h].T, axis=0, keepdims=True)


def adjoint(ga, k, v, states, c, b, ridge, x, p_all, m_all, scal):
    tokens = k.shape[1]
    steps = pl.BlockSpec((ITERS, GROUP, HEAD_DIM, tokens), lambda g: (0, g, 0, 0))
    square = pltpu.VMEM((GROUP, HEAD_DIM, tokens), f32)
    return pl.pallas_call(
        adjoint_kernel,
        grid=(HEADS // GROUP,),
        in_specs=[
            pl.BlockSpec((tokens, GROUP * HEAD_DIM), lambda g: (0, g)),
            grouped(tokens, HEAD_DIM),
            grouped(tokens, HEAD_DIM),
            grouped(2, HEAD_DIM, HEAD_DIM),
            whole(HEADS, tokens),
            whole(HEADS, tokens),
            whole(HEADS, HEAD_DIM),
            grouped(HEAD_DIM, tokens),
            steps,
            steps,
            grouped(2 * ITERS, tokens),
        ],
        out_specs=[
            grouped(HEAD_DIM, tokens),
            grouped(tokens, HEAD_DIM),
            grouped(tokens, HEAD_DIM),
            grouped(2, HEAD_DIM, HEAD_DIM),
            grouped(1, HEAD_DIM),
        ],
        out_shape=[
            jax.ShapeDtypeStruct((HEADS, HEAD_DIM, tokens), f32),
            jax.ShapeDtypeStruct((HEADS, tokens, HEAD_DIM), f32),
            jax.ShapeDtypeStruct((HEADS, tokens, HEAD_DIM), f32),
            jax.ShapeDtypeStruct((HEADS, 2, HEAD_DIM, HEAD_DIM), bf16),
            jax.ShapeDtypeStruct((HEADS, 1, HEAD_DIM), f32),
        ],
        scratch_shapes=[
            pltpu.VMEM((GROUP, HEAD_DIM + tokens, HEAD_DIM), bf16),
            pltpu.VMEM((GROUP, HEAD_DIM, tokens), bf16),
            pltpu.VMEM((GROUP, tokens, tokens), f32),
            pltpu.VMEM((GROUP, 8, tokens), f32),
            square, square, square, square, square,
            pltpu.VMEM((GROUP, tokens, (2 * ITERS + 1) * tokens), bf16),
            pltpu.VMEM((GROUP, HEAD_DIM, (2 * ITERS + 1) * tokens), bf16),
            pltpu.VMEM((GROUP, HEAD_DIM, ITERS * tokens), bf16),
        ],
        compiler_params=pltpu.CompilerParams(vmem_limit_bytes=VMEM_LIMIT),
        cost_estimate=pl.CostEstimate(flops=1_800_000_000, bytes_accessed=12_000_000, transcendentals=200_000),
        name="adjoint",
    )(ga, k, v, states, c, b, ridge, x, p_all, m_all, scal)


def features_back_kernel(
    pq, pk, pv, hq, hk, hv, tq, tk, tv, c_ref, b_ref, dq_ref, dk_ref, dv_ref, dst_ref,
    gq, gk, gv, bq, bk, bv, dtq, dtk, dtv,
):
    head = pl.program_id(0)
    tokens = pq.shape[0]
    c = c_ref[pl.ds(head, 1), :]
    b = b_ref[pl.ds(head, 1), :]
    ending = column(jnp.exp(c[:, tokens - 1 :] - c) * b, (HEAD_DIM, tokens))

    def forward(p, h, t):
        total, shifted = conv_parts(p[...], h[...], t[...])
        sig = jax.nn.sigmoid(total)
        act = total * sig
        return shifted, sig * (1.0 + total * (1.0 - sig)), act

    def unit_back(act, grad):
        scale = lax.rsqrt(jnp.sum(act * act, axis=-1, keepdims=True) + 1e-06)
        unit = act * scale
        return scale * (grad - unit * jnp.sum(unit * grad, axis=-1, keepdims=True))

    def conv_back(dconv, shifted, t, g, before, dt):
        taps = t[...]
        padded = jnp.concatenate([dconv, jnp.zeros((8, HEAD_DIM), f32)], axis=0)
        total = taps[KW - 1 : KW] * dconv
        for j in range(KW - 1):
            total = total + taps[j : j + 1] * padded[KW - 1 - j : KW - 1 - j + tokens]
        g[...] = total
        ahead = jnp.concatenate([jnp.zeros((8, HEAD_DIM), f32), dconv[:8]], axis=0)
        lead = taps[0:1] * ahead[8:16]
        for j in range(1, KW - 1):
            lead = lead + taps[j : j + 1] * ahead[8 - j : 16 - j]
        before[...] = lead
        dt[...] = jnp.concatenate(
            [jnp.sum(dconv * shifted[j], axis=0, keepdims=True) for j in range(KW)], axis=0
        )

    sh_q, slope_q, act_q = forward(pq, hq, tq)
    sh_k, slope_k, act_k = forward(pk, hk, tk)
    sh_v, slope_v, act_v = forward(pv, hv, tv)
    k = act_k * lax.rsqrt(jnp.sum(act_k * act_k, axis=-1, keepdims=True) + 1e-06)
    k_low = k.astype(bf16)
    v_low = act_v.astype(bf16)
    both = dst_ref[0, 0].astype(f32)
    both = (both + both.T).astype(bf16)
    rv = dst_ref[0, 1].astype(bf16)
    dk = dk_ref[0] + ending * (nn(k_low, both) + nn(v_low, rv))
    dv = dv_ref[0] + ending * nt(k_low, rv)
    conv_back(unit_back(act_q, dq_ref[0].T) * slope_q, sh_q, tq, gq, bq, dtq)
    conv_back(unit_back(act_k, dk) * slope_k, sh_k, tk, gk, bk, dtk)
    conv_back(dv * slope_v, sh_v, tv, gv, bv, dtv)


def features_back(proj, halo, taps, c, b, dq, dk, dv, dst):
    tokens = proj.shape[0]

    def third(rows):
        return pl.BlockSpec((rows, HEAD_DIM), lambda h: (0, h))

    return pl.pallas_call(
        features_back_kernel,
        grid=(HEADS,),
        in_specs=thirds(tokens) + thirds(8) + thirds(KW) + [whole(HEADS, tokens)] * 2
        + [per_head(HEAD_DIM, tokens), per_head(tokens, HEAD_DIM), per_head(tokens, HEAD_DIM), per_head(2, HEAD_DIM, HEAD_DIM)],
        out_specs=[third(tokens)] * 3 + [third(8)] * 3 + [third(KW)] * 3,
        out_shape=[jax.ShapeDtypeStruct((tokens, D), f32)] * 3
        + [jax.ShapeDtypeStruct((8, D), f32)] * 3
        + [jax.ShapeDtypeStruct((KW, D), f32)] * 3,
        cost_estimate=pl.CostEstimate(flops=100_000_000, bytes_accessed=8_000_000, transcendentals=400_000),
        name="features_back",
    )(proj, proj, proj, halo, halo, halo, taps, taps, taps, c, b, dq, dk, dv, dst)


def neighbour(axis, bit):
    return [(i, i ^ bit) for i in range(lax.axis_size(axis))]


def partner(x, axis, bit=1):
    return lax.ppermute(x, axis, neighbour(axis, bit))


def shifted(x, axis, by):
    peers = lax.axis_size(axis)
    return lax.ppermute(x, axis, [(i, i + by) for i in range(peers) if 0 <= i + by < peers])


def pick(x, index, axis=0):
    return lax.dynamic_index_in_dim(x, index, axis, keepdims=False)


def entering(own, logs, axis, reverse):
    peers = lax.axis_size(axis)
    here = lax.axis_index(axis)
    if reverse:
        here = peers - 1 - here
        logs = logs[::-1]
    at = jnp.arange(peers)
    heads = own.shape[0]

    def total_decay(start, stop):
        inside = (at >= start) & (at < stop)
        return jnp.exp(jnp.sum(jnp.where(inside[:, None], logs, 0.0), axis=0))

    def times(coefficients, first, count):
        part = lax.dynamic_slice_in_dim(coefficients, first, count, 0)
        return part[:, None, None, None]

    levels = peers.bit_length() - 1
    halving = min(2, levels)
    now = own
    first, count = 0, heads
    saved = []
    for level in range(halving):
        size = 1 << level
        bit = (here >> level) & 1
        base = (here >> (level + 1)) << (level + 1)
        halves = now.reshape((2, count // 2) + now.shape[1:])
        keep = pick(halves, bit)
        received = partner(pick(halves, 1 - bit), axis, size)
        count = count // 2
        first = first + bit * count
        low = jnp.where(bit == 1, received, keep).astype(f32)
        high = jnp.where(bit == 1, keep, received).astype(f32)
        now = (times(total_decay(base + size, base + 2 * size), first, count) * low + high).astype(bf16)
        saved.append((bit, low, times(total_decay(base, base + size), first, count)))
    unit = (here >> halving) << halving
    before = jnp.zeros(now.shape, f32)
    for level in range(halving, levels):
        size = 1 << level
        bit = (here >> level) & 1
        base = (here >> (level + 1)) << (level + 1)
        start = (here >> level) << level
        received = partner(now, axis, size).astype(f32)
        mine = now.astype(f32)
        before = jnp.where(bit == 1, times(total_decay(start, unit), first, count) * received + before, before)
        low = jnp.where(bit == 1, received, mine)
        high = jnp.where(bit == 1, mine, received)
        now = (times(total_decay(base + size, base + 2 * size), first, count) * low + high).astype(bf16)
    for level in reversed(range(halving)):
        bit, low, decay = saved[level]
        after = decay * before + low
        mine = jnp.where(bit == 1, after, before).astype(bf16)
        other = jnp.where(bit == 1, before, after).astype(bf16)
        received = partner(other, axis, 1 << level)
        before = jnp.concatenate(
            [jnp.where(bit == 1, received, mine), jnp.where(bit == 1, mine, received)], axis=0
        ).astype(f32)
    return before.astype(bf16)


def rms_scale(values, gain):
    return values * lax.rsqrt(jnp.mean(values * values, axis=-1, keepdims=True) + 1e-05) * gain


def right_product(left, right):
    return nt(left, right)


def local(
    inputs,
    qkv_weight,
    gate_weight,
    out_weight,
    up_weight,
    down_weight,
    conv_taps,
    gain_attn,
    gain_ffn,
    ridge_terms,
    forget,
    cotangent,
):
    tokens = inputs[0]
    rows = tokens.shape[0]
    y = lax.axis_index("fsdp")
    peers = lax.axis_size("ctx")
    owners = peers * 2
    small = jnp.concatenate(
        [conv_taps.reshape(-1), gain_attn, gain_ffn, ridge_terms]
    )
    both = lax.all_gather(small, "fsdp", axis=0)
    split = KW * 3 * D // 2
    taps = both[:, :split].reshape(2, KW, 3 * D // 2).transpose(1, 0, 2).reshape(KW, 3 * D).astype(f32)
    rest = both[:, split:].reshape(2, 3, D // 2).transpose(1, 0, 2).reshape(3, D).astype(f32)
    gain_first, gain_second = rest[0], rest[1]
    ridge = rest[2].reshape(HEADS, HEAD_DIM)
    out_full = lax.all_gather(out_weight, "fsdp", axis=0, tiled=True)
    up_full = lax.all_gather(up_weight, "fsdp", axis=0, tiled=True)
    down_full = lax.all_gather(down_weight, "fsdp", axis=0, tiled=True)
    cumulative = jnp.cumsum(jnp.log(forget[0]).T, axis=-1)
    strength = (1.0 - forget[0]).T
    logs = lax.all_gather(cumulative[:, -1], "ctx", axis=0)

    normed_low = rms_scale(tokens, gain_first).astype(bf16)
    halves = normed_low.reshape(rows, 2, D // 2)
    mine = pick(halves, y, 1)
    theirs = partner(pick(halves, 1 - y, 1), "fsdp")
    lent = nn(theirs, qkv_weight).astype(bf16)
    projected = nn(mine, qkv_weight) + partner(lent, "fsdp").astype(f32)
    lent = nn(theirs, gate_weight).astype(bf16)
    gate_logit = nn(mine, gate_weight) + partner(lent, "fsdp").astype(f32)
    tail = shifted(projected[rows - (KW - 1) :].astype(bf16), "ctx", 1).astype(f32)
    halo = jnp.concatenate([jnp.zeros((8 - KW + 1, 3 * D), f32), tail], axis=0)
    queries, keys, values, own = features(projected, halo, taps, cumulative, strength)
    states = entering(own, logs, "ctx", False)
    attended, x, p_all, m_all, scal = solve(queries, keys, values, states, cumulative, strength, ridge)

    gate_sig = jax.nn.sigmoid(gate_logit)
    gated_mix = (attended * gate_sig).astype(bf16)
    hidden = tokens + nn(gated_mix, out_full)
    normed_ffn, second_pull = jax.vjp(rms_scale, hidden, gain_second)
    normed_ffn_low = normed_ffn.astype(bf16)
    gate_up = nn(normed_ffn_low, up_full)
    gate_part = gate_up[:, :FF]
    up_part = gate_up[:, FF:]
    inner = (jax.nn.silu(gate_part) * up_part).astype(bf16)
    output = hidden + nn(inner, down_full)
    grad_output = cotangent[0]
    grad_branch = grad_output.astype(bf16)
    grad_inner = nt(grad_branch, down_full)
    gate_sigmoid = jax.nn.sigmoid(gate_part)
    grad_gate_part = grad_inner * up_part * gate_sigmoid * (1.0 + gate_part * (1.0 - gate_sigmoid))
    grad_up_part = grad_inner * gate_part * gate_sigmoid
    grad_gate_up = jnp.concatenate([grad_gate_part, grad_up_part], axis=1).astype(bf16)
    grad_normed_ffn = nt(grad_gate_up, up_full)
    grad_hidden_norm, grad_second_gain = second_pull(grad_normed_ffn)
    grad_hidden = grad_output + grad_hidden_norm
    grad_attn_branch = grad_hidden.astype(bf16)
    grad_mixed = nt(grad_attn_branch, out_full)
    grad_attended = grad_mixed * gate_sig
    grad_logit = (grad_mixed * attended * gate_sig * (1.0 - gate_sig)).astype(bf16)

    def parity(left):
        flat = left.T.reshape(peers, 2, left.shape[1] // owners, rows)
        kept = pick(flat, y, 1).reshape(-1, rows)
        sent = pick(flat, 1 - y, 1).reshape(-1, rows)
        return jnp.concatenate([kept, partner(sent, "fsdp")], axis=1)

    def share(right):
        return jnp.concatenate([right, partner(right, "fsdp")], axis=0)

    def reduced(left, right):
        return lax.psum_scatter(
            nn(left, right).astype(bf16), "ctx", scatter_dimension=0, tiled=True
        ).astype(f32)

    grad_down = reduced(parity(inner), share(grad_branch))
    grad_up = reduced(parity(normed_ffn_low), share(grad_gate_up))
    grad_out = reduced(parity(gated_mix), share(grad_attn_branch))
    both_logit = share(grad_logit)
    normed_parity = parity(normed_low)
    grad_gate = reduced(normed_parity, both_logit)

    dq, dk, dv, dst, dridge = adjoint(
        grad_attended, keys, values, states, cumulative, strength, ridge, x, p_all, m_all, scal
    )
    returned = entering(dst, logs, "ctx", True)
    parts = features_back(projected, halo, taps, cumulative, strength, dq, dk, dv, returned)
    grad_projected = jnp.concatenate(parts[:3], axis=1)
    grad_before = jnp.concatenate(parts[3:6], axis=1)[: KW - 1]
    grad_taps = jnp.concatenate(parts[6:], axis=1)
    from_next = shifted(grad_before.astype(bf16), "ctx", -1).astype(f32)
    grad_projected = grad_projected + jnp.pad(from_next, ((rows - KW + 1, 0), (0, 0)))
    both_projected = share(grad_projected.astype(bf16))
    grad_qkv = reduced(normed_parity, both_projected)
    lent = nt(both_projected, qkv_weight) + nt(both_logit, gate_weight)
    back = partner(lent[rows:].astype(bf16), "fsdp").astype(f32)
    kept = lent[:rows]
    grad_normed = jnp.where(
        y == 0, jnp.concatenate([kept, back], axis=1), jnp.concatenate([back, kept], axis=1)
    )
    _, first_pull = jax.vjp(rms_scale, tokens, gain_first)
    grad_tokens_norm, grad_first_gain = first_pull(grad_normed)
    grad_tokens = grad_hidden + grad_tokens_norm
    width = 3 * D // owners
    vector = jnp.concatenate(
        [
            grad_taps.reshape(KW, owners, width).transpose(1, 0, 2).reshape(owners, KW * width),
            grad_first_gain.reshape(owners, D // owners),
            grad_second_gain.reshape(owners, D // owners),
            dridge.reshape(owners, D // owners),
        ],
        axis=1,
    )
    vector = lax.psum_scatter(vector, ("ctx", "fsdp"), scatter_dimension=0, tiled=True)[0]
    taps_end = KW * width
    size = D // owners
    return (
        output[None],
        grad_tokens[None],
        grad_qkv,
        grad_gate,
        grad_out,
        grad_up,
        grad_down,
        vector[:taps_end].reshape(KW, width),
        vector[taps_end : taps_end + size],
        vector[taps_end + size : taps_end + 2 * size],
        vector[taps_end + 2 * size :],
    )


def solution(mesh):
    tokens = P("fsdp", "ctx", None)
    rows = P("fsdp", None)
    vector = P("fsdp")
    owned = P(("ctx", "fsdp"), None)
    owned_vector = P(("ctx", "fsdp"))
    return jax.shard_map(
        local,
        mesh=mesh,
        in_specs=(
            tokens, rows, rows, rows, rows, rows, P(None, "fsdp"), vector, vector, vector, tokens, tokens,
        ),
        out_specs=(
            tokens, tokens, owned, owned, owned, owned, owned, P(None, ("ctx", "fsdp")),
            owned_vector, owned_vector, owned_vector,
        ),
        check_vma=False,
    )
```

```python
import functools
import jax
import jax.numpy as jnp
from jax import lax
from jax.experimental import pallas as pl
from jax.experimental.pallas import tpu as pltpu
from jax.sharding import PartitionSpec as P

D = 1024
HEADS = 8
FF = 2816
KW = 4
ITERS = 8
HEAD_DIM = 128
GROUP = 4

f32 = jnp.float32
bf16 = jnp.bfloat16
VMEM_LIMIT = 56 * 1024 * 1024


def nn(a, b):
    return lax.dot_general(a, b, (((1,), (0,)), ((), ())), preferred_element_type=f32)


def nt(a, b):
    return lax.dot_general(a, b, (((1,), (1,)), ((), ())), preferred_element_type=f32)


def tn(a, b):
    return lax.dot_general(a, b, (((0,), (0,)), ((), ())), preferred_element_type=f32)


def column(row, like):
    return jnp.broadcast_to(row, like).T


def decay_mask(c, b, tokens):
    shape = (tokens, tokens)
    late = lax.broadcasted_iota(jnp.int32, shape, 1) >= lax.broadcasted_iota(jnp.int32, shape, 0)
    spread = jnp.broadcast_to(c, shape) - column(c, shape)
    return jnp.where(late, jnp.exp(jnp.where(late, spread, 0.0)), 0.0) * column(b, shape)


def conv_parts(proj, halo, taps):
    padded = jnp.concatenate([halo, proj], axis=0)
    rows = proj.shape[0]
    shifted = [padded[8 - KW + 1 + j : 8 - KW + 1 + j + rows] for j in range(KW)]
    total = taps[0:1] * shifted[0]
    for j in range(1, KW):
        total = total + taps[j : j + 1] * shifted[j]
    return total, shifted


def features_kernel(pq, pk, pv, hq, hk, hv, tq, tk, tv, c_ref, b_ref, q_out, k_out, v_out, st_out):
    head = pl.program_id(0)
    tokens = pq.shape[0]
    shape = (tokens, HEAD_DIM)

    def activated(p, h, t):
        total, _ = conv_parts(p[...], h[...], t[...])
        return total * jax.nn.sigmoid(total)

    def unit(a):
        return a * lax.rsqrt(jnp.sum(a * a, axis=-1, keepdims=True) + 1e-06)

    c = c_ref[pl.ds(head, 1), :]
    b = b_ref[pl.ds(head, 1), :]
    ending = column(jnp.exp(c[:, tokens - 1 :] - c) * b, (HEAD_DIM, tokens))
    q = unit(activated(pq, hq, tq))
    k = unit(activated(pk, hk, tk))
    v = activated(pv, hv, tv)
    k_low = k.astype(bf16)
    q_out[0] = q.T
    k_out[0] = k_low
    v_out[0] = v.astype(bf16)
    st_out[0, 0] = tn((k * ending).astype(bf16), k_low).astype(bf16)
    st_out[0, 1] = tn((v * ending).astype(bf16), k_low).astype(bf16)


def thirds(rows):
    return [pl.BlockSpec((rows, HEAD_DIM), lambda h, i=i: (0, i * HEADS + h)) for i in range(3)]


def whole(*shape):
    return pl.BlockSpec(shape, lambda h: (0,) * len(shape))


def per_head(*shape):
    return pl.BlockSpec((1,) + shape, lambda h: (h,) + (0,) * len(shape))


def features(proj, halo, taps, c, b):
    tokens = proj.shape[0]
    square = (HEADS, HEAD_DIM, tokens)
    return pl.pallas_call(
        features_kernel,
        grid=(HEADS,),
        in_specs=thirds(tokens) + thirds(8) + thirds(KW) + [whole(HEADS, tokens)] * 2,
        out_specs=[
            per_head(HEAD_DIM, tokens),
            per_head(tokens, HEAD_DIM),
            per_head(tokens, HEAD_DIM),
            per_head(2, HEAD_DIM, HEAD_DIM),
        ],
        out_shape=[
            jax.ShapeDtypeStruct(square, f32),
            jax.ShapeDtypeStruct((HEADS, tokens, HEAD_DIM), bf16),
            jax.ShapeDtypeStruct((HEADS, tokens, HEAD_DIM), bf16),
            jax.ShapeDtypeStruct((HEADS, 2, HEAD_DIM, HEAD_DIM), bf16),
        ],
        cost_estimate=pl.CostEstimate(flops=70_000_000, bytes_accessed=4_000_000, transcendentals=400_000),
        name="features",
    )(proj, proj, proj, halo, halo, halo, taps, taps, taps, c, b)


def solve_kernel(
    q_ref, k_ref, v_ref, st_ref, c_ref, b_ref, ridge_ref,
    att_ref, x_out, p_out, m_out, scal_out,
    left, kt, mask, decay, ridge, x_s, r_s, p_s,
):
    group = pl.program_id(0)
    tokens = q_ref.shape[2]
    shape = (HEAD_DIM, tokens)
    first = []
    for h in range(GROUP):
        c = c_ref[pl.ds(group * GROUP + h, 1), :]
        b = b_ref[pl.ds(group * GROUP + h, 1), :]
        left[h, :HEAD_DIM] = st_ref[h, 0]
        left[h, HEAD_DIM:] = k_ref[h]
        kt[h] = k_ref[h].T
        mask[h] = decay_mask(c, b, tokens)
        decay[h] = jnp.broadcast_to(jnp.exp(c), (8, tokens))
        ridge[h] = column(ridge_ref[pl.ds(group * GROUP + h, 1), :], (tokens, HEAD_DIM))
        q = q_ref[h]
        x_s[h] = jnp.zeros(shape, f32)
        r_s[h] = q
        p_s[h] = q
        first.append(jnp.sum(q * q, axis=0, keepdims=True))

    def step(i, norms):
        after = []
        for h in range(GROUP):
            p = p_s[h]
            p_low = p.astype(bf16)
            both = nn(left[h], p_low)
            scores = (both[HEAD_DIM:] * mask[h]).astype(bf16)
            image = decay[h, 0:1] * both[:HEAD_DIM] + nn(kt[h], scores) + ridge[h] * p
            dot = jnp.sum(p * image, axis=0, keepdims=True)
            size = norms[h] / dot
            p_out[i, h] = p
            m_out[i, h] = image
            scal_out[h, pl.ds(i, 1)] = norms[h]
            scal_out[h, pl.ds(ITERS + i, 1)] = dot
            x_s[h] = x_s[h] + size * p
            r = r_s[h] - size * image
            r_s[h] = r
            norm = jnp.sum(r * r, axis=0, keepdims=True)
            p_s[h] = r + (norm / norms[h]) * p
            after.append(norm)
        return tuple(after)

    lax.fori_loop(0, ITERS, step, tuple(first))
    for h in range(GROUP):
        x_low = x_s[h].astype(bf16)
        x_out[h] = x_low
        scores = (nn(k_ref[h], x_low) * mask[h]).astype(bf16)
        out = decay[h, 0:1] * nn(st_ref[h, 1], x_low) + tn(v_ref[h], scores)
        att_ref[:, h * HEAD_DIM : (h + 1) * HEAD_DIM] = out.T


def grouped(*shape):
    return pl.BlockSpec((GROUP,) + shape, lambda g: (g,) + (0,) * len(shape))


def solve(q, k, v, states, c, b, ridge):
    tokens = q.shape[2]
    steps = pl.BlockSpec((ITERS, GROUP, HEAD_DIM, tokens), lambda g: (0, g, 0, 0))
    square = pltpu.VMEM((GROUP, HEAD_DIM, tokens), f32)
    return pl.pallas_call(
        solve_kernel,
        grid=(HEADS // GROUP,),
        in_specs=[
            grouped(HEAD_DIM, tokens),
            grouped(tokens, HEAD_DIM),
            grouped(tokens, HEAD_DIM),
            grouped(2, HEAD_DIM, HEAD_DIM),
            whole(HEADS, tokens),
            whole(HEADS, tokens),
            whole(HEADS, HEAD_DIM),
        ],
        out_specs=[
            pl.BlockSpec((tokens, GROUP * HEAD_DIM), lambda g: (0, g)),
            grouped(HEAD_DIM, tokens),
            steps,
            steps,
            grouped(2 * ITERS, tokens),
        ],
        out_shape=[
            jax.ShapeDtypeStruct((tokens, D), f32),
            jax.ShapeDtypeStruct((HEADS, HEAD_DIM, tokens), bf16),
            jax.ShapeDtypeStruct((ITERS, HEADS, HEAD_DIM, tokens), f32),
            jax.ShapeDtypeStruct((ITERS, HEADS, HEAD_DIM, tokens), f32),
            jax.ShapeDtypeStruct((HEADS, 2 * ITERS, tokens), f32),
        ],
        scratch_shapes=[
            pltpu.VMEM((GROUP, HEAD_DIM + tokens, HEAD_DIM), bf16),
            pltpu.VMEM((GROUP, HEAD_DIM, tokens), bf16),
            pltpu.VMEM((GROUP, tokens, tokens), f32),
            pltpu.VMEM((GROUP, 8, tokens), f32),
            square, square, square, square,
        ],
        compiler_params=pltpu.CompilerParams(vmem_limit_bytes=VMEM_LIMIT),
        cost_estimate=pl.CostEstimate(flops=900_000_000, bytes_accessed=12_000_000, transcendentals=200_000),
        name="solve",
    )(q, k, v, states, c, b, ridge)


def adjoint_kernel(
    ga_ref, k_ref, v_ref, st_ref, c_ref, b_ref, ridge_ref, x_ref, p_ref, m_ref, scal_ref,
    dq_ref, dk_ref, dv_ref, dst_ref, dridge_ref,
    left, kt, mask, decay, ridge, gx_s, gr_s, gp_s, acc_s, wide, rows, scaled,
):
    group = pl.program_id(0)
    tokens = k_ref.shape[1]
    steps = ITERS * tokens
    first = []
    for h in range(GROUP):
        c = c_ref[pl.ds(group * GROUP + h, 1), :]
        b = b_ref[pl.ds(group * GROUP + h, 1), :]
        k = k_ref[h]
        left[h, :HEAD_DIM] = st_ref[h, 0]
        left[h, HEAD_DIM:] = k
        kt[h] = k.T
        mask[h] = decay_mask(c, b, tokens)
        decay[h] = jnp.broadcast_to(jnp.exp(c), (8, tokens))
        ridge[h] = column(ridge_ref[pl.ds(group * GROUP + h, 1), :], (tokens, HEAD_DIM))
        e = decay[h, 0:1]
        ga = ga_ref[:, h * HEAD_DIM : (h + 1) * HEAD_DIM].T
        ga_low = ga.astype(bf16)
        x = x_ref[h]
        scores = (nn(k, x) * mask[h]).astype(bf16)
        dscores = (nn(v_ref[h], ga_low) * mask[h]).astype(bf16)
        gx = e * tn(st_ref[h, 1], ga_low) + nn(kt[h], dscores)
        gx_s[h] = gx
        dv_ref[h] = nt(scores, ga_low)
        dst_ref[h, 1] = nt((e * ga).astype(bf16), x).astype(bf16)
        wide[h, :, 2 * steps :] = dscores
        rows[h, :, 2 * steps :] = x
        for i in range(ITERS):
            low = p_ref[i, h].astype(bf16)
            rows[h, :, steps + i * tokens : steps + (i + 1) * tokens] = low
            wide[h, :, i * tokens : (i + 1) * tokens] = (nn(k, low) * mask[h]).astype(bf16)
        i = ITERS - 1
        p, m = p_ref[i, h], m_ref[i, h]
        norm = scal_ref[h, i : i + 1]
        dot = scal_ref[h, ITERS + i : ITERS + i + 1]
        size = norm / dot
        gsize = jnp.sum(gx * p, axis=0, keepdims=True)
        gdot = -gsize * size / dot
        gm = gdot * p
        low = gm.astype(bf16)
        gp_s[h] = size * gx + 2.0 * gdot * m
        gr_s[h] = jnp.zeros_like(gx)
        acc_s[h] = gm * p
        rows[h, :, i * tokens : (i + 1) * tokens] = low
        wide[h, :, steps + i * tokens : steps + (i + 1) * tokens] = (nn(k, low) * mask[h]).astype(bf16)
        scaled[h, :, i * tokens : (i + 1) * tokens] = (e * gm).astype(bf16)
        first.append(gsize / dot)

    def step(back, gnorms):
        i = ITERS - 2 - back
        at = pl.multiple_of(i * tokens, tokens)
        after = []
        for h in range(GROUP):
            e = decay[h, 0:1]
            p, m = p_ref[i, h], m_ref[i, h]
            norm = scal_ref[h, pl.ds(i, 1)]
            norm_next = scal_ref[h, pl.ds(i + 1, 1)]
            dot = scal_ref[h, pl.ds(ITERS + i, 1)]
            size = norm / dot
            ratio = norm_next / norm
            gp = gp_s[h]
            gx = gx_s[h]
            gratio = jnp.sum(gp * p, axis=0, keepdims=True)
            gnext = gnorms[h] + gratio / norm
            residual = p_ref[i + 1, h] - ratio * p
            gr = gr_s[h] + gp + 2.0 * gnext * residual
            gsize = jnp.sum(gx * p - gr * m, axis=0, keepdims=True)
            gdot = -gsize * size / dot
            gm = gdot * p - size * gr
            low = gm.astype(bf16)
            both = nn(left[h], low)
            dscores = (both[HEAD_DIM:] * mask[h]).astype(bf16)
            image = e * both[:HEAD_DIM] + nn(kt[h], dscores) + ridge[h] * gm
            gp_s[h] = ratio * gp + size * gx + gdot * m + image
            gr_s[h] = gr
            acc_s[h] = acc_s[h] + gm * p
            rows[h, :, pl.ds(at, tokens)] = low
            wide[h, :, pl.ds(steps + at, tokens)] = dscores
            scaled[h, :, pl.ds(at, tokens)] = (e * gm).astype(bf16)
            after.append(gsize / dot - gratio * ratio / norm)
        return tuple(after)

    gnorms = lax.fori_loop(0, ITERS - 1, step, tuple(first))
    for h in range(GROUP):
        dq_ref[h] = gr_s[h] + gp_s[h] + 2.0 * gnorms[h] * p_ref[0, h]
        dk_ref[h] = nt(wide[h], rows[h])
        dst_ref[h, 0] = nt(scaled[h], rows[h, :, steps : 2 * steps]).astype(bf16)
        dridge_ref[h] = jnp.sum(acc_s[h].T, axis=0, keepdims=True)


def adjoint(ga, k, v, states, c, b, ridge, x, p_all, m_all, scal):
    tokens = k.shape[1]
    steps = pl.BlockSpec((ITERS, GROUP, HEAD_DIM, tokens), lambda g: (0, g, 0, 0))
    square = pltpu.VMEM((GROUP, HEAD_DIM, tokens), f32)
    return pl.pallas_call(
        adjoint_kernel,
        grid=(HEADS // GROUP,),
        in_specs=[
            pl.BlockSpec((tokens, GROUP * HEAD_DIM), lambda g: (0, g)),
            grouped(tokens, HEAD_DIM),
            grouped(tokens, HEAD_DIM),
            grouped(2, HEAD_DIM, HEAD_DIM),
            whole(HEADS, tokens),
            whole(HEADS, tokens),
            whole(HEADS, HEAD_DIM),
            grouped(HEAD_DIM, tokens),
            steps,
            steps,
            grouped(2 * ITERS, tokens),
        ],
        out_specs=[
            grouped(HEAD_DIM, tokens),
            grouped(tokens, HEAD_DIM),
            grouped(tokens, HEAD_DIM),
            grouped(2, HEAD_DIM, HEAD_DIM),
            grouped(1, HEAD_DIM),
        ],
        out_shape=[
            jax.ShapeDtypeStruct((HEADS, HEAD_DIM, tokens), f32),
            jax.ShapeDtypeStruct((HEADS, tokens, HEAD_DIM), f32),
            jax.ShapeDtypeStruct((HEADS, tokens, HEAD_DIM), f32),
            jax.ShapeDtypeStruct((HEADS, 2, HEAD_DIM, HEAD_DIM), bf16),
            jax.ShapeDtypeStruct((HEADS, 1, HEAD_DIM), f32),
        ],
        scratch_shapes=[
            pltpu.VMEM((GROUP, HEAD_DIM + tokens, HEAD_DIM), bf16),
            pltpu.VMEM((GROUP, HEAD_DIM, tokens), bf16),
            pltpu.VMEM((GROUP, tokens, tokens), f32),
            pltpu.VMEM((GROUP, 8, tokens), f32),
            square, square, square, square, square,
            pltpu.VMEM((GROUP, tokens, (2 * ITERS + 1) * tokens), bf16),
            pltpu.VMEM((GROUP, HEAD_DIM, (2 * ITERS + 1) * tokens), bf16),
            pltpu.VMEM((GROUP, HEAD_DIM, ITERS * tokens), bf16),
        ],
        compiler_params=pltpu.CompilerParams(vmem_limit_bytes=VMEM_LIMIT),
        cost_estimate=pl.CostEstimate(flops=1_800_000_000, bytes_accessed=12_000_000, transcendentals=200_000),
        name="adjoint",
    )(ga, k, v, states, c, b, ridge, x, p_all, m_all, scal)


def features_back_kernel(
    pq, pk, pv, hq, hk, hv, tq, tk, tv, c_ref, b_ref, dq_ref, dk_ref, dv_ref, dst_ref,
    gq, gk, gv, bq, bk, bv, dtq, dtk, dtv,
):
    head = pl.program_id(0)
    tokens = pq.shape[0]
    c = c_ref[pl.ds(head, 1), :]
    b = b_ref[pl.ds(head, 1), :]
    ending = column(jnp.exp(c[:, tokens - 1 :] - c) * b, (HEAD_DIM, tokens))

    def forward(p, h, t):
        total, shifted = conv_parts(p[...], h[...], t[...])
        sig = jax.nn.sigmoid(total)
        act = total * sig
        return shifted, sig * (1.0 + total * (1.0 - sig)), act

    def unit_back(act, grad):
        scale = lax.rsqrt(jnp.sum(act * act, axis=-1, keepdims=True) + 1e-06)
        unit = act * scale
        return scale * (grad - unit * jnp.sum(unit * grad, axis=-1, keepdims=True))

    def conv_back(dconv, shifted, t, g, before, dt):
        taps = t[...]
        padded = jnp.concatenate([dconv, jnp.zeros((8, HEAD_DIM), f32)], axis=0)
        total = taps[KW - 1 : KW] * dconv
        for j in range(KW - 1):
            total = total + taps[j : j + 1] * padded[KW - 1 - j : KW - 1 - j + tokens]
        g[...] = total
        ahead = jnp.concatenate([jnp.zeros((8, HEAD_DIM), f32), dconv[:8]], axis=0)
        lead = taps[0:1] * ahead[8:16]
        for j in range(1, KW - 1):
            lead = lead + taps[j : j + 1] * ahead[8 - j : 16 - j]
        before[...] = lead
        dt[...] = jnp.concatenate(
            [jnp.sum(dconv * shifted[j], axis=0, keepdims=True) for j in range(KW)], axis=0
        )

    sh_q, slope_q, act_q = forward(pq, hq, tq)
    sh_k, slope_k, act_k = forward(pk, hk, tk)
    sh_v, slope_v, act_v = forward(pv, hv, tv)
    k = act_k * lax.rsqrt(jnp.sum(act_k * act_k, axis=-1, keepdims=True) + 1e-06)
    k_low = k.astype(bf16)
    v_low = act_v.astype(bf16)
    both = dst_ref[0, 0].astype(f32)
    both = (both + both.T).astype(bf16)
    rv = dst_ref[0, 1].astype(bf16)
    dk = dk_ref[0] + ending * (nn(k_low, both) + nn(v_low, rv))
    dv = dv_ref[0] + ending * nt(k_low, rv)
    conv_back(unit_back(act_q, dq_ref[0].T) * slope_q, sh_q, tq, gq, bq, dtq)
    conv_back(unit_back(act_k, dk) * slope_k, sh_k, tk, gk, bk, dtk)
    conv_back(dv * slope_v, sh_v, tv, gv, bv, dtv)


def features_back(proj, halo, taps, c, b, dq, dk, dv, dst):
    tokens = proj.shape[0]

    def third(rows):
        return pl.BlockSpec((rows, HEAD_DIM), lambda h: (0, h))

    return pl.pallas_call(
        features_back_kernel,
        grid=(HEADS,),
        in_specs=thirds(tokens) + thirds(8) + thirds(KW) + [whole(HEADS, tokens)] * 2
        + [per_head(HEAD_DIM, tokens), per_head(tokens, HEAD_DIM), per_head(tokens, HEAD_DIM), per_head(2, HEAD_DIM, HEAD_DIM)],
        out_specs=[third(tokens)] * 3 + [third(8)] * 3 + [third(KW)] * 3,
        out_shape=[jax.ShapeDtypeStruct((tokens, D), f32)] * 3
        + [jax.ShapeDtypeStruct((8, D), f32)] * 3
        + [jax.ShapeDtypeStruct((KW, D), f32)] * 3,
        cost_estimate=pl.CostEstimate(flops=100_000_000, bytes_accessed=8_000_000, transcendentals=400_000),
        name="features_back",
    )(proj, proj, proj, halo, halo, halo, taps, taps, taps, c, b, dq, dk, dv, dst)


def middle_kernel(
    place, att_ref, logit_ref, tok_ref, cot_ref, gain_ref, own_out, out_a, out_b, out_c, out_d, *refs,
):
    own_up = refs[:4]
    up_parts = refs[4:8]
    own_down = refs[8]
    down_parts = refs[9:13]
    (out_o, hid_o, gab_o, gatt_o, glog_o, mix_o, nf_o, inner_o, ggu_o, dgain_o) = refs[13:23]
    out_s, up_s, down_s, nf_s, gb_s, hid_s, acc_s, gnf_s = refs[23:]
    j = pl.program_id(0)
    y = place[0]
    quarter = place[1]
    half = D // 2
    mine = pl.ds(pl.multiple_of(y * half, half), half)
    theirs = pl.ds(pl.multiple_of((1 - y) * half, half), half)
    order = [quarter, quarter ^ 2, quarter ^ 1, quarter ^ 3]
    tile = own_up[0].shape[1]

    def scale_of(hidden):
        return lax.rsqrt(jnp.mean(hidden * hidden, axis=-1, keepdims=True) + 1e-05)

    @pl.when(j == 0)
    def _():
        out_s[mine, :] = own_out[...]
        wide = out_a.shape[1]
        for part, q in zip((out_a, out_b, out_c, out_d), order):
            out_s[theirs, pl.ds(pl.multiple_of(q * wide, wide), wide)] = part[...]
        mix = (att_ref[...] * jax.nn.sigmoid(logit_ref[...])).astype(bf16)
        mix_o[...] = mix.T
        hidden = tok_ref[...] + nn(mix, out_s[...])
        hid_s[...] = hidden
        normed = (hidden * scale_of(hidden) * gain_ref[...]).astype(bf16)
        nf_s[...] = normed
        nf_o[...] = normed.T
        gb_s[...] = cot_ref[...].astype(bf16)
        acc_s[...] = jnp.zeros_like(acc_s)
        gnf_s[...] = jnp.zeros_like(gnf_s)

    for i in range(4):
        up_s[mine, i * tile : (i + 1) * tile] = own_up[i][...]
    for part, q in zip(up_parts, order):
        slot = (q >> 1) * 2 + ((q & 1) ^ y)
        up_s[theirs, pl.ds(pl.multiple_of(slot * tile, tile), tile)] = part[...]
    down_s[:tile, :] = own_down[...]
    wide = down_parts[0].shape[1]
    for part, q in zip(down_parts, order):
        down_s[tile:, pl.ds(pl.multiple_of(q * wide, wide), wide)] = part[...]
    product = nn(nf_s[...], up_s[...])
    gate, up = product[:, : 2 * tile], product[:, 2 * tile :]
    ginner = nt(gb_s[...], down_s[...])
    sig = jax.nn.sigmoid(gate)
    silu = gate * sig
    inner = (silu * up).astype(bf16)
    ggate = (ginner * up * (sig * (1.0 + gate * (1.0 - sig)))).astype(bf16)
    gup = (ginner * silu).astype(bf16)
    ggu = jnp.concatenate([ggate, gup], axis=1)
    acc_s[...] += nn(inner, down_s[...])
    gnf_s[...] += nt(ggu, up_s[...])
    inner_t = inner.T
    inner_o[y] = inner_t[:tile]
    inner_o[1 - y] = inner_t[tile:]
    ggu_o[y] = ggate[:, :tile]
    ggu_o[1 - y] = ggate[:, tile:]
    ggu_o[2 + y] = gup[:, :tile]
    ggu_o[3 - y] = gup[:, tile:]

    @pl.when(j == pl.num_programs(0) - 1)
    def _():
        hidden = hid_s[...]
        out_o[...] = hidden + acc_s[...]
        scale = scale_of(hidden)
        unit = hidden * scale
        gnf = gnf_s[...]
        dgain_o[...] = jnp.sum(gnf * unit, axis=0, keepdims=True)
        gunit = gnf * gain_ref[...]
        ghid = cot_ref[...] + scale * (gunit - unit * jnp.mean(gunit * unit, axis=-1, keepdims=True))
        hid_o[...] = ghid
        low = ghid.astype(bf16)
        gab_o[...] = low
        gmix = nt(low, out_s[...])
        sig = jax.nn.sigmoid(logit_ref[...])
        gatt = gmix * sig
        gatt_o[...] = gatt
        glog_o[...] = (gatt * att_ref[...] * (1.0 - sig)).astype(bf16)


def middle(place, att, logit, tok, cot, gain, out_parts, up_parts, down_parts):
    tokens = att.shape[0]
    tile = 128
    share = FF // 2 // tile
    half = D // 2

    def full(*shape):
        return pl.BlockSpec(shape, lambda j, s: (0,) * len(shape))

    rows = full(tokens, D)
    own_up = [
        pl.BlockSpec((half, tile), lambda j, s: (0, s[0] * share + j)),
        pl.BlockSpec((half, tile), lambda j, s: (0, (1 - s[0]) * share + j)),
        pl.BlockSpec((half, tile), lambda j, s: (0, (2 + s[0]) * share + j)),
        pl.BlockSpec((half, tile), lambda j, s: (0, (3 - s[0]) * share + j)),
    ]
    up_specs = [pl.BlockSpec((half, tile), lambda j, s: (0, j))] * 4
    own_down = pl.BlockSpec((tile, D), lambda j, s: (j, 0))
    down_specs = [pl.BlockSpec((tile, D // 4), lambda j, s: (j, 0))] * 4
    act = jax.ShapeDtypeStruct((tokens, D), f32)
    low = jax.ShapeDtypeStruct((tokens, D), bf16)
    turned = jax.ShapeDtypeStruct((D, tokens), bf16)
    return pl.pallas_call(
        middle_kernel,
        grid_spec=pltpu.PrefetchScalarGridSpec(
            num_scalar_prefetch=1,
            grid=(share,),
            in_specs=[rows] * 4 + [full(1, D), full(half, D)] + [full(half, D // 4)] * 4
            + own_up + up_specs + [own_down] + down_specs,
            out_specs=[
                rows, rows, rows, rows, rows, full(D, tokens), full(D, tokens),
                pl.BlockSpec((2, tile, tokens), lambda j, s: (0, j, 0)),
                pl.BlockSpec((4, tokens, tile), lambda j, s: (0, 0, j)),
                full(1, D),
            ],
            scratch_shapes=[
                pltpu.VMEM((D, D), bf16),
                pltpu.VMEM((D, 4 * tile), bf16),
                pltpu.VMEM((2 * tile, D), bf16),
                pltpu.VMEM((tokens, D), bf16),
                pltpu.VMEM((tokens, D), bf16),
                pltpu.VMEM((tokens, D), f32),
                pltpu.VMEM((tokens, D), f32),
                pltpu.VMEM((tokens, D), f32),
            ],
        ),
        out_shape=[
            act, act, low, act, low, turned, turned,
            jax.ShapeDtypeStruct((2, FF // 2, tokens), bf16),
            jax.ShapeDtypeStruct((4, tokens, FF // 2), bf16),
            jax.ShapeDtypeStruct((1, D), f32),
        ],
        compiler_params=pltpu.CompilerParams(vmem_limit_bytes=VMEM_LIMIT),
        cost_estimate=pl.CostEstimate(flops=5_000_000_000, bytes_accessed=24_000_000, transcendentals=600_000),
        name="middle",
    )(place, att, logit, tok, cot, gain, *out_parts, *[up_parts[0]] * 4, *up_parts[1:], *down_parts)


def neighbour(axis, bit):
    return [(i, i ^ bit) for i in range(lax.axis_size(axis))]


def partner(x, axis, bit=1):
    return lax.ppermute(x, axis, neighbour(axis, bit))


def shifted(x, axis, by):
    peers = lax.axis_size(axis)
    return lax.ppermute(x, axis, [(i, i + by) for i in range(peers) if 0 <= i + by < peers])


def pick(x, index, axis=0):
    return lax.dynamic_index_in_dim(x, index, axis, keepdims=False)


def collected(row, axis):
    here = lax.axis_index(axis)
    for level in range(lax.axis_size(axis).bit_length() - 1):
        other = partner(row, axis, 1 << level)
        late = ((here >> level) & 1) == 1
        row = jnp.where(late, jnp.concatenate([other, row]), jnp.concatenate([row, other]))
    return row


def after(value, *others):
    return lax.optimization_barrier((value,) + others)[0]


def entering(own, logs, axis, reverse):
    peers = lax.axis_size(axis)
    here = lax.axis_index(axis)
    if reverse:
        here = peers - 1 - here
        logs = logs[::-1]
    at = jnp.arange(peers)
    heads = own.shape[0]

    def total_decay(start, stop):
        inside = (at >= start) & (at < stop)
        return jnp.exp(jnp.sum(jnp.where(inside[:, None], logs, 0.0), axis=0))

    def times(coefficients, first, count):
        part = lax.dynamic_slice_in_dim(coefficients, first, count, 0)
        return part[:, None, None, None]

    levels = peers.bit_length() - 1
    halving = min(2, levels)
    now = own
    first, count = 0, heads
    saved = []
    for level in range(halving):
        size = 1 << level
        bit = (here >> level) & 1
        base = (here >> (level + 1)) << (level + 1)
        halves = now.reshape((2, count // 2) + now.shape[1:])
        keep = pick(halves, bit)
        received = partner(pick(halves, 1 - bit), axis, size)
        count = count // 2
        first = first + bit * count
        low = jnp.where(bit == 1, received, keep).astype(f32)
        high = jnp.where(bit == 1, keep, received).astype(f32)
        now = (times(total_decay(base + size, base + 2 * size), first, count) * low + high).astype(bf16)
        saved.append((bit, low, times(total_decay(base, base + size), first, count)))
    unit = (here >> halving) << halving
    before = jnp.zeros(now.shape, f32)
    for level in range(halving, levels):
        size = 1 << level
        bit = (here >> level) & 1
        base = (here >> (level + 1)) << (level + 1)
        start = (here >> level) << level
        received = partner(now, axis, size).astype(f32)
        mine = now.astype(f32)
        before = jnp.where(bit == 1, times(total_decay(start, unit), first, count) * received + before, before)
        low = jnp.where(bit == 1, received, mine)
        high = jnp.where(bit == 1, mine, received)
        now = (times(total_decay(base + size, base + 2 * size), first, count) * low + high).astype(bf16)
    for level in reversed(range(halving)):
        bit, low, decay = saved[level]
        after = decay * before + low
        mine = jnp.where(bit == 1, after, before).astype(bf16)
        other = jnp.where(bit == 1, before, after).astype(bf16)
        received = partner(other, axis, 1 << level)
        before = jnp.concatenate(
            [jnp.where(bit == 1, received, mine), jnp.where(bit == 1, mine, received)], axis=0
        ).astype(f32)
    return before.astype(bf16)


def gathered(shard):
    q = lax.axis_index("ctx") % 4
    wide = shard.shape[1] // 4
    direct = partner(lax.dynamic_slice_in_dim(shard, q * wide, wide, 1), "fsdp")
    across = partner(direct, "ctx", 2)
    return shard, direct, across, partner(direct, "ctx", 1), partner(across, "ctx", 1)


def scattered(left, right):
    peers = lax.axis_size("ctx")
    here = lax.axis_index("ctx")
    bit = here % 2
    shape = (peers // 2, left.shape[0] // peers, right.shape[1])
    halves = left.reshape(peers // 2, 2, left.shape[0] // peers, left.shape[1])
    sent = nn(pick(halves, 1 - bit, 1).reshape(-1, left.shape[1]), right).astype(bf16)
    kept = nn(pick(halves, bit, 1).reshape(-1, left.shape[1]), right)
    now = (kept + partner(sent, "ctx", 1).astype(f32)).astype(bf16).reshape(shape)
    return halved(now, "ctx", 1)


def halved(now, axis, level):
    here = lax.axis_index(axis)
    levels = lax.axis_size(axis).bit_length() - 1
    kind = now.dtype
    for level in range(level, levels):
        bit = (here >> level) & 1
        pairs = now.reshape((now.shape[0] // 2, 2) + now.shape[1:])
        total = pick(pairs, bit, 1).astype(f32) + partner(pick(pairs, 1 - bit, 1), axis, 1 << level).astype(f32)
        now = total if level == levels - 1 else total.astype(kind)
    return now[0]


def rms_scale(values, gain):
    return values * lax.rsqrt(jnp.mean(values * values, axis=-1, keepdims=True) + 1e-05) * gain


def local(
    inputs,
    qkv_weight,
    gate_weight,
    out_weight,
    up_weight,
    down_weight,
    conv_taps,
    gain_attn,
    gain_ffn,
    ridge_terms,
    forget,
    cotangent,
):
    tokens = inputs[0]
    rows = tokens.shape[0]
    y = lax.axis_index("fsdp")
    peers = lax.axis_size("ctx")
    owners = peers * 2
    place = jnp.stack([y, lax.axis_index("ctx") % 4]).astype(jnp.int32)
    small = jnp.concatenate([conv_taps.reshape(-1), gain_attn, gain_ffn, ridge_terms])
    theirs = partner(small, "fsdp")
    both = jnp.where(y == 0, jnp.stack([small, theirs]), jnp.stack([theirs, small])).astype(f32)
    split = KW * 3 * D // 2
    taps = both[:, :split].reshape(2, KW, 3 * D // 2).transpose(1, 0, 2).reshape(KW, 3 * D)
    rest = both[:, split:].reshape(2, 3, D // 2).transpose(1, 0, 2).reshape(3, D)
    gain_first, gain_second = rest[0], rest[1:2]
    ridge = rest[2].reshape(HEADS, HEAD_DIM)
    cumulative = jnp.cumsum(jnp.log(forget[0]).T, axis=-1)
    strength = (1.0 - forget[0]).T
    logs = collected(cumulative[:, -1][None], "ctx")

    normed_low = rms_scale(tokens, gain_first).astype(bf16)
    halves = normed_low.reshape(rows, 2, D // 2)
    mine = pick(halves, y, 1)
    theirs = partner(pick(halves, 1 - y, 1), "fsdp")
    lent = partner(nn(theirs, qkv_weight).astype(bf16), "fsdp")
    projected = nn(mine, qkv_weight) + lent.astype(f32)
    tail = shifted(projected[rows - (KW - 1) :].astype(bf16), "ctx", 1).astype(f32)
    halo = jnp.concatenate([jnp.zeros((8 - KW + 1, 3 * D), f32), tail], axis=0)
    out_parts = gathered(after(out_weight, theirs))
    up_parts = gathered(after(up_weight, lent))
    down_parts = gathered(after(down_weight, up_parts[1]))
    lent_gate = partner(nn(after(theirs, lent), gate_weight).astype(bf16), "fsdp")
    gate_logit = nn(mine, gate_weight) + lent_gate.astype(f32)
    queries, keys, values, own = features(projected, halo, taps, cumulative, strength)
    states = entering(own, logs, "ctx", False)
    attended, x, p_all, m_all, scal = solve(queries, keys, values, states, cumulative, strength, ridge)

    (output, grad_hidden, grad_attn_branch, grad_attended, grad_logit, mix_t, normed_ffn_t, inner_t,
     grad_gate_up, grad_second_gain) = middle(
        place, attended, gate_logit, tokens, cotangent[0], gain_second, out_parts, up_parts, down_parts
    )
    grad_branch = cotangent[0].astype(bf16)

    def parity(left):
        flat = left.reshape(peers, 2, left.shape[0] // owners, rows)
        kept = pick(flat, y, 1).reshape(-1, rows)
        sent = pick(flat, 1 - y, 1).reshape(-1, rows)
        return jnp.concatenate([kept, partner(sent, "fsdp")], axis=1)

    def share(right, axis=0):
        return jnp.concatenate([right, partner(right, "fsdp")], axis=axis)

    both_up = share(grad_gate_up, 1)
    normed_ffn_p = parity(normed_ffn_t)
    grad_up = jnp.concatenate([scattered(normed_ffn_p, both_up[i]) for i in range(4)], axis=1)
    grad_down = scattered(parity(inner_t.reshape(FF, rows)), share(grad_branch))
    grad_out = scattered(parity(mix_t), share(grad_attn_branch))
    both_logit = share(grad_logit)
    normed_parity = parity(normed_low.T)
    grad_gate = scattered(normed_parity, both_logit)

    dq, dk, dv, dst, dridge = adjoint(
        grad_attended, keys, values, states, cumulative, strength, ridge, x, p_all, m_all, scal
    )
    returned = entering(dst, logs, "ctx", True)
    parts = features_back(projected, halo, taps, cumulative, strength, dq, dk, dv, returned)
    grad_projected = jnp.concatenate(parts[:3], axis=1)
    grad_before = jnp.concatenate(parts[3:6], axis=1)[: KW - 1]
    grad_taps = jnp.concatenate(parts[6:], axis=1)
    from_next = shifted(grad_before.astype(bf16), "ctx", -1).astype(f32)
    grad_projected = grad_projected + jnp.pad(from_next, ((rows - KW + 1, 0), (0, 0)))
    both_projected = share(grad_projected.astype(bf16))
    grad_qkv = scattered(normed_parity, both_projected)
    lent = nt(both_projected, qkv_weight) + nt(both_logit, gate_weight)
    back = partner(lent[rows:].astype(bf16), "fsdp").astype(f32)
    kept = lent[:rows]
    grad_normed = jnp.where(
        y == 0, jnp.concatenate([kept, back], axis=1), jnp.concatenate([back, kept], axis=1)
    )
    _, first_pull = jax.vjp(rms_scale, tokens, gain_first)
    grad_tokens_norm, grad_first_gain = first_pull(grad_normed)
    grad_tokens = grad_hidden + grad_tokens_norm
    width = 3 * D // owners
    size = D // owners
    vector = jnp.concatenate(
        [
            grad_taps.reshape(KW, owners, width).transpose(1, 0, 2).reshape(owners, KW * width),
            grad_first_gain.reshape(owners, size),
            grad_second_gain.reshape(owners, size),
            dridge.reshape(owners, size),
        ],
        axis=1,
    ).reshape(peers, 2, -1)
    vector = pick(vector, y, 1) + partner(pick(vector, 1 - y, 1), "fsdp")
    vector = halved(vector, "ctx", 0)
    taps_end = KW * width
    return (
        output[None],
        grad_tokens[None],
        grad_qkv,
        grad_gate,
        grad_out,
        grad_up,
        grad_down,
        vector[:taps_end].reshape(KW, width),
        vector[taps_end : taps_end + size],
        vector[taps_end + size : taps_end + 2 * size],
        vector[taps_end + 2 * size :],
    )


def solution(mesh):
    tokens = P("fsdp", "ctx", None)
    rows = P("fsdp", None)
    vector = P("fsdp")
    owned = P(("ctx", "fsdp"), None)
    owned_vector = P(("ctx", "fsdp"))
    return jax.shard_map(
        local,
        mesh=mesh,
        in_specs=(
            tokens, rows, rows, rows, rows, rows, P(None, "fsdp"), vector, vector, vector, tokens, tokens,
        ),
        out_specs=(
            tokens, tokens, owned, owned, owned, owned, owned, P(None, ("ctx", "fsdp")),
            owned_vector, owned_vector, owned_vector,
        ),
        check_vma=False,
    )
```

```python
import functools
import jax
import jax.numpy as jnp
from jax import lax
from jax.experimental import pallas as pl
from jax.experimental.pallas import tpu as pltpu
from jax.sharding import PartitionSpec as P

D = 1024
HEADS = 8
FF = 2816
KW = 4
ITERS = 8
HEAD_DIM = 128
QUARTERS = 4
SHARE = HEADS // QUARTERS
HALO = 16

f32 = jnp.float32
bf16 = jnp.bfloat16
VMEM_LIMIT = 56 * 1024 * 1024


def nn(a, b):
    return lax.dot_general(a, b, (((1,), (0,)), ((), ())), preferred_element_type=f32)


def nt(a, b):
    return lax.dot_general(a, b, (((1,), (1,)), ((), ())), preferred_element_type=f32)


def tn(a, b):
    return lax.dot_general(a, b, (((0,), (0,)), ((), ())), preferred_element_type=f32)


def column(row, like):
    return jnp.broadcast_to(row, like).T


def decay_mask(c, b, tokens):
    shape = (tokens, tokens)
    late = lax.broadcasted_iota(jnp.int32, shape, 1) >= lax.broadcasted_iota(jnp.int32, shape, 0)
    spread = jnp.broadcast_to(c, shape) - column(c, shape)
    return jnp.where(late, jnp.exp(jnp.where(late, spread, 0.0)), 0.0) * column(b, shape)


def like(shape, kind=f32):
    return jax.ShapeDtypeStruct(shape, kind)


def smem():
    return pl.BlockSpec(memory_space=pltpu.SMEM)


EXTRA = 16


def norm_kernel(place, tok_ref, taps_ref, lines_ref, mine_o, theirs_o):
    half = D // 2
    y = place[0]
    a = tok_ref[...]
    unit = a * lax.rsqrt(jnp.mean(a * a, axis=-1, keepdims=True) + 1e-05)
    left, right = unit[:, :half], unit[:, half:]
    rows = a.shape[0]
    gain = lines_ref[0:1].astype(f32)
    mine_o[...] = (jnp.where(y == 0, left, right) * gain).astype(bf16)
    theirs_o[:rows] = jnp.where(y == 0, right, left)
    taps = taps_ref[...].astype(f32)
    lines = [taps[t : t + 1, i * half : (i + 1) * half] for t in range(KW) for i in range(3)]
    theirs_o[rows:] = jnp.concatenate(lines + [lines_ref[...].astype(f32)], axis=0)


def norm(place, tokens, taps, lines):
    rows = tokens.shape[0]
    vmem = pl.BlockSpec(memory_space=pltpu.VMEM)
    return pl.pallas_call(
        norm_kernel,
        in_specs=[smem()] + [vmem] * 3,
        out_specs=[vmem, vmem],
        out_shape=[like((rows, D // 2), bf16), like((rows + EXTRA, D // 2))],
        name="norm",
    )(place, tokens, taps, lines)


def with_halo(own, lent, halo):
    before = halo[...].astype(f32)
    blank = jnp.zeros((HALO - before.shape[0], before.shape[1]), f32)
    return jnp.concatenate([blank, before, own[...] + lent[...].astype(f32)], axis=0)


def conv_parts(padded, taps):
    rows = padded.shape[0] - HALO
    shifted = [padded[HALO - KW + 1 + j : HALO - KW + 1 + j + rows] for j in range(KW)]
    total = taps[0:1] * shifted[0]
    for j in range(1, KW):
        total = total + taps[j : j + 1] * shifted[j]
    return total, shifted


def unit(a):
    return a * lax.rsqrt(jnp.sum(a * a, axis=-1, keepdims=True) + 1e-06)


def ending_of(c_ref, b_ref, head):
    c = c_ref[pl.ds(head, 1), :]
    b = b_ref[pl.ds(head, 1), :]
    return column(jnp.exp(c[:, c.shape[1] - 1 :] - c) * b, (HEAD_DIM, c.shape[1]))


def position(spot):
    return spot[0] % FOUR


FOUR = 4
PAIR = (2 * SHARE, HEAD_DIM, HEAD_DIM)
MESSAGE = (2 * SHARE, HEAD_DIM + 16, HEAD_DIM)


def decay_rows(decay):
    shape = (16, HEAD_DIM)
    at = lax.broadcasted_iota(jnp.int32, shape, 0)
    decay = jnp.broadcast_to(decay, shape)
    high = decay.astype(bf16).astype(f32)
    return jnp.where(at == 0, high, jnp.where(at == 1, decay - high, 0.0)).astype(bf16)


def decay_of(message, m):
    rows = message[m, HEAD_DIM:].astype(f32)
    return rows[0:1] + rows[1:2]


def block_decay(c_ref, head):
    c = c_ref[pl.ds(head, 1), :]
    return jnp.broadcast_to(jnp.exp(c[:, c.shape[1] - 1 :]), (1, HEAD_DIM))


def store_quarter(spot, quarter, outs, states, c_ref):
    rows = [decay_rows(block_decay(c_ref, quarter * SHARE + m)) for m in range(SHARE)]
    for i, out in enumerate(outs):

        @pl.when((position(spot) ^ i) == quarter)
        def _():
            for m in range(2 * SHARE):
                out[m, :HEAD_DIM] = states[m]
                out[m, HEAD_DIM:] = rows[m % SHARE]


def cut(h):
    return slice(h * HEAD_DIM, (h + 1) * HEAD_DIM)


def keys_kernel(oq, ok, lq, lk, hq, hk, tq, tk, c_ref, b_ref, q_o, k_o, state_o):
    quarter = pl.program_id(0)
    sums = []
    for own, lent, halo, taps in ((oq, lq, hq, tq), (ok, lk, hk, tk)):
        total, _ = conv_parts(with_halo(own, lent, halo), taps[...])
        sums.append(total * jax.nn.sigmoid(total))
    for m in range(SHARE):
        k = unit(sums[1][:, cut(m)])
        k_low = k.astype(bf16)
        k_o[m] = k_low
        ending = ending_of(c_ref, b_ref, quarter * SHARE + m)
        state_o[m] = tn((k * ending).astype(bf16), k_low).astype(bf16)
        q_o[m] = unit(sums[0][:, cut(m)]).T


def values_kernel(spot, ov, lv, hv, tv, k_ref, ks_ref, c_ref, b_ref, v_o, *outs):
    quarter = pl.program_id(0)
    total, _ = conv_parts(with_halo(ov, lv, hv), tv[...])
    values = total * jax.nn.sigmoid(total)
    states = [ks_ref[m] for m in range(SHARE)]
    for m in range(SHARE):
        v = values[:, cut(m)]
        v_o[m] = v.astype(bf16)
        ending = ending_of(c_ref, b_ref, quarter * SHARE + m)
        states.append(tn((v * ending).astype(bf16), k_ref[m]).astype(bf16))
    store_quarter(spot, quarter, outs, states, c_ref)


def whole(*shape):
    return pl.BlockSpec(shape, lambda *g: (0,) * len(shape))


def per_quarter(*shape):
    return pl.BlockSpec((SHARE,) + shape, lambda p: (p,) + (0,) * len(shape))


def quarter_columns(rows, third):
    return pl.BlockSpec((rows, SHARE * HEAD_DIM), lambda p: (0, third * QUARTERS + p))


def keys(own, lent, halo, taps, c, b):
    tokens = own.shape[0]
    square = (HEADS, HEAD_DIM, HEAD_DIM)
    return pl.pallas_call(
        keys_kernel,
        grid=(QUARTERS,),
        in_specs=[quarter_columns(rows, i) for rows in (tokens, tokens, halo.shape[0], KW) for i in (0, 1)]
        + [whole(HEADS, tokens)] * 2,
        out_specs=[per_quarter(HEAD_DIM, tokens), per_quarter(tokens, HEAD_DIM), per_quarter(HEAD_DIM, HEAD_DIM)],
        out_shape=[like((HEADS, HEAD_DIM, tokens)), like((HEADS, tokens, HEAD_DIM), bf16), like(square, bf16)],
        cost_estimate=pl.CostEstimate(flops=1, bytes_accessed=1, transcendentals=0),
        name="keys",
    )(own, own, lent, lent, halo, halo, taps, taps, c, b)


def values(spot, own, lent, halo, taps, k, key_states, c, b):
    tokens = own.shape[0]
    return pl.pallas_call(
        values_kernel,
        grid=(QUARTERS,),
        in_specs=[smem()] + [quarter_columns(rows, 0) for rows in (tokens, tokens, halo.shape[0])] + [quarter_columns(KW, 2)]
        + [per_quarter(tokens, HEAD_DIM), per_quarter(HEAD_DIM, HEAD_DIM)] + [whole(HEADS, tokens)] * 2,
        out_specs=[per_quarter(tokens, HEAD_DIM)] + [whole(*MESSAGE)] * QUARTERS,
        out_shape=[like((HEADS, tokens, HEAD_DIM), bf16)] + [like(MESSAGE, bf16)] * QUARTERS,
        cost_estimate=pl.CostEstimate(flops=1, bytes_accessed=1, transcendentals=0),
        name="values",
    )(spot, own, lent, halo, taps, k, key_states, c, b)


def decay_between(indices, decays, low, high):
    total = None
    for index, decay in zip(indices, decays):
        one = jnp.where((index > low) & (index < high), decay, 1.0)
        total = one if total is None else total * one
    return total


def summed(factors, arrays, m):
    total = factors[0] * arrays[0][m, :HEAD_DIM].astype(f32)
    for factor, array in zip(factors[1:], arrays[1:]):
        total = total + factor * array[m, :HEAD_DIM].astype(f32)
    return total


def members(spot, unit, count):
    place = (spot[0] // unit) % count
    return place, [place ^ i for i in range(count)]


def whole_group(indices, arrays, m):
    decays = [decay_of(a, m) for a in arrays]
    count = len(arrays)
    state = summed([decay_between(indices, decays, i, count) for i in indices], arrays, m)
    return state, decay_between(indices, decays, -1, count)


def earlier(place, indices, arrays, m, before):
    decays = [decay_of(a, m) for a in arrays]
    factors = [jnp.where(i < place, decay_between(indices, decays, i, place), 0.0) for i in indices[1:]]
    state = summed(factors, arrays[1:], m)
    decay = decay_between(indices, decays, -1, place)
    if before is None:
        return state, decay
    old = before[m, HEAD_DIM : HEAD_DIM + 1]
    return before[m, :HEAD_DIM] + old * state, old * decay


def group_kernel(spot, *refs):
    arrays, out = refs[:FOUR], refs[FOUR]
    _, indices = members(spot, 1, FOUR)
    for m in range(2 * SHARE):
        state, decay = whole_group(indices, arrays, m)
        out[m, :HEAD_DIM] = state.astype(bf16)
        out[m, HEAD_DIM:] = decay_rows(decay)


def upper_kernel(unit, count, has_before, spot, *refs):
    arrays = refs[:count]
    before = refs[count] if has_before else None
    before_o, total_o = refs[-2:]
    place, indices = members(spot, unit, count)
    for m in range(2 * SHARE):
        state, decay = earlier(place, indices, arrays, m, before)
        before_o[m, :HEAD_DIM] = state
        before_o[m, HEAD_DIM:] = jnp.broadcast_to(decay, (16, HEAD_DIM))
        state, decay = whole_group(indices, arrays, m)
        total_o[m, :HEAD_DIM] = state.astype(bf16)
        total_o[m, HEAD_DIM:] = decay_rows(decay)


def spread_kernel(unit, count, has_before, spot, *refs):
    arrays, near = refs[:count], refs[count : count + FOUR]
    before = refs[count + FOUR] if has_before else None
    outs = refs[-FOUR:]
    place, upper = members(spot, unit, count)
    _, indices = members(spot, 1, FOUR)
    for m in range(2 * SHARE):
        state, _ = earlier(place, upper, arrays, m, before)
        decays = [decay_of(x, m) for x in near]
        for j in range(FOUR):
            at = indices[j]
            factors = [jnp.where(i < at, decay_between(indices, decays, i, at), 0.0) for i in indices]
            total = decay_between(indices, decays, -1, at) * state + summed(factors, near, m)
            outs[j][m] = total.astype(bf16)


def small_call(kernel, name, shapes, spot, *args):
    vmem = pl.BlockSpec(memory_space=pltpu.VMEM)
    return pl.pallas_call(
        kernel,
        in_specs=[smem()] + [vmem] * len(args),
        out_specs=[vmem] * len(shapes),
        out_shape=shapes,
        cost_estimate=pl.CostEstimate(flops=1, bytes_accessed=1, transcendentals=0),
        name=name,
    )(spot, *args)


def neighbour(axis, bit):
    return [(i, i ^ bit) for i in range(lax.axis_size(axis))]


def partner(x, axis, bit=1):
    return lax.ppermute(x, axis, neighbour(axis, bit))


def radices(peers):
    sizes = []
    left = peers // FOUR
    while left > 1:
        sizes.append(min(FOUR, left))
        left //= sizes[-1]
    return sizes


def swapped(arrays, axis, unit_size=1):
    return [arrays[0]] + [partner(a, axis, unit_size * i) for i, a in enumerate(arrays) if i]


class Scan:
    def __init__(self, spot, near, axis):
        self.spot, self.axis, self.near = spot, axis, near
        self.sizes = radices(lax.axis_size(axis))

    def group(self):
        message = like(MESSAGE, bf16)
        (self.total,) = small_call(group_kernel, "group", [message], self.spot, *self.near)
        self.before = ()
        self.unit = FOUR
        for radix in self.sizes[:-1]:
            arrays = swapped([self.total] * radix, self.axis, self.unit)
            kernel = functools.partial(upper_kernel, self.unit, radix, bool(self.before))
            before, self.total = small_call(kernel, "upper", [like(MESSAGE), message], self.spot, *arrays, *self.before)
            self.before = (before,)
            self.unit *= radix
        self.far = swapped([self.total] * self.sizes[-1], self.axis, self.unit)

    def spread(self):
        kernel = functools.partial(spread_kernel, self.unit, self.sizes[-1], bool(self.before))
        self.parts = small_call(
            kernel, "spread", [like(PAIR, bf16)] * FOUR, self.spot, *self.far, *self.near, *self.before
        )
        self.entering = swapped(self.parts, self.axis)
        return self.entering


def prepare(k_ref, c_ref, b_ref, ridge_ref, state_refs, place, left, wide, mask, decay, ridge, pair):
    tokens = k_ref.shape[1]
    for i, state in enumerate(state_refs):
        for m in range(SHARE):
            left[(place ^ i) * SHARE + m, :, :HEAD_DIM] = state[m]
    pair[...] = jnp.zeros_like(pair)
    for h in range(HEADS):
        k = k_ref[h]
        left[h, :, HEAD_DIM:] = k.T
        wide[h // 2, :, cut(h % 2)] = k
        mask[h] = decay_mask(c_ref[h : h + 1, :], b_ref[h : h + 1, :], tokens)
        decay[h] = jnp.broadcast_to(jnp.exp(c_ref[h : h + 1, :]), (8, tokens))
        ridge[h] = column(ridge_ref[h : h + 1, :], (tokens, HEAD_DIM))


def key_products(columns, wide, pair):
    products = []
    for h in range(0, HEADS, 2):
        pair[h // 2, :HEAD_DIM, :HEAD_DIM] = columns(h)
        pair[h // 2, HEAD_DIM:, HEAD_DIM:] = columns(h + 1)
        both = nn(wide[h // 2], pair[h // 2])
        products += [both[:, :HEAD_DIM], both[:, HEAD_DIM:]]
    return products


def solve_kernel(
    place, q_ref, k_ref, s0, s1, s2, s3, c_ref, b_ref, ridge_ref,
    x_out, p_out, m_out, score_out, scal_out,
    left, wide, mask, decay, ridge, pair, x_s, r_s, p_s,
):
    i = pl.program_id(0)

    @pl.when(i == 0)
    def _():
        prepare(k_ref, c_ref, b_ref, ridge_ref, (s0, s1, s2, s3), place[0], left, wide, mask, decay, ridge, pair)
        for h in range(HEADS):
            q = q_ref[h]
            x_s[h] = jnp.zeros_like(q)
            r_s[h] = q
            p_s[h] = q
            scal_out[h, 0:1] = jnp.sum(q * q, axis=0, keepdims=True)

    products = key_products(lambda h: p_s[h].astype(bf16), wide, pair)
    for h in range(HEADS):
        p = p_s[h]
        scores = (products[h] * mask[h]).astype(bf16)
        score_out[0, h] = scores
        stacked = jnp.concatenate([(decay[h, 0:1] * p).astype(bf16), scores], axis=0)
        image = nn(left[h], stacked) + ridge[h] * p
        norm = scal_out[h, pl.ds(i, 1)]
        dot = jnp.sum(p * image, axis=0, keepdims=True)
        size = norm / dot
        p_out[0, h] = p
        m_out[0, h] = image
        scal_out[h, pl.ds(2 * ITERS + i, 1)] = dot
        x_s[h] = x_s[h] + size * p
        r = r_s[h] - size * image
        r_s[h] = r
        norm_next = jnp.sum(r * r, axis=0, keepdims=True)
        scal_out[h, pl.ds(i + 1, 1)] = norm_next
        p_s[h] = r + (norm_next / norm) * p

    @pl.when(i == ITERS - 1)
    def _():
        for h in range(HEADS):
            x_out[h] = x_s[h].astype(bf16)


def common_scratch(tokens):
    square = pltpu.VMEM((HEADS, HEAD_DIM, tokens), f32)
    return [
        pltpu.VMEM((HEADS, HEAD_DIM, HEAD_DIM + tokens), bf16),
        pltpu.VMEM((HEADS // 2, tokens, 2 * HEAD_DIM), bf16),
        pltpu.VMEM((HEADS, tokens, tokens), f32),
        pltpu.VMEM((HEADS, 8, tokens), f32),
        square,
        pltpu.VMEM((HEADS // 2, 2 * HEAD_DIM, 2 * tokens), bf16),
        square, square, square,
    ]


def solve(place, q, k, states, c, b, ridge):
    tokens = q.shape[2]
    step = pl.BlockSpec((1, HEADS, HEAD_DIM, tokens), lambda i: (i, 0, 0, 0))
    steps = (ITERS, HEADS, HEAD_DIM, tokens)
    return pl.pallas_call(
        solve_kernel,
        grid=(ITERS,),
        in_specs=[smem(), whole(HEADS, HEAD_DIM, tokens), whole(HEADS, tokens, HEAD_DIM)] + [whole(*PAIR)] * FOUR
        + [whole(HEADS, tokens)] * 2 + [whole(HEADS, HEAD_DIM)],
        out_specs=[whole(HEADS, HEAD_DIM, tokens), step, step, step, whole(HEADS, 3 * ITERS, tokens)],
        out_shape=[
            like((HEADS, HEAD_DIM, tokens), bf16), like(steps), like(steps), like(steps, bf16),
            like((HEADS, 3 * ITERS, tokens)),
        ],
        scratch_shapes=common_scratch(tokens),
        compiler_params=pltpu.CompilerParams(vmem_limit_bytes=VMEM_LIMIT),
        cost_estimate=pl.CostEstimate(flops=1, bytes_accessed=1, transcendentals=0),
        name="solve",
    )(place, q, k, *states, c, b, ridge)


def attend_back_kernel(place, ga_ref, k_ref, v_ref, x_ref, s0, s1, s2, s3, c_ref, b_ref, gx_o, dk_o, dv_o, state_o):
    quarter = pl.program_id(0)
    tokens = k_ref.shape[1]
    for m in range(SHARE):
        head = quarter * SHARE + m
        c = c_ref[pl.ds(head, 1), :]
        b = b_ref[pl.ds(head, 1), :]
        mask = decay_mask(c, b, tokens)
        e = jnp.exp(c)
        state = s0[SHARE + m]
        for i, other in ((1, s1), (2, s2), (3, s3)):
            state = jnp.where((place[0] ^ i) == quarter, other[SHARE + m], state)
        ga = ga_ref[:, cut(m)].T
        low = ga.astype(bf16)
        x = x_ref[m]
        k = k_ref[m]
        scores = (nn(k, x) * mask).astype(bf16)
        dscores = (nn(v_ref[m], low) * mask).astype(bf16)
        ega = (e * ga).astype(bf16)
        gx_o[m] = tn(state, ega) + tn(k, dscores)
        dv_o[m] = nt(scores, low)
        dk_o[m] = nt(dscores, x)
        state_o[m] = nt(ega, x).astype(bf16)


def attend_back(place, ga, k, v, x, states, c, b):
    tokens = k.shape[1]
    square = like((HEADS, HEAD_DIM, tokens))
    return pl.pallas_call(
        attend_back_kernel,
        grid=(QUARTERS,),
        in_specs=[smem(), quarter_columns(tokens, 0)] + [per_quarter(tokens, HEAD_DIM)] * 2
        + [per_quarter(HEAD_DIM, tokens)] + [whole(*PAIR)] * FOUR + [whole(HEADS, tokens)] * 2,
        out_specs=[per_quarter(HEAD_DIM, tokens)] * 4,
        out_shape=[square] * 3 + [like((HEADS, HEAD_DIM, HEAD_DIM), bf16)],
        cost_estimate=pl.CostEstimate(flops=1, bytes_accessed=1, transcendentals=0),
        name="attend_back",
    )(place, ga, k, v, x, *states, c, b)


def adjoint_kernel(
    spot, place, gx_ref, k_ref, s0, s1, s2, s3, c_ref, b_ref, ridge_ref, p_ref, m_ref, score_ref, scal_ref, values_ref,
    dq_ref, dk_ref, dridge_ref, o0, o1, o2, o3,
    left, wide, mask, decay, ridge, pair, gr_s, gp_s, acc_s, next_s, gnorm_s, low_s, steps_p, steps_g, steps_s, stack,
):
    s = pl.program_id(0)
    i = ITERS - 1 - s
    tokens = k_ref.shape[1]
    at = pl.ds(pl.multiple_of(i * tokens, tokens), tokens)

    @pl.when(s == 0)
    def _():
        prepare(k_ref, c_ref, b_ref, ridge_ref, (s0, s1, s2, s3), place[0], left, wide, mask, decay, ridge, pair)
        gr_s[...] = jnp.zeros_like(gr_s)
        gp_s[...] = jnp.zeros_like(gp_s)
        acc_s[...] = jnp.zeros_like(acc_s)
        next_s[...] = jnp.zeros_like(next_s)
        gnorm_s[...] = jnp.zeros_like(gnorm_s)

    for h in range(HEADS):
        p, m, gx = p_ref[0, h], m_ref[0, h], gx_ref[h]
        norm = scal_ref[h, pl.ds(i, 1)]
        dot = scal_ref[h, pl.ds(2 * ITERS + i, 1)]
        size = norm / dot
        ratio = jnp.where(s == 0, 0.0, scal_ref[h, pl.ds(i + 1, 1)] / norm)
        gp = gp_s[h]
        gratio = jnp.sum(gp * p, axis=0, keepdims=True)
        gnext = gnorm_s[h, 0:1] + gratio / norm
        gr = gr_s[h] + gp + (2.0 * gnext) * (next_s[h] - ratio * p)
        gsize = jnp.sum(gx * p - gr * m, axis=0, keepdims=True)
        gdot = -gsize * size / dot
        gm = gdot * p - size * gr
        gr_s[h] = gr
        gp_s[h] = ratio * gp + size * gx + gdot * m + ridge[h] * gm
        acc_s[h] = acc_s[h] + gm * p
        next_s[h] = p
        gnorm_s[h, 0:1] = gsize / dot - gratio * ratio / norm
        low = gm.astype(bf16)
        low_s[h] = low
        egm = (decay[h, 0:1] * gm).astype(bf16)
        steps_g[h, :, at] = low
        steps_p[h, :, at] = p.astype(bf16)
        steps_s[h, :, at] = score_ref[0, h]
        stack[h, HEAD_DIM:, at] = egm
    products = key_products(lambda h: low_s[h], wide, pair)
    for h in range(HEADS):
        dscores = (products[h] * mask[h]).astype(bf16)
        stack[h, :HEAD_DIM, at] = dscores
        stacked = jnp.concatenate([stack[h, HEAD_DIM:, at], dscores], axis=0)
        gp_s[h] = gp_s[h] + nn(left[h], stacked)

    @pl.when(s == ITERS - 1)
    def _():
        for h in range(HEADS):
            dq_ref[h] = gr_s[h] + gp_s[h] + 2.0 * gnorm_s[h, 0:1] * p_ref[0, h]
            both = nt(steps_p[h], stack[h])
            dk_ref[h] = (nt(steps_g[h], steps_s[h]) + both[:, :HEAD_DIM]).T
            left[h, :, :HEAD_DIM] = both[:, HEAD_DIM:].T.astype(bf16)
            dridge_ref[h] = jnp.sum(acc_s[h].T, axis=0, keepdims=True)
        for j, out in enumerate((o0, o1, o2, o3)):
            for m in range(SHARE):
                head = (position(spot) ^ j) * SHARE + m
                decay = decay_rows(block_decay(c_ref, head))
                out[m, :HEAD_DIM] = left[head, :, :HEAD_DIM]
                out[m, HEAD_DIM:] = decay
                out[SHARE + m, :HEAD_DIM] = values_ref[head]
                out[SHARE + m, HEAD_DIM:] = decay


def adjoint(spot, place, gx, k, states, c, b, ridge, p_all, m_all, scores, scal, value_states):
    tokens = k.shape[1]
    step = pl.BlockSpec((1, HEADS, HEAD_DIM, tokens), lambda s: (ITERS - 1 - s, 0, 0, 0))
    square = pltpu.VMEM((HEADS, HEAD_DIM, tokens), f32)
    line = pltpu.VMEM((HEADS, HEAD_DIM, ITERS * tokens), bf16)
    return pl.pallas_call(
        adjoint_kernel,
        grid=(ITERS,),
        in_specs=[smem(), smem(), whole(HEADS, HEAD_DIM, tokens), whole(HEADS, tokens, HEAD_DIM)] + [whole(*PAIR)] * FOUR
        + [whole(HEADS, tokens)] * 2 + [whole(HEADS, HEAD_DIM), step, step, step, whole(HEADS, 3 * ITERS, tokens), whole(HEADS, HEAD_DIM, HEAD_DIM)],
        out_specs=[whole(HEADS, HEAD_DIM, tokens), whole(HEADS, tokens, HEAD_DIM), whole(HEADS, 1, HEAD_DIM)]
        + [whole(*MESSAGE)] * FOUR,
        out_shape=[like((HEADS, HEAD_DIM, tokens)), like((HEADS, tokens, HEAD_DIM)), like((HEADS, 1, HEAD_DIM))]
        + [like(MESSAGE, bf16)] * FOUR,
        scratch_shapes=common_scratch(tokens) + [
            square,
            pltpu.VMEM((HEADS, 8, tokens), f32),
            pltpu.VMEM((HEADS, HEAD_DIM, tokens), bf16),
            line, line, line,
            pltpu.VMEM((HEADS, 2 * HEAD_DIM, ITERS * tokens), bf16),
        ],
        compiler_params=pltpu.CompilerParams(vmem_limit_bytes=VMEM_LIMIT),
        cost_estimate=pl.CostEstimate(flops=1, bytes_accessed=1, transcendentals=0),
        name="adjoint",
    )(spot, place, gx, k, *states, c, b, ridge, p_all, m_all, scores, scal, value_states)


def conv_forward(own, lent, halo, t):
    total, shifted = conv_parts(with_halo(own, lent, halo), t[...])
    sig = jax.nn.sigmoid(total)
    return shifted, sig * (1.0 + total * (1.0 - sig)), total * sig


def unit_back(act, grad):
    scale = lax.rsqrt(jnp.sum(act * act, axis=-1, keepdims=True) + 1e-06)
    rows = act * scale
    return scale * (grad - rows * jnp.sum(rows * grad, axis=-1, keepdims=True))


def conv_back(dconv, shifted, t, g, dt):
    taps = t[...]
    tokens = dconv.shape[0]
    blank = jnp.zeros((HALO, dconv.shape[1]), f32)
    padded = jnp.concatenate([blank, dconv, blank], axis=0)
    rows = tokens + HALO
    total = taps[KW - 1 : KW] * padded[:rows]
    for j in range(KW - 1):
        total = total + taps[j : j + 1] * padded[KW - 1 - j : KW - 1 - j + rows]
    g[...] = total.astype(bf16)
    dt[...] = jnp.concatenate(
        [jnp.sum(dconv * shifted[j], axis=0, keepdims=True) for j in range(KW)], axis=0
    )


def queries_back_kernel(own, lent, halo, t, dq_ref, g, dt):
    shifted, slope, act = conv_forward(own, lent, halo, t)
    grads = [unit_back(act[:, cut(m)], dq_ref[m].T) for m in range(SHARE)]
    conv_back(jnp.concatenate(grads, axis=1) * slope, shifted, t, g, dt)


def returned(place, quarter, refs, m):
    state = refs[0][m]
    for i in range(1, FOUR):
        state = jnp.where((place ^ i) == quarter, refs[i][m], state)
    return state


def values_back_kernel(spot, own, lent, halo, t, dv_ref, k_ref, r0, r1, r2, r3, c_ref, b_ref, g, dt):
    quarter = pl.program_id(0)
    shifted, slope, _ = conv_forward(own, lent, halo, t)
    grads = []
    for m in range(SHARE):
        rv = returned(position(spot), quarter, (r0, r1, r2, r3), SHARE + m)
        grads.append(dv_ref[m] + ending_of(c_ref, b_ref, quarter * SHARE + m) * nt(k_ref[m], rv))
    conv_back(jnp.concatenate(grads, axis=1) * slope, shifted, t, g, dt)


def keys_back_kernel(
    spot, own, lent, halo, t, dk1, dk2, k_ref, v_ref, r0, r1, r2, r3, c_ref, b_ref, g, dt
):
    quarter = pl.program_id(0)
    shifted, slope, act = conv_forward(own, lent, halo, t)
    grads = []
    for m in range(SHARE):
        rv = returned(position(spot), quarter, (r0, r1, r2, r3), SHARE + m)
        rk = returned(position(spot), quarter, (r0, r1, r2, r3), m).astype(f32)
        rk = (rk + rk.T).astype(bf16)
        ending = ending_of(c_ref, b_ref, quarter * SHARE + m)
        dk = dk1[m] + dk2[m] + ending * (nn(k_ref[m], rk) + nn(v_ref[m], rv))
        grads.append(unit_back(act[:, cut(m)], dk))
    conv_back(jnp.concatenate(grads, axis=1) * slope, shifted, t, g, dt)


def third_back(kernel, name, which, taps_third, projected, taps, before, others, specs):
    own, lent, halo = projected
    tokens = own.shape[0]
    return pl.pallas_call(
        kernel,
        grid=(QUARTERS,),
        in_specs=[smem()] * len(before) + [quarter_columns(rows, which) for rows in (tokens, tokens, halo.shape[0])]
        + [quarter_columns(KW, taps_third)] + specs,
        out_specs=[quarter_columns(tokens + HALO, 0), quarter_columns(KW, 0)],
        out_shape=[like((tokens + HALO, D), bf16), like((KW, D))],
        cost_estimate=pl.CostEstimate(flops=1, bytes_accessed=1, transcendentals=0),
        name=name,
    )(*before, own, lent, halo, taps, *others)


def queries_back(projected, taps, dq):
    return third_back(queries_back_kernel, "queries_back", 0, 0, projected, taps, (), (dq,), [per_quarter(HEAD_DIM, HEAD_DIM)])


def values_back(spot, projected, taps, dv, k, states, c, b):
    square = per_quarter(HEAD_DIM, HEAD_DIM)
    return third_back(
        values_back_kernel, "values_back", 0, 2, projected, taps, (spot,), (dv, k, *states, c, b),
        [square] * 2 + [whole(*PAIR)] * FOUR + [whole(*c.shape)] * 2,
    )


def keys_back(spot, projected, taps, dk1, dk2, k, v, states, c, b):
    square = per_quarter(HEAD_DIM, HEAD_DIM)
    return third_back(
        keys_back_kernel, "keys_back", 1, 1, projected, taps, (spot,), (dk1, dk2, k, v, *states, c, b),
        [square] * 4 + [whole(*PAIR)] * FOUR + [whole(*c.shape)] * 2,
    )


def completed(ref, extra):
    more = extra[...].astype(f32)
    more = jnp.concatenate([jnp.zeros_like(more), more], axis=0)
    last = ref.shape[0] - 16
    return [ref[HALO:last], (ref[last:].astype(f32) + more).astype(bf16)]


def products_kernel(plan, joined, cuts, spot, *refs):
    count = len(plan)
    odd = spot[0] % 2 == 1
    outs, scratch = refs[-count - (1 if joined else 1 + len(cuts)) : -count], refs[-count:]

    @pl.when(pl.program_id(0) == 0)
    def _():
        for (lefts, _, _), both in zip(plan, scratch):
            both[...] = jnp.concatenate([refs[at][...] if rows is None else refs[at][rows] for at, rows in lefts], axis=1)

    start = 0
    def right(at, stacked):
        if not stacked:
            return refs[at][...]
        return jnp.concatenate([refs[at][i : i + stacked] for i in range(0, refs[at].shape[0], stacked)], axis=1)

    for (_, rights, size), both in zip(plan, scratch):
        if len(rights) == 4:
            rows = [part for i in (0, 1) for part in completed(refs[rights[i][0]], refs[rights[2 + i][0]])]
        else:
            rows = [right(*at) for at in rights]
        product = nn(both[...], jnp.concatenate(rows, axis=0))
        at = slice(start, start + size)
        start += size
        if joined:
            outs[0][:, at, :] = product.reshape(product.shape[0] // size, size, product.shape[1]).astype(bf16)
            continue
        blocks = product.reshape(product.shape[0] // (2 * size), 2, size, product.shape[1])
        outs[0][:, at, :] = jnp.where(odd, blocks[:, 1], blocks[:, 0]).astype(bf16)
        other = jnp.where(odd, blocks[:, 0], blocks[:, 1]).astype(bf16)
        for out, cut_at in zip(outs[1:], cuts):
            first, last = max(at.start, cut_at.start), min(at.stop, cut_at.stop)
            if first < last:
                out[:, first - cut_at.start : last - cut_at.start, :] = other[:, first - at.start : last - at.start]


def unstacked(array, index):
    row, tokens = index
    return jnp.concatenate([array[row + i * tokens : row + (i + 1) * tokens] for i in range(D // HEAD_DIM)], axis=1)


def products(spot, peers, lefts, rights, tile, joined=False, messages=1):
    sizes = [(part[0][1].stop - part[0][1].start) // peers for part in lefts]
    width = rights[0][0][0].shape[1] if rights[0][0][1] is None else D
    count, number = (peers, 1) if joined else (peers // 2, 2)
    shape = (count, sum(sizes), width)
    cuts = [slice(i * shape[1] // messages, (i + 1) * shape[1] // messages) for i in range(messages)]
    if any(size % 8 for size in sizes):
        odd = spot[0] % 2
        sides = []
        for side in range(number):
            parts = []
            for left, right in zip(lefts, rights):
                if len(right) == 4:
                    rows = []
                    for i in (0, 1):
                        (array, third), (extra, _) = right[i], right[2 + i]
                        size = array.shape[0] // 3
                        rows += completed(array[third * size : (third + 1) * size], extra[:, third * D : (third + 1) * D])
                else:
                    rows = [unstacked(array, index) if index else array for array, index in right]
                blocks = nn(jnp.concatenate([array[at] for array, at in left], axis=1), jnp.concatenate(rows, axis=0))
                blocks = blocks.astype(bf16).reshape(count, number, -1, width)
                parts.append(lax.dynamic_index_in_dim(blocks, 0 if joined else odd ^ side, 1, keepdims=False))
            sides.append(jnp.concatenate(parts, axis=1))
        return sides if joined else sides[:1] + [sides[1][:, at] for at in cuts]
    arrays, specs, plan = [], [], []

    def place_of(array, spec):
        for at, other in enumerate(arrays):
            if other is array and specs[at] is None and spec is None:
                return at
        arrays.append(array)
        specs.append(spec)
        return len(arrays) - 1

    def columns(array, index):
        if index is None:
            return pl.BlockSpec((array.shape[0], tile), lambda j: (0, j))
        if isinstance(index, int) and array.shape[1] == D:
            return pl.BlockSpec((array.shape[0] // 3, tile), lambda j: (index, j))
        if isinstance(index, int):
            return pl.BlockSpec((array.shape[0], tile), lambda j: (0, index * (D // tile) + j))
        size = index[1] * tile // HEAD_DIM
        return pl.BlockSpec((size, HEAD_DIM), lambda j: (index[0] // size + j, 0))

    def left_part(array, rows):
        size = rows.stop - rows.start
        if rows.start % size:
            return place_of(array, None), rows
        at = rows.start // size
        return place_of(array, pl.BlockSpec((size, array.shape[1]), lambda j: (at, 0))), None

    for left, right, size in zip(lefts, rights, sizes):
        plan.append((
            [left_part(array, rows) for array, rows in left],
            [(place_of(array, columns(array, index)), index[1] if isinstance(index, tuple) else None) for array, index in right],
            size,
        ))
    heights = [shape[1]] + ([] if joined else [at.stop - at.start for at in cuts])
    return pl.pallas_call(
        functools.partial(products_kernel, plan, joined, cuts),
        grid=(width // tile,),
        in_specs=[smem()] + [spec or whole(*array.shape) for array, spec in zip(arrays, specs)],
        out_specs=[pl.BlockSpec((count, height, tile), lambda j: (0, 0, j)) for height in heights],
        out_shape=[like((count, height, width), bf16) for height in heights],
        scratch_shapes=[
            pltpu.VMEM((left[0][1].stop - left[0][1].start, sum(array.shape[1] for array, _ in left)), bf16) for left in lefts
        ],
        compiler_params=pltpu.CompilerParams(vmem_limit_bytes=VMEM_LIMIT),
        cost_estimate=pl.CostEstimate(flops=1, bytes_accessed=1, transcendentals=0),
        name="products",
    )(spot, *arrays)


def lent_kernel(own, peer, extra1, extra2, logit1, logit2, qkv_ref, gate_ref, own_o, theirs_o):
    rows = own_o.shape[0]
    logits = [unstacked(ref, (D // HEAD_DIM * rows, rows)) for ref in (logit1, logit2)]
    total = nt(jnp.concatenate(logits, axis=0), gate_ref[...])
    size = rows + HALO
    for third in range(3):
        at, columns = slice(third * size, (third + 1) * size), slice(third * D, (third + 1) * D)
        both = completed(own.at[at], extra1[:, columns]) + completed(peer.at[at], extra2[:, columns])
        total = total + nt(jnp.concatenate(both, axis=0), qkv_ref[:, columns])
    own_o[...] = total[:rows]
    theirs_o[...] = total[rows:].astype(bf16)


def lent_rows(own, peer, extras, logits, qkv_weight, gate_weight):
    rows = own.shape[0] // 3 - HALO
    half = qkv_weight.shape[0]
    vmem = pl.BlockSpec(memory_space=pltpu.VMEM)
    return pl.pallas_call(
        lent_kernel,
        in_specs=[vmem] * 8,
        out_specs=[vmem] * 2,
        out_shape=[like((rows, half)), like((rows, half), bf16)],
        compiler_params=pltpu.CompilerParams(vmem_limit_bytes=VMEM_LIMIT),
        cost_estimate=pl.CostEstimate(flops=1, bytes_accessed=1, transcendentals=0),
        name="lent_rows",
    )(own, peer, *extras, *logits, qkv_weight, gate_weight)


def norm_back_kernel(place, own, back, tok_ref, gain_ref, hid_ref, tq, tk, tv, second_ref, ridge_ref, tok_o, vec_o):
    mine, other = own[...], back[...].astype(f32)
    grad = jnp.where(
        place[0] == 0, jnp.concatenate([mine, other], axis=1), jnp.concatenate([other, mine], axis=1)
    )
    tokens = tok_ref[...]
    scale = lax.rsqrt(jnp.mean(tokens * tokens, axis=-1, keepdims=True) + 1e-05)
    rows = tokens * scale
    grows = grad * gain_ref[...]
    tok_o[...] = hid_ref[...] + scale * (grows - rows * jnp.mean(grows * rows, axis=-1, keepdims=True))
    vec_o[:KW] = jnp.concatenate([tq[...], tk[...], tv[...]], axis=1)
    ridge = jnp.concatenate([ridge_ref[h] for h in range(HEADS)], axis=1)
    first = jnp.sum(grad * rows, axis=0, keepdims=True)
    vec_o[KW : KW + 1] = jnp.concatenate([first, second_ref[...], ridge], axis=1)
    vec_o[KW + 1 :] = jnp.zeros((8 - KW - 1, 3 * D), f32)


def norm_back(place, own, back, tokens, gain, hidden, taps, second, ridge):
    vmem = pl.BlockSpec(memory_space=pltpu.VMEM)
    return pl.pallas_call(
        norm_back_kernel,
        in_specs=[smem()] + [vmem] * 10,
        out_specs=[vmem] * 2,
        out_shape=[like(tokens.shape), like((8, 3 * D))],
        cost_estimate=pl.CostEstimate(flops=1, bytes_accessed=1, transcendentals=0),
        name="norm_back",
    )(place, own, back, tokens, gain, hidden, *taps, second, ridge)


def step_kernel(bit, kept_mine, kept_other, *refs):
    mine_o, other_o = refs[-2:]
    start = 0
    for mine, other in zip(refs[0:-2:2], refs[1:-2:2]):
        at = slice(start, start + mine.shape[1])
        start += mine.shape[1]
        mine_o[0, at] = (kept_mine[0, at].astype(f32) + mine[0].astype(f32)).astype(bf16)
        other_o[0, at] = (kept_other[0, at].astype(f32) + other[0].astype(f32)).astype(bf16)


def halving_step(bit, below, kept, got):
    count, size, width = kept.shape

    def half(side, rows):
        def index(i, s):
            return ((i // below) * 2 * below + (s[0] if side == 0 else 1 - s[0]) * below + i % below, 0, 0)

        return pl.BlockSpec((1, rows, width), index)

    out = pl.BlockSpec((1, size, width), lambda i, s: (i, 0, 0))
    arrays = [kept] + list(got)
    return pl.pallas_call(
        step_kernel,
        grid_spec=pltpu.PrefetchScalarGridSpec(
            num_scalar_prefetch=1,
            grid=(count // 2,),
            in_specs=[half(side, x.shape[1]) for x in arrays for side in (0, 1)],
            out_specs=[out, out],
        ),
        out_shape=[like((count // 2, size, width), bf16)] * 2,
        cost_estimate=pl.CostEstimate(flops=1, bytes_accessed=1, transcendentals=0),
        name="halving",
    )(bit, *[x for x in arrays for _ in (0, 1)])


BLOCKS = D // HEAD_DIM


def middle_kernel(
    owners, place, x_ref, s0, s1, s2, s3, k_ref, v_ref, c_ref, b_ref, own_logit, lent_logit, tok_ref, cot_ref, gain_ref, first_ref,
    own_out, out_a, out_b, out_c, out_d, *refs,
):
    own_up = refs[:4]
    up_parts = (refs[4:8], refs[8:12])
    own_down = refs[12]
    down_parts = refs[13:17]
    (out_o, hid_o, gatt_o, own_o, sent_o, ggu_o, dgain_o) = refs[17:24]
    out_s, up_s, down_s, nf_s, gb_s, att_s, sig_s, hid_s, acc_s, gnf_s, inner_s = refs[24:]
    j = pl.program_id(0)
    y = place[0]
    half = D // 2

    def aligned(at, by):
        return pl.multiple_of(at, by)

    mine = pl.ds(aligned(y * half, half), half)
    theirs = pl.ds(aligned((1 - y) * half, half), half)

    def order(q):
        return [q, q ^ 2, q ^ 1, q ^ 3]

    tile = own_up[0].shape[1]
    tokens = tok_ref.shape[0]

    def spread_rows(rows, start):
        total = rows.shape[0]
        size = total // owners
        own_at = slice(start, start + total // 2)
        sent_at = slice(3 * BLOCKS * tokens + start, 3 * BLOCKS * tokens + start + total // 2)
        if size % 8:
            own_o[own_at], sent_o[sent_at] = rows[: total // 2].astype(bf16), rows[total // 2 :].astype(bf16)
            return
        blocks = rows.reshape(owners // 2, 2, size, rows.shape[1])
        for out, at, odd in ((own_o, own_at, y == 1), (sent_o, sent_at, y == 0)):
            out[at] = jnp.where(odd, blocks[:, 1], blocks[:, 0]).reshape(total // 2, rows.shape[1]).astype(bf16)

    def stack_right(value, index):
        for i in range(BLOCKS):
            sent_o[(index * BLOCKS + i) * tokens : (index * BLOCKS + i + 1) * tokens] = value[:, cut(i)]

    def scale_of(hidden):
        return lax.rsqrt(jnp.mean(hidden * hidden, axis=-1, keepdims=True) + 1e-05)

    @pl.when(j == 0)
    def _():
        for i, state in enumerate((s0, s1, s2, s3)):
            for m in range(SHARE):
                head = (place[1] ^ i) * SHARE + m
                c = c_ref[pl.ds(head, 1), :]
                b = b_ref[pl.ds(head, 1), :]
                x = x_ref[head]
                scores = (nn(k_ref[head], x) * decay_mask(c, b, tokens)).astype(bf16)
                part = jnp.exp(c) * nn(state[SHARE + m], x) + tn(v_ref[head], scores)
                att_s[:, pl.ds(aligned(head * HEAD_DIM, HEAD_DIM), HEAD_DIM)] = part.T
        out_s[mine, :] = own_out[...]
        wide = out_a.shape[1]
        for part, q in zip((out_a, out_b, out_c, out_d), order(place[1])):
            out_s[theirs, pl.ds(aligned(q * wide, wide), wide)] = part[...]
        sig = jax.nn.sigmoid(own_logit[...] + lent_logit[...].astype(f32))
        sig_s[...] = sig
        mix = (att_s[...] * sig).astype(bf16)
        spread_rows(mix.astype(f32).T, half)
        normed = tok_ref[...] * scale_of(tok_ref[...]) * first_ref[...]
        spread_rows(normed.astype(bf16).astype(f32).T, 2 * half)
        hidden = tok_ref[...] + nn(mix, out_s[...])
        hid_s[...] = hidden
        normed = (hidden * scale_of(hidden) * gain_ref[...]).astype(bf16)
        nf_s[...] = normed
        spread_rows(normed.astype(f32).T, 0)
        gb_s[...] = cot_ref[...].astype(bf16)
        stack_right(gb_s[...], 2)
        acc_s[...] = jnp.zeros_like(acc_s)
        gnf_s[...] = jnp.zeros_like(gnf_s)

    for i in range(4):
        up_s[mine, i * tile : (i + 1) * tile] = own_up[i][...]
    start = 0
    for parts, q0 in zip(up_parts, (place[2], place[1])):
        count = parts[0].shape[0]
        at = pl.ds(aligned((1 - y) * half + start, 16), count)
        for part, q in zip(parts, order(q0)):
            slot = (q >> 1) * 2 + ((q & 1) ^ y)
            up_s[at, pl.ds(aligned(slot * tile, tile), tile)] = part[...]
        start += count
    down_s[:tile, :] = own_down[...]
    wide = down_parts[0].shape[1]
    for part, q in zip(down_parts, order(place[1])):
        down_s[tile:, pl.ds(aligned(q * wide, wide), wide)] = part[...]
    product = nn(nf_s[...], up_s[...])
    gate, up = product[:, : 2 * tile], product[:, 2 * tile :]
    ginner = nt(gb_s[...], down_s[...])
    sig = jax.nn.sigmoid(gate)
    silu = gate * sig
    inner = (silu * up).astype(bf16)
    ggate = (ginner * up * (sig * (1.0 + gate * (1.0 - sig)))).astype(bf16)
    gup = (ginner * silu).astype(bf16)
    ggu = jnp.concatenate([ggate, gup], axis=1)
    acc_s[...] += nn(inner, down_s[...])
    gnf_s[...] += nt(ggu, up_s[...])
    inner_t = inner.astype(f32).T
    for slot, value in ((y, inner_t[:tile]), (1 - y, inner_t[tile:])):
        inner_s[pl.ds(aligned(slot * (FF // 2) + j * tile, tile), tile), :] = value
    share = FF // 2
    for i, (slot, value) in enumerate(((y, ggate), (1 - y, ggate), (2 + y, gup), (3 - y, gup))):
        at = pl.ds(aligned(slot * share + j * tile, tile), tile)
        ggu_o[:, at] = value[:, (i % 2) * tile : (i % 2 + 1) * tile]

    @pl.when(j == pl.num_programs(0) - 1)
    def _():
        spread_rows(inner_s[...], 3 * half)
        hidden = hid_s[...]
        out_o[...] = hidden + acc_s[...]
        scale = scale_of(hidden)
        rows = hidden * scale
        gnf = gnf_s[...]
        dgain_o[...] = jnp.sum(gnf * rows, axis=0, keepdims=True)
        grows = gnf * gain_ref[...]
        ghid = cot_ref[...] + scale * (grows - rows * jnp.mean(grows * rows, axis=-1, keepdims=True))
        hid_o[...] = ghid
        low = ghid.astype(bf16)
        stack_right(low, 0)
        gmix = nt(low, out_s[...])
        sig = sig_s[...]
        gatt = gmix * sig
        gatt_o[...] = gatt
        stack_right((gatt * att_s[...] * (1.0 - sig)).astype(bf16), 1)


def middle(owners, place, attention, own_logit, lent_logit, tok, cot, gain, gain_first, out_weight, up_weight, down_weight, up_parts, rest_parts):
    tokens = tok.shape[0]
    tile = 128
    share = FF // 2 // tile
    half = D // 2
    left_rows = 3 * half + FF // 2

    def full(*shape):
        return pl.BlockSpec(shape, lambda j, s: (0,) * len(shape))

    rows = full(tokens, D)
    own_up = [
        pl.BlockSpec((half, tile), lambda j, s: (0, s[0] * share + j)),
        pl.BlockSpec((half, tile), lambda j, s: (0, (1 - s[0]) * share + j)),
        pl.BlockSpec((half, tile), lambda j, s: (0, (2 + s[0]) * share + j)),
        pl.BlockSpec((half, tile), lambda j, s: (0, (3 - s[0]) * share + j)),
    ]
    up_specs = [pl.BlockSpec((p.shape[0], tile), lambda j, s: (0, j)) for p in up_parts]
    own_down = pl.BlockSpec((tile, D), lambda j, s: (j, 0))
    down_specs = [pl.BlockSpec((tile, D // 4), lambda j, s: (half // tile + j, 0))] * 4
    square = (HEAD_DIM, HEAD_DIM)
    return pl.pallas_call(
        functools.partial(middle_kernel, owners),
        grid_spec=pltpu.PrefetchScalarGridSpec(
            num_scalar_prefetch=1,
            grid=(share,),
            in_specs=[full(HEADS, HEAD_DIM, tokens)] + [full(*PAIR)] * FOUR + [full(HEADS, tokens, HEAD_DIM)] * 2
            + [full(HEADS, tokens)] * 2
            + [rows, pl.BlockSpec((tokens, D), lambda j, s: (0, 1))]
            + [rows] * 2 + [full(1, D), full(1, D), full(half, D)] + [full(half, D // 4)] * 4
            + own_up + up_specs + [own_down] + down_specs,
            out_specs=[
                rows, rows, rows, full(left_rows, tokens), full(3 * BLOCKS * tokens + left_rows, tokens),
                full(tokens, 2 * FF),
                full(1, D),
            ],
            scratch_shapes=[
                pltpu.VMEM((D, D), bf16),
                pltpu.VMEM((D, 4 * tile), bf16),
                pltpu.VMEM((2 * tile, D), bf16),
                pltpu.VMEM((tokens, D), bf16),
                pltpu.VMEM((tokens, D), bf16),
                pltpu.VMEM((tokens, D), f32),
                pltpu.VMEM((tokens, D), f32),
                pltpu.VMEM((tokens, D), f32),
                pltpu.VMEM((tokens, D), f32),
                pltpu.VMEM((tokens, D), f32),
                pltpu.VMEM((FF, tokens), f32),
            ],
        ),
        out_shape=[
            like((tokens, D)), like((tokens, D)), like((tokens, D)),
            like((left_rows, tokens), bf16), like((3 * BLOCKS * tokens + left_rows, tokens), bf16),
            like((tokens, 2 * FF), bf16),
            like((1, D)),
        ],
        compiler_params=pltpu.CompilerParams(vmem_limit_bytes=VMEM_LIMIT),
        cost_estimate=pl.CostEstimate(flops=1, bytes_accessed=1, transcendentals=0),
        name="middle",
    )(
        place, *attention, own_logit, lent_logit, tok, cot, gain, gain_first, out_weight, *rest_parts,
        *[up_weight] * 4, *up_parts, down_weight, *rest_parts,
    )


def shifted(x, axis, by):
    peers = lax.axis_size(axis)
    return lax.ppermute(x, axis, [(i, i + by) for i in range(peers) if 0 <= i + by < peers])


def crossed(x, by):
    peers, pair = lax.axis_size("ctx"), 2
    return lax.ppermute(
        x,
        ("ctx", "fsdp"),
        [(i * pair + s, (i + by) * pair + 1 - s) for i in range(peers) if 0 <= i + by < peers for s in range(pair)],
    )


def pick(x, index, axis=0):
    return lax.dynamic_index_in_dim(x, index, axis, keepdims=False)


def part(x, index, axis):
    size = x.shape[axis] // 2
    return lax.dynamic_slice_in_dim(x, index * size, size, axis)


def quarter(shard, q, start=0, count=None):
    wide = shard.shape[1] // 4
    return lax.dynamic_slice(shard, (start, q * wide), (count or shard.shape[0], wide))


class Reduction:
    def __init__(self, order, blocks):
        self.here = lax.axis_index("ctx")
        levels = lax.axis_size("ctx").bit_length() - 1
        self.order = list(order) + [level for level in range(levels) if level not in order]
        self.left = list(range(levels))
        self.kept, *sent = blocks
        self.send(sent)

    def bit(self):
        return (self.here >> self.order[0]) & 1

    def send(self, arrays):
        level = self.order.pop(0)
        self.left.remove(level)
        self.got = [partner(array, "ctx", 1 << level) for array in arrays]

    def step(self):
        below = 1 << self.left.index(self.order[0])
        self.kept, sent = halving_step(self.bit().astype(jnp.int32)[None], below, self.kept, self.got)
        self.send([sent])
        return sent

    def result(self, sizes):
        while self.order:
            self.step()
        total = (self.kept.astype(f32) + self.got[0].astype(f32))[0]
        ends = [sum(sizes[: i + 1]) for i in range(len(sizes))]
        return [total[end - size : end] for end, size in zip(ends, sizes)]


class Sequence:
    def __init__(self):
        self.last = ()

    def gate(self, *values):
        return lax.optimization_barrier(values + self.last)[: len(values)]

    def mark(self, *values):
        self.last = values


def added(value, axis):
    for level in range(lax.axis_size(axis).bit_length() - 1):
        value = value + partner(value, axis, 1 << level)
    return value


def rms_scale(values, gain):
    return values * lax.rsqrt(jnp.mean(values * values, axis=-1, keepdims=True) + 1e-05) * gain


def sided(mine, theirs, y, axis):
    return jnp.where(
        y == 0, jnp.concatenate([mine, theirs], axis=axis), jnp.concatenate([theirs, mine], axis=axis)
    )


UP_ROWS = (0, 320, 512)


def local(
    inputs,
    qkv_weight,
    gate_weight,
    out_weight,
    up_weight,
    down_weight,
    conv_taps,
    gain_attn,
    gain_ffn,
    ridge_terms,
    forget,
    cotangent,
):
    tokens = inputs[0]
    rows = tokens.shape[0]
    y = lax.axis_index("fsdp")
    here = lax.axis_index("ctx")
    peers = lax.axis_size("ctx")
    owners = peers * 2
    near_x = here % 4
    near_z = here % 2 + 2 * ((here // 4) % 2)
    place = jnp.stack([y, near_x, near_z]).astype(jnp.int32)
    spot = here.astype(jnp.int32)[None]
    spot_back = (peers - 1 - here).astype(jnp.int32)[None]
    ring = near_x.astype(jnp.int32)[None]
    seq = Sequence()

    lines = jnp.stack([gain_attn, gain_ffn, ridge_terms, ridge_terms])
    mine, theirs = norm(place, tokens, conv_taps, lines)
    theirs = partner(theirs, "fsdp")
    gain_mine = gain_attn.astype(f32)
    peer_extra, left_theirs = lax.optimization_barrier((theirs[rows:], (theirs[:rows] * gain_mine).astype(bf16)))
    lent_qk = nn(left_theirs, qkv_weight[:, : 2 * D]).astype(bf16)
    seq.mark(lent_qk)
    lent_qk = partner(lent_qk, "fsdp")
    (left,) = seq.gate(left_theirs)
    lent_v = jnp.concatenate([nn(left, qkv_weight[:, 2 * D :]).astype(bf16), nn(left, gate_weight).astype(bf16)], axis=1)
    seq.mark(lent_v)
    lent_v = partner(lent_v, "fsdp")
    (left,) = seq.gate(mine)
    own_qk = nn(left, qkv_weight[:, : 2 * D])
    own_v = nn(left, qkv_weight[:, 2 * D :])
    own_gate = nn(left, gate_weight)
    (peer_extra,) = seq.gate(peer_extra)
    taps_rows = KW * 3
    vectors = sided(lines[:3].astype(f32), peer_extra[taps_rows : taps_rows + 3], y, 1)
    taps = sided(conv_taps.astype(f32), peer_extra[:taps_rows].reshape(conv_taps.shape), y, 1)
    gain_first, gain_second = vectors[0], vectors[1:2]
    ridge = vectors[2].reshape(HEADS, HEAD_DIM)
    cumulative = jnp.cumsum(jnp.log(forget[0]).T, axis=-1)
    strength = (1.0 - forget[0]).T
    out_here, up_here, down_here = seq.gate(out_weight, up_weight, down_weight)
    rest_quarter = jnp.concatenate([quarter(out_here, near_x), quarter(down_here, near_x)], axis=0)
    seq.mark(own_qk, own_v, own_gate, rest_quarter, taps, cumulative, strength)
    rest_direct = partner(rest_quarter, "fsdp")
    (up_here,) = seq.gate(up_here)
    up_quarters = [
        quarter(up_here, near, start, stop - start)
        for near, start, stop in zip((near_z, near_x), UP_ROWS, UP_ROWS[1:])
    ]
    seq.mark(*up_quarters)

    own_qk, lent_qk = seq.gate(own_qk, lent_qk)

    def halo_of(own, lent):
        return shifted((own[rows - 8 :] + lent[rows - 8 :].astype(f32)).astype(bf16), "ctx", 1)

    halo_qk = halo_of(own_qk, lent_qk)
    queries, keys_low, key_states = keys(own_qk, lent_qk, halo_qk, taps, cumulative, strength)
    seq.mark(key_states)
    own_v, lent_v, up_first = seq.gate(own_v, lent_v, up_quarters[0])
    halo_v = halo_of(own_v, lent_v[:, :D])
    values_low, *own = values(spot, own_v, lent_v, halo_v, taps, keys_low, key_states, cumulative, strength)
    seq.mark(*own)
    scan = Scan(spot, swapped(own, "ctx"), "ctx")
    up_first = partner(up_first, "fsdp")

    def split(left):
        flat = left.reshape(peers, 2, left.shape[0] // owners, left.shape[1])
        return [pick(flat, side, 1).reshape(-1, left.shape[1]) for side in (y, 1 - y)]

    scan.near = list(seq.gate(*scan.near))
    scan.group()
    seq.mark(scan.total)
    (rest_direct,) = seq.gate(rest_direct)
    rest_across = partner(rest_direct, "ctx", 2)
    scan.far = list(seq.gate(*scan.far))
    states = scan.spread()
    seq.mark(scan.parts[0])
    up_first, up_second = seq.gate(up_first, up_quarters[1])
    up_second = partner(up_second, "fsdp")
    first_across = partner(up_first, "ctx", 4)
    *states, queries = seq.gate(*states, queries)
    seq.mark(states[1], states[2], states[3])
    rest_direct, rest_across, up_first, up_second = seq.gate(rest_direct, rest_across, up_first, up_second)
    second_across = partner(up_second, "ctx", 2)
    rest_core, rest_far, first_core = partner(rest_direct, "ctx", 1), partner(rest_across, "ctx", 1), partner(up_first, "ctx", 1)
    (queries,) = seq.gate(queries)
    x, p_all, m_all, scores, scal = solve(ring, queries, keys_low, states, cumulative, strength, ridge)
    seq.mark(x)

    def share(right):
        return right, partner(right, "fsdp")

    def below(pair):
        return jnp.concatenate(pair, axis=0)

    rest_core, rest_far, first_core, first_across, up_second, second_across = seq.gate(
        rest_core, rest_far, first_core, first_across, up_second, second_across
    )
    rest_parts = (rest_direct, rest_across, rest_core, rest_far)
    up_parts = (up_first, first_across, first_core, partner(first_across, "ctx", 1))
    up_parts += (up_second, second_across, partner(up_second, "ctx", 1), partner(second_across, "ctx", 1))

    output, grad_hidden, grad_attended, lefts, message, grad_gate_up, grad_second_gain = middle(
        owners, place, (x, *states, keys_low, values_low, cumulative, strength), own_gate, lent_v,
        tokens, cotangent[0], gain_second, gain_first[None], out_weight, up_weight, down_weight, up_parts, rest_parts
    )
    size = D // 2
    parts = [slice(0, size), slice(size, 2 * size), slice(2 * size, 3 * size), slice(3 * size, 3 * size + FF // 2)]
    start = 3 * BLOCKS * rows
    peer_parts = [slice(start + at.start, start + at.stop) for at in parts]
    if (D // owners) % 8 or (FF // owners) % 8:
        pairs = [split(jnp.concatenate([lefts[at], message[there]], axis=0)) for at, there in zip(parts, peer_parts)]
        lefts = jnp.concatenate([own for own, _ in pairs], axis=0)
        message = jnp.concatenate([message[:start]] + [sent for _, sent in pairs], axis=0)
    seq.mark(grad_second_gain)
    message_peer = partner(message, "fsdp")
    (grad_attended,) = seq.gate(grad_attended)
    gx, dk_attend, dv, value_states = attend_back(
        ring, grad_attended, keys_low, values_low, x, states, cumulative, strength
    )
    dq, dk_solve, grad_ridge, *own = adjoint(
        spot_back, ring, gx, keys_low, states, cumulative, strength, ridge, p_all, m_all, scores, scal, value_states
    )
    seq.mark(*own)
    back = Scan(spot_back, swapped(own, "ctx"), "ctx")
    (up_here,) = seq.gate(grad_gate_up)
    both_up = share(up_here)
    dq, back.near[1] = seq.gate(dq, back.near[1])
    low_q, taps_q = queries_back((own_qk, lent_qk, halo_qk), taps, dq)
    seq.mark(low_q)
    back.near = list(seq.gate(*back.near))
    back.group()
    seq.mark(back.total)
    lefts_here, message_peer, back.far[1] = seq.gate(lefts, message_peer, back.far[1])
    rights = [(i * BLOCKS * rows, rows) for i in range(3)]
    (early,) = products(
        spot, peers, [[(lefts_here, parts[i]), (message_peer, peer_parts[i])] for i in (1, 2, 3)],
        [[(message, at), (message_peer, at)] for at in rights], 256, joined=True
    )
    seq.mark(early)
    early = lax.psum_scatter(early.reshape(-1, D), "ctx", scatter_dimension=0, tiled=True)
    back.far = list(seq.gate(*back.far))
    states_back = back.spread()
    seq.mark(back.parts[0])
    dv, *states_back = seq.gate(dv, *states_back)
    low_v, taps_v = values_back(
        spot_back, (own_v, lent_v, halo_v), taps, dv, keys_low, states_back, cumulative, strength
    )
    seq.mark(low_v)
    (dk_attend,) = seq.gate(dk_attend)
    low_k, taps_k = keys_back(
        spot_back, (own_qk, lent_qk, halo_qk), taps, dk_attend, dk_solve, keys_low, values_low, states_back, cumulative, strength
    )
    seq.mark(low_k)
    ahead = jnp.concatenate([low[HALO - 8 : HALO] for low in (low_q, low_k, low_v)], axis=1)
    extra = shifted(ahead, "ctx", -1), crossed(ahead, -1)
    thirds = jnp.concatenate([low_q, low_k, low_v], axis=0)
    seq.mark(thirds)
    thirds_peer = partner(thirds, "fsdp")
    up_peer, *extra = seq.gate(both_up[1], *extra)
    blocks = products(
        spot, peers, [[(lefts, parts[0]), (message_peer, peer_parts[0])]], [[(both_up[0], None), (up_peer, None)]], 512
    )
    seq.mark(blocks[0])
    ups = Reduction((0, 1, 2), blocks)
    ups.got = seq.gate(*ups.got)
    seq.mark(ups.step())
    lefts_here, thirds_peer = seq.gate(lefts, thirds_peer)
    left = [(lefts_here, parts[2]), (message_peer, peer_parts[2])]
    rights = [[(thirds, i), (thirds_peer, i), (extra[0], i), (extra[1], i)] for i in range(3)]
    blocks = products(spot, peers, [left] * 3, rights, 256, messages=2)
    seq.mark(blocks[0])
    late = Reduction((0, 1, 2), blocks)
    late.got = seq.gate(*late.got)
    seq.mark(late.step())
    ups.got = seq.gate(*ups.got)
    seq.mark(ups.step())
    (thirds_here,) = seq.gate(thirds)
    kept, lent = lent_rows(thirds_here, thirds_peer, extra, (message, message_peer), qkv_weight, gate_weight)
    seq.mark(lent)
    arriving = partner(lent, "fsdp")
    late.got = seq.gate(*late.got)
    seq.mark(late.step())
    (arriving,) = seq.gate(arriving)
    grad_tokens, vector = norm_back(
        place, kept, arriving, tokens, gain_first[None], grad_hidden, (taps_q, taps_k, taps_v), grad_second_gain, grad_ridge
    )
    seq.mark(vector)
    size, width = D // owners, 3 * D // owners
    vector = jnp.concatenate(
        [vector[:KW].reshape(KW, owners, width).transpose(1, 0, 2).reshape(owners, KW * width),
         vector[KW].reshape(3, owners, size).transpose(1, 0, 2).reshape(owners, 3 * size)], axis=1
    ).reshape(peers, 2, KW * width + 3 * size)
    vector_kept, vector_sent = pick(vector, y, 1), pick(vector, 1 - y, 1)
    seq.mark(vector_sent)
    arriving = partner(vector_sent, "fsdp")
    *ups.got, early = seq.gate(*ups.got, early)
    seq.mark(ups.step())
    vector_kept, arriving = seq.gate(vector_kept, arriving)
    vector = vector_kept + arriving
    seq.mark(vector)
    vector = lax.all_to_all(vector, "ctx", 0, 0, tiled=True)
    late.got = seq.gate(*late.got)
    seq.mark(late.step())
    vector = jnp.sum(seq.gate(vector)[0], axis=0)
    size = D // owners
    grad_up = ups.result([size])[0]
    grad_q, grad_k, grad_v = late.result([size] * 3)
    grad_qkv = jnp.concatenate([grad_q, grad_k, grad_v], axis=1)
    early = early.astype(f32)
    grad_out, grad_gate, grad_down = early[:size], early[size : 2 * size], early[2 * size :]
    return (
        output[None],
        grad_tokens[None],
        grad_qkv,
        grad_gate,
        grad_out,
        grad_up,
        grad_down,
        vector[: KW * width].reshape(KW, width),
        vector[KW * width : KW * width + size],
        vector[KW * width + size : KW * width + 2 * size],
        vector[KW * width + 2 * size :],
    )


def solution(mesh):
    tokens = P("fsdp", "ctx", None)
    rows = P("fsdp", None)
    vector = P("fsdp")
    owned = P(("ctx", "fsdp"), None)
    owned_vector = P(("ctx", "fsdp"))
    return jax.shard_map(
        local,
        mesh=mesh,
        in_specs=(
            tokens, rows, rows, rows, rows, rows, P(None, "fsdp"), vector, vector, vector, tokens, tokens,
        ),
        out_specs=(
            tokens, tokens, owned, owned, owned, owned, owned, P(None, ("ctx", "fsdp")),
            owned_vector, owned_vector, owned_vector,
        ),
        check_vma=False,
    )
```

```python
import functools
import jax
import jax.numpy as jnp
from jax import lax
from jax.experimental import pallas as pl
from jax.experimental.pallas import tpu as pltpu
from jax.sharding import PartitionSpec as P

D = 1024
HEADS = 8
FF = 2816
KW = 4
ITERS = 8
HEAD_DIM = 128
QUARTERS = 4
SHARE = HEADS // QUARTERS
HALO = 16

f32 = jnp.float32
bf16 = jnp.bfloat16
VMEM_LIMIT = 56 * 1024 * 1024


def nn(a, b):
    return lax.dot_general(a, b, (((1,), (0,)), ((), ())), preferred_element_type=f32)


def nt(a, b):
    return lax.dot_general(a, b, (((1,), (1,)), ((), ())), preferred_element_type=f32)


def tn(a, b):
    return lax.dot_general(a, b, (((0,), (0,)), ((), ())), preferred_element_type=f32)


def column(row, like):
    return jnp.broadcast_to(row, like).T


def decay_mask(c, b, tokens):
    shape = (tokens, tokens)
    late = lax.broadcasted_iota(jnp.int32, shape, 1) >= lax.broadcasted_iota(jnp.int32, shape, 0)
    spread = jnp.broadcast_to(c, shape) - column(c, shape)
    return jnp.where(late, jnp.exp(jnp.where(late, spread, 0.0)), 0.0) * column(b, shape)


def like(shape, kind=f32):
    return jax.ShapeDtypeStruct(shape, kind)


def smem():
    return pl.BlockSpec(memory_space=pltpu.SMEM)


EXTRA = 16


def norm_kernel(place, tok_ref, taps_ref, lines_ref, mine_o, theirs_o):
    half = D // 2
    y = place[0]
    a = tok_ref[...]
    unit = a * lax.rsqrt(jnp.mean(a * a, axis=-1, keepdims=True) + 1e-05)
    left, right = unit[:, :half], unit[:, half:]
    rows = a.shape[0]
    gain = lines_ref[0:1].astype(f32)
    mine_o[...] = (jnp.where(y == 0, left, right) * gain).astype(bf16)
    theirs_o[:rows] = jnp.where(y == 0, right, left)
    taps = taps_ref[...].astype(f32)
    lines = [taps[t : t + 1, i * half : (i + 1) * half] for t in range(KW) for i in range(3)]
    theirs_o[rows:] = jnp.concatenate(lines + [lines_ref[...].astype(f32)], axis=0)


def norm(place, tokens, taps, lines):
    rows = tokens.shape[0]
    vmem = pl.BlockSpec(memory_space=pltpu.VMEM)
    return pl.pallas_call(
        norm_kernel,
        in_specs=[smem()] + [vmem] * 3,
        out_specs=[vmem, vmem],
        out_shape=[like((rows, D // 2), bf16), like((rows + EXTRA, D // 2))],
        name="norm",
    )(place, tokens, taps, lines)


def weigh_kernel(scaled, left_ref, gain_ref, qkv_ref, gate_ref, out, left):
    j = pl.program_id(0)

    @pl.when(j == 0)
    def _():
        rows = left_ref[: left.shape[0]]
        left[...] = (rows * gain_ref[...].astype(f32)).astype(bf16) if scaled else rows

    steps = 3 * D // out.shape[1]

    @pl.when(j < steps)
    def _():
        out[...] = nn(left[...], qkv_ref[...]).astype(out.dtype)

    @pl.when(j >= steps)
    def _():
        out[...] = nn(left[...], gate_ref[...]).astype(out.dtype)


def weigh(left, rows, gain, qkv_weight, gate_weight, kind):
    half = left.shape[1]
    tile = 1024
    steps = 3 * D // tile
    return pl.pallas_call(
        functools.partial(weigh_kernel, left.dtype == f32),
        grid=(4 * D // tile,),
        in_specs=[
            whole(*left.shape), whole(1, half),
            pl.BlockSpec((half, tile), lambda j: (0, jnp.minimum(j, steps - 1))),
            pl.BlockSpec((half, tile), lambda j: (0, jnp.maximum(j - steps, 0))),
        ],
        out_specs=pl.BlockSpec((rows, tile), lambda j: (0, j)),
        out_shape=like((rows, 4 * D), kind),
        scratch_shapes=[pltpu.VMEM((rows, half), bf16)],
        cost_estimate=pl.CostEstimate(flops=1, bytes_accessed=1, transcendentals=0),
        name="weigh",
    )(left, gain, qkv_weight, gate_weight)


def tables_kernel(c_ref, b_ref, ridge_ref, mask_o, ending_o, ridge_o):
    tokens = c_ref.shape[1]
    head = pl.program_id(0)
    c, b = c_ref[pl.ds(head, 1), :], b_ref[pl.ds(head, 1), :]
    mask_o[0] = decay_mask(c, b, tokens)
    ending_o[0] = column(jnp.exp(c[:, tokens - 1 :] - c) * b, (HEAD_DIM, tokens))
    ridge_o[0] = column(ridge_ref[pl.ds(head, 1), :], (tokens, HEAD_DIM))


def tables(c, b, ridge):
    tokens = c.shape[1]
    shapes = [(tokens, tokens), (tokens, HEAD_DIM), (HEAD_DIM, tokens)]
    return pl.pallas_call(
        tables_kernel,
        grid=(HEADS,),
        in_specs=[whole(HEADS, tokens)] * 2 + [whole(HEADS, HEAD_DIM)],
        out_specs=[pl.BlockSpec((1,) + shape, lambda h: (h, 0, 0)) for shape in shapes],
        out_shape=[like((HEADS,) + shape) for shape in shapes],
        cost_estimate=pl.CostEstimate(flops=1, bytes_accessed=1, transcendentals=0),
        name="tables",
    )(c, b, ridge)


def with_halo(own, lent, halo):
    before = halo[...].astype(f32)
    blank = jnp.zeros((HALO - before.shape[0], before.shape[1]), f32)
    return jnp.concatenate([blank, before, own[...] + lent[...].astype(f32)], axis=0)


def conv_parts(padded, taps):
    rows = padded.shape[0] - HALO
    shifted = [padded[HALO - KW + 1 + j : HALO - KW + 1 + j + rows] for j in range(KW)]
    total = taps[0:1] * shifted[0]
    for j in range(1, KW):
        total = total + taps[j : j + 1] * shifted[j]
    return total, shifted


def unit(a):
    return a * lax.rsqrt(jnp.sum(a * a, axis=-1, keepdims=True) + 1e-06)


def position(spot):
    return spot[0] % FOUR


FOUR = 4
PAIR = (2 * SHARE, HEAD_DIM, HEAD_DIM)
MESSAGE = (2 * SHARE, HEAD_DIM + 16, HEAD_DIM)


def decay_rows(decay):
    shape = (16, HEAD_DIM)
    at = lax.broadcasted_iota(jnp.int32, shape, 0)
    decay = jnp.broadcast_to(decay, shape)
    high = decay.astype(bf16).astype(f32)
    return jnp.where(at == 0, high, jnp.where(at == 1, decay - high, 0.0)).astype(bf16)


def decay_of(message, m):
    rows = message[m, HEAD_DIM:].astype(f32)
    return rows[0:1] + rows[1:2]


def block_decay(c_ref, head):
    c = c_ref[pl.ds(head, 1), :]
    return jnp.broadcast_to(jnp.exp(c[:, c.shape[1] - 1 :]), (1, HEAD_DIM))


def store_quarter(spot, quarter, outs, states, c_ref):
    rows = [decay_rows(block_decay(c_ref, quarter * SHARE + m)) for m in range(SHARE)]
    for i, out in enumerate(outs):

        @pl.when((position(spot) ^ i) == quarter)
        def _():
            for m in range(2 * SHARE):
                out[m, :HEAD_DIM] = states[m]
                out[m, HEAD_DIM:] = rows[m % SHARE]


def cut(h):
    return slice(h * HEAD_DIM, (h + 1) * HEAD_DIM)


def features_kernel(
    spot, oq, ok, ov, lq, lk, lv, hq, hk, hv, tq, tk, tv, ending_ref, c_ref, q_o, k_o, v_o, *outs
):
    quarter = pl.program_id(0)

    def activated(own, lent, halo, taps):
        total, _ = conv_parts(with_halo(own, lent, halo), taps[...])
        return total * jax.nn.sigmoid(total)

    queries, keys, values = activated(oq, lq, hq, tq), activated(ok, lk, hk, tk), activated(ov, lv, hv, tv)
    key_states, value_states = [], []
    for m in range(SHARE):
        k, v = unit(keys[:, cut(m)]), values[:, cut(m)]
        k_low = k.astype(bf16)
        k_o[m] = k_low
        v_o[m] = v.astype(bf16)
        q_o[m] = unit(queries[:, cut(m)]).T
        ending = ending_ref[m]
        key_states.append(tn((k * ending).astype(bf16), k_low).astype(bf16))
        value_states.append(tn((v * ending).astype(bf16), k_low).astype(bf16))
    store_quarter(spot, quarter, outs, key_states + value_states, c_ref)


def whole(*shape):
    return pl.BlockSpec(shape, lambda *g: (0,) * len(shape))


def per_quarter(*shape):
    return pl.BlockSpec((SHARE,) + shape, lambda p: (p,) + (0,) * len(shape))


def quarter_columns(rows, third):
    return pl.BlockSpec((rows, SHARE * HEAD_DIM), lambda p: (0, third * QUARTERS + p))


def features(spot, projected, taps, ending, c):
    own, lent, halo = projected
    tokens = own.shape[0]
    return pl.pallas_call(
        features_kernel,
        grid=(QUARTERS,),
        in_specs=[smem()] + [quarter_columns(x, i) for x in (tokens, tokens, halo.shape[0], KW) for i in range(3)]
        + [per_quarter(tokens, HEAD_DIM), whole(HEADS, tokens)],
        out_specs=[per_quarter(HEAD_DIM, tokens)] + [per_quarter(tokens, HEAD_DIM)] * 2 + [whole(*MESSAGE)] * QUARTERS,
        out_shape=[like((HEADS, HEAD_DIM, tokens))] + [like((HEADS, tokens, HEAD_DIM), bf16)] * 2
        + [like(MESSAGE, bf16)] * QUARTERS,
        cost_estimate=pl.CostEstimate(flops=1, bytes_accessed=1, transcendentals=0),
        name="features",
    )(spot, own, own, own, lent, lent, lent, halo, halo, halo, taps, taps, taps, ending, c)


def decay_between(indices, decays, low, high):
    total = None
    for index, decay in zip(indices, decays):
        one = jnp.where((index > low) & (index < high), decay, 1.0)
        total = one if total is None else total * one
    return total


def summed(factors, arrays, m):
    total = factors[0] * arrays[0][m, :HEAD_DIM].astype(f32)
    for factor, array in zip(factors[1:], arrays[1:]):
        total = total + factor * array[m, :HEAD_DIM].astype(f32)
    return total


def members(spot, unit, count):
    place = (spot[0] // unit) % count
    return place, [place ^ i for i in range(count)]


def whole_group(indices, arrays, m):
    decays = [decay_of(a, m) for a in arrays]
    count = len(arrays)
    state = summed([decay_between(indices, decays, i, count) for i in indices], arrays, m)
    return state, decay_between(indices, decays, -1, count)


def earlier(place, indices, arrays, m, before):
    decays = [decay_of(a, m) for a in arrays]
    factors = [jnp.where(i < place, decay_between(indices, decays, i, place), 0.0) for i in indices[1:]]
    state = summed(factors, arrays[1:], m)
    decay = decay_between(indices, decays, -1, place)
    if before is None:
        return state, decay
    old = before[m, HEAD_DIM : HEAD_DIM + 1]
    return before[m, :HEAD_DIM] + old * state, old * decay


def group_kernel(spot, *refs):
    arrays, out = refs[:FOUR], refs[FOUR]
    _, indices = members(spot, 1, FOUR)
    for m in range(2 * SHARE):
        state, decay = whole_group(indices, arrays, m)
        out[m, :HEAD_DIM] = state.astype(bf16)
        out[m, HEAD_DIM:] = decay_rows(decay)


def upper_kernel(unit, count, has_before, spot, *refs):
    arrays = refs[:count]
    before = refs[count] if has_before else None
    before_o, total_o = refs[-2:]
    place, indices = members(spot, unit, count)
    for m in range(2 * SHARE):
        state, decay = earlier(place, indices, arrays, m, before)
        before_o[m, :HEAD_DIM] = state
        before_o[m, HEAD_DIM:] = jnp.broadcast_to(decay, (16, HEAD_DIM))
        state, decay = whole_group(indices, arrays, m)
        total_o[m, :HEAD_DIM] = state.astype(bf16)
        total_o[m, HEAD_DIM:] = decay_rows(decay)


def spread_kernel(unit, count, has_before, spot, *refs):
    arrays, near = refs[:count], refs[count : count + FOUR]
    before = refs[count + FOUR] if has_before else None
    outs = refs[-FOUR:]
    place, upper = members(spot, unit, count)
    _, indices = members(spot, 1, FOUR)
    for m in range(2 * SHARE):
        state, _ = earlier(place, upper, arrays, m, before)
        decays = [decay_of(x, m) for x in near]
        for j in range(FOUR):
            at = indices[j]
            factors = [jnp.where(i < at, decay_between(indices, decays, i, at), 0.0) for i in indices]
            total = decay_between(indices, decays, -1, at) * state + summed(factors, near, m)
            outs[j][m] = total.astype(bf16)


def small_call(kernel, name, shapes, spot, *args):
    vmem = pl.BlockSpec(memory_space=pltpu.VMEM)
    return pl.pallas_call(
        kernel,
        in_specs=[smem()] + [vmem] * len(args),
        out_specs=[vmem] * len(shapes),
        out_shape=shapes,
        cost_estimate=pl.CostEstimate(flops=1, bytes_accessed=1, transcendentals=0),
        name=name,
    )(spot, *args)


def neighbour(axis, bit):
    return [(i, i ^ bit) for i in range(lax.axis_size(axis))]


def partner(x, axis, bit=1):
    return lax.ppermute(x, axis, neighbour(axis, bit))


def radices(peers):
    sizes = []
    left = peers // FOUR
    while left > 1:
        sizes.append(min(FOUR, left))
        left //= sizes[-1]
    return sizes


def swapped(arrays, axis, unit_size=1):
    return [arrays[0]] + [partner(a, axis, unit_size * i) for i, a in enumerate(arrays) if i]


class Scan:
    def __init__(self, spot, near, axis):
        self.spot, self.axis, self.near = spot, axis, near
        self.sizes = radices(lax.axis_size(axis))

    def group(self):
        message = like(MESSAGE, bf16)
        (self.total,) = small_call(group_kernel, "group", [message], self.spot, *self.near)
        self.before = ()
        self.unit = FOUR
        for radix in self.sizes[:-1]:
            arrays = swapped([self.total] * radix, self.axis, self.unit)
            kernel = functools.partial(upper_kernel, self.unit, radix, bool(self.before))
            before, self.total = small_call(kernel, "upper", [like(MESSAGE), message], self.spot, *arrays, *self.before)
            self.before = (before,)
            self.unit *= radix
        self.far = swapped([self.total] * self.sizes[-1], self.axis, self.unit)

    def spread(self):
        kernel = functools.partial(spread_kernel, self.unit, self.sizes[-1], bool(self.before))
        self.parts = small_call(
            kernel, "spread", [like(PAIR, bf16)] * FOUR, self.spot, *self.far, *self.near, *self.before
        )
        self.entering = swapped(self.parts, self.axis)
        return self.entering


def prepare(k_ref, c_ref, state_refs, place, left, wide, decay, pair):
    tokens = k_ref.shape[1]
    for i, state in enumerate(state_refs):
        for m in range(SHARE):
            left[(place ^ i) * SHARE + m, :, :HEAD_DIM] = state[m]
    pair[...] = jnp.zeros_like(pair)
    for h in range(HEADS):
        k = k_ref[h]
        left[h, :, HEAD_DIM:] = k.T
        wide[h // 2, :, cut(h % 2)] = k
        decay[h] = jnp.broadcast_to(jnp.exp(c_ref[h : h + 1, :]), (8, tokens))


def key_products(columns, wide, pair):
    products = []
    for h in range(0, HEADS, 2):
        pair[h // 2, :HEAD_DIM, :HEAD_DIM] = columns(h)
        pair[h // 2, HEAD_DIM:, HEAD_DIM:] = columns(h + 1)
        both = nn(wide[h // 2], pair[h // 2])
        products += [both[:, :HEAD_DIM], both[:, HEAD_DIM:]]
    return products


def solve_kernel(
    place, q_ref, k_ref, s0, s1, s2, s3, c_ref, mask, ridge,
    x_out, p_out, m_out, score_out, scal_out,
    left, wide, decay, pair, x_s, r_s, p_s,
):
    i = pl.program_id(0)

    @pl.when(i == 0)
    def _():
        prepare(k_ref, c_ref, (s0, s1, s2, s3), place[0], left, wide, decay, pair)
        for h in range(HEADS):
            q = q_ref[h]
            x_s[h] = jnp.zeros_like(q)
            r_s[h] = q
            p_s[h] = q
            scal_out[h, 0:1] = jnp.sum(q * q, axis=0, keepdims=True)

    products = key_products(lambda h: p_s[h].astype(bf16), wide, pair)
    for h in range(HEADS):
        p = p_s[h]
        scores = (products[h] * mask[h]).astype(bf16)
        score_out[0, h] = scores
        stacked = jnp.concatenate([(decay[h, 0:1] * p).astype(bf16), scores], axis=0)
        image = nn(left[h], stacked) + ridge[h] * p
        norm = scal_out[h, pl.ds(i, 1)]
        dot = jnp.sum(p * image, axis=0, keepdims=True)
        size = norm / dot
        p_out[0, h] = p
        m_out[0, h] = image
        scal_out[h, pl.ds(2 * ITERS + i, 1)] = dot
        x_s[h] = x_s[h] + size * p
        r = r_s[h] - size * image
        r_s[h] = r
        norm_next = jnp.sum(r * r, axis=0, keepdims=True)
        scal_out[h, pl.ds(i + 1, 1)] = norm_next
        p_s[h] = r + (norm_next / norm) * p

    @pl.when(i == ITERS - 1)
    def _():
        for h in range(HEADS):
            x_out[h] = x_s[h].astype(bf16)


def common_scratch(tokens):
    square = pltpu.VMEM((HEADS, HEAD_DIM, tokens), f32)
    return [
        pltpu.VMEM((HEADS, HEAD_DIM, HEAD_DIM + tokens), bf16),
        pltpu.VMEM((HEADS // 2, tokens, 2 * HEAD_DIM), bf16),
        pltpu.VMEM((HEADS, 8, tokens), f32),
        pltpu.VMEM((HEADS // 2, 2 * HEAD_DIM, 2 * tokens), bf16),
        square, square, square,
    ]


def solve(place, q, k, states, c, mask, ridge):
    tokens = q.shape[2]
    step = pl.BlockSpec((1, HEADS, HEAD_DIM, tokens), lambda i: (i, 0, 0, 0))
    steps = (ITERS, HEADS, HEAD_DIM, tokens)
    return pl.pallas_call(
        solve_kernel,
        grid=(ITERS,),
        in_specs=[smem(), whole(HEADS, HEAD_DIM, tokens), whole(HEADS, tokens, HEAD_DIM)] + [whole(*PAIR)] * FOUR
        + [whole(HEADS, tokens), whole(HEADS, tokens, tokens), whole(HEADS, HEAD_DIM, tokens)],
        out_specs=[whole(HEADS, HEAD_DIM, tokens), step, step, step, whole(HEADS, 3 * ITERS, tokens)],
        out_shape=[
            like((HEADS, HEAD_DIM, tokens), bf16), like(steps), like(steps), like(steps, bf16),
            like((HEADS, 3 * ITERS, tokens)),
        ],
        scratch_shapes=common_scratch(tokens),
        compiler_params=pltpu.CompilerParams(vmem_limit_bytes=VMEM_LIMIT),
        cost_estimate=pl.CostEstimate(flops=1, bytes_accessed=1, transcendentals=0),
        name="solve",
    )(place, q, k, *states, c, mask, ridge)


def attend_back_kernel(place, ga_ref, k_ref, v_ref, x_ref, s0, s1, s2, s3, c_ref, mask_ref, gx_o, dk_o, dv_o, state_o):
    quarter = pl.program_id(0)
    tokens = k_ref.shape[1]
    for m in range(SHARE):
        head = quarter * SHARE + m
        c = c_ref[pl.ds(head, 1), :]
        mask = mask_ref[m]
        e = jnp.exp(c)
        state = s0[SHARE + m]
        for i, other in ((1, s1), (2, s2), (3, s3)):
            state = jnp.where((place[0] ^ i) == quarter, other[SHARE + m], state)
        ga = ga_ref[:, cut(m)].T
        low = ga.astype(bf16)
        x = x_ref[m]
        k = k_ref[m]
        scores = (nn(k, x) * mask).astype(bf16)
        dscores = (nn(v_ref[m], low) * mask).astype(bf16)
        ega = (e * ga).astype(bf16)
        gx_o[m] = tn(state, ega) + tn(k, dscores)
        dv_o[m] = nt(scores, low)
        dk_o[m] = nt(dscores, x)
        state_o[m] = nt(ega, x).astype(bf16)


def attend_back(place, ga, k, v, x, states, c, mask):
    tokens = k.shape[1]
    square = like((HEADS, HEAD_DIM, tokens))
    return pl.pallas_call(
        attend_back_kernel,
        grid=(QUARTERS,),
        in_specs=[smem(), quarter_columns(tokens, 0)] + [per_quarter(tokens, HEAD_DIM)] * 2
        + [per_quarter(HEAD_DIM, tokens)] + [whole(*PAIR)] * FOUR + [whole(HEADS, tokens), per_quarter(tokens, tokens)],
        out_specs=[per_quarter(HEAD_DIM, tokens)] * 4,
        out_shape=[square] * 3 + [like((HEADS, HEAD_DIM, HEAD_DIM), bf16)],
        cost_estimate=pl.CostEstimate(flops=1, bytes_accessed=1, transcendentals=0),
        name="attend_back",
    )(place, ga, k, v, x, *states, c, mask)


def adjoint_kernel(
    spot, place, gx_ref, k_ref, s0, s1, s2, s3, c_ref, mask, ridge, p_ref, m_ref, score_ref, scal_ref, values_ref,
    dq_ref, dk_ref, dridge_ref, o0, o1, o2, o3,
    left, wide, decay, pair, gr_s, gp_s, acc_s, next_s, gnorm_s, low_s, steps_p, steps_g, steps_s, stack,
):
    s = pl.program_id(0)
    i = ITERS - 1 - s
    tokens = k_ref.shape[1]
    at = pl.ds(pl.multiple_of(i * tokens, tokens), tokens)

    @pl.when(s == 0)
    def _():
        prepare(k_ref, c_ref, (s0, s1, s2, s3), place[0], left, wide, decay, pair)
        gr_s[...] = jnp.zeros_like(gr_s)
        gp_s[...] = jnp.zeros_like(gp_s)
        acc_s[...] = jnp.zeros_like(acc_s)
        next_s[...] = jnp.zeros_like(next_s)
        gnorm_s[...] = jnp.zeros_like(gnorm_s)

    for h in range(HEADS):
        p, m, gx = p_ref[0, h], m_ref[0, h], gx_ref[h]
        norm = scal_ref[h, pl.ds(i, 1)]
        dot = scal_ref[h, pl.ds(2 * ITERS + i, 1)]
        size = norm / dot
        ratio = jnp.where(s == 0, 0.0, scal_ref[h, pl.ds(i + 1, 1)] / norm)
        gp = gp_s[h]
        gratio = jnp.sum(gp * p, axis=0, keepdims=True)
        gnext = gnorm_s[h, 0:1] + gratio / norm
        gr = gr_s[h] + gp + (2.0 * gnext) * (next_s[h] - ratio * p)
        gsize = jnp.sum(gx * p - gr * m, axis=0, keepdims=True)
        gdot = -gsize * size / dot
        gm = gdot * p - size * gr
        gr_s[h] = gr
        gp_s[h] = ratio * gp + size * gx + gdot * m + ridge[h] * gm
        acc_s[h] = acc_s[h] + gm * p
        next_s[h] = p
        gnorm_s[h, 0:1] = gsize / dot - gratio * ratio / norm
        low = gm.astype(bf16)
        low_s[h] = low
        egm = (decay[h, 0:1] * gm).astype(bf16)
        steps_g[h, :, at] = low
        steps_p[h, :, at] = p.astype(bf16)
        steps_s[h, :, at] = score_ref[0, h]
        stack[h, HEAD_DIM:, at] = egm
    products = key_products(lambda h: low_s[h], wide, pair)
    for h in range(HEADS):
        dscores = (products[h] * mask[h]).astype(bf16)
        stack[h, :HEAD_DIM, at] = dscores
        stacked = jnp.concatenate([stack[h, HEAD_DIM:, at], dscores], axis=0)
        gp_s[h] = gp_s[h] + nn(left[h], stacked)

    @pl.when(s == ITERS - 1)
    def _():
        for h in range(HEADS):
            dq_ref[h] = gr_s[h] + gp_s[h] + 2.0 * gnorm_s[h, 0:1] * p_ref[0, h]
            both = nt(steps_p[h], stack[h])
            dk_ref[h] = (nt(steps_g[h], steps_s[h]) + both[:, :HEAD_DIM]).T
            left[h, :, :HEAD_DIM] = both[:, HEAD_DIM:].T.astype(bf16)
            dridge_ref[h] = jnp.sum(acc_s[h].T, axis=0, keepdims=True)
        for j, out in enumerate((o0, o1, o2, o3)):
            for m in range(SHARE):
                head = (position(spot) ^ j) * SHARE + m
                decay = decay_rows(block_decay(c_ref, head))
                out[m, :HEAD_DIM] = left[head, :, :HEAD_DIM]
                out[m, HEAD_DIM:] = decay
                out[SHARE + m, :HEAD_DIM] = values_ref[head]
                out[SHARE + m, HEAD_DIM:] = decay


def adjoint(spot, place, gx, k, states, c, mask, ridge, p_all, m_all, scores, scal, value_states):
    tokens = k.shape[1]
    step = pl.BlockSpec((1, HEADS, HEAD_DIM, tokens), lambda s: (ITERS - 1 - s, 0, 0, 0))
    square = pltpu.VMEM((HEADS, HEAD_DIM, tokens), f32)
    line = pltpu.VMEM((HEADS, HEAD_DIM, ITERS * tokens), bf16)
    return pl.pallas_call(
        adjoint_kernel,
        grid=(ITERS,),
        in_specs=[smem(), smem(), whole(HEADS, HEAD_DIM, tokens), whole(HEADS, tokens, HEAD_DIM)] + [whole(*PAIR)] * FOUR
        + [whole(HEADS, tokens), whole(HEADS, tokens, tokens), whole(HEADS, HEAD_DIM, tokens), step, step, step, whole(HEADS, 3 * ITERS, tokens), whole(HEADS, HEAD_DIM, HEAD_DIM)],
        out_specs=[whole(HEADS, HEAD_DIM, tokens), whole(HEADS, tokens, HEAD_DIM), whole(HEADS, 1, HEAD_DIM)]
        + [whole(*MESSAGE)] * FOUR,
        out_shape=[like((HEADS, HEAD_DIM, tokens)), like((HEADS, tokens, HEAD_DIM)), like((HEADS, 1, HEAD_DIM))]
        + [like(MESSAGE, bf16)] * FOUR,
        scratch_shapes=common_scratch(tokens) + [
            square,
            pltpu.VMEM((HEADS, 8, tokens), f32),
            pltpu.VMEM((HEADS, HEAD_DIM, tokens), bf16),
            line, line, line,
            pltpu.VMEM((HEADS, 2 * HEAD_DIM, ITERS * tokens), bf16),
        ],
        compiler_params=pltpu.CompilerParams(vmem_limit_bytes=VMEM_LIMIT),
        cost_estimate=pl.CostEstimate(flops=1, bytes_accessed=1, transcendentals=0),
        name="adjoint",
    )(spot, place, gx, k, *states, c, mask, ridge, p_all, m_all, scores, scal, value_states)


def conv_forward(own, lent, halo, t):
    total, shifted = conv_parts(with_halo(own, lent, halo), t[...])
    sig = jax.nn.sigmoid(total)
    return shifted, sig * (1.0 + total * (1.0 - sig)), total * sig


def unit_back(act, grad):
    scale = lax.rsqrt(jnp.sum(act * act, axis=-1, keepdims=True) + 1e-06)
    rows = act * scale
    return scale * (grad - rows * jnp.sum(rows * grad, axis=-1, keepdims=True))


def conv_back(dconv, shifted, t, g, dt):
    taps = t[...]
    tokens = dconv.shape[0]
    blank = jnp.zeros((HALO, dconv.shape[1]), f32)
    padded = jnp.concatenate([blank, dconv, blank], axis=0)
    rows = tokens + HALO
    total = taps[KW - 1 : KW] * padded[:rows]
    for j in range(KW - 1):
        total = total + taps[j : j + 1] * padded[KW - 1 - j : KW - 1 - j + rows]
    g[...] = total.astype(bf16)
    dt[...] = jnp.concatenate(
        [jnp.sum(dconv * shifted[j], axis=0, keepdims=True) for j in range(KW)], axis=0
    )


def queries_back_kernel(own, lent, halo, t, dq_ref, g, dt):
    shifted, slope, act = conv_forward(own, lent, halo, t)
    grads = [unit_back(act[:, cut(m)], dq_ref[m].T) for m in range(SHARE)]
    conv_back(jnp.concatenate(grads, axis=1) * slope, shifted, t, g, dt)


def returned(place, quarter, refs, m):
    state = refs[0][m]
    for i in range(1, FOUR):
        state = jnp.where((place ^ i) == quarter, refs[i][m], state)
    return state


def values_back_kernel(spot, own, lent, halo, t, dv_ref, k_ref, r0, r1, r2, r3, ending_ref, g, dt):
    quarter = pl.program_id(0)
    shifted, slope, _ = conv_forward(own, lent, halo, t)
    grads = []
    for m in range(SHARE):
        rv = returned(position(spot), quarter, (r0, r1, r2, r3), SHARE + m)
        grads.append(dv_ref[m] + ending_ref[m] * nt(k_ref[m], rv))
    conv_back(jnp.concatenate(grads, axis=1) * slope, shifted, t, g, dt)


def keys_back_kernel(
    spot, own, lent, halo, t, dk1, dk2, k_ref, v_ref, r0, r1, r2, r3, ending_ref, g, dt
):
    quarter = pl.program_id(0)
    shifted, slope, act = conv_forward(own, lent, halo, t)
    grads = []
    for m in range(SHARE):
        rv = returned(position(spot), quarter, (r0, r1, r2, r3), SHARE + m)
        rk = returned(position(spot), quarter, (r0, r1, r2, r3), m).astype(f32)
        rk = (rk + rk.T).astype(bf16)
        ending = ending_ref[m]
        dk = dk1[m] + dk2[m] + ending * (nn(k_ref[m], rk) + nn(v_ref[m], rv))
        grads.append(unit_back(act[:, cut(m)], dk))
    conv_back(jnp.concatenate(grads, axis=1) * slope, shifted, t, g, dt)


def third_back(kernel, name, which, taps_third, projected, taps, before, others, specs):
    own, lent, halo = projected
    tokens = own.shape[0]
    return pl.pallas_call(
        kernel,
        grid=(QUARTERS,),
        in_specs=[smem()] * len(before) + [quarter_columns(rows, which) for rows in (tokens, tokens, halo.shape[0])]
        + [quarter_columns(KW, taps_third)] + specs,
        out_specs=[quarter_columns(tokens + HALO, 0), quarter_columns(KW, 0)],
        out_shape=[like((tokens + HALO, D), bf16), like((KW, D))],
        cost_estimate=pl.CostEstimate(flops=1, bytes_accessed=1, transcendentals=0),
        name=name,
    )(*before, own, lent, halo, taps, *others)


def queries_back(projected, taps, dq):
    return third_back(queries_back_kernel, "queries_back", 0, 0, projected, taps, (), (dq,), [per_quarter(HEAD_DIM, HEAD_DIM)])


def values_back(spot, projected, taps, dv, k, states, ending):
    square = per_quarter(HEAD_DIM, HEAD_DIM)
    return third_back(
        values_back_kernel, "values_back", 2, 2, projected, taps, (spot,), (dv, k, *states, ending),
        [square] * 2 + [whole(*PAIR)] * FOUR + [square],
    )


def keys_back(spot, projected, taps, dk1, dk2, k, v, states, ending):
    square = per_quarter(HEAD_DIM, HEAD_DIM)
    return third_back(
        keys_back_kernel, "keys_back", 1, 1, projected, taps, (spot,), (dk1, dk2, k, v, *states, ending),
        [square] * 4 + [whole(*PAIR)] * FOUR + [square],
    )


def completed(ref, extra):
    more = extra[...].astype(f32)
    more = jnp.concatenate([jnp.zeros_like(more), more], axis=0)
    last = ref.shape[0] - 16
    return [ref[HALO:last], (ref[last:].astype(f32) + more).astype(bf16)]


def products_kernel(plan, joined, cuts, spot, *refs):
    count = len(plan)
    odd = spot[0] % 2 == 1
    outs, scratch = refs[-count - (1 if joined else 1 + len(cuts)) : -count], refs[-count:]

    @pl.when(pl.program_id(0) == 0)
    def _():
        for (lefts, _, _), both in zip(plan, scratch):
            both[...] = jnp.concatenate([refs[at][...] if rows is None else refs[at][rows] for at, rows in lefts], axis=1)

    start = 0
    def right(at, stacked):
        if not stacked:
            return refs[at][...]
        return jnp.concatenate([refs[at][i : i + stacked] for i in range(0, refs[at].shape[0], stacked)], axis=1)

    for (_, rights, size), both in zip(plan, scratch):
        if len(rights) == 4:
            rows = [part for i in (0, 1) for part in completed(refs[rights[i][0]], refs[rights[2 + i][0]])]
        else:
            rows = [right(*at) for at in rights]
        product = nn(both[...], jnp.concatenate(rows, axis=0))
        at = slice(start, start + size)
        start += size
        if joined:
            outs[0][:, at, :] = product.reshape(product.shape[0] // size, size, product.shape[1]).astype(bf16)
            continue
        blocks = product.reshape(product.shape[0] // (2 * size), 2, size, product.shape[1])
        outs[0][:, at, :] = jnp.where(odd, blocks[:, 1], blocks[:, 0]).astype(bf16)
        other = jnp.where(odd, blocks[:, 0], blocks[:, 1]).astype(bf16)
        for out, cut_at in zip(outs[1:], cuts):
            first, last = max(at.start, cut_at.start), min(at.stop, cut_at.stop)
            if first < last:
                out[:, first - cut_at.start : last - cut_at.start, :] = other[:, first - at.start : last - at.start]


def unstacked(array, index):
    row, tokens = index
    return jnp.concatenate([array[row + i * tokens : row + (i + 1) * tokens] for i in range(D // HEAD_DIM)], axis=1)


def products(spot, peers, lefts, rights, tile, joined=False, messages=1):
    sizes = [(part[0][1].stop - part[0][1].start) // peers for part in lefts]
    width = rights[0][0][0].shape[1] if rights[0][0][1] is None else D
    count, number = (peers, 1) if joined else (peers // 2, 2)
    shape = (count, sum(sizes), width)
    cuts = [slice(i * shape[1] // messages, (i + 1) * shape[1] // messages) for i in range(messages)]
    if any(size % 8 for size in sizes):
        odd = spot[0] % 2
        sides = []
        for side in range(number):
            parts = []
            for left, right in zip(lefts, rights):
                if len(right) == 4:
                    rows = []
                    for i in (0, 1):
                        (array, third), (extra, _) = right[i], right[2 + i]
                        size = array.shape[0] // 3
                        rows += completed(array[third * size : (third + 1) * size], extra[:, third * D : (third + 1) * D])
                else:
                    rows = [unstacked(array, index) if index else array for array, index in right]
                blocks = nn(jnp.concatenate([array[at] for array, at in left], axis=1), jnp.concatenate(rows, axis=0))
                blocks = blocks.astype(bf16).reshape(count, number, -1, width)
                parts.append(lax.dynamic_index_in_dim(blocks, 0 if joined else odd ^ side, 1, keepdims=False))
            sides.append(jnp.concatenate(parts, axis=1))
        return sides if joined else sides[:1] + [sides[1][:, at] for at in cuts]
    arrays, specs, plan = [], [], []

    def place_of(array, spec):
        for at, other in enumerate(arrays):
            if other is array and specs[at] is None and spec is None:
                return at
        arrays.append(array)
        specs.append(spec)
        return len(arrays) - 1

    def columns(array, index):
        if index is None:
            return pl.BlockSpec((array.shape[0], tile), lambda j: (0, j))
        if isinstance(index, int) and array.shape[1] == D:
            return pl.BlockSpec((array.shape[0] // 3, tile), lambda j: (index, j))
        if isinstance(index, int):
            return pl.BlockSpec((array.shape[0], tile), lambda j: (0, index * (D // tile) + j))
        size = index[1] * tile // HEAD_DIM
        return pl.BlockSpec((size, HEAD_DIM), lambda j: (index[0] // size + j, 0))

    def left_part(array, rows):
        size = rows.stop - rows.start
        if rows.start % size:
            return place_of(array, None), rows
        at = rows.start // size
        return place_of(array, pl.BlockSpec((size, array.shape[1]), lambda j: (at, 0))), None

    for left, right, size in zip(lefts, rights, sizes):
        plan.append((
            [left_part(array, rows) for array, rows in left],
            [(place_of(array, columns(array, index)), index[1] if isinstance(index, tuple) else None) for array, index in right],
            size,
        ))
    heights = [shape[1]] + ([] if joined else [at.stop - at.start for at in cuts])
    return pl.pallas_call(
        functools.partial(products_kernel, plan, joined, cuts),
        grid=(width // tile,),
        in_specs=[smem()] + [spec or whole(*array.shape) for array, spec in zip(arrays, specs)],
        out_specs=[pl.BlockSpec((count, height, tile), lambda j: (0, 0, j)) for height in heights],
        out_shape=[like((count, height, width), bf16) for height in heights],
        scratch_shapes=[
            pltpu.VMEM((left[0][1].stop - left[0][1].start, sum(array.shape[1] for array, _ in left)), bf16) for left in lefts
        ],
        compiler_params=pltpu.CompilerParams(vmem_limit_bytes=VMEM_LIMIT),
        cost_estimate=pl.CostEstimate(flops=1, bytes_accessed=1, transcendentals=0),
        name="products",
    )(spot, *arrays)


def lent_kernel(own, peer, extra1, extra2, logit1, logit2, qkv_ref, gate_ref, own_o, theirs_o):
    rows = own_o.shape[0]
    logits = [unstacked(ref, (D // HEAD_DIM * rows, rows)) for ref in (logit1, logit2)]
    total = nt(jnp.concatenate(logits, axis=0), gate_ref[...])
    size = rows + HALO
    for third in range(3):
        at, columns = slice(third * size, (third + 1) * size), slice(third * D, (third + 1) * D)
        both = completed(own.at[at], extra1[:, columns]) + completed(peer.at[at], extra2[:, columns])
        total = total + nt(jnp.concatenate(both, axis=0), qkv_ref[:, columns])
    own_o[...] = total[:rows]
    theirs_o[...] = total[rows:].astype(bf16)


def lent_rows(own, peer, extras, logits, qkv_weight, gate_weight):
    rows = own.shape[0] // 3 - HALO
    half = qkv_weight.shape[0]
    vmem = pl.BlockSpec(memory_space=pltpu.VMEM)
    return pl.pallas_call(
        lent_kernel,
        in_specs=[vmem] * 8,
        out_specs=[vmem] * 2,
        out_shape=[like((rows, half)), like((rows, half), bf16)],
        compiler_params=pltpu.CompilerParams(vmem_limit_bytes=VMEM_LIMIT),
        cost_estimate=pl.CostEstimate(flops=1, bytes_accessed=1, transcendentals=0),
        name="lent_rows",
    )(own, peer, *extras, *logits, qkv_weight, gate_weight)


def norm_back_kernel(place, own, back, tok_ref, gain_ref, hid_ref, tq, tk, tv, second_ref, ridge_ref, tok_o, vec_o):
    mine, other = own[...], back[...].astype(f32)
    grad = jnp.where(
        place[0] == 0, jnp.concatenate([mine, other], axis=1), jnp.concatenate([other, mine], axis=1)
    )
    tokens = tok_ref[...]
    scale = lax.rsqrt(jnp.mean(tokens * tokens, axis=-1, keepdims=True) + 1e-05)
    rows = tokens * scale
    grows = grad * gain_ref[...]
    tok_o[...] = hid_ref[...] + scale * (grows - rows * jnp.mean(grows * rows, axis=-1, keepdims=True))
    vec_o[:KW] = jnp.concatenate([tq[...], tk[...], tv[...]], axis=1)
    ridge = jnp.concatenate([ridge_ref[h] for h in range(HEADS)], axis=1)
    first = jnp.sum(grad * rows, axis=0, keepdims=True)
    vec_o[KW : KW + 1] = jnp.concatenate([first, second_ref[...], ridge], axis=1)
    vec_o[KW + 1 :] = jnp.zeros((8 - KW - 1, 3 * D), f32)


def norm_back(place, own, back, tokens, gain, hidden, taps, second, ridge):
    vmem = pl.BlockSpec(memory_space=pltpu.VMEM)
    return pl.pallas_call(
        norm_back_kernel,
        in_specs=[smem()] + [vmem] * 10,
        out_specs=[vmem] * 2,
        out_shape=[like(tokens.shape), like((8, 3 * D))],
        cost_estimate=pl.CostEstimate(flops=1, bytes_accessed=1, transcendentals=0),
        name="norm_back",
    )(place, own, back, tokens, gain, hidden, *taps, second, ridge)


def step_kernel(bit, kept_mine, kept_other, *refs):
    mine_o, other_o = refs[-2:]
    start = 0
    for mine, other in zip(refs[0:-2:2], refs[1:-2:2]):
        at = slice(start, start + mine.shape[1])
        start += mine.shape[1]
        mine_o[0, at] = (kept_mine[0, at].astype(f32) + mine[0].astype(f32)).astype(bf16)
        other_o[0, at] = (kept_other[0, at].astype(f32) + other[0].astype(f32)).astype(bf16)


def halving_step(bit, below, kept, got):
    count, size, width = kept.shape

    def half(side, rows):
        def index(i, s):
            return ((i // below) * 2 * below + (s[0] if side == 0 else 1 - s[0]) * below + i % below, 0, 0)

        return pl.BlockSpec((1, rows, width), index)

    out = pl.BlockSpec((1, size, width), lambda i, s: (i, 0, 0))
    arrays = [kept] + list(got)
    return pl.pallas_call(
        step_kernel,
        grid_spec=pltpu.PrefetchScalarGridSpec(
            num_scalar_prefetch=1,
            grid=(count // 2,),
            in_specs=[half(side, x.shape[1]) for x in arrays for side in (0, 1)],
            out_specs=[out, out],
        ),
        out_shape=[like((count // 2, size, width), bf16)] * 2,
        cost_estimate=pl.CostEstimate(flops=1, bytes_accessed=1, transcendentals=0),
        name="halving",
    )(bit, *[x for x in arrays for _ in (0, 1)])


BLOCKS = D // HEAD_DIM


def middle_kernel(
    owners, place, x_ref, s0, s1, s2, s3, k_ref, v_ref, c_ref, mask_ref, own_logit, lent_logit, tok_ref, cot_ref, gain_ref, first_ref,
    own_out, out_a, out_b, out_c, out_d, *refs,
):
    own_up = refs[:4]
    up_parts = (refs[4:8], refs[8:12])
    own_down = refs[12]
    down_parts = refs[13:17]
    (out_o, hid_o, gatt_o, own_o, sent_o, ggu_o, dgain_o) = refs[17:24]
    out_s, up_s, down_s, nf_s, gb_s, att_s, sig_s, hid_s, acc_s, gnf_s, inner_s = refs[24:]
    j = pl.program_id(0)
    y = place[0]
    half = D // 2

    def aligned(at, by):
        return pl.multiple_of(at, by)

    mine = pl.ds(aligned(y * half, half), half)
    theirs = pl.ds(aligned((1 - y) * half, half), half)

    def order(q):
        return [q, q ^ 2, q ^ 1, q ^ 3]

    tile = own_up[0].shape[1]
    tokens = tok_ref.shape[0]

    def spread_rows(rows, start):
        total = rows.shape[0]
        size = total // owners
        own_at = slice(start, start + total // 2)
        sent_at = slice(3 * BLOCKS * tokens + start, 3 * BLOCKS * tokens + start + total // 2)
        if size % 8:
            own_o[own_at], sent_o[sent_at] = rows[: total // 2].astype(bf16), rows[total // 2 :].astype(bf16)
            return
        blocks = rows.reshape(owners // 2, 2, size, rows.shape[1])
        for out, at, odd in ((own_o, own_at, y == 1), (sent_o, sent_at, y == 0)):
            out[at] = jnp.where(odd, blocks[:, 1], blocks[:, 0]).reshape(total // 2, rows.shape[1]).astype(bf16)

    def stack_right(value, index):
        for i in range(BLOCKS):
            sent_o[(index * BLOCKS + i) * tokens : (index * BLOCKS + i + 1) * tokens] = value[:, cut(i)]

    def scale_of(hidden):
        return lax.rsqrt(jnp.mean(hidden * hidden, axis=-1, keepdims=True) + 1e-05)

    @pl.when(j == 0)
    def _():
        for i, state in enumerate((s0, s1, s2, s3)):
            for m in range(SHARE):
                head = (place[1] ^ i) * SHARE + m
                c = c_ref[pl.ds(head, 1), :]
                x = x_ref[head]
                scores = (nn(k_ref[head], x) * mask_ref[head]).astype(bf16)
                part = jnp.exp(c) * nn(state[SHARE + m], x) + tn(v_ref[head], scores)
                att_s[:, pl.ds(aligned(head * HEAD_DIM, HEAD_DIM), HEAD_DIM)] = part.T
        out_s[mine, :] = own_out[...]
        wide = out_a.shape[1]
        for part, q in zip((out_a, out_b, out_c, out_d), order(place[1])):
            out_s[theirs, pl.ds(aligned(q * wide, wide), wide)] = part[...]
        sig = jax.nn.sigmoid(own_logit[...] + lent_logit[...].astype(f32))
        sig_s[...] = sig
        mix = (att_s[...] * sig).astype(bf16)
        spread_rows(mix.astype(f32).T, half)
        normed = tok_ref[...] * scale_of(tok_ref[...]) * first_ref[...]
        spread_rows(normed.astype(bf16).astype(f32).T, 2 * half)
        hidden = tok_ref[...] + nn(mix, out_s[...])
        hid_s[...] = hidden
        normed = (hidden * scale_of(hidden) * gain_ref[...]).astype(bf16)
        nf_s[...] = normed
        spread_rows(normed.astype(f32).T, 0)
        gb_s[...] = cot_ref[...].astype(bf16)
        stack_right(gb_s[...], 2)
        acc_s[...] = jnp.zeros_like(acc_s)
        gnf_s[...] = jnp.zeros_like(gnf_s)

    for i in range(4):
        up_s[mine, i * tile : (i + 1) * tile] = own_up[i][...]
    count = up_parts[0][0].shape[0]
    at = pl.ds(aligned((1 - y) * half, 16), count)
    for part, q in zip(up_parts[0], order(place[2])):
        slot = (q >> 1) * 2 + ((q & 1) ^ y)
        up_s[at, pl.ds(aligned(slot * tile, tile), tile)] = part[...]
    at = pl.ds(aligned((1 - y) * half + count, 16), half - count)
    for i, part in enumerate(up_parts[1]):
        slot = ((place[1] ^ (i // 2)) & 1) * 2 + i % 2
        up_s[at, pl.ds(aligned(slot * tile, tile), tile)] = part[...]
    down_s[:tile, :] = own_down[...]
    wide = down_parts[0].shape[1]
    for part, q in zip(down_parts, order(place[1])):
        down_s[tile:, pl.ds(aligned(q * wide, wide), wide)] = part[...]
    product = nn(nf_s[...], up_s[...])
    gate, up = product[:, : 2 * tile], product[:, 2 * tile :]
    ginner = nt(gb_s[...], down_s[...])
    sig = jax.nn.sigmoid(gate)
    silu = gate * sig
    inner = (silu * up).astype(bf16)
    ggate = (ginner * up * (sig * (1.0 + gate * (1.0 - sig)))).astype(bf16)
    gup = (ginner * silu).astype(bf16)
    ggu = jnp.concatenate([ggate, gup], axis=1)
    acc_s[...] += nn(inner, down_s[...])
    gnf_s[...] += nt(ggu, up_s[...])
    inner_t = inner.astype(f32).T
    for slot, value in ((y, inner_t[:tile]), (1 - y, inner_t[tile:])):
        inner_s[pl.ds(aligned(slot * (FF // 2) + j * tile, tile), tile), :] = value
    share = FF // 2
    for i, (slot, value) in enumerate(((y, ggate), (1 - y, ggate), (2 + y, gup), (3 - y, gup))):
        at = pl.ds(aligned(slot * share + j * tile, tile), tile)
        ggu_o[:, at] = value[:, (i % 2) * tile : (i % 2 + 1) * tile]

    @pl.when(j == pl.num_programs(0) - 1)
    def _():
        spread_rows(inner_s[...], 3 * half)
        hidden = hid_s[...]
        out_o[...] = hidden + acc_s[...]
        scale = scale_of(hidden)
        rows = hidden * scale
        gnf = gnf_s[...]
        dgain_o[...] = jnp.sum(gnf * rows, axis=0, keepdims=True)
        grows = gnf * gain_ref[...]
        ghid = cot_ref[...] + scale * (grows - rows * jnp.mean(grows * rows, axis=-1, keepdims=True))
        hid_o[...] = ghid
        low = ghid.astype(bf16)
        stack_right(low, 0)
        gmix = nt(low, out_s[...])
        sig = sig_s[...]
        gatt = gmix * sig
        gatt_o[...] = gatt
        stack_right((gatt * att_s[...] * (1.0 - sig)).astype(bf16), 1)


def middle(owners, place, attention, own_logit, lent_logit, tok, cot, gain, gain_first, out_weight, up_weight, down_weight, up_parts, rest_parts):
    tokens = tok.shape[0]
    tile = 128
    share = FF // 2 // tile
    half = D // 2
    left_rows = 3 * half + FF // 2

    def full(*shape):
        return pl.BlockSpec(shape, lambda j, s: (0,) * len(shape))

    rows = full(tokens, D)
    own_up = [
        pl.BlockSpec((half, tile), lambda j, s: (0, s[0] * share + j)),
        pl.BlockSpec((half, tile), lambda j, s: (0, (1 - s[0]) * share + j)),
        pl.BlockSpec((half, tile), lambda j, s: (0, (2 + s[0]) * share + j)),
        pl.BlockSpec((half, tile), lambda j, s: (0, (3 - s[0]) * share + j)),
    ]
    up_specs = [pl.BlockSpec((p.shape[0], tile), lambda j, s: (0, j)) for p in up_parts[:4]]
    rest_rows = up_parts[4].shape[0]
    up_specs += [
        pl.BlockSpec((rest_rows, tile), lambda j, s: (0, s[0] * share + j)),
        pl.BlockSpec((rest_rows, tile), lambda j, s: (0, (1 - s[0]) * share + j)),
    ] * 2
    up_parts = up_parts[:4] + (up_parts[4],) * 2 + (up_parts[5],) * 2
    own_down = pl.BlockSpec((tile, D), lambda j, s: (j, 0))
    down_specs = [pl.BlockSpec((tile, D // 4), lambda j, s: (half // tile + j, 0))] * 4
    square = (HEAD_DIM, HEAD_DIM)
    return pl.pallas_call(
        functools.partial(middle_kernel, owners),
        grid_spec=pltpu.PrefetchScalarGridSpec(
            num_scalar_prefetch=1,
            grid=(share,),
            in_specs=[full(HEADS, HEAD_DIM, tokens)] + [full(*PAIR)] * FOUR + [full(HEADS, tokens, HEAD_DIM)] * 2
            + [full(HEADS, tokens), full(HEADS, tokens, tokens)]
            + [pl.BlockSpec((tokens, D), lambda j, s: (0, 3))] * 2
            + [rows] * 2 + [full(1, D), full(1, D), full(half, D)] + [full(half, D // 4)] * 4
            + own_up + up_specs + [own_down] + down_specs,
            out_specs=[
                rows, rows, rows, full(left_rows, tokens), full(3 * BLOCKS * tokens + left_rows, tokens),
                full(tokens, 2 * FF),
                full(1, D),
            ],
            scratch_shapes=[
                pltpu.VMEM((D, D), bf16),
                pltpu.VMEM((D, 4 * tile), bf16),
                pltpu.VMEM((2 * tile, D), bf16),
                pltpu.VMEM((tokens, D), bf16),
                pltpu.VMEM((tokens, D), bf16),
                pltpu.VMEM((tokens, D), f32),
                pltpu.VMEM((tokens, D), f32),
                pltpu.VMEM((tokens, D), f32),
                pltpu.VMEM((tokens, D), f32),
                pltpu.VMEM((tokens, D), f32),
                pltpu.VMEM((FF, tokens), f32),
            ],
        ),
        out_shape=[
            like((tokens, D)), like((tokens, D)), like((tokens, D)),
            like((left_rows, tokens), bf16), like((3 * BLOCKS * tokens + left_rows, tokens), bf16),
            like((tokens, 2 * FF), bf16),
            like((1, D)),
        ],
        compiler_params=pltpu.CompilerParams(vmem_limit_bytes=VMEM_LIMIT),
        cost_estimate=pl.CostEstimate(flops=1, bytes_accessed=1, transcendentals=0),
        name="middle",
    )(
        place, *attention, own_logit, lent_logit, tok, cot, gain, gain_first, out_weight, *rest_parts,
        *[up_weight] * 4, *up_parts, down_weight, *rest_parts,
    )


def shifted(x, axis, by):
    peers = lax.axis_size(axis)
    return lax.ppermute(x, axis, [(i, i + by) for i in range(peers) if 0 <= i + by < peers])


def crossed(x, by):
    peers, pair = lax.axis_size("ctx"), 2
    return lax.ppermute(
        x,
        ("ctx", "fsdp"),
        [(i * pair + s, (i + by) * pair + 1 - s) for i in range(peers) if 0 <= i + by < peers for s in range(pair)],
    )


def pick(x, index, axis=0):
    return lax.dynamic_index_in_dim(x, index, axis, keepdims=False)


def part(x, index, axis):
    size = x.shape[axis] // 2
    return lax.dynamic_slice_in_dim(x, index * size, size, axis)


def quarter(shard, q, start=0, count=None):
    wide = shard.shape[1] // 4
    return lax.dynamic_slice(shard, (start, q * wide), (count or shard.shape[0], wide))


class Reduction:
    def __init__(self, order, blocks):
        self.here = lax.axis_index("ctx")
        levels = lax.axis_size("ctx").bit_length() - 1
        self.order = list(order) + [level for level in range(levels) if level not in order]
        self.left = list(range(levels))
        self.kept, *sent = blocks
        self.send(sent)

    def bit(self):
        return (self.here >> self.order[0]) & 1

    def send(self, arrays):
        level = self.order.pop(0)
        self.left.remove(level)
        self.got = [partner(array, "ctx", 1 << level) for array in arrays]

    def step(self):
        below = 1 << self.left.index(self.order[0])
        self.kept, sent = halving_step(self.bit().astype(jnp.int32)[None], below, self.kept, self.got)
        self.send([sent])
        return sent

    def result(self, sizes):
        while self.order:
            self.step()
        total = (self.kept.astype(f32) + self.got[0].astype(f32))[0]
        ends = [sum(sizes[: i + 1]) for i in range(len(sizes))]
        return [total[end - size : end] for end, size in zip(ends, sizes)]


class Sequence:
    def __init__(self):
        self.last = ()

    def gate(self, *values):
        return lax.optimization_barrier(values + self.last)[: len(values)]

    def mark(self, *values):
        self.last = values


def added(value, axis):
    for level in range(lax.axis_size(axis).bit_length() - 1):
        value = value + partner(value, axis, 1 << level)
    return value


def rms_scale(values, gain):
    return values * lax.rsqrt(jnp.mean(values * values, axis=-1, keepdims=True) + 1e-05) * gain


def sided(mine, theirs, y, axis):
    return jnp.where(
        y == 0, jnp.concatenate([mine, theirs], axis=axis), jnp.concatenate([theirs, mine], axis=axis)
    )


UP_ROWS = 384


def local(
    inputs,
    qkv_weight,
    gate_weight,
    out_weight,
    up_weight,
    down_weight,
    conv_taps,
    gain_attn,
    gain_ffn,
    ridge_terms,
    forget,
    cotangent,
):
    tokens = inputs[0]
    rows = tokens.shape[0]
    y = lax.axis_index("fsdp")
    here = lax.axis_index("ctx")
    peers = lax.axis_size("ctx")
    owners = peers * 2
    near_x = here % 4
    near_z = here % 2 + 2 * ((here // 4) % 2)
    place = jnp.stack([y, near_x, near_z]).astype(jnp.int32)
    spot = here.astype(jnp.int32)[None]
    spot_back = (peers - 1 - here).astype(jnp.int32)[None]
    ring = near_x.astype(jnp.int32)[None]
    seq = Sequence()

    lines = jnp.stack([gain_attn, gain_ffn, ridge_terms, ridge_terms])
    mine, theirs = norm(place, tokens, conv_taps, lines)
    theirs = partner(theirs, "fsdp")
    lent = weigh(theirs, rows, gain_attn[None], qkv_weight, gate_weight, bf16)
    seq.mark(lent)
    lent = partner(lent, "fsdp")
    peer_extra = theirs[rows:]
    (peer_extra,) = seq.gate(peer_extra)
    taps_rows = KW * 3
    vectors = sided(lines[:3].astype(f32), peer_extra[taps_rows : taps_rows + 3], y, 1)
    taps = sided(conv_taps.astype(f32), peer_extra[:taps_rows].reshape(conv_taps.shape), y, 1)
    gain_first, gain_second = vectors[0], vectors[1:2]
    ridge = vectors[2].reshape(HEADS, HEAD_DIM)
    cumulative = jnp.cumsum(jnp.log(forget[0]).T, axis=-1)
    strength = (1.0 - forget[0]).T
    out_here, up_here, down_here = seq.gate(out_weight, up_weight, down_weight)
    rest_quarter = jnp.concatenate([quarter(out_here, near_x), quarter(down_here, near_x)], axis=0)
    seq.mark(rest_quarter)
    rest_direct = partner(rest_quarter, "fsdp")
    (up_here,) = seq.gate(up_here)
    up_quarters = [
        quarter(up_here, near_z, 0, UP_ROWS),
        lax.dynamic_slice(up_here, (UP_ROWS, (here % 2) * FF), (D // 2 - UP_ROWS, FF)),
    ]
    seq.mark(*up_quarters)
    cumulative, strength, ridge, taps, mine = seq.gate(cumulative, strength, ridge, taps, mine)
    own = weigh(mine, rows, gain_attn[None], qkv_weight, gate_weight, f32)
    mask, ending, ridge = tables(cumulative, strength, ridge)
    seq.mark(mask, own)

    own, lent, up_first = seq.gate(own, lent, up_quarters[0])
    halo = shifted((own[rows - 8 :, : 3 * D] + lent[rows - 8 :, : 3 * D].astype(f32)).astype(bf16), "ctx", 1)
    projected = own, lent, halo
    queries, keys_low, values_low, *near = features(spot, projected, taps, ending, cumulative)
    seq.mark(*near)
    scan = Scan(spot, swapped(near, "ctx"), "ctx")
    up_first = partner(up_first, "fsdp")

    def split(left):
        flat = left.reshape(peers, 2, left.shape[0] // owners, left.shape[1])
        return [pick(flat, side, 1).reshape(-1, left.shape[1]) for side in (y, 1 - y)]

    scan.near = list(seq.gate(*scan.near))
    scan.group()
    seq.mark(scan.total)
    (rest_direct,) = seq.gate(rest_direct)
    rest_across = partner(rest_direct, "ctx", 2)
    scan.far = list(seq.gate(*scan.far))
    states = scan.spread()
    seq.mark(scan.parts[0])
    up_first, up_second = seq.gate(up_first, up_quarters[1])
    up_second = partner(up_second, "fsdp")
    first_across = partner(up_first, "ctx", 4)
    *states, queries = seq.gate(*states, queries)
    seq.mark(states[1], states[2], states[3])
    rest_direct, rest_across, up_first = seq.gate(rest_direct, rest_across, up_first)
    rest_core, rest_far, first_core = partner(rest_direct, "ctx", 1), partner(rest_across, "ctx", 1), partner(up_first, "ctx", 1)
    (queries,) = seq.gate(queries)
    x, p_all, m_all, scores, scal = solve(ring, queries, keys_low, states, cumulative, mask, ridge)
    seq.mark(x)

    def split(left):
        flat = left.reshape(peers, 2, left.shape[0] // owners, left.shape[1])
        return [pick(flat, side, 1).reshape(-1, left.shape[1]) for side in (y, 1 - y)]

    def share(right):
        return right, partner(right, "fsdp")

    up_second, rest_core, rest_far = seq.gate(up_second, rest_core, rest_far)
    second_core = partner(up_second, "ctx", 1)
    (first_across,) = seq.gate(first_across)
    rest_parts = (rest_direct, rest_across, rest_core, rest_far)
    up_parts = (up_first, first_across, first_core, partner(first_across, "ctx", 1))
    up_parts += (up_second, second_core)

    output, grad_hidden, grad_attended, lefts, message, grad_gate_up, grad_second_gain = middle(
        owners, place, (x, *states, keys_low, values_low, cumulative, mask), own, lent,
        tokens, cotangent[0], gain_second, gain_first[None], out_weight, up_weight, down_weight, up_parts, rest_parts
    )
    size = D // 2
    parts = [slice(0, size), slice(size, 2 * size), slice(2 * size, 3 * size), slice(3 * size, 3 * size + FF // 2)]
    start = 3 * BLOCKS * rows
    peer_parts = [slice(start + at.start, start + at.stop) for at in parts]
    if (D // owners) % 8 or (FF // owners) % 8:
        pairs = [split(jnp.concatenate([lefts[at], message[there]], axis=0)) for at, there in zip(parts, peer_parts)]
        lefts = jnp.concatenate([own for own, _ in pairs], axis=0)
        message = jnp.concatenate([message[:start]] + [sent for _, sent in pairs], axis=0)
    seq.mark(grad_second_gain)
    message_peer = partner(message, "fsdp")
    (grad_attended,) = seq.gate(grad_attended)
    gx, dk_attend, dv, value_states = attend_back(
        ring, grad_attended, keys_low, values_low, x, states, cumulative, mask
    )
    dq, dk_solve, grad_ridge, *own = adjoint(
        spot_back, ring, gx, keys_low, states, cumulative, mask, ridge, p_all, m_all, scores, scal, value_states
    )
    seq.mark(*own)
    back = Scan(spot_back, swapped(own, "ctx"), "ctx")
    (up_here,) = seq.gate(grad_gate_up)
    both_up = share(up_here)
    dq, back.near[1] = seq.gate(dq, back.near[1])
    low_q, taps_q = queries_back(projected, taps, dq)
    seq.mark(low_q)
    back.near = list(seq.gate(*back.near))
    back.group()
    seq.mark(back.total)
    lefts_here, message_peer, back.far[1] = seq.gate(lefts, message_peer, back.far[1])
    rights = [(i * BLOCKS * rows, rows) for i in range(3)]
    (early,) = products(
        spot, peers, [[(lefts_here, parts[i]), (message_peer, peer_parts[i])] for i in (1, 2, 3)],
        [[(message, at), (message_peer, at)] for at in rights], 512, joined=True
    )
    seq.mark(early)
    early = lax.psum_scatter(early.reshape(-1, D), "ctx", scatter_dimension=0, tiled=True)
    back.far = list(seq.gate(*back.far))
    states_back = back.spread()
    seq.mark(back.parts[0])
    dv, *states_back = seq.gate(dv, *states_back)
    low_v, taps_v = values_back(
        spot_back, projected, taps, dv, keys_low, states_back, ending
    )
    seq.mark(low_v)
    (dk_attend,) = seq.gate(dk_attend)
    low_k, taps_k = keys_back(
        spot_back, projected, taps, dk_attend, dk_solve, keys_low, values_low, states_back, ending
    )
    seq.mark(low_k)
    ahead = jnp.concatenate([low[HALO - 8 : HALO] for low in (low_q, low_k, low_v)], axis=1)
    extra = shifted(ahead, "ctx", -1), crossed(ahead, -1)
    thirds = jnp.concatenate([low_q, low_k, low_v], axis=0)
    seq.mark(thirds)
    thirds_peer = partner(thirds, "fsdp")
    up_peer, *extra = seq.gate(both_up[1], *extra)
    blocks = products(
        spot, peers, [[(lefts, parts[0]), (message_peer, peer_parts[0])]], [[(both_up[0], None), (up_peer, None)]], 1408
    )
    seq.mark(blocks[0])
    ups = Reduction((0, 1, 2), blocks)
    ups.got = seq.gate(*ups.got)
    seq.mark(ups.step())
    lefts_here, thirds_peer = seq.gate(lefts, thirds_peer)
    left = [(lefts_here, parts[2]), (message_peer, peer_parts[2])]
    rights = [[(thirds, i), (thirds_peer, i), (extra[0], i), (extra[1], i)] for i in range(3)]
    blocks = products(spot, peers, [left] * 3, rights, 512, messages=2)
    seq.mark(blocks[0])
    late = Reduction((0, 1, 2), blocks)
    late.got = seq.gate(*late.got)
    seq.mark(late.step())
    (thirds_here,) = seq.gate(thirds)
    kept, lent = lent_rows(thirds_here, thirds_peer, extra, (message, message_peer), qkv_weight, gate_weight)
    seq.mark(lent)
    arriving = partner(lent, "fsdp")
    ups.got = seq.gate(*ups.got)
    seq.mark(ups.step())
    (arriving,) = seq.gate(arriving)
    grad_tokens, vector = norm_back(
        place, kept, arriving, tokens, gain_first[None], grad_hidden, (taps_q, taps_k, taps_v), grad_second_gain, grad_ridge
    )
    seq.mark(vector)
    size, width = D // owners, 3 * D // owners
    vector = jnp.concatenate(
        [vector[:KW].reshape(KW, owners, width).transpose(1, 0, 2).reshape(owners, KW * width),
         vector[KW].reshape(3, owners, size).transpose(1, 0, 2).reshape(owners, 3 * size)], axis=1
    ).reshape(peers, 2, KW * width + 3 * size)
    vector_kept, vector_sent = pick(vector, y, 1), pick(vector, 1 - y, 1)
    seq.mark(vector_sent)
    arriving = partner(vector_sent, "fsdp")
    late.got = seq.gate(*late.got)
    seq.mark(late.step())
    *ups.got, early = seq.gate(*ups.got, early)
    seq.mark(ups.step())
    vector_kept, arriving = seq.gate(vector_kept, arriving)
    vector = vector_kept + arriving
    seq.mark(vector)
    vector = lax.all_to_all(vector, "ctx", 0, 0, tiled=True)
    late.got = seq.gate(*late.got)
    seq.mark(late.step())
    vector = jnp.sum(seq.gate(vector)[0], axis=0)
    size = D // owners
    grad_up = ups.result([size])[0]
    grad_q, grad_k, grad_v = late.result([size] * 3)
    grad_qkv = jnp.concatenate([grad_q, grad_k, grad_v], axis=1)
    early = early.astype(f32)
    grad_out, grad_gate, grad_down = early[:size], early[size : 2 * size], early[2 * size :]
    return (
        output[None],
        grad_tokens[None],
        grad_qkv,
        grad_gate,
        grad_out,
        grad_up,
        grad_down,
        vector[: KW * width].reshape(KW, width),
        vector[KW * width : KW * width + size],
        vector[KW * width + size : KW * width + 2 * size],
        vector[KW * width + 2 * size :],
    )


def solution(mesh):
    tokens = P("fsdp", "ctx", None)
    rows = P("fsdp", None)
    vector = P("fsdp")
    owned = P(("ctx", "fsdp"), None)
    owned_vector = P(("ctx", "fsdp"))
    return jax.shard_map(
        local,
        mesh=mesh,
        in_specs=(
            tokens, rows, rows, rows, rows, rows, P(None, "fsdp"), vector, vector, vector, tokens, tokens,
        ),
        out_specs=(
            tokens, tokens, owned, owned, owned, owned, owned, P(None, ("ctx", "fsdp")),
            owned_vector, owned_vector, owned_vector,
        ),
        check_vma=False,
    )
```

```python
import functools
import jax
import jax.numpy as jnp
from jax import lax
from jax.experimental import pallas as pl
from jax.experimental.pallas import tpu as pltpu
from jax.sharding import PartitionSpec as P

D = 1024
HEADS = 8
FF = 2816
KW = 4
ITERS = 8
HEAD_DIM = 128
QUARTERS = 4
SHARE = HEADS // QUARTERS
HALO = 16

f32 = jnp.float32
bf16 = jnp.bfloat16
VMEM_LIMIT = 56 * 1024 * 1024


def nn(a, b):
    return lax.dot_general(a, b, (((1,), (0,)), ((), ())), preferred_element_type=f32)


def nt(a, b):
    return lax.dot_general(a, b, (((1,), (1,)), ((), ())), preferred_element_type=f32)


def tn(a, b):
    return lax.dot_general(a, b, (((0,), (0,)), ((), ())), preferred_element_type=f32)


def column(row, like):
    return jnp.broadcast_to(row, like).T


def decay_mask(c, b, tokens):
    shape = (tokens, tokens)
    late = lax.broadcasted_iota(jnp.int32, shape, 1) >= lax.broadcasted_iota(jnp.int32, shape, 0)
    spread = jnp.broadcast_to(c, shape) - column(c, shape)
    return jnp.where(late, jnp.exp(jnp.where(late, spread, 0.0)), 0.0) * column(b, shape)


def like(shape, kind=f32):
    return jax.ShapeDtypeStruct(shape, kind)


def smem():
    return pl.BlockSpec(memory_space=pltpu.SMEM)


EXTRA = 16


def norm_kernel(place, tok_ref, taps_ref, lines_ref, mine_o, theirs_o):
    half = D // 2
    y = place[0]
    a = tok_ref[...]
    unit = a * lax.rsqrt(jnp.mean(a * a, axis=-1, keepdims=True) + 1e-05)
    left, right = unit[:, :half], unit[:, half:]
    rows = a.shape[0]
    gain = lines_ref[0:1].astype(f32)
    mine_o[...] = (jnp.where(y == 0, left, right) * gain).astype(bf16)
    theirs_o[:rows] = jnp.where(y == 0, right, left).astype(bf16)
    taps = taps_ref[...]
    lines = [taps[t : t + 1, i * half : (i + 1) * half] for t in range(KW) for i in range(3)]
    theirs_o[rows:] = jnp.concatenate(lines + [lines_ref[...]], axis=0)


def norm(place, tokens, taps, lines):
    rows = tokens.shape[0]
    vmem = pl.BlockSpec(memory_space=pltpu.VMEM)
    return pl.pallas_call(
        norm_kernel,
        in_specs=[smem()] + [vmem] * 3,
        out_specs=[vmem, vmem],
        out_shape=[like((rows, D // 2), bf16), like((rows + EXTRA, D // 2), bf16)],
        name="norm",
    )(place, tokens, taps, lines)


def weigh_kernel(scaled, left_ref, gain_ref, qkv_ref, gate_ref, out, left):
    j = pl.program_id(0)

    @pl.when(j == 0)
    def _():
        rows = left_ref[: left.shape[0]]
        left[...] = (rows.astype(f32) * gain_ref[...].astype(f32)).astype(bf16) if scaled else rows

    steps = 3 * D // out.shape[1]

    @pl.when(j < steps)
    def _():
        out[...] = nn(left[...], qkv_ref[...]).astype(out.dtype)

    @pl.when(j >= steps)
    def _():
        out[...] = nn(left[...], gate_ref[...]).astype(out.dtype)


def weigh(left, rows, gain, qkv_weight, gate_weight, kind):
    half = left.shape[1]
    tile = 1024
    steps = 3 * D // tile
    return pl.pallas_call(
        functools.partial(weigh_kernel, left.shape[0] > rows),
        grid=(4 * D // tile,),
        in_specs=[
            whole(*left.shape), whole(1, half),
            pl.BlockSpec((half, tile), lambda j: (0, jnp.minimum(j, steps - 1))),
            pl.BlockSpec((half, tile), lambda j: (0, jnp.maximum(j - steps, 0))),
        ],
        out_specs=pl.BlockSpec((rows, tile), lambda j: (0, j)),
        out_shape=like((rows, 4 * D), kind),
        scratch_shapes=[pltpu.VMEM((rows, half), bf16)],
        cost_estimate=pl.CostEstimate(flops=1, bytes_accessed=1, transcendentals=0),
        name="weigh",
    )(left, gain, qkv_weight, gate_weight)


def tables_kernel(c_ref, b_ref, ridge_ref, mask_o, ending_o, ridge_o):
    tokens = c_ref.shape[1]
    head = pl.program_id(0)
    c, b = c_ref[pl.ds(head, 1), :], b_ref[pl.ds(head, 1), :]
    mask_o[0] = decay_mask(c, b, tokens)
    ending_o[0] = column(jnp.exp(c[:, tokens - 1 :] - c) * b, (HEAD_DIM, tokens))
    ridge_o[0] = column(ridge_ref[pl.ds(head, 1), :], (tokens, HEAD_DIM))


def tables(c, b, ridge):
    tokens = c.shape[1]
    shapes = [(tokens, tokens), (tokens, HEAD_DIM), (HEAD_DIM, tokens)]
    return pl.pallas_call(
        tables_kernel,
        grid=(HEADS,),
        in_specs=[whole(HEADS, tokens)] * 2 + [whole(HEADS, HEAD_DIM)],
        out_specs=[pl.BlockSpec((1,) + shape, lambda h: (h, 0, 0)) for shape in shapes],
        out_shape=[like((HEADS,) + shape) for shape in shapes],
        cost_estimate=pl.CostEstimate(flops=1, bytes_accessed=1, transcendentals=0),
        name="tables",
    )(c, b, ridge)


def with_halo(own, lent, halo):
    before = halo[...].astype(f32)
    blank = jnp.zeros((HALO - before.shape[0], before.shape[1]), f32)
    return jnp.concatenate([blank, before, own[...] + lent[...].astype(f32)], axis=0)


def conv_parts(padded, taps):
    rows = padded.shape[0] - HALO
    shifted = [padded[HALO - KW + 1 + j : HALO - KW + 1 + j + rows] for j in range(KW)]
    total = taps[0:1] * shifted[0]
    for j in range(1, KW):
        total = total + taps[j : j + 1] * shifted[j]
    return total, shifted


def unit(a):
    return a * lax.rsqrt(jnp.sum(a * a, axis=-1, keepdims=True) + 1e-06)


def position(spot):
    return spot[0] % FOUR


FOUR = 4
PAIR = (2 * SHARE, HEAD_DIM, HEAD_DIM)
MESSAGE = (2 * SHARE, HEAD_DIM + 16, HEAD_DIM)


def decay_rows(decay):
    shape = (16, HEAD_DIM)
    at = lax.broadcasted_iota(jnp.int32, shape, 0)
    decay = jnp.broadcast_to(decay, shape)
    high = decay.astype(bf16).astype(f32)
    return jnp.where(at == 0, high, jnp.where(at == 1, decay - high, 0.0)).astype(bf16)


def decay_of(message, m):
    rows = message[m, HEAD_DIM:].astype(f32)
    return rows[0:1] + rows[1:2]


def block_decay(c_ref, head):
    c = c_ref[pl.ds(head, 1), :]
    return jnp.broadcast_to(jnp.exp(c[:, c.shape[1] - 1 :]), (1, HEAD_DIM))


def store_quarter(spot, quarter, outs, states, c_ref):
    rows = [decay_rows(block_decay(c_ref, quarter * SHARE + m)) for m in range(SHARE)]
    for i, out in enumerate(outs):

        @pl.when((position(spot) ^ i) == quarter)
        def _():
            for m in range(2 * SHARE):
                out[m, :HEAD_DIM] = states[m]
                out[m, HEAD_DIM:] = rows[m % SHARE]


def cut(h):
    return slice(h * HEAD_DIM, (h + 1) * HEAD_DIM)


def features_kernel(
    spot, oq, ok, ov, lq, lk, lv, hq, hk, hv, tq, tk, tv, ending_ref, c_ref, q_o, k_o, v_o, *outs
):
    quarter = pl.program_id(0)

    def activated(own, lent, halo, taps):
        total, _ = conv_parts(with_halo(own, lent, halo), taps[...])
        return total * jax.nn.sigmoid(total)

    queries, keys, values = activated(oq, lq, hq, tq), activated(ok, lk, hk, tk), activated(ov, lv, hv, tv)
    key_states, value_states = [], []
    for m in range(SHARE):
        k, v = unit(keys[:, cut(m)]), values[:, cut(m)]
        k_low = k.astype(bf16)
        k_o[m] = k_low
        v_o[m] = v.astype(bf16)
        q_o[m] = unit(queries[:, cut(m)]).T
        ending = ending_ref[m]
        key_states.append(tn((k * ending).astype(bf16), k_low).astype(bf16))
        value_states.append(tn((v * ending).astype(bf16), k_low).astype(bf16))
    store_quarter(spot, quarter, outs, key_states + value_states, c_ref)


def whole(*shape):
    return pl.BlockSpec(shape, lambda *g: (0,) * len(shape))


def per_quarter(*shape):
    return pl.BlockSpec((SHARE,) + shape, lambda p: (p,) + (0,) * len(shape))


def quarter_columns(rows, third):
    return pl.BlockSpec((rows, SHARE * HEAD_DIM), lambda p: (0, third * QUARTERS + p))


def features(spot, projected, taps, ending, c):
    own, lent, halo = projected
    tokens = own.shape[0]
    return pl.pallas_call(
        features_kernel,
        grid=(QUARTERS,),
        in_specs=[smem()] + [quarter_columns(x, i) for x in (tokens, tokens, halo.shape[0], KW) for i in range(3)]
        + [per_quarter(tokens, HEAD_DIM), whole(HEADS, tokens)],
        out_specs=[per_quarter(HEAD_DIM, tokens)] + [per_quarter(tokens, HEAD_DIM)] * 2 + [whole(*MESSAGE)] * QUARTERS,
        out_shape=[like((HEADS, HEAD_DIM, tokens))] + [like((HEADS, tokens, HEAD_DIM), bf16)] * 2
        + [like(MESSAGE, bf16)] * QUARTERS,
        cost_estimate=pl.CostEstimate(flops=1, bytes_accessed=1, transcendentals=0),
        name="features",
    )(spot, own, own, own, lent, lent, lent, halo, halo, halo, taps, taps, taps, ending, c)


def decay_between(indices, decays, low, high):
    total = None
    for index, decay in zip(indices, decays):
        one = jnp.where((index > low) & (index < high), decay, 1.0)
        total = one if total is None else total * one
    return total


def summed(factors, arrays, m):
    total = factors[0] * arrays[0][m, :HEAD_DIM].astype(f32)
    for factor, array in zip(factors[1:], arrays[1:]):
        total = total + factor * array[m, :HEAD_DIM].astype(f32)
    return total


def members(spot, unit, count):
    place = (spot[0] // unit) % count
    return place, [place ^ i for i in range(count)]


def whole_group(indices, arrays, m):
    decays = [decay_of(a, m) for a in arrays]
    count = len(arrays)
    state = summed([decay_between(indices, decays, i, count) for i in indices], arrays, m)
    return state, decay_between(indices, decays, -1, count)


def earlier(place, indices, arrays, m, before):
    decays = [decay_of(a, m) for a in arrays]
    factors = [jnp.where(i < place, decay_between(indices, decays, i, place), 0.0) for i in indices[1:]]
    state = summed(factors, arrays[1:], m)
    decay = decay_between(indices, decays, -1, place)
    if before is None:
        return state, decay
    old = before[m, HEAD_DIM : HEAD_DIM + 1]
    return before[m, :HEAD_DIM] + old * state, old * decay


def group_kernel(spot, *refs):
    arrays, out = refs[:FOUR], refs[FOUR]
    _, indices = members(spot, 1, FOUR)
    for m in range(2 * SHARE):
        state, decay = whole_group(indices, arrays, m)
        out[m, :HEAD_DIM] = state.astype(bf16)
        out[m, HEAD_DIM:] = decay_rows(decay)


def upper_kernel(unit, count, has_before, spot, *refs):
    arrays = refs[:count]
    before = refs[count] if has_before else None
    before_o, total_o = refs[-2:]
    place, indices = members(spot, unit, count)
    for m in range(2 * SHARE):
        state, decay = earlier(place, indices, arrays, m, before)
        before_o[m, :HEAD_DIM] = state
        before_o[m, HEAD_DIM:] = jnp.broadcast_to(decay, (16, HEAD_DIM))
        state, decay = whole_group(indices, arrays, m)
        total_o[m, :HEAD_DIM] = state.astype(bf16)
        total_o[m, HEAD_DIM:] = decay_rows(decay)


def spread_kernel(unit, count, has_before, spot, *refs):
    arrays, near = refs[:count], refs[count : count + FOUR]
    before = refs[count + FOUR] if has_before else None
    outs = refs[-FOUR:]
    place, upper = members(spot, unit, count)
    _, indices = members(spot, 1, FOUR)
    for m in range(2 * SHARE):
        state, _ = earlier(place, upper, arrays, m, before)
        decays = [decay_of(x, m) for x in near]
        for j in range(FOUR):
            at = indices[j]
            factors = [jnp.where(i < at, decay_between(indices, decays, i, at), 0.0) for i in indices]
            total = decay_between(indices, decays, -1, at) * state + summed(factors, near, m)
            outs[j][m] = total.astype(bf16)


def small_call(kernel, name, shapes, spot, *args):
    vmem = pl.BlockSpec(memory_space=pltpu.VMEM)
    return pl.pallas_call(
        kernel,
        in_specs=[smem()] + [vmem] * len(args),
        out_specs=[vmem] * len(shapes),
        out_shape=shapes,
        cost_estimate=pl.CostEstimate(flops=1, bytes_accessed=1, transcendentals=0),
        name=name,
    )(spot, *args)


def neighbour(axis, bit):
    return [(i, i ^ bit) for i in range(lax.axis_size(axis))]


def partner(x, axis, bit=1):
    return lax.ppermute(x, axis, neighbour(axis, bit))


def radices(peers):
    sizes = []
    left = peers // FOUR
    while left > 1:
        sizes.append(min(FOUR, left))
        left //= sizes[-1]
    return sizes


def swapped(arrays, axis, unit_size=1):
    return [arrays[0]] + [partner(a, axis, unit_size * i) for i, a in enumerate(arrays) if i]


class Scan:
    def __init__(self, spot, near, axis):
        self.spot, self.axis, self.near = spot, axis, near
        self.sizes = radices(lax.axis_size(axis))

    def group(self):
        message = like(MESSAGE, bf16)
        (self.total,) = small_call(group_kernel, "group", [message], self.spot, *self.near)
        self.before = ()
        self.unit = FOUR
        for radix in self.sizes[:-1]:
            arrays = swapped([self.total] * radix, self.axis, self.unit)
            kernel = functools.partial(upper_kernel, self.unit, radix, bool(self.before))
            before, self.total = small_call(kernel, "upper", [like(MESSAGE), message], self.spot, *arrays, *self.before)
            self.before = (before,)
            self.unit *= radix
        self.far = swapped([self.total] * self.sizes[-1], self.axis, self.unit)

    def spread(self):
        kernel = functools.partial(spread_kernel, self.unit, self.sizes[-1], bool(self.before))
        self.parts = small_call(
            kernel, "spread", [like(PAIR, bf16)] * FOUR, self.spot, *self.far, *self.near, *self.before
        )
        self.entering = swapped(self.parts, self.axis)
        return self.entering


def prepare(k_ref, c_ref, state_refs, place, left, wide, decay, pair):
    tokens = k_ref.shape[1]
    for i, state in enumerate(state_refs):
        for m in range(SHARE):
            left[(place ^ i) * SHARE + m, :, :HEAD_DIM] = state[m]
    pair[...] = jnp.zeros_like(pair)
    for h in range(HEADS):
        k = k_ref[h]
        left[h, :, HEAD_DIM:] = k.T
        wide[h // 2, :, cut(h % 2)] = k
        decay[h] = jnp.broadcast_to(jnp.exp(c_ref[h : h + 1, :]), (8, tokens))


def key_products(columns, wide, pair):
    products = []
    for h in range(0, HEADS, 2):
        pair[h // 2, :HEAD_DIM, :HEAD_DIM] = columns(h)
        pair[h // 2, HEAD_DIM:, HEAD_DIM:] = columns(h + 1)
        both = nn(wide[h // 2], pair[h // 2])
        products += [both[:, :HEAD_DIM], both[:, HEAD_DIM:]]
    return products


def solve_kernel(
    place, q_ref, k_ref, s0, s1, s2, s3, c_ref, mask, ridge,
    x_out, p_out, m_out, score_out, scal_out,
    left, wide, decay, pair, x_s, r_s, p_s,
):
    i = pl.program_id(0)

    @pl.when(i == 0)
    def _():
        prepare(k_ref, c_ref, (s0, s1, s2, s3), place[0], left, wide, decay, pair)
        for h in range(HEADS):
            q = q_ref[h]
            x_s[h] = jnp.zeros_like(q)
            r_s[h] = q
            p_s[h] = q
            scal_out[h, 0:1] = jnp.sum(q * q, axis=0, keepdims=True)

    products = key_products(lambda h: p_s[h].astype(bf16), wide, pair)
    for h in range(HEADS):
        p = p_s[h]
        scores = (products[h] * mask[h]).astype(bf16)
        score_out[0, h] = scores
        stacked = jnp.concatenate([(decay[h, 0:1] * p).astype(bf16), scores], axis=0)
        image = nn(left[h], stacked) + ridge[h] * p
        norm = scal_out[h, pl.ds(i, 1)]
        dot = jnp.sum(p * image, axis=0, keepdims=True)
        size = norm / dot
        p_out[0, h] = p
        m_out[0, h] = image
        scal_out[h, pl.ds(2 * ITERS + i, 1)] = dot
        x_s[h] = x_s[h] + size * p
        r = r_s[h] - size * image
        r_s[h] = r
        norm_next = jnp.sum(r * r, axis=0, keepdims=True)
        scal_out[h, pl.ds(i + 1, 1)] = norm_next
        p_s[h] = r + (norm_next / norm) * p

    @pl.when(i == ITERS - 1)
    def _():
        for h in range(HEADS):
            x_out[h] = x_s[h].astype(bf16)


def common_scratch(tokens):
    square = pltpu.VMEM((HEADS, HEAD_DIM, tokens), f32)
    return [
        pltpu.VMEM((HEADS, HEAD_DIM, HEAD_DIM + tokens), bf16),
        pltpu.VMEM((HEADS // 2, tokens, 2 * HEAD_DIM), bf16),
        pltpu.VMEM((HEADS, 8, tokens), f32),
        pltpu.VMEM((HEADS // 2, 2 * HEAD_DIM, 2 * tokens), bf16),
        square, square, square,
    ]


def solve(place, q, k, states, c, mask, ridge):
    tokens = q.shape[2]
    step = pl.BlockSpec((1, HEADS, HEAD_DIM, tokens), lambda i: (i, 0, 0, 0))
    steps = (ITERS, HEADS, HEAD_DIM, tokens)
    return pl.pallas_call(
        solve_kernel,
        grid=(ITERS,),
        in_specs=[smem(), whole(HEADS, HEAD_DIM, tokens), whole(HEADS, tokens, HEAD_DIM)] + [whole(*PAIR)] * FOUR
        + [whole(HEADS, tokens), whole(HEADS, tokens, tokens), whole(HEADS, HEAD_DIM, tokens)],
        out_specs=[whole(HEADS, HEAD_DIM, tokens), step, step, step, whole(HEADS, 3 * ITERS, tokens)],
        out_shape=[
            like((HEADS, HEAD_DIM, tokens), bf16), like(steps), like(steps), like(steps, bf16),
            like((HEADS, 3 * ITERS, tokens)),
        ],
        scratch_shapes=common_scratch(tokens),
        compiler_params=pltpu.CompilerParams(vmem_limit_bytes=VMEM_LIMIT),
        cost_estimate=pl.CostEstimate(flops=1, bytes_accessed=1, transcendentals=0),
        name="solve",
    )(place, q, k, *states, c, mask, ridge)


def attend_back_kernel(place, ga_ref, k_ref, v_ref, x_ref, s0, s1, s2, s3, c_ref, mask_ref, gx_o, dk_o, dv_o, state_o):
    quarter = pl.program_id(0)
    tokens = k_ref.shape[1]
    for m in range(SHARE):
        head = quarter * SHARE + m
        c = c_ref[pl.ds(head, 1), :]
        mask = mask_ref[m]
        e = jnp.exp(c)
        state = s0[SHARE + m]
        for i, other in ((1, s1), (2, s2), (3, s3)):
            state = jnp.where((place[0] ^ i) == quarter, other[SHARE + m], state)
        ga = ga_ref[:, cut(m)].T
        low = ga.astype(bf16)
        x = x_ref[m]
        k = k_ref[m]
        scores = (nn(k, x) * mask).astype(bf16)
        dscores = (nn(v_ref[m], low) * mask).astype(bf16)
        ega = (e * ga).astype(bf16)
        gx_o[m] = tn(state, ega) + tn(k, dscores)
        dv_o[m] = nt(scores, low)
        dk_o[m] = nt(dscores, x)
        state_o[m] = nt(ega, x).astype(bf16)


def attend_back(place, ga, k, v, x, states, c, mask):
    tokens = k.shape[1]
    square = like((HEADS, HEAD_DIM, tokens))
    return pl.pallas_call(
        attend_back_kernel,
        grid=(QUARTERS,),
        in_specs=[smem(), quarter_columns(tokens, 0)] + [per_quarter(tokens, HEAD_DIM)] * 2
        + [per_quarter(HEAD_DIM, tokens)] + [whole(*PAIR)] * FOUR + [whole(HEADS, tokens), per_quarter(tokens, tokens)],
        out_specs=[per_quarter(HEAD_DIM, tokens)] * 4,
        out_shape=[square] * 3 + [like((HEADS, HEAD_DIM, HEAD_DIM), bf16)],
        cost_estimate=pl.CostEstimate(flops=1, bytes_accessed=1, transcendentals=0),
        name="attend_back",
    )(place, ga, k, v, x, *states, c, mask)


def adjoint_kernel(
    spot, place, gx_ref, k_ref, s0, s1, s2, s3, c_ref, mask, ridge, p_ref, m_ref, score_ref, scal_ref, values_ref,
    dq_ref, dk_ref, dridge_ref, o0, o1, o2, o3,
    left, wide, decay, pair, gr_s, gp_s, acc_s, next_s, gnorm_s, low_s, steps_p, steps_g, steps_s, stack,
):
    s = pl.program_id(0)
    i = ITERS - 1 - s
    tokens = k_ref.shape[1]
    at = pl.ds(pl.multiple_of(i * tokens, tokens), tokens)

    @pl.when(s == 0)
    def _():
        prepare(k_ref, c_ref, (s0, s1, s2, s3), place[0], left, wide, decay, pair)
        gr_s[...] = jnp.zeros_like(gr_s)
        gp_s[...] = jnp.zeros_like(gp_s)
        acc_s[...] = jnp.zeros_like(acc_s)
        next_s[...] = jnp.zeros_like(next_s)
        gnorm_s[...] = jnp.zeros_like(gnorm_s)

    for h in range(HEADS):
        p, m, gx = p_ref[0, h], m_ref[0, h], gx_ref[h]
        norm = scal_ref[h, pl.ds(i, 1)]
        dot = scal_ref[h, pl.ds(2 * ITERS + i, 1)]
        size = norm / dot
        ratio = jnp.where(s == 0, 0.0, scal_ref[h, pl.ds(i + 1, 1)] / norm)
        gp = gp_s[h]
        gratio = jnp.sum(gp * p, axis=0, keepdims=True)
        gnext = gnorm_s[h, 0:1] + gratio / norm
        gr = gr_s[h] + gp + (2.0 * gnext) * (next_s[h] - ratio * p)
        gsize = jnp.sum(gx * p - gr * m, axis=0, keepdims=True)
        gdot = -gsize * size / dot
        gm = gdot * p - size * gr
        gr_s[h] = gr
        gp_s[h] = ratio * gp + size * gx + gdot * m + ridge[h] * gm
        acc_s[h] = acc_s[h] + gm * p
        next_s[h] = p
        gnorm_s[h, 0:1] = gsize / dot - gratio * ratio / norm
        low = gm.astype(bf16)
        low_s[h] = low
        egm = (decay[h, 0:1] * gm).astype(bf16)
        steps_g[h, :, at] = low
        steps_p[h, :, at] = p.astype(bf16)
        steps_s[h, :, at] = score_ref[0, h]
        stack[h, HEAD_DIM:, at] = egm
    products = key_products(lambda h: low_s[h], wide, pair)
    for h in range(HEADS):
        dscores = (products[h] * mask[h]).astype(bf16)
        stack[h, :HEAD_DIM, at] = dscores
        stacked = jnp.concatenate([stack[h, HEAD_DIM:, at], dscores], axis=0)
        gp_s[h] = gp_s[h] + nn(left[h], stacked)

    @pl.when(s == ITERS - 1)
    def _():
        for h in range(HEADS):
            dq_ref[h] = gr_s[h] + gp_s[h] + 2.0 * gnorm_s[h, 0:1] * p_ref[0, h]
            both = nt(steps_p[h], stack[h])
            dk_ref[h] = (nt(steps_g[h], steps_s[h]) + both[:, :HEAD_DIM]).T
            left[h, :, :HEAD_DIM] = both[:, HEAD_DIM:].T.astype(bf16)
            dridge_ref[h] = jnp.sum(acc_s[h].T, axis=0, keepdims=True)
        for j, out in enumerate((o0, o1, o2, o3)):
            for m in range(SHARE):
                head = (position(spot) ^ j) * SHARE + m
                decay = decay_rows(block_decay(c_ref, head))
                out[m, :HEAD_DIM] = left[head, :, :HEAD_DIM]
                out[m, HEAD_DIM:] = decay
                out[SHARE + m, :HEAD_DIM] = values_ref[head]
                out[SHARE + m, HEAD_DIM:] = decay


def adjoint(spot, place, gx, k, states, c, mask, ridge, p_all, m_all, scores, scal, value_states):
    tokens = k.shape[1]
    step = pl.BlockSpec((1, HEADS, HEAD_DIM, tokens), lambda s: (ITERS - 1 - s, 0, 0, 0))
    square = pltpu.VMEM((HEADS, HEAD_DIM, tokens), f32)
    line = pltpu.VMEM((HEADS, HEAD_DIM, ITERS * tokens), bf16)
    return pl.pallas_call(
        adjoint_kernel,
        grid=(ITERS,),
        in_specs=[smem(), smem(), whole(HEADS, HEAD_DIM, tokens), whole(HEADS, tokens, HEAD_DIM)] + [whole(*PAIR)] * FOUR
        + [whole(HEADS, tokens), whole(HEADS, tokens, tokens), whole(HEADS, HEAD_DIM, tokens), step, step, step, whole(HEADS, 3 * ITERS, tokens), whole(HEADS, HEAD_DIM, HEAD_DIM)],
        out_specs=[whole(HEADS, HEAD_DIM, tokens), whole(HEADS, tokens, HEAD_DIM), whole(HEADS, 1, HEAD_DIM)]
        + [whole(*MESSAGE)] * FOUR,
        out_shape=[like((HEADS, HEAD_DIM, tokens)), like((HEADS, tokens, HEAD_DIM)), like((HEADS, 1, HEAD_DIM))]
        + [like(MESSAGE, bf16)] * FOUR,
        scratch_shapes=common_scratch(tokens) + [
            square,
            pltpu.VMEM((HEADS, 8, tokens), f32),
            pltpu.VMEM((HEADS, HEAD_DIM, tokens), bf16),
            line, line, line,
            pltpu.VMEM((HEADS, 2 * HEAD_DIM, ITERS * tokens), bf16),
        ],
        compiler_params=pltpu.CompilerParams(vmem_limit_bytes=VMEM_LIMIT),
        cost_estimate=pl.CostEstimate(flops=1, bytes_accessed=1, transcendentals=0),
        name="adjoint",
    )(spot, place, gx, k, *states, c, mask, ridge, p_all, m_all, scores, scal, value_states)


def conv_forward(own, lent, halo, t):
    total, shifted = conv_parts(with_halo(own, lent, halo), t[...])
    sig = jax.nn.sigmoid(total)
    return shifted, sig * (1.0 + total * (1.0 - sig)), total * sig


def unit_back(act, grad):
    scale = lax.rsqrt(jnp.sum(act * act, axis=-1, keepdims=True) + 1e-06)
    rows = act * scale
    return scale * (grad - rows * jnp.sum(rows * grad, axis=-1, keepdims=True))


def conv_back(dconv, shifted, t, g, dt):
    taps = t[...]
    tokens = dconv.shape[0]
    blank = jnp.zeros((HALO, dconv.shape[1]), f32)
    padded = jnp.concatenate([blank, dconv, blank], axis=0)
    rows = tokens + HALO
    total = taps[KW - 1 : KW] * padded[:rows]
    for j in range(KW - 1):
        total = total + taps[j : j + 1] * padded[KW - 1 - j : KW - 1 - j + rows]
    g[...] = total.astype(bf16)
    dt[...] = jnp.concatenate(
        [jnp.sum(dconv * shifted[j], axis=0, keepdims=True) for j in range(KW)], axis=0
    )


def queries_back_kernel(own, lent, halo, t, dq_ref, g, dt):
    shifted, slope, act = conv_forward(own, lent, halo, t)
    grads = [unit_back(act[:, cut(m)], dq_ref[m].T) for m in range(SHARE)]
    conv_back(jnp.concatenate(grads, axis=1) * slope, shifted, t, g, dt)


def returned(place, quarter, refs, m):
    state = refs[0][m]
    for i in range(1, FOUR):
        state = jnp.where((place ^ i) == quarter, refs[i][m], state)
    return state


def values_back_kernel(spot, own, lent, halo, t, dv_ref, k_ref, r0, r1, r2, r3, ending_ref, g, dt):
    quarter = pl.program_id(0)
    shifted, slope, _ = conv_forward(own, lent, halo, t)
    grads = []
    for m in range(SHARE):
        rv = returned(position(spot), quarter, (r0, r1, r2, r3), SHARE + m)
        grads.append(dv_ref[m] + ending_ref[m] * nt(k_ref[m], rv))
    conv_back(jnp.concatenate(grads, axis=1) * slope, shifted, t, g, dt)


def keys_back_kernel(
    spot, own, lent, halo, t, dk1, dk2, k_ref, v_ref, r0, r1, r2, r3, ending_ref, g, dt
):
    quarter = pl.program_id(0)
    shifted, slope, act = conv_forward(own, lent, halo, t)
    grads = []
    for m in range(SHARE):
        rv = returned(position(spot), quarter, (r0, r1, r2, r3), SHARE + m)
        rk = returned(position(spot), quarter, (r0, r1, r2, r3), m).astype(f32)
        rk = (rk + rk.T).astype(bf16)
        ending = ending_ref[m]
        dk = dk1[m] + dk2[m] + ending * (nn(k_ref[m], rk) + nn(v_ref[m], rv))
        grads.append(unit_back(act[:, cut(m)], dk))
    conv_back(jnp.concatenate(grads, axis=1) * slope, shifted, t, g, dt)


def third_back(kernel, name, which, taps_third, projected, taps, before, others, specs):
    own, lent, halo = projected
    tokens = own.shape[0]
    return pl.pallas_call(
        kernel,
        grid=(QUARTERS,),
        in_specs=[smem()] * len(before) + [quarter_columns(rows, which) for rows in (tokens, tokens, halo.shape[0])]
        + [quarter_columns(KW, taps_third)] + specs,
        out_specs=[quarter_columns(tokens + HALO, 0), quarter_columns(KW, 0)],
        out_shape=[like((tokens + HALO, D), bf16), like((KW, D))],
        cost_estimate=pl.CostEstimate(flops=1, bytes_accessed=1, transcendentals=0),
        name=name,
    )(*before, own, lent, halo, taps, *others)


def queries_back(projected, taps, dq):
    return third_back(queries_back_kernel, "queries_back", 0, 0, projected, taps, (), (dq,), [per_quarter(HEAD_DIM, HEAD_DIM)])


def values_back(spot, projected, taps, dv, k, states, ending):
    square = per_quarter(HEAD_DIM, HEAD_DIM)
    return third_back(
        values_back_kernel, "values_back", 2, 2, projected, taps, (spot,), (dv, k, *states, ending),
        [square] * 2 + [whole(*PAIR)] * FOUR + [square],
    )


def keys_back(spot, projected, taps, dk1, dk2, k, v, states, ending):
    square = per_quarter(HEAD_DIM, HEAD_DIM)
    return third_back(
        keys_back_kernel, "keys_back", 1, 1, projected, taps, (spot,), (dk1, dk2, k, v, *states, ending),
        [square] * 4 + [whole(*PAIR)] * FOUR + [square],
    )


def completed(ref, extra):
    more = extra[...].astype(f32)
    more = jnp.concatenate([jnp.zeros_like(more), more], axis=0)
    last = ref.shape[0] - 16
    return [ref[HALO:last], (ref[last:].astype(f32) + more).astype(bf16)]


def products_kernel(plan, joined, cuts, spot, *refs):
    count = len(plan)
    odd = spot[0] % 2 == 1
    outs, scratch = refs[-count - (1 if joined else 1 + len(cuts)) : -count], refs[-count:]

    @pl.when(pl.program_id(0) == 0)
    def _():
        for (lefts, _, _), both in zip(plan, scratch):
            both[...] = jnp.concatenate([refs[at][...] if rows is None else refs[at][rows] for at, rows in lefts], axis=1)

    start = 0
    def right(at, stacked):
        if not stacked:
            return refs[at][...]
        return jnp.concatenate([refs[at][i : i + stacked] for i in range(0, refs[at].shape[0], stacked)], axis=1)

    for (_, rights, size), both in zip(plan, scratch):
        if len(rights) == 4:
            rows = [part for i in (0, 1) for part in completed(refs[rights[i][0]], refs[rights[2 + i][0]])]
        else:
            rows = [right(*at) for at in rights]
        product = nn(both[...], jnp.concatenate(rows, axis=0))
        at = slice(start, start + size)
        start += size
        if joined:
            outs[0][:, at, :] = product.reshape(product.shape[0] // size, size, product.shape[1]).astype(bf16)
            continue
        blocks = product.reshape(product.shape[0] // (2 * size), 2, size, product.shape[1])
        outs[0][:, at, :] = jnp.where(odd, blocks[:, 1], blocks[:, 0]).astype(bf16)
        other = jnp.where(odd, blocks[:, 0], blocks[:, 1]).astype(bf16)
        for out, cut_at in zip(outs[1:], cuts):
            first, last = max(at.start, cut_at.start), min(at.stop, cut_at.stop)
            if first < last:
                out[:, first - cut_at.start : last - cut_at.start, :] = other[:, first - at.start : last - at.start]


def unstacked(array, index):
    row, tokens = index
    return jnp.concatenate([array[row + i * tokens : row + (i + 1) * tokens] for i in range(D // HEAD_DIM)], axis=1)


def products(spot, peers, lefts, rights, tile, joined=False, messages=1):
    sizes = [(part[0][1].stop - part[0][1].start) // peers for part in lefts]
    width = rights[0][0][0].shape[1] if rights[0][0][1] is None else D
    count, number = (peers, 1) if joined else (peers // 2, 2)
    shape = (count, sum(sizes), width)
    cuts = [slice(i * shape[1] // messages, (i + 1) * shape[1] // messages) for i in range(messages)]
    if any(size % 8 for size in sizes):
        odd = spot[0] % 2
        sides = []
        for side in range(number):
            parts = []
            for left, right in zip(lefts, rights):
                if len(right) == 4:
                    rows = []
                    for i in (0, 1):
                        (array, third), (extra, _) = right[i], right[2 + i]
                        size = array.shape[0] // 3
                        rows += completed(array[third * size : (third + 1) * size], extra[:, third * D : (third + 1) * D])
                else:
                    rows = [unstacked(array, index) if index else array for array, index in right]
                blocks = nn(jnp.concatenate([array[at] for array, at in left], axis=1), jnp.concatenate(rows, axis=0))
                blocks = blocks.astype(bf16).reshape(count, number, -1, width)
                parts.append(lax.dynamic_index_in_dim(blocks, 0 if joined else odd ^ side, 1, keepdims=False))
            sides.append(jnp.concatenate(parts, axis=1))
        return sides if joined else sides[:1] + [sides[1][:, at] for at in cuts]
    arrays, specs, plan = [], [], []

    def place_of(array, spec):
        for at, other in enumerate(arrays):
            if other is array and specs[at] is None and spec is None:
                return at
        arrays.append(array)
        specs.append(spec)
        return len(arrays) - 1

    def columns(array, index):
        if index is None:
            return pl.BlockSpec((array.shape[0], tile), lambda j: (0, j))
        if isinstance(index, int) and array.shape[1] == D:
            return pl.BlockSpec((array.shape[0] // 3, tile), lambda j: (index, j))
        if isinstance(index, int):
            return pl.BlockSpec((array.shape[0], tile), lambda j: (0, index * (D // tile) + j))
        size = index[1] * tile // HEAD_DIM
        return pl.BlockSpec((size, HEAD_DIM), lambda j: (index[0] // size + j, 0))

    def left_part(array, rows):
        size = rows.stop - rows.start
        if rows.start % size:
            return place_of(array, None), rows
        at = rows.start // size
        return place_of(array, pl.BlockSpec((size, array.shape[1]), lambda j: (at, 0))), None

    for left, right, size in zip(lefts, rights, sizes):
        plan.append((
            [left_part(array, rows) for array, rows in left],
            [(place_of(array, columns(array, index)), index[1] if isinstance(index, tuple) else None) for array, index in right],
            size,
        ))
    heights = [shape[1]] + ([] if joined else [at.stop - at.start for at in cuts])
    return pl.pallas_call(
        functools.partial(products_kernel, plan, joined, cuts),
        grid=(width // tile,),
        in_specs=[smem()] + [spec or whole(*array.shape) for array, spec in zip(arrays, specs)],
        out_specs=[pl.BlockSpec((count, height, tile), lambda j: (0, 0, j)) for height in heights],
        out_shape=[like((count, height, width), bf16) for height in heights],
        scratch_shapes=[
            pltpu.VMEM((left[0][1].stop - left[0][1].start, sum(array.shape[1] for array, _ in left)), bf16) for left in lefts
        ],
        compiler_params=pltpu.CompilerParams(vmem_limit_bytes=VMEM_LIMIT),
        cost_estimate=pl.CostEstimate(flops=1, bytes_accessed=1, transcendentals=0),
        name="products",
    )(spot, *arrays)


def lent_kernel(own, peer, extra1, extra2, logit1, logit2, qkv_ref, gate_ref, own_o, theirs_o):
    rows = own_o.shape[0]
    logits = [unstacked(ref, (D // HEAD_DIM * rows, rows)) for ref in (logit1, logit2)]
    total = nt(jnp.concatenate(logits, axis=0), gate_ref[...])
    size = rows + HALO
    for third in range(3):
        at, columns = slice(third * size, (third + 1) * size), slice(third * D, (third + 1) * D)
        both = completed(own.at[at], extra1[:, columns]) + completed(peer.at[at], extra2[:, columns])
        total = total + nt(jnp.concatenate(both, axis=0), qkv_ref[:, columns])
    own_o[...] = total[:rows]
    theirs_o[...] = total[rows:].astype(bf16)


def lent_rows(own, peer, extras, logits, qkv_weight, gate_weight):
    rows = own.shape[0] // 3 - HALO
    half = qkv_weight.shape[0]
    vmem = pl.BlockSpec(memory_space=pltpu.VMEM)
    return pl.pallas_call(
        lent_kernel,
        in_specs=[vmem] * 8,
        out_specs=[vmem] * 2,
        out_shape=[like((rows, half)), like((rows, half), bf16)],
        compiler_params=pltpu.CompilerParams(vmem_limit_bytes=VMEM_LIMIT),
        cost_estimate=pl.CostEstimate(flops=1, bytes_accessed=1, transcendentals=0),
        name="lent_rows",
    )(own, peer, *extras, *logits, qkv_weight, gate_weight)


def norm_back_kernel(place, own, back, tok_ref, gain_ref, hid_ref, tq, tk, tv, second_ref, ridge_ref, tok_o, vec_o):
    mine, other = own[...], back[...].astype(f32)
    grad = jnp.where(
        place[0] == 0, jnp.concatenate([mine, other], axis=1), jnp.concatenate([other, mine], axis=1)
    )
    tokens = tok_ref[...]
    scale = lax.rsqrt(jnp.mean(tokens * tokens, axis=-1, keepdims=True) + 1e-05)
    rows = tokens * scale
    grows = grad * gain_ref[...]
    tok_o[...] = hid_ref[...] + scale * (grows - rows * jnp.mean(grows * rows, axis=-1, keepdims=True))
    vec_o[:KW] = jnp.concatenate([tq[...], tk[...], tv[...]], axis=1)
    ridge = jnp.concatenate([ridge_ref[h] for h in range(HEADS)], axis=1)
    first = jnp.sum(grad * rows, axis=0, keepdims=True)
    vec_o[KW : KW + 1] = jnp.concatenate([first, second_ref[...], ridge], axis=1)
    vec_o[KW + 1 :] = jnp.zeros((8 - KW - 1, 3 * D), f32)


def norm_back(place, own, back, tokens, gain, hidden, taps, second, ridge):
    vmem = pl.BlockSpec(memory_space=pltpu.VMEM)
    return pl.pallas_call(
        norm_back_kernel,
        in_specs=[smem()] + [vmem] * 10,
        out_specs=[vmem] * 2,
        out_shape=[like(tokens.shape), like((8, 3 * D))],
        cost_estimate=pl.CostEstimate(flops=1, bytes_accessed=1, transcendentals=0),
        name="norm_back",
    )(place, own, back, tokens, gain, hidden, *taps, second, ridge)


def step_kernel(bit, kept_mine, kept_other, *refs):
    mine_o, other_o = refs[-2:]
    start = 0
    for mine, other in zip(refs[0:-2:2], refs[1:-2:2]):
        at = slice(start, start + mine.shape[1])
        start += mine.shape[1]
        mine_o[0, at] = (kept_mine[0, at].astype(f32) + mine[0].astype(f32)).astype(bf16)
        other_o[0, at] = (kept_other[0, at].astype(f32) + other[0].astype(f32)).astype(bf16)


def halving_step(bit, below, kept, got):
    count, size, width = kept.shape

    def half(side, rows):
        def index(i, s):
            return ((i // below) * 2 * below + (s[0] if side == 0 else 1 - s[0]) * below + i % below, 0, 0)

        return pl.BlockSpec((1, rows, width), index)

    out = pl.BlockSpec((1, size, width), lambda i, s: (i, 0, 0))
    arrays = [kept] + list(got)
    return pl.pallas_call(
        step_kernel,
        grid_spec=pltpu.PrefetchScalarGridSpec(
            num_scalar_prefetch=1,
            grid=(count // 2,),
            in_specs=[half(side, x.shape[1]) for x in arrays for side in (0, 1)],
            out_specs=[out, out],
        ),
        out_shape=[like((count // 2, size, width), bf16)] * 2,
        cost_estimate=pl.CostEstimate(flops=1, bytes_accessed=1, transcendentals=0),
        name="halving",
    )(bit, *[x for x in arrays for _ in (0, 1)])


BLOCKS = D // HEAD_DIM


def middle_kernel(
    owners, place, x_ref, s0, s1, s2, s3, k_ref, v_ref, c_ref, mask_ref, own_logit, lent_logit, tok_ref, cot_ref, gain_ref, first_ref,
    own_out, out_a, out_b, out_c, out_d, *refs,
):
    own_up = refs[:4]
    up_parts = (refs[4:8], refs[8:12])
    own_down = refs[12]
    down_parts = refs[13:17]
    (out_o, hid_o, gatt_o, own_o, sent_o, ggu_o, dgain_o) = refs[17:24]
    out_s, up_s, down_s, nf_s, gb_s, att_s, sig_s, hid_s, acc_s, gnf_s, inner_s = refs[24:]
    j = pl.program_id(0)
    y = place[0]
    half = D // 2

    def aligned(at, by):
        return pl.multiple_of(at, by)

    mine = pl.ds(aligned(y * half, half), half)
    theirs = pl.ds(aligned((1 - y) * half, half), half)

    def order(q):
        return [q, q ^ 2, q ^ 1, q ^ 3]

    tile = own_up[0].shape[1]
    tokens = tok_ref.shape[0]

    def spread_rows(rows, start):
        total = rows.shape[0]
        size = total // owners
        own_at = slice(start, start + total // 2)
        sent_at = slice(3 * BLOCKS * tokens + start, 3 * BLOCKS * tokens + start + total // 2)
        if size % 8:
            own_o[own_at], sent_o[sent_at] = rows[: total // 2].astype(bf16), rows[total // 2 :].astype(bf16)
            return
        blocks = rows.reshape(owners // 2, 2, size, rows.shape[1])
        for out, at, odd in ((own_o, own_at, y == 1), (sent_o, sent_at, y == 0)):
            out[at] = jnp.where(odd, blocks[:, 1], blocks[:, 0]).reshape(total // 2, rows.shape[1]).astype(bf16)

    def stack_right(value, index):
        for i in range(BLOCKS):
            sent_o[(index * BLOCKS + i) * tokens : (index * BLOCKS + i + 1) * tokens] = value[:, cut(i)]

    def scale_of(hidden):
        return lax.rsqrt(jnp.mean(hidden * hidden, axis=-1, keepdims=True) + 1e-05)

    @pl.when(j == 0)
    def _():
        for i, state in enumerate((s0, s1, s2, s3)):
            for m in range(SHARE):
                head = (place[1] ^ i) * SHARE + m
                c = c_ref[pl.ds(head, 1), :]
                x = x_ref[head]
                scores = (nn(k_ref[head], x) * mask_ref[head]).astype(bf16)
                part = jnp.exp(c) * nn(state[SHARE + m], x) + tn(v_ref[head], scores)
                att_s[:, pl.ds(aligned(head * HEAD_DIM, HEAD_DIM), HEAD_DIM)] = part.T
        out_s[mine, :] = own_out[...]
        wide = out_a.shape[1]
        for part, q in zip((out_a, out_b, out_c, out_d), order(place[1])):
            out_s[theirs, pl.ds(aligned(q * wide, wide), wide)] = part[...]
        sig = jax.nn.sigmoid(own_logit[...] + lent_logit[...].astype(f32))
        sig_s[...] = sig
        mix = (att_s[...] * sig).astype(bf16)
        spread_rows(mix.astype(f32).T, half)
        normed = tok_ref[...] * scale_of(tok_ref[...]) * first_ref[...]
        spread_rows(normed.astype(bf16).astype(f32).T, 2 * half)
        hidden = tok_ref[...] + nn(mix, out_s[...])
        hid_s[...] = hidden
        normed = (hidden * scale_of(hidden) * gain_ref[...]).astype(bf16)
        nf_s[...] = normed
        spread_rows(normed.astype(f32).T, 0)
        gb_s[...] = cot_ref[...].astype(bf16)
        stack_right(gb_s[...], 2)
        acc_s[...] = jnp.zeros_like(acc_s)
        gnf_s[...] = jnp.zeros_like(gnf_s)

    for i in range(4):
        up_s[mine, i * tile : (i + 1) * tile] = own_up[i][...]
    count = up_parts[0][0].shape[0]
    at = pl.ds(aligned((1 - y) * half, 16), count)
    for part, q in zip(up_parts[0], order(place[2])):
        slot = (q >> 1) * 2 + ((q & 1) ^ y)
        up_s[at, pl.ds(aligned(slot * tile, tile), tile)] = part[...]
    at = pl.ds(aligned((1 - y) * half + count, 16), half - count)
    for i, part in enumerate(up_parts[1]):
        slot = ((place[1] ^ (i // 2)) & 1) * 2 + i % 2
        up_s[at, pl.ds(aligned(slot * tile, tile), tile)] = part[...]
    down_s[:tile, :] = own_down[...]
    wide = down_parts[0].shape[1]
    for part, q in zip(down_parts, order(place[1])):
        down_s[tile:, pl.ds(aligned(q * wide, wide), wide)] = part[...]
    product = nn(nf_s[...], up_s[...])
    gate, up = product[:, : 2 * tile], product[:, 2 * tile :]
    ginner = nt(gb_s[...], down_s[...])
    sig = jax.nn.sigmoid(gate)
    silu = gate * sig
    inner = (silu * up).astype(bf16)
    ggate = (ginner * up * (sig * (1.0 + gate * (1.0 - sig)))).astype(bf16)
    gup = (ginner * silu).astype(bf16)
    ggu = jnp.concatenate([ggate, gup], axis=1)
    acc_s[...] += nn(inner, down_s[...])
    gnf_s[...] += nt(ggu, up_s[...])
    inner_t = inner.astype(f32).T
    for slot, value in ((y, inner_t[:tile]), (1 - y, inner_t[tile:])):
        inner_s[pl.ds(aligned(slot * (FF // 2) + j * tile, tile), tile), :] = value
    share = FF // 2
    for i, (slot, value) in enumerate(((y, ggate), (1 - y, ggate), (2 + y, gup), (3 - y, gup))):
        at = pl.ds(aligned(slot * share + j * tile, tile), tile)
        ggu_o[:, at] = value[:, (i % 2) * tile : (i % 2 + 1) * tile]

    @pl.when(j == pl.num_programs(0) - 1)
    def _():
        spread_rows(inner_s[...], 3 * half)
        hidden = hid_s[...]
        out_o[...] = hidden + acc_s[...]
        scale = scale_of(hidden)
        rows = hidden * scale
        gnf = gnf_s[...]
        dgain_o[...] = jnp.sum(gnf * rows, axis=0, keepdims=True)
        grows = gnf * gain_ref[...]
        ghid = cot_ref[...] + scale * (grows - rows * jnp.mean(grows * rows, axis=-1, keepdims=True))
        hid_o[...] = ghid
        low = ghid.astype(bf16)
        stack_right(low, 0)
        gmix = nt(low, out_s[...])
        sig = sig_s[...]
        gatt = gmix * sig
        gatt_o[...] = gatt
        stack_right((gatt * att_s[...] * (1.0 - sig)).astype(bf16), 1)


def middle(owners, place, attention, own_logit, lent_logit, tok, cot, gain, gain_first, out_weight, up_weight, down_weight, up_parts, rest_parts):
    tokens = tok.shape[0]
    tile = 128
    share = FF // 2 // tile
    half = D // 2
    left_rows = 3 * half + FF // 2

    def full(*shape):
        return pl.BlockSpec(shape, lambda j, s: (0,) * len(shape))

    rows = full(tokens, D)
    own_up = [
        pl.BlockSpec((half, tile), lambda j, s: (0, s[0] * share + j)),
        pl.BlockSpec((half, tile), lambda j, s: (0, (1 - s[0]) * share + j)),
        pl.BlockSpec((half, tile), lambda j, s: (0, (2 + s[0]) * share + j)),
        pl.BlockSpec((half, tile), lambda j, s: (0, (3 - s[0]) * share + j)),
    ]
    up_specs = [pl.BlockSpec((p.shape[0], tile), lambda j, s: (0, j)) for p in up_parts[:4]]
    rest_rows = up_parts[4].shape[0]
    up_specs += [
        pl.BlockSpec((rest_rows, tile), lambda j, s: (0, s[0] * share + j)),
        pl.BlockSpec((rest_rows, tile), lambda j, s: (0, (1 - s[0]) * share + j)),
    ] * 2
    up_parts = up_parts[:4] + (up_parts[4],) * 2 + (up_parts[5],) * 2
    own_down = pl.BlockSpec((tile, D), lambda j, s: (j, 0))
    down_specs = [pl.BlockSpec((tile, D // 4), lambda j, s: (half // tile + j, 0))] * 4
    square = (HEAD_DIM, HEAD_DIM)
    return pl.pallas_call(
        functools.partial(middle_kernel, owners),
        grid_spec=pltpu.PrefetchScalarGridSpec(
            num_scalar_prefetch=1,
            grid=(share,),
            in_specs=[full(HEADS, HEAD_DIM, tokens)] + [full(*PAIR)] * FOUR + [full(HEADS, tokens, HEAD_DIM)] * 2
            + [full(HEADS, tokens), full(HEADS, tokens, tokens)]
            + [pl.BlockSpec((tokens, D), lambda j, s: (0, 3))] * 2
            + [rows] * 2 + [full(1, D), full(1, D), full(half, D)] + [full(half, D // 4)] * 4
            + own_up + up_specs + [own_down] + down_specs,
            out_specs=[
                rows, rows, rows, full(left_rows, tokens), full(3 * BLOCKS * tokens + left_rows, tokens),
                full(tokens, 2 * FF),
                full(1, D),
            ],
            scratch_shapes=[
                pltpu.VMEM((D, D), bf16),
                pltpu.VMEM((D, 4 * tile), bf16),
                pltpu.VMEM((2 * tile, D), bf16),
                pltpu.VMEM((tokens, D), bf16),
                pltpu.VMEM((tokens, D), bf16),
                pltpu.VMEM((tokens, D), f32),
                pltpu.VMEM((tokens, D), f32),
                pltpu.VMEM((tokens, D), f32),
                pltpu.VMEM((tokens, D), f32),
                pltpu.VMEM((tokens, D), f32),
                pltpu.VMEM((FF, tokens), f32),
            ],
        ),
        out_shape=[
            like((tokens, D)), like((tokens, D)), like((tokens, D)),
            like((left_rows, tokens), bf16), like((3 * BLOCKS * tokens + left_rows, tokens), bf16),
            like((tokens, 2 * FF), bf16),
            like((1, D)),
        ],
        compiler_params=pltpu.CompilerParams(vmem_limit_bytes=VMEM_LIMIT),
        cost_estimate=pl.CostEstimate(flops=1, bytes_accessed=1, transcendentals=0),
        name="middle",
    )(
        place, *attention, own_logit, lent_logit, tok, cot, gain, gain_first, out_weight, *rest_parts,
        *[up_weight] * 4, *up_parts, down_weight, *rest_parts,
    )


def shifted(x, axis, by):
    peers = lax.axis_size(axis)
    return lax.ppermute(x, axis, [(i, i + by) for i in range(peers) if 0 <= i + by < peers])


def crossed(x, by):
    peers, pair = lax.axis_size("ctx"), 2
    return lax.ppermute(
        x,
        ("ctx", "fsdp"),
        [(i * pair + s, (i + by) * pair + 1 - s) for i in range(peers) if 0 <= i + by < peers for s in range(pair)],
    )


def pick(x, index, axis=0):
    return lax.dynamic_index_in_dim(x, index, axis, keepdims=False)


def part(x, index, axis):
    size = x.shape[axis] // 2
    return lax.dynamic_slice_in_dim(x, index * size, size, axis)


def quarter(shard, q, start=0, count=None):
    wide = shard.shape[1] // 4
    return lax.dynamic_slice(shard, (start, q * wide), (count or shard.shape[0], wide))


class Reduction:
    def __init__(self, order, blocks):
        self.here = lax.axis_index("ctx")
        levels = lax.axis_size("ctx").bit_length() - 1
        self.order = list(order) + [level for level in range(levels) if level not in order]
        self.left = list(range(levels))
        self.kept, *sent = blocks
        self.send(sent)

    def bit(self):
        return (self.here >> self.order[0]) & 1

    def send(self, arrays):
        level = self.order.pop(0)
        self.left.remove(level)
        self.got = [partner(array, "ctx", 1 << level) for array in arrays]

    def step(self):
        below = 1 << self.left.index(self.order[0])
        self.kept, sent = halving_step(self.bit().astype(jnp.int32)[None], below, self.kept, self.got)
        self.send([sent])
        return sent

    def result(self, sizes):
        while self.order:
            self.step()
        total = (self.kept.astype(f32) + self.got[0].astype(f32))[0]
        ends = [sum(sizes[: i + 1]) for i in range(len(sizes))]
        return [total[end - size : end] for end, size in zip(ends, sizes)]


class Sequence:
    def __init__(self):
        self.last = ()

    def gate(self, *values):
        return lax.optimization_barrier(values + self.last)[: len(values)]

    def mark(self, *values):
        self.last = values


def added(value, axis):
    for level in range(lax.axis_size(axis).bit_length() - 1):
        value = value + partner(value, axis, 1 << level)
    return value


def rms_scale(values, gain):
    return values * lax.rsqrt(jnp.mean(values * values, axis=-1, keepdims=True) + 1e-05) * gain


def sided(mine, theirs, y, axis):
    return jnp.where(
        y == 0, jnp.concatenate([mine, theirs], axis=axis), jnp.concatenate([theirs, mine], axis=axis)
    )


UP_ROWS = 384


def local(
    inputs,
    qkv_weight,
    gate_weight,
    out_weight,
    up_weight,
    down_weight,
    conv_taps,
    gain_attn,
    gain_ffn,
    ridge_terms,
    forget,
    cotangent,
):
    tokens = inputs[0]
    rows = tokens.shape[0]
    y = lax.axis_index("fsdp")
    here = lax.axis_index("ctx")
    peers = lax.axis_size("ctx")
    owners = peers * 2
    near_x = here % 4
    near_z = here % 2 + 2 * ((here // 4) % 2)
    place = jnp.stack([y, near_x, near_z]).astype(jnp.int32)
    spot = here.astype(jnp.int32)[None]
    spot_back = (peers - 1 - here).astype(jnp.int32)[None]
    ring = near_x.astype(jnp.int32)[None]
    seq = Sequence()

    lines = jnp.stack([gain_attn, gain_ffn, ridge_terms, ridge_terms])
    mine, theirs = norm(place, tokens, conv_taps, lines)
    theirs = partner(theirs, "fsdp")
    lent = weigh(theirs, rows, gain_attn[None], qkv_weight, gate_weight, bf16)
    seq.mark(lent)
    lent = partner(lent, "fsdp")
    peer_extra = theirs[rows:].astype(f32)
    (peer_extra,) = seq.gate(peer_extra)
    taps_rows = KW * 3
    vectors = sided(lines[:3].astype(f32), peer_extra[taps_rows : taps_rows + 3], y, 1)
    taps = sided(conv_taps.astype(f32), peer_extra[:taps_rows].reshape(conv_taps.shape), y, 1)
    gain_first, gain_second = vectors[0], vectors[1:2]
    ridge = vectors[2].reshape(HEADS, HEAD_DIM)
    cumulative = jnp.cumsum(jnp.log(forget[0]).T, axis=-1)
    strength = (1.0 - forget[0]).T
    out_here, up_here, down_here = seq.gate(out_weight, up_weight, down_weight)
    rest_quarter = jnp.concatenate([quarter(out_here, near_x), quarter(down_here, near_x)], axis=0)
    seq.mark(rest_quarter)
    rest_direct = partner(rest_quarter, "fsdp")
    (up_here,) = seq.gate(up_here)
    up_quarters = [
        quarter(up_here, near_z, 0, UP_ROWS),
        lax.dynamic_slice(up_here, (UP_ROWS, (here % 2) * FF), (D // 2 - UP_ROWS, FF)),
    ]
    seq.mark(*up_quarters)
    cumulative, strength, ridge, taps, mine = seq.gate(cumulative, strength, ridge, taps, mine)
    own = weigh(mine, rows, gain_attn[None], qkv_weight, gate_weight, f32)
    mask, ending, ridge = tables(cumulative, strength, ridge)
    seq.mark(mask, own)

    own, lent, up_first = seq.gate(own, lent, up_quarters[0])
    halo = shifted((own[rows - 8 :, : 3 * D] + lent[rows - 8 :, : 3 * D].astype(f32)).astype(bf16), "ctx", 1)
    projected = own, lent, halo
    queries, keys_low, values_low, *near = features(spot, projected, taps, ending, cumulative)
    seq.mark(*near)
    scan = Scan(spot, swapped(near, "ctx"), "ctx")
    up_first = partner(up_first, "fsdp")

    def split(left):
        flat = left.reshape(peers, 2, left.shape[0] // owners, left.shape[1])
        return [pick(flat, side, 1).reshape(-1, left.shape[1]) for side in (y, 1 - y)]

    scan.near = list(seq.gate(*scan.near))
    scan.group()
    seq.mark(scan.total)
    (rest_direct,) = seq.gate(rest_direct)
    rest_across = partner(rest_direct, "ctx", 2)
    scan.far = list(seq.gate(*scan.far))
    states = scan.spread()
    seq.mark(scan.parts[0])
    up_first, up_second = seq.gate(up_first, up_quarters[1])
    up_second = partner(up_second, "fsdp")
    first_across = partner(up_first, "ctx", 4)
    *states, queries = seq.gate(*states, queries)
    seq.mark(states[1], states[2], states[3])
    rest_direct, rest_across, up_first = seq.gate(rest_direct, rest_across, up_first)
    rest_core, rest_far, first_core = partner(rest_direct, "ctx", 1), partner(rest_across, "ctx", 1), partner(up_first, "ctx", 1)
    (queries,) = seq.gate(queries)
    x, p_all, m_all, scores, scal = solve(ring, queries, keys_low, states, cumulative, mask, ridge)
    seq.mark(x)

    def split(left):
        flat = left.reshape(peers, 2, left.shape[0] // owners, left.shape[1])
        return [pick(flat, side, 1).reshape(-1, left.shape[1]) for side in (y, 1 - y)]

    def share(right):
        return right, partner(right, "fsdp")

    up_second, rest_core, rest_far = seq.gate(up_second, rest_core, rest_far)
    second_core = partner(up_second, "ctx", 1)
    (first_across,) = seq.gate(first_across)
    rest_parts = (rest_direct, rest_across, rest_core, rest_far)
    up_parts = (up_first, first_across, first_core, partner(first_across, "ctx", 1))
    up_parts += (up_second, second_core)

    output, grad_hidden, grad_attended, lefts, message, grad_gate_up, grad_second_gain = middle(
        owners, place, (x, *states, keys_low, values_low, cumulative, mask), own, lent,
        tokens, cotangent[0], gain_second, gain_first[None], out_weight, up_weight, down_weight, up_parts, rest_parts
    )
    size = D // 2
    parts = [slice(0, size), slice(size, 2 * size), slice(2 * size, 3 * size), slice(3 * size, 3 * size + FF // 2)]
    start = 3 * BLOCKS * rows
    peer_parts = [slice(start + at.start, start + at.stop) for at in parts]
    if (D // owners) % 8 or (FF // owners) % 8:
        pairs = [split(jnp.concatenate([lefts[at], message[there]], axis=0)) for at, there in zip(parts, peer_parts)]
        lefts = jnp.concatenate([own for own, _ in pairs], axis=0)
        message = jnp.concatenate([message[:start]] + [sent for _, sent in pairs], axis=0)
    seq.mark(grad_second_gain)
    message_peer = partner(message, "fsdp")
    (grad_attended,) = seq.gate(grad_attended)
    gx, dk_attend, dv, value_states = attend_back(
        ring, grad_attended, keys_low, values_low, x, states, cumulative, mask
    )
    dq, dk_solve, grad_ridge, *own = adjoint(
        spot_back, ring, gx, keys_low, states, cumulative, mask, ridge, p_all, m_all, scores, scal, value_states
    )
    seq.mark(*own)
    back = Scan(spot_back, swapped(own, "ctx"), "ctx")
    (up_here,) = seq.gate(grad_gate_up)
    both_up = share(up_here)
    dq, back.near[1] = seq.gate(dq, back.near[1])
    low_q, taps_q = queries_back(projected, taps, dq)
    seq.mark(low_q)
    back.near = list(seq.gate(*back.near))
    back.group()
    seq.mark(back.total)
    lefts_here, message_peer, back.far[1] = seq.gate(lefts, message_peer, back.far[1])
    rights = [(i * BLOCKS * rows, rows) for i in range(3)]
    (early,) = products(
        spot, peers, [[(lefts_here, parts[i]), (message_peer, peer_parts[i])] for i in (1, 2, 3)],
        [[(message, at), (message_peer, at)] for at in rights], 512, joined=True
    )
    seq.mark(early)
    early = lax.psum_scatter(early.reshape(-1, D), "ctx", scatter_dimension=0, tiled=True)
    back.far = list(seq.gate(*back.far))
    states_back = back.spread()
    seq.mark(back.parts[0])
    dv, *states_back = seq.gate(dv, *states_back)
    low_v, taps_v = values_back(
        spot_back, projected, taps, dv, keys_low, states_back, ending
    )
    seq.mark(low_v)
    (dk_attend,) = seq.gate(dk_attend)
    low_k, taps_k = keys_back(
        spot_back, projected, taps, dk_attend, dk_solve, keys_low, values_low, states_back, ending
    )
    seq.mark(low_k)
    (up_peer,) = seq.gate(both_up[1])
    blocks = products(
        spot, peers, [[(lefts, parts[0]), (message_peer, peer_parts[0])]], [[(both_up[0], None), (up_peer, None)]], 1408
    )
    seq.mark(blocks[0])
    ups = Reduction((0, 1, 2), blocks)
    low_q, low_k, low_v = seq.gate(low_q, low_k, low_v)
    ahead = jnp.concatenate([low[HALO - 8 : HALO] for low in (low_q, low_k, low_v)], axis=1)
    extra = shifted(ahead, "ctx", -1), crossed(ahead, -1)
    thirds = jnp.concatenate([low_q, low_k, low_v], axis=0)
    thirds, *extra = lax.optimization_barrier((thirds, *extra))
    thirds_peer = partner(thirds, "fsdp")
    *ups.got, extra1, extra2 = seq.gate(*ups.got, *extra)
    extra = extra1, extra2
    seq.mark(ups.step())
    lefts_here, thirds_peer = seq.gate(lefts, thirds_peer)
    left = [(lefts_here, parts[2]), (message_peer, peer_parts[2])]
    rights = [[(thirds, i), (thirds_peer, i), (extra[0], i), (extra[1], i)] for i in range(3)]
    blocks = products(spot, peers, [left] * 3, rights, 512, messages=2)
    seq.mark(blocks[0])
    late = Reduction((0, 1, 2), blocks)
    late.got = seq.gate(*late.got)
    seq.mark(late.step())
    (thirds_here,) = seq.gate(thirds)
    kept, lent = lent_rows(thirds_here, thirds_peer, extra, (message, message_peer), qkv_weight, gate_weight)
    seq.mark(lent)
    arriving = partner(lent, "fsdp")
    ups.got = seq.gate(*ups.got)
    seq.mark(ups.step())
    (arriving,) = seq.gate(arriving)
    grad_tokens, vector = norm_back(
        place, kept, arriving, tokens, gain_first[None], grad_hidden, (taps_q, taps_k, taps_v), grad_second_gain, grad_ridge
    )
    seq.mark(vector)
    size, width = D // owners, 3 * D // owners
    vector = jnp.concatenate(
        [vector[:KW].reshape(KW, owners, width).transpose(1, 0, 2).reshape(owners, KW * width),
         vector[KW].reshape(3, owners, size).transpose(1, 0, 2).reshape(owners, 3 * size)], axis=1
    ).reshape(peers, 2, KW * width + 3 * size)
    vector_kept, vector_sent = pick(vector, y, 1), pick(vector, 1 - y, 1)
    seq.mark(vector_sent)
    arriving = partner(vector_sent, "fsdp")
    late.got = seq.gate(*late.got)
    seq.mark(late.step())
    *ups.got, early = seq.gate(*ups.got, early)
    seq.mark(ups.step())
    vector_kept, arriving = seq.gate(vector_kept, arriving)
    vector = vector_kept + arriving
    seq.mark(vector)
    vector = lax.all_to_all(vector, "ctx", 0, 0, tiled=True)
    late.got = seq.gate(*late.got)
    seq.mark(late.step())
    vector = jnp.sum(seq.gate(vector)[0], axis=0)
    size = D // owners
    grad_up = ups.result([size])[0]
    grad_q, grad_k, grad_v = late.result([size] * 3)
    grad_qkv = jnp.concatenate([grad_q, grad_k, grad_v], axis=1)
    early = early.astype(f32)
    grad_out, grad_gate, grad_down = early[:size], early[size : 2 * size], early[2 * size :]
    return (
        output[None],
        grad_tokens[None],
        grad_qkv,
        grad_gate,
        grad_out,
        grad_up,
        grad_down,
        vector[: KW * width].reshape(KW, width),
        vector[KW * width : KW * width + size],
        vector[KW * width + size : KW * width + 2 * size],
        vector[KW * width + 2 * size :],
    )


def solution(mesh):
    tokens = P("fsdp", "ctx", None)
    rows = P("fsdp", None)
    vector = P("fsdp")
    owned = P(("ctx", "fsdp"), None)
    owned_vector = P(("ctx", "fsdp"))
    return jax.shard_map(
        local,
        mesh=mesh,
        in_specs=(
            tokens, rows, rows, rows, rows, rows, P(None, "fsdp"), vector, vector, vector, tokens, tokens,
        ),
        out_specs=(
            tokens, tokens, owned, owned, owned, owned, owned, P(None, ("ctx", "fsdp")),
            owned_vector, owned_vector, owned_vector,
        ),
        check_vma=False,
    )
```

```python
import functools
import jax
import jax.numpy as jnp
from jax import lax
from jax.experimental import pallas as pl
from jax.experimental.pallas import tpu as pltpu
from jax.sharding import PartitionSpec as P

D = 1024
HEADS = 8
FF = 2816
KW = 4
ITERS = 8
AT_ONCE = 2
HEAD_DIM = 128
QUARTERS = 4
SHARE = HEADS // QUARTERS
HALO = 16

f32 = jnp.float32
bf16 = jnp.bfloat16
VMEM_LIMIT = 56 * 1024 * 1024


def nn(a, b):
    return lax.dot_general(a, b, (((1,), (0,)), ((), ())), preferred_element_type=f32)


def nt(a, b):
    return lax.dot_general(a, b, (((1,), (1,)), ((), ())), preferred_element_type=f32)


def tn(a, b):
    return lax.dot_general(a, b, (((0,), (0,)), ((), ())), preferred_element_type=f32)


def column(row, like):
    return jnp.broadcast_to(row, like).T


def decay_mask(c, b, tokens):
    shape = (tokens, tokens)
    late = lax.broadcasted_iota(jnp.int32, shape, 1) >= lax.broadcasted_iota(jnp.int32, shape, 0)
    spread = jnp.broadcast_to(c, shape) - column(c, shape)
    return jnp.where(late, jnp.exp(jnp.where(late, spread, 0.0)), 0.0) * column(b, shape)


def like(shape, kind=f32):
    return jax.ShapeDtypeStruct(shape, kind)


def smem():
    return pl.BlockSpec(memory_space=pltpu.SMEM)


EXTRA = 16


def norm_kernel(place, tok_ref, taps_ref, lines_ref, mine_o, theirs_o):
    half = D // 2
    y = place[0]
    a = tok_ref[...]
    unit = a * lax.rsqrt(jnp.mean(a * a, axis=-1, keepdims=True) + 1e-05)
    left, right = unit[:, :half], unit[:, half:]
    rows = a.shape[0]
    gain = lines_ref[0:1].astype(f32)
    mine_o[...] = (jnp.where(y == 0, left, right) * gain).astype(bf16)
    theirs_o[:rows] = jnp.where(y == 0, right, left).astype(bf16)
    taps = taps_ref[...]
    lines = [taps[t : t + 1, i * half : (i + 1) * half] for t in range(KW) for i in range(3)]
    theirs_o[rows:] = jnp.concatenate(lines + [lines_ref[...]], axis=0)


def norm(place, tokens, taps, lines):
    rows = tokens.shape[0]
    vmem = pl.BlockSpec(memory_space=pltpu.VMEM)
    return pl.pallas_call(
        norm_kernel,
        in_specs=[smem()] + [vmem] * 3,
        out_specs=[vmem, vmem],
        out_shape=[like((rows, D // 2), bf16), like((rows + EXTRA, D // 2), bf16)],
        name="norm",
    )(place, tokens, taps, lines)


def weigh_kernel(scaled, left_ref, gain_ref, qkv_ref, gate_ref, out, left):
    j = pl.program_id(0)

    @pl.when(j == 0)
    def _():
        rows = left_ref[: left.shape[0]]
        left[...] = (rows.astype(f32) * gain_ref[...].astype(f32)).astype(bf16) if scaled else rows

    steps = 3 * D // out.shape[1]

    @pl.when(j < steps)
    def _():
        out[...] = nn(left[...], qkv_ref[...]).astype(out.dtype)

    @pl.when(j >= steps)
    def _():
        out[...] = nn(left[...], gate_ref[...]).astype(out.dtype)


def weigh(left, rows, gain, qkv_weight, gate_weight, kind):
    half = left.shape[1]
    tile = 1024
    steps = 3 * D // tile
    return pl.pallas_call(
        functools.partial(weigh_kernel, left.shape[0] > rows),
        grid=(4 * D // tile,),
        in_specs=[
            whole(*left.shape), whole(1, half),
            pl.BlockSpec((half, tile), lambda j: (0, jnp.minimum(j, steps - 1))),
            pl.BlockSpec((half, tile), lambda j: (0, jnp.maximum(j - steps, 0))),
        ],
        out_specs=pl.BlockSpec((rows, tile), lambda j: (0, j)),
        out_shape=like((rows, 4 * D), kind),
        scratch_shapes=[pltpu.VMEM((rows, half), bf16)],
        cost_estimate=pl.CostEstimate(flops=1, bytes_accessed=1, transcendentals=0),
        name="weigh",
    )(left, gain, qkv_weight, gate_weight)


def tables_kernel(c_ref, b_ref, ridge_ref, mask_o, ending_o, ridge_o):
    tokens = c_ref.shape[1]
    head = pl.program_id(0)
    c, b = c_ref[pl.ds(head, 1), :], b_ref[pl.ds(head, 1), :]
    mask_o[0] = decay_mask(c, b, tokens)
    ending_o[0] = column(jnp.exp(c[:, tokens - 1 :] - c) * b, (HEAD_DIM, tokens))
    ridge_o[0] = column(ridge_ref[pl.ds(head, 1), :], (tokens, HEAD_DIM))


def tables(c, b, ridge):
    tokens = c.shape[1]
    shapes = [(tokens, tokens), (tokens, HEAD_DIM), (HEAD_DIM, tokens)]
    return pl.pallas_call(
        tables_kernel,
        grid=(HEADS,),
        in_specs=[whole(HEADS, tokens)] * 2 + [whole(HEADS, HEAD_DIM)],
        out_specs=[pl.BlockSpec((1,) + shape, lambda h: (h, 0, 0)) for shape in shapes],
        out_shape=[like((HEADS,) + shape) for shape in shapes],
        cost_estimate=pl.CostEstimate(flops=1, bytes_accessed=1, transcendentals=0),
        name="tables",
    )(c, b, ridge)


def with_halo(own, lent, halo):
    before = halo[...].astype(f32)
    blank = jnp.zeros((HALO - before.shape[0], before.shape[1]), f32)
    return jnp.concatenate([blank, before, own[...] + lent[...].astype(f32)], axis=0)


def conv_parts(padded, taps):
    rows = padded.shape[0] - HALO
    shifted = [padded[HALO - KW + 1 + j : HALO - KW + 1 + j + rows] for j in range(KW)]
    total = taps[0:1] * shifted[0]
    for j in range(1, KW):
        total = total + taps[j : j + 1] * shifted[j]
    return total, shifted


def unit(a):
    return a * lax.rsqrt(jnp.sum(a * a, axis=-1, keepdims=True) + 1e-06)


def position(spot):
    return spot[0] % FOUR


FOUR = 4
PAIR = (2 * SHARE, HEAD_DIM, HEAD_DIM)
MESSAGE = (2 * SHARE, HEAD_DIM + 16, HEAD_DIM)


def decay_rows(decay):
    shape = (16, HEAD_DIM)
    at = lax.broadcasted_iota(jnp.int32, shape, 0)
    decay = jnp.broadcast_to(decay, shape)
    high = decay.astype(bf16).astype(f32)
    return jnp.where(at == 0, high, jnp.where(at == 1, decay - high, 0.0)).astype(bf16)


def decay_of(message, m):
    rows = message[m, HEAD_DIM:].astype(f32)
    return rows[0:1] + rows[1:2]


def block_decay(c_ref, head):
    c = c_ref[pl.ds(head, 1), :]
    return jnp.broadcast_to(jnp.exp(c[:, c.shape[1] - 1 :]), (1, HEAD_DIM))


def store_quarter(spot, quarter, outs, states, c_ref):
    rows = [decay_rows(block_decay(c_ref, quarter * SHARE + m)) for m in range(SHARE)]
    for i, out in enumerate(outs):

        @pl.when((position(spot) ^ i) == quarter)
        def _():
            for m in range(2 * SHARE):
                out[m, :HEAD_DIM] = states[m]
                out[m, HEAD_DIM:] = rows[m % SHARE]


def cut(h):
    return slice(h * HEAD_DIM, (h + 1) * HEAD_DIM)


def features_kernel(
    spot, oq, ok, ov, lq, lk, lv, hq, hk, hv, tq, tk, tv, ending_ref, c_ref, q_o, k_o, v_o, *outs
):
    quarter = pl.program_id(0)

    def activated(own, lent, halo, taps):
        total, _ = conv_parts(with_halo(own, lent, halo), taps[...])
        return total * jax.nn.sigmoid(total)

    queries, keys, values = activated(oq, lq, hq, tq), activated(ok, lk, hk, tk), activated(ov, lv, hv, tv)
    key_states, value_states = [], []
    for m in range(SHARE):
        k, v = unit(keys[:, cut(m)]), values[:, cut(m)]
        k_low = k.astype(bf16)
        k_o[m] = k_low
        v_o[m] = v.astype(bf16)
        q_o[m] = unit(queries[:, cut(m)]).T
        ending = ending_ref[m]
        key_states.append(tn((k * ending).astype(bf16), k_low).astype(bf16))
        value_states.append(tn((v * ending).astype(bf16), k_low).astype(bf16))
    store_quarter(spot, quarter, outs, key_states + value_states, c_ref)


def whole(*shape):
    return pl.BlockSpec(shape, lambda *g: (0,) * len(shape))


def per_quarter(*shape):
    return pl.BlockSpec((SHARE,) + shape, lambda p: (p,) + (0,) * len(shape))


def quarter_columns(rows, third):
    return pl.BlockSpec((rows, SHARE * HEAD_DIM), lambda p: (0, third * QUARTERS + p))


def features(spot, projected, taps, ending, c):
    own, lent, halo = projected
    tokens = own.shape[0]
    return pl.pallas_call(
        features_kernel,
        grid=(QUARTERS,),
        in_specs=[smem()] + [quarter_columns(x, i) for x in (tokens, tokens, halo.shape[0], KW) for i in range(3)]
        + [per_quarter(tokens, HEAD_DIM), whole(HEADS, tokens)],
        out_specs=[per_quarter(HEAD_DIM, tokens)] + [per_quarter(tokens, HEAD_DIM)] * 2 + [whole(*MESSAGE)] * QUARTERS,
        out_shape=[like((HEADS, HEAD_DIM, tokens))] + [like((HEADS, tokens, HEAD_DIM), bf16)] * 2
        + [like(MESSAGE, bf16)] * QUARTERS,
        cost_estimate=pl.CostEstimate(flops=1, bytes_accessed=1, transcendentals=0),
        name="features",
    )(spot, own, own, own, lent, lent, lent, halo, halo, halo, taps, taps, taps, ending, c)


def decay_between(indices, decays, low, high):
    total = None
    for index, decay in zip(indices, decays):
        one = jnp.where((index > low) & (index < high), decay, 1.0)
        total = one if total is None else total * one
    return total


def summed(factors, arrays, m):
    total = factors[0] * arrays[0][m, :HEAD_DIM].astype(f32)
    for factor, array in zip(factors[1:], arrays[1:]):
        total = total + factor * array[m, :HEAD_DIM].astype(f32)
    return total


def members(spot, unit, count):
    place = (spot[0] // unit) % count
    return place, [place ^ i for i in range(count)]


def whole_group(indices, arrays, m):
    decays = [decay_of(a, m) for a in arrays]
    count = len(arrays)
    state = summed([decay_between(indices, decays, i, count) for i in indices], arrays, m)
    return state, decay_between(indices, decays, -1, count)


def earlier(place, indices, arrays, m, before):
    decays = [decay_of(a, m) for a in arrays]
    factors = [jnp.where(i < place, decay_between(indices, decays, i, place), 0.0) for i in indices[1:]]
    state = summed(factors, arrays[1:], m)
    decay = decay_between(indices, decays, -1, place)
    if before is None:
        return state, decay
    old = before[m, HEAD_DIM : HEAD_DIM + 1]
    return before[m, :HEAD_DIM] + old * state, old * decay


def group_kernel(spot, *refs):
    arrays, out = refs[:FOUR], refs[FOUR]
    _, indices = members(spot, 1, FOUR)
    for m in range(2 * SHARE):
        state, decay = whole_group(indices, arrays, m)
        out[m, :HEAD_DIM] = state.astype(bf16)
        out[m, HEAD_DIM:] = decay_rows(decay)


def upper_kernel(unit, count, has_before, spot, *refs):
    arrays = refs[:count]
    before = refs[count] if has_before else None
    before_o, total_o = refs[-2:]
    place, indices = members(spot, unit, count)
    for m in range(2 * SHARE):
        state, decay = earlier(place, indices, arrays, m, before)
        before_o[m, :HEAD_DIM] = state
        before_o[m, HEAD_DIM:] = jnp.broadcast_to(decay, (16, HEAD_DIM))
        state, decay = whole_group(indices, arrays, m)
        total_o[m, :HEAD_DIM] = state.astype(bf16)
        total_o[m, HEAD_DIM:] = decay_rows(decay)


def spread_kernel(unit, count, has_before, spot, *refs):
    arrays, near = refs[:count], refs[count : count + FOUR]
    before = refs[count + FOUR] if has_before else None
    outs = refs[-FOUR:]
    place, upper = members(spot, unit, count)
    _, indices = members(spot, 1, FOUR)
    for m in range(2 * SHARE):
        state, _ = earlier(place, upper, arrays, m, before)
        decays = [decay_of(x, m) for x in near]
        for j in range(FOUR):
            at = indices[j]
            factors = [jnp.where(i < at, decay_between(indices, decays, i, at), 0.0) for i in indices]
            total = decay_between(indices, decays, -1, at) * state + summed(factors, near, m)
            outs[j][m] = total.astype(bf16)


def small_call(kernel, name, shapes, spot, *args):
    vmem = pl.BlockSpec(memory_space=pltpu.VMEM)
    return pl.pallas_call(
        kernel,
        in_specs=[smem()] + [vmem] * len(args),
        out_specs=[vmem] * len(shapes),
        out_shape=shapes,
        cost_estimate=pl.CostEstimate(flops=1, bytes_accessed=1, transcendentals=0),
        name=name,
    )(spot, *args)


def neighbour(axis, bit):
    return [(i, i ^ bit) for i in range(lax.axis_size(axis))]


def partner(x, axis, bit=1):
    return lax.ppermute(x, axis, neighbour(axis, bit))


def radices(peers):
    sizes = []
    left = peers // FOUR
    while left > 1:
        sizes.append(min(FOUR, left))
        left //= sizes[-1]
    return sizes


def swapped(arrays, axis, unit_size=1):
    return [arrays[0]] + [partner(a, axis, unit_size * i) for i, a in enumerate(arrays) if i]


class Scan:
    def __init__(self, spot, near, axis):
        self.spot, self.axis, self.near = spot, axis, near
        self.sizes = radices(lax.axis_size(axis))

    def group(self):
        message = like(MESSAGE, bf16)
        (self.total,) = small_call(group_kernel, "group", [message], self.spot, *self.near)
        self.before = ()
        self.unit = FOUR
        for radix in self.sizes[:-1]:
            arrays = swapped([self.total] * radix, self.axis, self.unit)
            kernel = functools.partial(upper_kernel, self.unit, radix, bool(self.before))
            before, self.total = small_call(kernel, "upper", [like(MESSAGE), message], self.spot, *arrays, *self.before)
            self.before = (before,)
            self.unit *= radix
        self.far = swapped([self.total] * self.sizes[-1], self.axis, self.unit)

    def spread(self):
        kernel = functools.partial(spread_kernel, self.unit, self.sizes[-1], bool(self.before))
        self.parts = small_call(
            kernel, "spread", [like(PAIR, bf16)] * FOUR, self.spot, *self.far, *self.near, *self.before
        )
        self.entering = swapped(self.parts, self.axis)
        return self.entering


def prepare(k_ref, c_ref, state_refs, place, left, wide, decay, pair):
    tokens = k_ref.shape[1]
    for i, state in enumerate(state_refs):
        for m in range(SHARE):
            left[(place ^ i) * SHARE + m, :, :HEAD_DIM] = state[m]
    pair[...] = jnp.zeros_like(pair)
    for h in range(HEADS):
        k = k_ref[h]
        left[h, :, HEAD_DIM:] = k.T
        wide[h // 2, :, cut(h % 2)] = k
        decay[h] = jnp.broadcast_to(jnp.exp(c_ref[h : h + 1, :]), (8, tokens))


def key_products(columns, wide, pair):
    products = []
    for h in range(0, HEADS, 2):
        pair[h // 2, :HEAD_DIM, :HEAD_DIM] = columns(h)
        pair[h // 2, HEAD_DIM:, HEAD_DIM:] = columns(h + 1)
        both = nn(wide[h // 2], pair[h // 2])
        products += [both[:, :HEAD_DIM], both[:, HEAD_DIM:]]
    return products


def solve_kernel(
    place, q_ref, k_ref, s0, s1, s2, s3, c_ref, mask, ridge,
    x_out, p_out, m_out, score_out, scal_out,
    left, wide, decay, pair, x_s, r_s, p_s,
):
    @pl.when(pl.program_id(0) == 0)
    def _():
        prepare(k_ref, c_ref, (s0, s1, s2, s3), place[0], left, wide, decay, pair)
        for h in range(HEADS):
            q = q_ref[h]
            x_s[h] = jnp.zeros_like(q)
            r_s[h] = q
            p_s[h] = q
            scal_out[h, 0:1] = jnp.sum(q * q, axis=0, keepdims=True)

    for t in range(AT_ONCE):
        i = pl.program_id(0) * AT_ONCE + t
        products = key_products(lambda h: p_s[h].astype(bf16), wide, pair)
        for h in range(HEADS):
            p = p_s[h]
            scores = (products[h] * mask[h]).astype(bf16)
            score_out[t, h] = scores
            stacked = jnp.concatenate([(decay[h, 0:1] * p).astype(bf16), scores], axis=0)
            image = nn(left[h], stacked) + ridge[h] * p
            norm = scal_out[h, pl.ds(i, 1)]
            dot = jnp.sum(p * image, axis=0, keepdims=True)
            size = norm / dot
            p_out[t, h] = p
            m_out[t, h] = image
            scal_out[h, pl.ds(2 * ITERS + i, 1)] = dot
            x_s[h] = x_s[h] + size * p
            r = r_s[h] - size * image
            r_s[h] = r
            norm_next = jnp.sum(r * r, axis=0, keepdims=True)
            scal_out[h, pl.ds(i + 1, 1)] = norm_next
            p_s[h] = r + (norm_next / norm) * p

    @pl.when(i == ITERS - 1)
    def _():
        for h in range(HEADS):
            x_out[h] = x_s[h].astype(bf16)


def common_scratch(tokens):
    square = pltpu.VMEM((HEADS, HEAD_DIM, tokens), f32)
    return [
        pltpu.VMEM((HEADS, HEAD_DIM, HEAD_DIM + tokens), bf16),
        pltpu.VMEM((HEADS // 2, tokens, 2 * HEAD_DIM), bf16),
        pltpu.VMEM((HEADS, 8, tokens), f32),
        pltpu.VMEM((HEADS // 2, 2 * HEAD_DIM, 2 * tokens), bf16),
        square, square, square,
    ]


def solve(place, q, k, states, c, mask, ridge):
    tokens = q.shape[2]
    step = pl.BlockSpec((AT_ONCE, HEADS, HEAD_DIM, tokens), lambda i: (i, 0, 0, 0))
    steps = (ITERS, HEADS, HEAD_DIM, tokens)
    return pl.pallas_call(
        solve_kernel,
        grid=(ITERS // AT_ONCE,),
        in_specs=[smem(), whole(HEADS, HEAD_DIM, tokens), whole(HEADS, tokens, HEAD_DIM)] + [whole(*PAIR)] * FOUR
        + [whole(HEADS, tokens), whole(HEADS, tokens, tokens), whole(HEADS, HEAD_DIM, tokens)],
        out_specs=[whole(HEADS, HEAD_DIM, tokens), step, step, step, whole(HEADS, 3 * ITERS, tokens)],
        out_shape=[
            like((HEADS, HEAD_DIM, tokens), bf16), like(steps), like(steps), like(steps, bf16),
            like((HEADS, 3 * ITERS, tokens)),
        ],
        scratch_shapes=common_scratch(tokens),
        compiler_params=pltpu.CompilerParams(vmem_limit_bytes=VMEM_LIMIT),
        cost_estimate=pl.CostEstimate(flops=1, bytes_accessed=1, transcendentals=0),
        name="solve",
    )(place, q, k, *states, c, mask, ridge)


def attend_back_kernel(place, ga_ref, k_ref, v_ref, x_ref, s0, s1, s2, s3, c_ref, mask_ref, gx_o, dk_o, dv_o, state_o):
    quarter = pl.program_id(0)
    tokens = k_ref.shape[1]
    for m in range(SHARE):
        head = quarter * SHARE + m
        c = c_ref[pl.ds(head, 1), :]
        mask = mask_ref[m]
        e = jnp.exp(c)
        state = s0[SHARE + m]
        for i, other in ((1, s1), (2, s2), (3, s3)):
            state = jnp.where((place[0] ^ i) == quarter, other[SHARE + m], state)
        ga = ga_ref[:, cut(m)].T
        low = ga.astype(bf16)
        x = x_ref[m]
        k = k_ref[m]
        scores = (nn(k, x) * mask).astype(bf16)
        dscores = (nn(v_ref[m], low) * mask).astype(bf16)
        ega = (e * ga).astype(bf16)
        gx_o[m] = tn(state, ega) + tn(k, dscores)
        dv_o[m] = nt(scores, low)
        dk_o[m] = nt(dscores, x)
        state_o[m] = nt(ega, x).astype(bf16)


def attend_back(place, ga, k, v, x, states, c, mask):
    tokens = k.shape[1]
    square = like((HEADS, HEAD_DIM, tokens))
    return pl.pallas_call(
        attend_back_kernel,
        grid=(QUARTERS,),
        in_specs=[smem(), quarter_columns(tokens, 0)] + [per_quarter(tokens, HEAD_DIM)] * 2
        + [per_quarter(HEAD_DIM, tokens)] + [whole(*PAIR)] * FOUR + [whole(HEADS, tokens), per_quarter(tokens, tokens)],
        out_specs=[per_quarter(HEAD_DIM, tokens)] * 4,
        out_shape=[square] * 3 + [like((HEADS, HEAD_DIM, HEAD_DIM), bf16)],
        cost_estimate=pl.CostEstimate(flops=1, bytes_accessed=1, transcendentals=0),
        name="attend_back",
    )(place, ga, k, v, x, *states, c, mask)


def adjoint_kernel(
    spot, place, gx_ref, k_ref, s0, s1, s2, s3, c_ref, mask, ridge, p_ref, m_ref, score_ref, scal_ref, values_ref,
    dq_ref, dk_ref, dridge_ref, o0, o1, o2, o3,
    left, wide, decay, pair, gr_s, gp_s, acc_s, next_s, gnorm_s, low_s, steps_p, steps_g, steps_s, stack,
):
    s = pl.program_id(0)
    tokens = k_ref.shape[1]

    @pl.when(s == 0)
    def _():
        prepare(k_ref, c_ref, (s0, s1, s2, s3), place[0], left, wide, decay, pair)
        gr_s[...] = jnp.zeros_like(gr_s)
        gp_s[...] = jnp.zeros_like(gp_s)
        acc_s[...] = jnp.zeros_like(acc_s)
        next_s[...] = jnp.zeros_like(next_s)
        gnorm_s[...] = jnp.zeros_like(gnorm_s)

    for t in reversed(range(AT_ONCE)):
        i = ITERS - AT_ONCE * (s + 1) + t
        at = pl.ds(pl.multiple_of(i * tokens, tokens), tokens)
        for h in range(HEADS):
            p, m, gx = p_ref[t, h], m_ref[t, h], gx_ref[h]
            norm = scal_ref[h, pl.ds(i, 1)]
            dot = scal_ref[h, pl.ds(2 * ITERS + i, 1)]
            size = norm / dot
            ratio = jnp.where(i == ITERS - 1, 0.0, scal_ref[h, pl.ds(i + 1, 1)] / norm)
            gp = gp_s[h]
            gratio = jnp.sum(gp * p, axis=0, keepdims=True)
            gnext = gnorm_s[h, 0:1] + gratio / norm
            gr = gr_s[h] + gp + (2.0 * gnext) * (next_s[h] - ratio * p)
            gsize = jnp.sum(gx * p - gr * m, axis=0, keepdims=True)
            gdot = -gsize * size / dot
            gm = gdot * p - size * gr
            gr_s[h] = gr
            gp_s[h] = ratio * gp + size * gx + gdot * m + ridge[h] * gm
            acc_s[h] = acc_s[h] + gm * p
            next_s[h] = p
            gnorm_s[h, 0:1] = gsize / dot - gratio * ratio / norm
            low = gm.astype(bf16)
            low_s[h] = low
            egm = (decay[h, 0:1] * gm).astype(bf16)
            steps_g[h, :, at] = low
            steps_p[h, :, at] = p.astype(bf16)
            steps_s[h, :, at] = score_ref[t, h]
            stack[h, HEAD_DIM:, at] = egm
        products = key_products(lambda h: low_s[h], wide, pair)
        for h in range(HEADS):
            dscores = (products[h] * mask[h]).astype(bf16)
            stack[h, :HEAD_DIM, at] = dscores
            stacked = jnp.concatenate([stack[h, HEAD_DIM:, at], dscores], axis=0)
            gp_s[h] = gp_s[h] + nn(left[h], stacked)

    @pl.when(s == ITERS // AT_ONCE - 1)
    def _():
        for h in range(HEADS):
            dq_ref[h] = gr_s[h] + gp_s[h] + 2.0 * gnorm_s[h, 0:1] * p_ref[0, h]
            both = nt(steps_p[h], stack[h])
            dk_ref[h] = (nt(steps_g[h], steps_s[h]) + both[:, :HEAD_DIM]).T
            left[h, :, :HEAD_DIM] = both[:, HEAD_DIM:].T.astype(bf16)
            dridge_ref[h] = jnp.sum(acc_s[h].T, axis=0, keepdims=True)
        for j, out in enumerate((o0, o1, o2, o3)):
            for m in range(SHARE):
                head = (position(spot) ^ j) * SHARE + m
                decay = decay_rows(block_decay(c_ref, head))
                out[m, :HEAD_DIM] = left[head, :, :HEAD_DIM]
                out[m, HEAD_DIM:] = decay
                out[SHARE + m, :HEAD_DIM] = values_ref[head]
                out[SHARE + m, HEAD_DIM:] = decay


def adjoint(spot, place, gx, k, states, c, mask, ridge, p_all, m_all, scores, scal, value_states):
    tokens = k.shape[1]
    step = pl.BlockSpec((AT_ONCE, HEADS, HEAD_DIM, tokens), lambda s: (ITERS // AT_ONCE - 1 - s, 0, 0, 0))
    square = pltpu.VMEM((HEADS, HEAD_DIM, tokens), f32)
    line = pltpu.VMEM((HEADS, HEAD_DIM, ITERS * tokens), bf16)
    return pl.pallas_call(
        adjoint_kernel,
        grid=(ITERS // AT_ONCE,),
        in_specs=[smem(), smem(), whole(HEADS, HEAD_DIM, tokens), whole(HEADS, tokens, HEAD_DIM)] + [whole(*PAIR)] * FOUR
        + [whole(HEADS, tokens), whole(HEADS, tokens, tokens), whole(HEADS, HEAD_DIM, tokens), step, step, step, whole(HEADS, 3 * ITERS, tokens), whole(HEADS, HEAD_DIM, HEAD_DIM)],
        out_specs=[whole(HEADS, HEAD_DIM, tokens), whole(HEADS, tokens, HEAD_DIM), whole(HEADS, 1, HEAD_DIM)]
        + [whole(*MESSAGE)] * FOUR,
        out_shape=[like((HEADS, HEAD_DIM, tokens)), like((HEADS, tokens, HEAD_DIM)), like((HEADS, 1, HEAD_DIM))]
        + [like(MESSAGE, bf16)] * FOUR,
        scratch_shapes=common_scratch(tokens) + [
            square,
            pltpu.VMEM((HEADS, 8, tokens), f32),
            pltpu.VMEM((HEADS, HEAD_DIM, tokens), bf16),
            line, line, line,
            pltpu.VMEM((HEADS, 2 * HEAD_DIM, ITERS * tokens), bf16),
        ],
        compiler_params=pltpu.CompilerParams(vmem_limit_bytes=VMEM_LIMIT),
        cost_estimate=pl.CostEstimate(flops=1, bytes_accessed=1, transcendentals=0),
        name="adjoint",
    )(spot, place, gx, k, *states, c, mask, ridge, p_all, m_all, scores, scal, value_states)


def conv_forward(own, lent, halo, t):
    total, shifted = conv_parts(with_halo(own, lent, halo), t[...])
    sig = jax.nn.sigmoid(total)
    return shifted, sig * (1.0 + total * (1.0 - sig)), total * sig


def unit_back(act, grad):
    scale = lax.rsqrt(jnp.sum(act * act, axis=-1, keepdims=True) + 1e-06)
    rows = act * scale
    return scale * (grad - rows * jnp.sum(rows * grad, axis=-1, keepdims=True))


def conv_back(dconv, shifted, t, g, dt):
    taps = t[...]
    tokens = dconv.shape[0]
    blank = jnp.zeros((HALO, dconv.shape[1]), f32)
    padded = jnp.concatenate([blank, dconv, blank], axis=0)
    rows = tokens + HALO
    total = taps[KW - 1 : KW] * padded[:rows]
    for j in range(KW - 1):
        total = total + taps[j : j + 1] * padded[KW - 1 - j : KW - 1 - j + rows]
    g[...] = total.astype(bf16)
    dt[...] = jnp.concatenate(
        [jnp.sum(dconv * shifted[j], axis=0, keepdims=True) for j in range(KW)], axis=0
    )


def queries_back_kernel(own, lent, halo, t, dq_ref, g, dt):
    shifted, slope, act = conv_forward(own, lent, halo, t)
    grads = [unit_back(act[:, cut(m)], dq_ref[m].T) for m in range(SHARE)]
    conv_back(jnp.concatenate(grads, axis=1) * slope, shifted, t, g, dt)


def returned(place, quarter, refs, m):
    state = refs[0][m]
    for i in range(1, FOUR):
        state = jnp.where((place ^ i) == quarter, refs[i][m], state)
    return state


def values_back_kernel(spot, own, lent, halo, t, dv_ref, k_ref, r0, r1, r2, r3, ending_ref, g, dt):
    quarter = pl.program_id(0)
    shifted, slope, _ = conv_forward(own, lent, halo, t)
    grads = []
    for m in range(SHARE):
        rv = returned(position(spot), quarter, (r0, r1, r2, r3), SHARE + m)
        grads.append(dv_ref[m] + ending_ref[m] * nt(k_ref[m], rv))
    conv_back(jnp.concatenate(grads, axis=1) * slope, shifted, t, g, dt)


def keys_back_kernel(
    spot, own, lent, halo, t, dk1, dk2, k_ref, v_ref, r0, r1, r2, r3, ending_ref, g, dt
):
    quarter = pl.program_id(0)
    shifted, slope, act = conv_forward(own, lent, halo, t)
    grads = []
    for m in range(SHARE):
        rv = returned(position(spot), quarter, (r0, r1, r2, r3), SHARE + m)
        rk = returned(position(spot), quarter, (r0, r1, r2, r3), m).astype(f32)
        rk = (rk + rk.T).astype(bf16)
        ending = ending_ref[m]
        dk = dk1[m] + dk2[m] + ending * (nn(k_ref[m], rk) + nn(v_ref[m], rv))
        grads.append(unit_back(act[:, cut(m)], dk))
    conv_back(jnp.concatenate(grads, axis=1) * slope, shifted, t, g, dt)


def third_back(kernel, name, which, taps_third, projected, taps, before, others, specs):
    own, lent, halo = projected
    tokens = own.shape[0]
    return pl.pallas_call(
        kernel,
        grid=(QUARTERS,),
        in_specs=[smem()] * len(before) + [quarter_columns(rows, which) for rows in (tokens, tokens, halo.shape[0])]
        + [quarter_columns(KW, taps_third)] + specs,
        out_specs=[quarter_columns(tokens + HALO, 0), quarter_columns(KW, 0)],
        out_shape=[like((tokens + HALO, D), bf16), like((KW, D))],
        cost_estimate=pl.CostEstimate(flops=1, bytes_accessed=1, transcendentals=0),
        name=name,
    )(*before, own, lent, halo, taps, *others)


def queries_back(projected, taps, dq):
    return third_back(queries_back_kernel, "queries_back", 0, 0, projected, taps, (), (dq,), [per_quarter(HEAD_DIM, HEAD_DIM)])


def values_back(spot, projected, taps, dv, k, states, ending):
    square = per_quarter(HEAD_DIM, HEAD_DIM)
    return third_back(
        values_back_kernel, "values_back", 2, 2, projected, taps, (spot,), (dv, k, *states, ending),
        [square] * 2 + [whole(*PAIR)] * FOUR + [square],
    )


def keys_back(spot, projected, taps, dk1, dk2, k, v, states, ending):
    square = per_quarter(HEAD_DIM, HEAD_DIM)
    return third_back(
        keys_back_kernel, "keys_back", 1, 1, projected, taps, (spot,), (dk1, dk2, k, v, *states, ending),
        [square] * 4 + [whole(*PAIR)] * FOUR + [square],
    )


def keys_values_back_kernel(
    spot, ok, lk, hk, tk, ov, lv, hv, tv, dk1, dk2, dv_ref, k_ref, v_ref, r0, r1, r2, r3, ending_ref, gk, dtk, gv, dtv
):
    values_back_kernel(spot, ov, lv, hv, tv, dv_ref, k_ref, r0, r1, r2, r3, ending_ref, gv, dtv)
    keys_back_kernel(spot, ok, lk, hk, tk, dk1, dk2, k_ref, v_ref, r0, r1, r2, r3, ending_ref, gk, dtk)


def keys_values_back(spot, projected, taps, dk1, dk2, dv, k, v, states, ending):
    own, lent, halo = projected
    tokens = own.shape[0]
    square = per_quarter(HEAD_DIM, HEAD_DIM)
    out = [quarter_columns(tokens + HALO, 0), quarter_columns(KW, 0)]
    return pl.pallas_call(
        keys_values_back_kernel,
        grid=(QUARTERS,),
        in_specs=[smem()]
        + [quarter_columns(rows, third) for third in (1, 2) for rows in (tokens, tokens, halo.shape[0], KW)]
        + [square] * 5 + [whole(*PAIR)] * FOUR + [square],
        out_specs=out * 2,
        out_shape=[like((tokens + HALO, D), bf16), like((KW, D))] * 2,
        cost_estimate=pl.CostEstimate(flops=1, bytes_accessed=1, transcendentals=0),
        name="keys_values_back",
    )(spot, own, lent, halo, taps, own, lent, halo, taps, dk1, dk2, dv, k, v, *states, ending)


def completed(ref, extra):
    more = extra[...].astype(f32)
    more = jnp.concatenate([jnp.zeros_like(more), more], axis=0)
    last = ref.shape[0] - 16
    return [ref[HALO:last], (ref[last:].astype(f32) + more).astype(bf16)]


def products_kernel(plan, joined, cuts, spot, *refs):
    count = len(plan)
    odd = spot[0] % 2 == 1
    outs, scratch = refs[-count - (1 if joined else 1 + len(cuts)) : -count], refs[-count:]

    @pl.when(pl.program_id(0) == 0)
    def _():
        for (lefts, _, _), both in zip(plan, scratch):
            both[...] = jnp.concatenate([refs[at][...] if rows is None else refs[at][rows] for at, rows in lefts], axis=1)

    start = 0
    def right(at, stacked):
        if not stacked:
            return refs[at][...]
        return jnp.concatenate([refs[at][i : i + stacked] for i in range(0, refs[at].shape[0], stacked)], axis=1)

    for (_, rights, size), both in zip(plan, scratch):
        if len(rights) == 4:
            rows = [part for i in (0, 1) for part in completed(refs[rights[i][0]], refs[rights[2 + i][0]])]
        else:
            rows = [right(*at) for at in rights]
        product = nn(both[...], jnp.concatenate(rows, axis=0))
        at = slice(start, start + size)
        start += size
        if joined:
            outs[0][:, at, :] = product.reshape(product.shape[0] // size, size, product.shape[1]).astype(bf16)
            continue
        blocks = product.reshape(product.shape[0] // (2 * size), 2, size, product.shape[1])
        outs[0][:, at, :] = jnp.where(odd, blocks[:, 1], blocks[:, 0]).astype(bf16)
        other = jnp.where(odd, blocks[:, 0], blocks[:, 1]).astype(bf16)
        for out, cut_at in zip(outs[1:], cuts):
            first, last = max(at.start, cut_at.start), min(at.stop, cut_at.stop)
            if first < last:
                out[:, first - cut_at.start : last - cut_at.start, :] = other[:, first - at.start : last - at.start]


def unstacked(array, index):
    row, tokens = index
    return jnp.concatenate([array[row + i * tokens : row + (i + 1) * tokens] for i in range(D // HEAD_DIM)], axis=1)


def products(spot, peers, lefts, rights, tile, joined=False, messages=1):
    sizes = [(part[0][1].stop - part[0][1].start) // peers for part in lefts]
    width = rights[0][0][0].shape[1] if rights[0][0][1] is None else D
    count, number = (peers, 1) if joined else (peers // 2, 2)
    shape = (count, sum(sizes), width)
    cuts = [slice(i * shape[1] // messages, (i + 1) * shape[1] // messages) for i in range(messages)]
    if any(size % 8 for size in sizes):
        odd = spot[0] % 2
        sides = []
        for side in range(number):
            parts = []
            for left, right in zip(lefts, rights):
                if len(right) == 4:
                    rows = []
                    for i in (0, 1):
                        (array, third), (extra, _) = right[i], right[2 + i]
                        size = array.shape[0] // 3
                        rows += completed(array[third * size : (third + 1) * size], extra[:, third * D : (third + 1) * D])
                else:
                    rows = [unstacked(array, index) if index else array for array, index in right]
                blocks = nn(jnp.concatenate([array[at] for array, at in left], axis=1), jnp.concatenate(rows, axis=0))
                blocks = blocks.astype(bf16).reshape(count, number, -1, width)
                parts.append(lax.dynamic_index_in_dim(blocks, 0 if joined else odd ^ side, 1, keepdims=False))
            sides.append(jnp.concatenate(parts, axis=1))
        return sides if joined else sides[:1] + [sides[1][:, at] for at in cuts]
    arrays, specs, plan = [], [], []

    def place_of(array, spec):
        for at, other in enumerate(arrays):
            if other is array and specs[at] is None and spec is None:
                return at
        arrays.append(array)
        specs.append(spec)
        return len(arrays) - 1

    def columns(array, index):
        if index is None:
            return pl.BlockSpec((array.shape[0], tile), lambda j: (0, j))
        if isinstance(index, int) and array.shape[1] == D:
            return pl.BlockSpec((array.shape[0] // 3, tile), lambda j: (index, j))
        if isinstance(index, int):
            return pl.BlockSpec((array.shape[0], tile), lambda j: (0, index * (D // tile) + j))
        size = index[1] * tile // HEAD_DIM
        return pl.BlockSpec((size, HEAD_DIM), lambda j: (index[0] // size + j, 0))

    def left_part(array, rows):
        size = rows.stop - rows.start
        if rows.start % size:
            return place_of(array, None), rows
        at = rows.start // size
        return place_of(array, pl.BlockSpec((size, array.shape[1]), lambda j: (at, 0))), None

    for left, right, size in zip(lefts, rights, sizes):
        plan.append((
            [left_part(array, rows) for array, rows in left],
            [(place_of(array, columns(array, index)), index[1] if isinstance(index, tuple) else None) for array, index in right],
            size,
        ))
    heights = [shape[1]] + ([] if joined else [at.stop - at.start for at in cuts])
    return pl.pallas_call(
        functools.partial(products_kernel, plan, joined, cuts),
        grid=(width // tile,),
        in_specs=[smem()] + [spec or whole(*array.shape) for array, spec in zip(arrays, specs)],
        out_specs=[pl.BlockSpec((count, height, tile), lambda j: (0, 0, j)) for height in heights],
        out_shape=[like((count, height, width), bf16) for height in heights],
        scratch_shapes=[
            pltpu.VMEM((left[0][1].stop - left[0][1].start, sum(array.shape[1] for array, _ in left)), bf16) for left in lefts
        ],
        compiler_params=pltpu.CompilerParams(vmem_limit_bytes=VMEM_LIMIT),
        cost_estimate=pl.CostEstimate(flops=1, bytes_accessed=1, transcendentals=0),
        name="products",
    )(spot, *arrays)


def lent_kernel(own, peer, extra1, extra2, logit1, logit2, qkv_ref, gate_ref, own_o, theirs_o):
    rows = own_o.shape[0]
    logits = [unstacked(ref, (D // HEAD_DIM * rows, rows)) for ref in (logit1, logit2)]
    total = nt(jnp.concatenate(logits, axis=0), gate_ref[...])
    size = rows + HALO
    for third in range(3):
        at, columns = slice(third * size, (third + 1) * size), slice(third * D, (third + 1) * D)
        both = completed(own.at[at], extra1[:, columns]) + completed(peer.at[at], extra2[:, columns])
        total = total + nt(jnp.concatenate(both, axis=0), qkv_ref[:, columns])
    own_o[...] = total[:rows]
    theirs_o[...] = total[rows:].astype(bf16)


def lent_rows(own, peer, extras, logits, qkv_weight, gate_weight):
    rows = own.shape[0] // 3 - HALO
    half = qkv_weight.shape[0]
    vmem = pl.BlockSpec(memory_space=pltpu.VMEM)
    return pl.pallas_call(
        lent_kernel,
        in_specs=[vmem] * 8,
        out_specs=[vmem] * 2,
        out_shape=[like((rows, half)), like((rows, half), bf16)],
        compiler_params=pltpu.CompilerParams(vmem_limit_bytes=VMEM_LIMIT),
        cost_estimate=pl.CostEstimate(flops=1, bytes_accessed=1, transcendentals=0),
        name="lent_rows",
    )(own, peer, *extras, *logits, qkv_weight, gate_weight)


def norm_back_kernel(place, own, back, tok_ref, gain_ref, hid_ref, tq, tk, tv, second_ref, ridge_ref, tok_o, vec_o):
    mine, other = own[...], back[...].astype(f32)
    grad = jnp.where(
        place[0] == 0, jnp.concatenate([mine, other], axis=1), jnp.concatenate([other, mine], axis=1)
    )
    tokens = tok_ref[...]
    scale = lax.rsqrt(jnp.mean(tokens * tokens, axis=-1, keepdims=True) + 1e-05)
    rows = tokens * scale
    grows = grad * gain_ref[...]
    tok_o[...] = hid_ref[...] + scale * (grows - rows * jnp.mean(grows * rows, axis=-1, keepdims=True))
    vec_o[:KW] = jnp.concatenate([tq[...], tk[...], tv[...]], axis=1)
    ridge = jnp.concatenate([ridge_ref[h] for h in range(HEADS)], axis=1)
    first = jnp.sum(grad * rows, axis=0, keepdims=True)
    vec_o[KW : KW + 1] = jnp.concatenate([first, second_ref[...], ridge], axis=1)
    vec_o[KW + 1 :] = jnp.zeros((8 - KW - 1, 3 * D), f32)


def norm_back(place, own, back, tokens, gain, hidden, taps, second, ridge):
    vmem = pl.BlockSpec(memory_space=pltpu.VMEM)
    return pl.pallas_call(
        norm_back_kernel,
        in_specs=[smem()] + [vmem] * 10,
        out_specs=[vmem] * 2,
        out_shape=[like(tokens.shape), like((8, 3 * D))],
        cost_estimate=pl.CostEstimate(flops=1, bytes_accessed=1, transcendentals=0),
        name="norm_back",
    )(place, own, back, tokens, gain, hidden, *taps, second, ridge)


def step_kernel(bit, kept_mine, kept_other, *refs):
    mine_o, other_o = refs[-2:]
    start = 0
    for mine, other in zip(refs[0:-2:2], refs[1:-2:2]):
        at = slice(start, start + mine.shape[1])
        start += mine.shape[1]
        mine_o[0, at] = (kept_mine[0, at].astype(f32) + mine[0].astype(f32)).astype(bf16)
        other_o[0, at] = (kept_other[0, at].astype(f32) + other[0].astype(f32)).astype(bf16)


def halving_step(bit, below, kept, got):
    count, size, width = kept.shape

    def half(side, rows):
        def index(i, s):
            return ((i // below) * 2 * below + (s[0] if side == 0 else 1 - s[0]) * below + i % below, 0, 0)

        return pl.BlockSpec((1, rows, width), index)

    out = pl.BlockSpec((1, size, width), lambda i, s: (i, 0, 0))
    arrays = [kept] + list(got)
    return pl.pallas_call(
        step_kernel,
        grid_spec=pltpu.PrefetchScalarGridSpec(
            num_scalar_prefetch=1,
            grid=(count // 2,),
            in_specs=[half(side, x.shape[1]) for x in arrays for side in (0, 1)],
            out_specs=[out, out],
        ),
        out_shape=[like((count // 2, size, width), bf16)] * 2,
        cost_estimate=pl.CostEstimate(flops=1, bytes_accessed=1, transcendentals=0),
        name="halving",
    )(bit, *[x for x in arrays for _ in (0, 1)])


BLOCKS = D // HEAD_DIM


def middle_kernel(
    owners, place, x_ref, s0, s1, s2, s3, k_ref, v_ref, c_ref, mask_ref, own_logit, lent_logit, tok_ref, cot_ref, gain_ref, first_ref,
    own_out, out_a, out_b, out_c, out_d, *refs,
):
    own_up = refs[:4]
    up_parts = (refs[4:8], refs[8:12])
    own_down = refs[12]
    down_parts = refs[13:17]
    (out_o, hid_o, gatt_o, own_o, sent_o, ggu_o, dgain_o) = refs[17:24]
    out_s, up_s, down_s, nf_s, gb_s, att_s, sig_s, hid_s, acc_s, gnf_s, inner_s = refs[24:]
    j = pl.program_id(0)
    y = place[0]
    half = D // 2

    def aligned(at, by):
        return pl.multiple_of(at, by)

    mine = pl.ds(aligned(y * half, half), half)
    theirs = pl.ds(aligned((1 - y) * half, half), half)

    def order(q):
        return [q, q ^ 2, q ^ 1, q ^ 3]

    tile = own_up[0].shape[1]
    tokens = tok_ref.shape[0]

    def spread_rows(rows, start):
        total = rows.shape[0]
        size = total // owners
        own_at = slice(start, start + total // 2)
        sent_at = slice(3 * BLOCKS * tokens + start, 3 * BLOCKS * tokens + start + total // 2)
        if size % 8:
            own_o[own_at], sent_o[sent_at] = rows[: total // 2].astype(bf16), rows[total // 2 :].astype(bf16)
            return
        blocks = rows.reshape(owners // 2, 2, size, rows.shape[1])
        for out, at, odd in ((own_o, own_at, y == 1), (sent_o, sent_at, y == 0)):
            out[at] = jnp.where(odd, blocks[:, 1], blocks[:, 0]).reshape(total // 2, rows.shape[1]).astype(bf16)

    def stack_right(value, index):
        for i in range(BLOCKS):
            sent_o[(index * BLOCKS + i) * tokens : (index * BLOCKS + i + 1) * tokens] = value[:, cut(i)]

    def scale_of(hidden):
        return lax.rsqrt(jnp.mean(hidden * hidden, axis=-1, keepdims=True) + 1e-05)

    @pl.when(j == 0)
    def _():
        for i, state in enumerate((s0, s1, s2, s3)):
            for m in range(SHARE):
                head = (place[1] ^ i) * SHARE + m
                c = c_ref[pl.ds(head, 1), :]
                x = x_ref[head]
                scores = (nn(k_ref[head], x) * mask_ref[head]).astype(bf16)
                part = jnp.exp(c) * nn(state[SHARE + m], x) + tn(v_ref[head], scores)
                att_s[:, pl.ds(aligned(head * HEAD_DIM, HEAD_DIM), HEAD_DIM)] = part.T
        out_s[mine, :] = own_out[...]
        wide = out_a.shape[1]
        for part, q in zip((out_a, out_b, out_c, out_d), order(place[1])):
            out_s[theirs, pl.ds(aligned(q * wide, wide), wide)] = part[...]
        sig = jax.nn.sigmoid(own_logit[...] + lent_logit[...].astype(f32))
        sig_s[...] = sig
        mix = (att_s[...] * sig).astype(bf16)
        spread_rows(mix.astype(f32).T, half)
        normed = tok_ref[...] * scale_of(tok_ref[...]) * first_ref[...]
        spread_rows(normed.astype(bf16).astype(f32).T, 2 * half)
        hidden = tok_ref[...] + nn(mix, out_s[...])
        hid_s[...] = hidden
        normed = (hidden * scale_of(hidden) * gain_ref[...]).astype(bf16)
        nf_s[...] = normed
        spread_rows(normed.astype(f32).T, 0)
        gb_s[...] = cot_ref[...].astype(bf16)
        stack_right(gb_s[...], 2)
        acc_s[...] = jnp.zeros_like(acc_s)
        gnf_s[...] = jnp.zeros_like(gnf_s)

    for i in range(4):
        up_s[mine, i * tile : (i + 1) * tile] = own_up[i][...]
    count = up_parts[0][0].shape[0]
    at = pl.ds(aligned((1 - y) * half, 16), count)
    for part, q in zip(up_parts[0], order(place[2])):
        slot = (q >> 1) * 2 + ((q & 1) ^ y)
        up_s[at, pl.ds(aligned(slot * tile, tile), tile)] = part[...]
    at = pl.ds(aligned((1 - y) * half + count, 16), half - count)
    for i, part in enumerate(up_parts[1]):
        slot = ((place[1] ^ (i // 2)) & 1) * 2 + i % 2
        up_s[at, pl.ds(aligned(slot * tile, tile), tile)] = part[...]
    down_s[:tile, :] = own_down[...]
    wide = down_parts[0].shape[1]
    for part, q in zip(down_parts, order(place[1])):
        down_s[tile:, pl.ds(aligned(q * wide, wide), wide)] = part[...]
    product = nn(nf_s[...], up_s[...])
    gate, up = product[:, : 2 * tile], product[:, 2 * tile :]
    ginner = nt(gb_s[...], down_s[...])
    sig = jax.nn.sigmoid(gate)
    silu = gate * sig
    inner = (silu * up).astype(bf16)
    ggate = (ginner * up * (sig * (1.0 + gate * (1.0 - sig)))).astype(bf16)
    gup = (ginner * silu).astype(bf16)
    ggu = jnp.concatenate([ggate, gup], axis=1)
    acc_s[...] += nn(inner, down_s[...])
    gnf_s[...] += nt(ggu, up_s[...])
    inner_t = inner.astype(f32).T
    for slot, value in ((y, inner_t[:tile]), (1 - y, inner_t[tile:])):
        inner_s[pl.ds(aligned(slot * (FF // 2) + j * tile, tile), tile), :] = value
    share = FF // 2
    for i, (slot, value) in enumerate(((y, ggate), (1 - y, ggate), (2 + y, gup), (3 - y, gup))):
        at = pl.ds(aligned(slot * share + j * tile, tile), tile)
        ggu_o[:, at] = value[:, (i % 2) * tile : (i % 2 + 1) * tile]

    @pl.when(j == pl.num_programs(0) - 1)
    def _():
        spread_rows(inner_s[...], 3 * half)
        hidden = hid_s[...]
        out_o[...] = hidden + acc_s[...]
        scale = scale_of(hidden)
        rows = hidden * scale
        gnf = gnf_s[...]
        dgain_o[...] = jnp.sum(gnf * rows, axis=0, keepdims=True)
        grows = gnf * gain_ref[...]
        ghid = cot_ref[...] + scale * (grows - rows * jnp.mean(grows * rows, axis=-1, keepdims=True))
        hid_o[...] = ghid
        low = ghid.astype(bf16)
        stack_right(low, 0)
        gmix = nt(low, out_s[...])
        sig = sig_s[...]
        gatt = gmix * sig
        gatt_o[...] = gatt
        stack_right((gatt * att_s[...] * (1.0 - sig)).astype(bf16), 1)


def middle(owners, place, attention, own_logit, lent_logit, tok, cot, gain, gain_first, out_weight, up_weight, down_weight, up_parts, rest_parts):
    tokens = tok.shape[0]
    tile = 128
    share = FF // 2 // tile
    half = D // 2
    left_rows = 3 * half + FF // 2

    def full(*shape):
        return pl.BlockSpec(shape, lambda j, s: (0,) * len(shape))

    rows = full(tokens, D)
    own_up = [
        pl.BlockSpec((half, tile), lambda j, s: (0, s[0] * share + j)),
        pl.BlockSpec((half, tile), lambda j, s: (0, (1 - s[0]) * share + j)),
        pl.BlockSpec((half, tile), lambda j, s: (0, (2 + s[0]) * share + j)),
        pl.BlockSpec((half, tile), lambda j, s: (0, (3 - s[0]) * share + j)),
    ]
    up_specs = [pl.BlockSpec((p.shape[0], tile), lambda j, s: (0, j)) for p in up_parts[:4]]
    rest_rows = up_parts[4].shape[0]
    up_specs += [
        pl.BlockSpec((rest_rows, tile), lambda j, s: (0, s[0] * share + j)),
        pl.BlockSpec((rest_rows, tile), lambda j, s: (0, (1 - s[0]) * share + j)),
    ] * 2
    up_parts = up_parts[:4] + (up_parts[4],) * 2 + (up_parts[5],) * 2
    own_down = pl.BlockSpec((tile, D), lambda j, s: (j, 0))
    down_specs = [pl.BlockSpec((tile, D // 4), lambda j, s: (half // tile + j, 0))] * 4
    square = (HEAD_DIM, HEAD_DIM)
    return pl.pallas_call(
        functools.partial(middle_kernel, owners),
        grid_spec=pltpu.PrefetchScalarGridSpec(
            num_scalar_prefetch=1,
            grid=(share,),
            in_specs=[full(HEADS, HEAD_DIM, tokens)] + [full(*PAIR)] * FOUR + [full(HEADS, tokens, HEAD_DIM)] * 2
            + [full(HEADS, tokens), full(HEADS, tokens, tokens)]
            + [pl.BlockSpec((tokens, D), lambda j, s: (0, 3))] * 2
            + [rows] * 2 + [full(1, D), full(1, D), full(half, D)] + [full(half, D // 4)] * 4
            + own_up + up_specs + [own_down] + down_specs,
            out_specs=[
                rows, rows, rows, full(left_rows, tokens), full(3 * BLOCKS * tokens + left_rows, tokens),
                full(tokens, 2 * FF),
                full(1, D),
            ],
            scratch_shapes=[
                pltpu.VMEM((D, D), bf16),
                pltpu.VMEM((D, 4 * tile), bf16),
                pltpu.VMEM((2 * tile, D), bf16),
                pltpu.VMEM((tokens, D), bf16),
                pltpu.VMEM((tokens, D), bf16),
                pltpu.VMEM((tokens, D), f32),
                pltpu.VMEM((tokens, D), f32),
                pltpu.VMEM((tokens, D), f32),
                pltpu.VMEM((tokens, D), f32),
                pltpu.VMEM((tokens, D), f32),
                pltpu.VMEM((FF, tokens), f32),
            ],
        ),
        out_shape=[
            like((tokens, D)), like((tokens, D)), like((tokens, D)),
            like((left_rows, tokens), bf16), like((3 * BLOCKS * tokens + left_rows, tokens), bf16),
            like((tokens, 2 * FF), bf16),
            like((1, D)),
        ],
        compiler_params=pltpu.CompilerParams(vmem_limit_bytes=VMEM_LIMIT),
        cost_estimate=pl.CostEstimate(flops=1, bytes_accessed=1, transcendentals=0),
        name="middle",
    )(
        place, *attention, own_logit, lent_logit, tok, cot, gain, gain_first, out_weight, *rest_parts,
        *[up_weight] * 4, *up_parts, down_weight, *rest_parts,
    )


def shifted(x, axis, by):
    peers = lax.axis_size(axis)
    return lax.ppermute(x, axis, [(i, i + by) for i in range(peers) if 0 <= i + by < peers])


def crossed(x, by):
    peers, pair = lax.axis_size("ctx"), 2
    return lax.ppermute(
        x,
        ("ctx", "fsdp"),
        [(i * pair + s, (i + by) * pair + 1 - s) for i in range(peers) if 0 <= i + by < peers for s in range(pair)],
    )


def pick(x, index, axis=0):
    return lax.dynamic_index_in_dim(x, index, axis, keepdims=False)


def part(x, index, axis):
    size = x.shape[axis] // 2
    return lax.dynamic_slice_in_dim(x, index * size, size, axis)


def quarter(shard, q, start=0, count=None):
    wide = shard.shape[1] // 4
    return lax.dynamic_slice(shard, (start, q * wide), (count or shard.shape[0], wide))


class Reduction:
    def __init__(self, order, blocks):
        self.here = lax.axis_index("ctx")
        levels = lax.axis_size("ctx").bit_length() - 1
        self.order = list(order) + [level for level in range(levels) if level not in order]
        self.left = list(range(levels))
        self.kept, *sent = blocks
        self.send(sent)

    def bit(self):
        return (self.here >> self.order[0]) & 1

    def send(self, arrays):
        level = self.order.pop(0)
        self.left.remove(level)
        self.got = [partner(array, "ctx", 1 << level) for array in arrays]

    def step(self):
        below = 1 << self.left.index(self.order[0])
        self.kept, sent = halving_step(self.bit().astype(jnp.int32)[None], below, self.kept, self.got)
        self.send([sent])
        return sent

    def result(self, sizes):
        while self.order:
            self.step()
        total = (self.kept.astype(f32) + self.got[0].astype(f32))[0]
        ends = [sum(sizes[: i + 1]) for i in range(len(sizes))]
        return [total[end - size : end] for end, size in zip(ends, sizes)]


class Sequence:
    def __init__(self):
        self.last = ()

    def gate(self, *values):
        return lax.optimization_barrier(values + self.last)[: len(values)]

    def mark(self, *values):
        self.last = values


def added(value, axis):
    for level in range(lax.axis_size(axis).bit_length() - 1):
        value = value + partner(value, axis, 1 << level)
    return value


def rms_scale(values, gain):
    return values * lax.rsqrt(jnp.mean(values * values, axis=-1, keepdims=True) + 1e-05) * gain


def sided(mine, theirs, y, axis):
    return jnp.where(
        y == 0, jnp.concatenate([mine, theirs], axis=axis), jnp.concatenate([theirs, mine], axis=axis)
    )


UP_ROWS = 400


def local(
    inputs,
    qkv_weight,
    gate_weight,
    out_weight,
    up_weight,
    down_weight,
    conv_taps,
    gain_attn,
    gain_ffn,
    ridge_terms,
    forget,
    cotangent,
):
    tokens = inputs[0]
    rows = tokens.shape[0]
    y = lax.axis_index("fsdp")
    here = lax.axis_index("ctx")
    peers = lax.axis_size("ctx")
    owners = peers * 2
    near_x = here % 4
    near_z = here % 2 + 2 * ((here // 4) % 2)
    place = jnp.stack([y, near_x, near_z]).astype(jnp.int32)
    spot = here.astype(jnp.int32)[None]
    spot_back = (peers - 1 - here).astype(jnp.int32)[None]
    ring = near_x.astype(jnp.int32)[None]
    seq = Sequence()

    lines = jnp.stack([gain_attn, gain_ffn, ridge_terms, ridge_terms])
    mine, theirs = norm(place, tokens, conv_taps, lines)
    theirs = partner(theirs, "fsdp")
    lent = weigh(theirs, rows, gain_attn[None], qkv_weight, gate_weight, bf16)
    seq.mark(lent)
    lent = partner(lent, "fsdp")
    peer_extra = theirs[rows:].astype(f32)
    (peer_extra,) = seq.gate(peer_extra)
    taps_rows = KW * 3
    vectors = sided(lines[:3].astype(f32), peer_extra[taps_rows : taps_rows + 3], y, 1)
    taps = sided(conv_taps.astype(f32), peer_extra[:taps_rows].reshape(conv_taps.shape), y, 1)
    gain_first, gain_second = vectors[0], vectors[1:2]
    ridge = vectors[2].reshape(HEADS, HEAD_DIM)
    cumulative = jnp.cumsum(jnp.log(forget[0]).T, axis=-1)
    strength = (1.0 - forget[0]).T
    out_here, up_here, down_here = seq.gate(out_weight, up_weight, down_weight)
    rest_quarter = jnp.concatenate([quarter(out_here, near_x), quarter(down_here, near_x)], axis=0)
    seq.mark(rest_quarter)
    rest_direct = partner(rest_quarter, "fsdp")
    (up_here,) = seq.gate(up_here)
    up_quarters = [
        quarter(up_here, near_z, 0, UP_ROWS),
        lax.dynamic_slice(up_here, (UP_ROWS, (here % 2) * FF), (D // 2 - UP_ROWS, FF)),
    ]
    seq.mark(*up_quarters)
    cumulative, strength, ridge, taps, mine = seq.gate(cumulative, strength, ridge, taps, mine)
    own = weigh(mine, rows, gain_attn[None], qkv_weight, gate_weight, f32)
    mask, ending, ridge = tables(cumulative, strength, ridge)
    seq.mark(mask, own)

    own, lent, up_first = seq.gate(own, lent, up_quarters[0])
    halo = shifted((own[rows - 8 :, : 3 * D] + lent[rows - 8 :, : 3 * D].astype(f32)).astype(bf16), "ctx", 1)
    projected = own, lent, halo
    queries, keys_low, values_low, *near = features(spot, projected, taps, ending, cumulative)
    seq.mark(*near)
    scan = Scan(spot, swapped(near, "ctx"), "ctx")
    up_first = partner(up_first, "fsdp")

    def split(left):
        flat = left.reshape(peers, 2, left.shape[0] // owners, left.shape[1])
        return [pick(flat, side, 1).reshape(-1, left.shape[1]) for side in (y, 1 - y)]

    scan.near = list(seq.gate(*scan.near))
    scan.group()
    seq.mark(scan.total)
    (rest_direct,) = seq.gate(rest_direct)
    rest_across = partner(rest_direct, "ctx", 2)
    scan.far = list(seq.gate(*scan.far))
    states = scan.spread()
    seq.mark(scan.parts[0])
    up_first, up_second = seq.gate(up_first, up_quarters[1])
    up_second = partner(up_second, "fsdp")
    first_across = partner(up_first, "ctx", 4)
    *states, queries = seq.gate(*states, queries)
    seq.mark(states[1], states[2], states[3])
    rest_direct, rest_across, up_first = seq.gate(rest_direct, rest_across, up_first)
    rest_core, rest_far, first_core = partner(rest_direct, "ctx", 1), partner(rest_across, "ctx", 1), partner(up_first, "ctx", 1)
    (queries,) = seq.gate(queries)
    x, p_all, m_all, scores, scal = solve(ring, queries, keys_low, states, cumulative, mask, ridge)
    seq.mark(x)

    def split(left):
        flat = left.reshape(peers, 2, left.shape[0] // owners, left.shape[1])
        return [pick(flat, side, 1).reshape(-1, left.shape[1]) for side in (y, 1 - y)]

    def share(right):
        return right, partner(right, "fsdp")

    up_second, rest_core, rest_far = seq.gate(up_second, rest_core, rest_far)
    second_core = partner(up_second, "ctx", 1)
    (first_across,) = seq.gate(first_across)
    rest_parts = (rest_direct, rest_across, rest_core, rest_far)
    up_parts = (up_first, first_across, first_core, partner(first_across, "ctx", 1))
    up_parts += (up_second, second_core)

    output, grad_hidden, grad_attended, lefts, message, grad_gate_up, grad_second_gain = middle(
        owners, place, (x, *states, keys_low, values_low, cumulative, mask), own, lent,
        tokens, cotangent[0], gain_second, gain_first[None], out_weight, up_weight, down_weight, up_parts, rest_parts
    )
    size = D // 2
    parts = [slice(0, size), slice(size, 2 * size), slice(2 * size, 3 * size), slice(3 * size, 3 * size + FF // 2)]
    start = 3 * BLOCKS * rows
    peer_parts = [slice(start + at.start, start + at.stop) for at in parts]
    if (D // owners) % 8 or (FF // owners) % 8:
        pairs = [split(jnp.concatenate([lefts[at], message[there]], axis=0)) for at, there in zip(parts, peer_parts)]
        lefts = jnp.concatenate([own for own, _ in pairs], axis=0)
        message = jnp.concatenate([message[:start]] + [sent for _, sent in pairs], axis=0)
    seq.mark(grad_second_gain)
    message_peer = partner(message, "fsdp")
    (grad_attended,) = seq.gate(grad_attended)
    gx, dk_attend, dv, value_states = attend_back(
        ring, grad_attended, keys_low, values_low, x, states, cumulative, mask
    )
    dq, dk_solve, grad_ridge, *own = adjoint(
        spot_back, ring, gx, keys_low, states, cumulative, mask, ridge, p_all, m_all, scores, scal, value_states
    )
    seq.mark(*own)
    back = Scan(spot_back, swapped(own, "ctx"), "ctx")
    (up_here,) = seq.gate(grad_gate_up)
    both_up = share(up_here)
    dq, back.near[1] = seq.gate(dq, back.near[1])
    low_q, taps_q = queries_back(projected, taps, dq)
    seq.mark(low_q)
    back.near = list(seq.gate(*back.near))
    back.group()
    seq.mark(back.total)
    lefts_here, message_peer, back.far[1] = seq.gate(lefts, message_peer, back.far[1])
    rights = [(i * BLOCKS * rows, rows) for i in range(3)]
    (early,) = products(
        spot, peers, [[(lefts_here, parts[i]), (message_peer, peer_parts[i])] for i in (1, 2, 3)],
        [[(message, at), (message_peer, at)] for at in rights], 512, joined=True
    )
    seq.mark(early)
    early = lax.psum_scatter(early.reshape(-1, D), "ctx", scatter_dimension=0, tiled=True)
    back.far = list(seq.gate(*back.far))
    states_back = back.spread()
    seq.mark(back.parts[0])
    dv, *states_back = seq.gate(dv, *states_back)
    low_k, taps_k, low_v, taps_v = keys_values_back(
        spot_back, projected, taps, dk_attend, dk_solve, dv, keys_low, values_low, states_back, ending
    )
    seq.mark(low_k)
    (up_peer,) = seq.gate(both_up[1])
    blocks = products(
        spot, peers, [[(lefts, parts[0]), (message_peer, peer_parts[0])]], [[(both_up[0], None), (up_peer, None)]], 1408
    )
    seq.mark(blocks[0])
    ups = Reduction((0, 1, 2), blocks)
    low_q, low_k, low_v = seq.gate(low_q, low_k, low_v)
    ahead = jnp.concatenate([low[HALO - 8 : HALO] for low in (low_q, low_k, low_v)], axis=1)
    extra = shifted(ahead, "ctx", -1), crossed(ahead, -1)
    thirds = jnp.concatenate([low_q, low_k, low_v], axis=0)
    thirds, *extra = lax.optimization_barrier((thirds, *extra))
    thirds_peer = partner(thirds, "fsdp")
    *ups.got, extra1, extra2 = seq.gate(*ups.got, *extra)
    extra = extra1, extra2
    seq.mark(ups.step())
    lefts_here, thirds_peer = seq.gate(lefts, thirds_peer)
    left = [(lefts_here, parts[2]), (message_peer, peer_parts[2])]
    rights = [[(thirds, i), (thirds_peer, i), (extra[0], i), (extra[1], i)] for i in range(3)]
    blocks = products(spot, peers, [left] * 3, rights, 512, messages=2)
    seq.mark(blocks[0])
    late = Reduction((0, 1, 2), blocks)
    late.got = seq.gate(*late.got)
    seq.mark(late.step())
    (thirds_here,) = seq.gate(thirds)
    kept, lent = lent_rows(thirds_here, thirds_peer, extra, (message, message_peer), qkv_weight, gate_weight)
    seq.mark(lent)
    arriving = partner(lent, "fsdp")
    ups.got = seq.gate(*ups.got)
    seq.mark(ups.step())
    (arriving,) = seq.gate(arriving)
    grad_tokens, vector = norm_back(
        place, kept, arriving, tokens, gain_first[None], grad_hidden, (taps_q, taps_k, taps_v), grad_second_gain, grad_ridge
    )
    seq.mark(vector)
    size, width = D // owners, 3 * D // owners
    vector = jnp.concatenate(
        [vector[:KW].reshape(KW, owners, width).transpose(1, 0, 2).reshape(owners, KW * width),
         vector[KW].reshape(3, owners, size).transpose(1, 0, 2).reshape(owners, 3 * size)], axis=1
    ).reshape(peers, 2, KW * width + 3 * size)
    vector_kept, vector_sent = pick(vector, y, 1), pick(vector, 1 - y, 1)
    seq.mark(vector_sent)
    arriving = partner(vector_sent, "fsdp")
    late.got = seq.gate(*late.got)
    seq.mark(late.step())
    *ups.got, early = seq.gate(*ups.got, early)
    seq.mark(ups.step())
    vector_kept, arriving = seq.gate(vector_kept, arriving)
    vector = vector_kept + arriving
    seq.mark(vector)
    vector = lax.all_to_all(vector, "ctx", 0, 0, tiled=True)
    late.got = seq.gate(*late.got)
    seq.mark(late.step())
    vector = jnp.sum(seq.gate(vector)[0], axis=0)
    size = D // owners
    grad_up = ups.result([size])[0]
    grad_q, grad_k, grad_v = late.result([size] * 3)
    grad_qkv = jnp.concatenate([grad_q, grad_k, grad_v], axis=1)
    early = early.astype(f32)
    grad_out, grad_gate, grad_down = early[:size], early[size : 2 * size], early[2 * size :]
    return (
        output[None],
        grad_tokens[None],
        grad_qkv,
        grad_gate,
        grad_out,
        grad_up,
        grad_down,
        vector[: KW * width].reshape(KW, width),
        vector[KW * width : KW * width + size],
        vector[KW * width + size : KW * width + 2 * size],
        vector[KW * width + 2 * size :],
    )


def solution(mesh):
    tokens = P("fsdp", "ctx", None)
    rows = P("fsdp", None)
    vector = P("fsdp")
    owned = P(("ctx", "fsdp"), None)
    owned_vector = P(("ctx", "fsdp"))
    return jax.shard_map(
        local,
        mesh=mesh,
        in_specs=(
            tokens, rows, rows, rows, rows, rows, P(None, "fsdp"), vector, vector, vector, tokens, tokens,
        ),
        out_specs=(
            tokens, tokens, owned, owned, owned, owned, owned, P(None, ("ctx", "fsdp")),
            owned_vector, owned_vector, owned_vector,
        ),
        check_vma=False,
    )
```

```python
import functools
import jax
import jax.numpy as jnp
from jax import lax
from jax.experimental import pallas as pl
from jax.experimental.pallas import tpu as pltpu
from jax.sharding import PartitionSpec as P

D = 1024
HEADS = 8
FF = 2816
KW = 4
ITERS = 8
AT_ONCE = 2
HEAD_DIM = 128
QUARTERS = 4
SHARE = HEADS // QUARTERS
HALO = 16

f32 = jnp.float32
bf16 = jnp.bfloat16
VMEM_LIMIT = 56 * 1024 * 1024


def nn(a, b):
    return lax.dot_general(a, b, (((1,), (0,)), ((), ())), preferred_element_type=f32)


def nt(a, b):
    return lax.dot_general(a, b, (((1,), (1,)), ((), ())), preferred_element_type=f32)


def tn(a, b):
    return lax.dot_general(a, b, (((0,), (0,)), ((), ())), preferred_element_type=f32)


def column(row, like):
    return jnp.broadcast_to(row, like).T


def decay_mask(c, b, tokens):
    shape = (tokens, tokens)
    late = lax.broadcasted_iota(jnp.int32, shape, 1) >= lax.broadcasted_iota(jnp.int32, shape, 0)
    spread = jnp.broadcast_to(c, shape) - column(c, shape)
    return jnp.where(late, jnp.exp(jnp.where(late, spread, 0.0)), 0.0) * column(b, shape)


def like(shape, kind=f32):
    return jax.ShapeDtypeStruct(shape, kind)


def smem():
    return pl.BlockSpec(memory_space=pltpu.SMEM)


EXTRA = 16


def norm_kernel(place, tok_ref, taps_ref, lines_ref, mine_o, theirs_o):
    half = D // 2
    y = place[0]
    a = tok_ref[...]
    unit = a * lax.rsqrt(jnp.mean(a * a, axis=-1, keepdims=True) + 1e-05)
    left, right = unit[:, :half], unit[:, half:]
    rows = a.shape[0]
    gain = lines_ref[0:1].astype(f32)
    mine_o[...] = (jnp.where(y == 0, left, right) * gain).astype(bf16)
    theirs_o[:rows] = jnp.where(y == 0, right, left).astype(bf16)
    taps = taps_ref[...]
    lines = [taps[t : t + 1, i * half : (i + 1) * half] for t in range(KW) for i in range(3)]
    theirs_o[rows:] = jnp.concatenate(lines + [lines_ref[...]], axis=0)


def norm(place, tokens, taps, lines):
    rows = tokens.shape[0]
    vmem = pl.BlockSpec(memory_space=pltpu.VMEM)
    return pl.pallas_call(
        norm_kernel,
        in_specs=[smem()] + [vmem] * 3,
        out_specs=[vmem, vmem],
        out_shape=[like((rows, D // 2), bf16), like((rows + EXTRA, D // 2), bf16)],
        name="norm",
    )(place, tokens, taps, lines)


def weigh_kernel(scaled, left_ref, gain_ref, qkv_ref, gate_ref, out, left):
    j = pl.program_id(0)

    @pl.when(j == 0)
    def _():
        rows = left_ref[: left.shape[0]]
        left[...] = (rows.astype(f32) * gain_ref[...].astype(f32)).astype(bf16) if scaled else rows

    steps = 3 * D // out.shape[1]

    @pl.when(j < steps)
    def _():
        out[...] = nn(left[...], qkv_ref[...]).astype(out.dtype)

    @pl.when(j >= steps)
    def _():
        out[...] = nn(left[...], gate_ref[...]).astype(out.dtype)


def weigh(left, rows, gain, qkv_weight, gate_weight, kind):
    half = left.shape[1]
    tile = 1024
    steps = 3 * D // tile
    return pl.pallas_call(
        functools.partial(weigh_kernel, left.shape[0] > rows),
        grid=(4 * D // tile,),
        in_specs=[
            whole(*left.shape), whole(1, half),
            pl.BlockSpec((half, tile), lambda j: (0, jnp.minimum(j, steps - 1))),
            pl.BlockSpec((half, tile), lambda j: (0, jnp.maximum(j - steps, 0))),
        ],
        out_specs=pl.BlockSpec((rows, tile), lambda j: (0, j)),
        out_shape=like((rows, 4 * D), kind),
        scratch_shapes=[pltpu.VMEM((rows, half), bf16)],
        cost_estimate=pl.CostEstimate(flops=1, bytes_accessed=1, transcendentals=0),
        name="weigh",
    )(left, gain, qkv_weight, gate_weight)


def tables_kernel(c_ref, b_ref, ridge_ref, mask_o, ending_o, ridge_o):
    tokens = c_ref.shape[1]
    head = pl.program_id(0)
    c, b = c_ref[pl.ds(head, 1), :], b_ref[pl.ds(head, 1), :]
    mask_o[0] = decay_mask(c, b, tokens)
    ending_o[0] = column(jnp.exp(c[:, tokens - 1 :] - c) * b, (HEAD_DIM, tokens))
    ridge_o[0] = column(ridge_ref[pl.ds(head, 1), :], (tokens, HEAD_DIM))


def tables(c, b, ridge):
    tokens = c.shape[1]
    shapes = [(tokens, tokens), (tokens, HEAD_DIM), (HEAD_DIM, tokens)]
    return pl.pallas_call(
        tables_kernel,
        grid=(HEADS,),
        in_specs=[whole(HEADS, tokens)] * 2 + [whole(HEADS, HEAD_DIM)],
        out_specs=[pl.BlockSpec((1,) + shape, lambda h: (h, 0, 0)) for shape in shapes],
        out_shape=[like((HEADS,) + shape) for shape in shapes],
        cost_estimate=pl.CostEstimate(flops=1, bytes_accessed=1, transcendentals=0),
        name="tables",
    )(c, b, ridge)


def with_halo(own, lent, halo):
    before = halo[...].astype(f32)
    blank = jnp.zeros((HALO - before.shape[0], before.shape[1]), f32)
    return jnp.concatenate([blank, before, own[...] + lent[...].astype(f32)], axis=0)


def conv_parts(padded, taps):
    rows = padded.shape[0] - HALO
    shifted = [padded[HALO - KW + 1 + j : HALO - KW + 1 + j + rows] for j in range(KW)]
    total = taps[0:1] * shifted[0]
    for j in range(1, KW):
        total = total + taps[j : j + 1] * shifted[j]
    return total, shifted


def unit(a):
    return a * lax.rsqrt(jnp.sum(a * a, axis=-1, keepdims=True) + 1e-06)


def position(spot):
    return spot[0] % FOUR


FOUR = 4
PAIR = (2 * SHARE, HEAD_DIM, HEAD_DIM)
MESSAGE = (2 * SHARE, HEAD_DIM + 16, HEAD_DIM)


def decay_rows(decay):
    shape = (16, HEAD_DIM)
    at = lax.broadcasted_iota(jnp.int32, shape, 0)
    decay = jnp.broadcast_to(decay, shape)
    high = decay.astype(bf16).astype(f32)
    return jnp.where(at == 0, high, jnp.where(at == 1, decay - high, 0.0)).astype(bf16)


def decay_of(message, m):
    rows = message[m, HEAD_DIM:].astype(f32)
    return rows[0:1] + rows[1:2]


def block_decay(c_ref, head):
    c = c_ref[pl.ds(head, 1), :]
    return jnp.broadcast_to(jnp.exp(c[:, c.shape[1] - 1 :]), (1, HEAD_DIM))


def store_quarter(spot, quarter, outs, states, c_ref):
    rows = [decay_rows(block_decay(c_ref, quarter * SHARE + m)) for m in range(SHARE)]
    for i, out in enumerate(outs):

        @pl.when((position(spot) ^ i) == quarter)
        def _():
            for m in range(2 * SHARE):
                out[m, :HEAD_DIM] = states[m]
                out[m, HEAD_DIM:] = rows[m % SHARE]


def cut(h):
    return slice(h * HEAD_DIM, (h + 1) * HEAD_DIM)


def features_kernel(
    spot, oq, ok, ov, lq, lk, lv, hq, hk, hv, tq, tk, tv, ending_ref, c_ref, q_o, k_o, v_o, *outs
):
    quarter = pl.program_id(0)

    def activated(own, lent, halo, taps):
        total, _ = conv_parts(with_halo(own, lent, halo), taps[...])
        return total * jax.nn.sigmoid(total)

    queries, keys, values = activated(oq, lq, hq, tq), activated(ok, lk, hk, tk), activated(ov, lv, hv, tv)
    key_states, value_states = [], []
    for m in range(SHARE):
        k, v = unit(keys[:, cut(m)]), values[:, cut(m)]
        k_low = k.astype(bf16)
        k_o[m] = k_low
        v_o[m] = v.astype(bf16)
        q_o[m] = unit(queries[:, cut(m)]).T
        ending = ending_ref[m]
        key_states.append(tn((k * ending).astype(bf16), k_low).astype(bf16))
        value_states.append(tn((v * ending).astype(bf16), k_low).astype(bf16))
    store_quarter(spot, quarter, outs, key_states + value_states, c_ref)


def whole(*shape):
    return pl.BlockSpec(shape, lambda *g: (0,) * len(shape))


def per_quarter(*shape):
    return pl.BlockSpec((SHARE,) + shape, lambda p: (p,) + (0,) * len(shape))


def quarter_columns(rows, third):
    return pl.BlockSpec((rows, SHARE * HEAD_DIM), lambda p: (0, third * QUARTERS + p))


def features(spot, projected, taps, ending, c):
    own, lent, halo = projected
    tokens = own.shape[0]
    return pl.pallas_call(
        features_kernel,
        grid=(QUARTERS,),
        in_specs=[smem()] + [quarter_columns(x, i) for x in (tokens, tokens, halo.shape[0], KW) for i in range(3)]
        + [per_quarter(tokens, HEAD_DIM), whole(HEADS, tokens)],
        out_specs=[per_quarter(HEAD_DIM, tokens)] + [per_quarter(tokens, HEAD_DIM)] * 2 + [whole(*MESSAGE)] * QUARTERS,
        out_shape=[like((HEADS, HEAD_DIM, tokens))] + [like((HEADS, tokens, HEAD_DIM), bf16)] * 2
        + [like(MESSAGE, bf16)] * QUARTERS,
        cost_estimate=pl.CostEstimate(flops=1, bytes_accessed=1, transcendentals=0),
        name="features",
    )(spot, own, own, own, lent, lent, lent, halo, halo, halo, taps, taps, taps, ending, c)


def decay_between(indices, decays, low, high):
    total = None
    for index, decay in zip(indices, decays):
        one = jnp.where((index > low) & (index < high), decay, 1.0)
        total = one if total is None else total * one
    return total


def summed(factors, arrays, m):
    total = factors[0] * arrays[0][m, :HEAD_DIM].astype(f32)
    for factor, array in zip(factors[1:], arrays[1:]):
        total = total + factor * array[m, :HEAD_DIM].astype(f32)
    return total


def members(spot, unit, count):
    place = (spot[0] // unit) % count
    return place, [place ^ i for i in range(count)]


def whole_group(indices, arrays, m):
    decays = [decay_of(a, m) for a in arrays]
    count = len(arrays)
    state = summed([decay_between(indices, decays, i, count) for i in indices], arrays, m)
    return state, decay_between(indices, decays, -1, count)


def earlier(place, indices, arrays, m, before):
    decays = [decay_of(a, m) for a in arrays]
    factors = [jnp.where(i < place, decay_between(indices, decays, i, place), 0.0) for i in indices[1:]]
    state = summed(factors, arrays[1:], m)
    decay = decay_between(indices, decays, -1, place)
    if before is None:
        return state, decay
    old = before[m, HEAD_DIM : HEAD_DIM + 1]
    return before[m, :HEAD_DIM] + old * state, old * decay


def group_kernel(spot, *refs):
    arrays, out = refs[:FOUR], refs[FOUR]
    _, indices = members(spot, 1, FOUR)
    for m in range(2 * SHARE):
        state, decay = whole_group(indices, arrays, m)
        out[m, :HEAD_DIM] = state.astype(bf16)
        out[m, HEAD_DIM:] = decay_rows(decay)


def upper_kernel(unit, count, has_before, spot, *refs):
    arrays = refs[:count]
    before = refs[count] if has_before else None
    before_o, total_o = refs[-2:]
    place, indices = members(spot, unit, count)
    for m in range(2 * SHARE):
        state, decay = earlier(place, indices, arrays, m, before)
        before_o[m, :HEAD_DIM] = state
        before_o[m, HEAD_DIM:] = jnp.broadcast_to(decay, (16, HEAD_DIM))
        state, decay = whole_group(indices, arrays, m)
        total_o[m, :HEAD_DIM] = state.astype(bf16)
        total_o[m, HEAD_DIM:] = decay_rows(decay)


def spread_kernel(unit, count, has_before, spot, *refs):
    arrays, near = refs[:count], refs[count : count + FOUR]
    before = refs[count + FOUR] if has_before else None
    outs = refs[-FOUR:]
    place, upper = members(spot, unit, count)
    _, indices = members(spot, 1, FOUR)
    for m in range(2 * SHARE):
        state, _ = earlier(place, upper, arrays, m, before)
        decays = [decay_of(x, m) for x in near]
        for j in range(FOUR):
            at = indices[j]
            factors = [jnp.where(i < at, decay_between(indices, decays, i, at), 0.0) for i in indices]
            total = decay_between(indices, decays, -1, at) * state + summed(factors, near, m)
            outs[j][m] = total.astype(bf16)


def small_call(kernel, name, shapes, spot, *args):
    vmem = pl.BlockSpec(memory_space=pltpu.VMEM)
    return pl.pallas_call(
        kernel,
        in_specs=[smem()] + [vmem] * len(args),
        out_specs=[vmem] * len(shapes),
        out_shape=shapes,
        cost_estimate=pl.CostEstimate(flops=1, bytes_accessed=1, transcendentals=0),
        name=name,
    )(spot, *args)


def neighbour(axis, bit):
    return [(i, i ^ bit) for i in range(lax.axis_size(axis))]


def partner(x, axis, bit=1):
    return lax.ppermute(x, axis, neighbour(axis, bit))


def radices(peers):
    sizes = []
    left = peers // FOUR
    while left > 1:
        sizes.append(min(FOUR, left))
        left //= sizes[-1]
    return sizes


def swapped(arrays, axis, unit_size=1):
    return [arrays[0]] + [partner(a, axis, unit_size * i) for i, a in enumerate(arrays) if i]


class Scan:
    def __init__(self, spot, near, axis):
        self.spot, self.axis, self.near = spot, axis, near
        self.sizes = radices(lax.axis_size(axis))

    def group(self):
        message = like(MESSAGE, bf16)
        (self.total,) = small_call(group_kernel, "group", [message], self.spot, *self.near)
        self.before = ()
        self.unit = FOUR
        for radix in self.sizes[:-1]:
            arrays = swapped([self.total] * radix, self.axis, self.unit)
            kernel = functools.partial(upper_kernel, self.unit, radix, bool(self.before))
            before, self.total = small_call(kernel, "upper", [like(MESSAGE), message], self.spot, *arrays, *self.before)
            self.before = (before,)
            self.unit *= radix
        self.far = swapped([self.total] * self.sizes[-1], self.axis, self.unit)

    def spread(self):
        kernel = functools.partial(spread_kernel, self.unit, self.sizes[-1], bool(self.before))
        self.parts = small_call(
            kernel, "spread", [like(PAIR, bf16)] * FOUR, self.spot, *self.far, *self.near, *self.before
        )
        self.entering = swapped(self.parts, self.axis)
        return self.entering


def prepare(k_ref, c_ref, state_refs, place, left, wide, decay, pair):
    tokens = k_ref.shape[1]
    for i, state in enumerate(state_refs):
        for m in range(SHARE):
            left[(place ^ i) * SHARE + m, :, :HEAD_DIM] = state[m]
    pair[...] = jnp.zeros_like(pair)
    for h in range(HEADS):
        k = k_ref[h]
        left[h, :, HEAD_DIM:] = k.T
        wide[h // 2, :, cut(h % 2)] = k
        decay[h] = jnp.broadcast_to(jnp.exp(c_ref[h : h + 1, :]), (8, tokens))


def key_products(columns, wide, pair):
    products = []
    for h in range(0, HEADS, 2):
        pair[h // 2, :HEAD_DIM, :HEAD_DIM] = columns(h)
        pair[h // 2, HEAD_DIM:, HEAD_DIM:] = columns(h + 1)
        both = nn(wide[h // 2], pair[h // 2])
        products += [both[:, :HEAD_DIM], both[:, HEAD_DIM:]]
    return products


def solve_kernel(
    place, q_ref, k_ref, s0, s1, s2, s3, c_ref, mask, ridge,
    x_out, p_out, m_out, score_out, scal_out,
    left, wide, decay, pair, x_s, r_s, p_s,
):
    @pl.when(pl.program_id(0) == 0)
    def _():
        prepare(k_ref, c_ref, (s0, s1, s2, s3), place[0], left, wide, decay, pair)
        for h in range(HEADS):
            q = q_ref[h]
            x_s[h] = jnp.zeros_like(q)
            r_s[h] = q
            p_s[h] = q
            scal_out[h, 0:1] = jnp.sum(q * q, axis=0, keepdims=True)

    for t in range(AT_ONCE):
        i = pl.program_id(0) * AT_ONCE + t
        products = key_products(lambda h: p_s[h].astype(bf16), wide, pair)
        for h in range(HEADS):
            p = p_s[h]
            scores = (products[h] * mask[h]).astype(bf16)
            score_out[t, h] = scores
            stacked = jnp.concatenate([(decay[h, 0:1] * p).astype(bf16), scores], axis=0)
            image = nn(left[h], stacked) + ridge[h] * p
            norm = scal_out[h, pl.ds(i, 1)]
            dot = jnp.sum(p * image, axis=0, keepdims=True)
            size = norm / dot
            p_out[t, h] = p
            m_out[t, h] = image
            scal_out[h, pl.ds(2 * ITERS + i, 1)] = dot
            x_s[h] = x_s[h] + size * p
            r = r_s[h] - size * image
            r_s[h] = r
            norm_next = jnp.sum(r * r, axis=0, keepdims=True)
            scal_out[h, pl.ds(i + 1, 1)] = norm_next
            p_s[h] = r + (norm_next / norm) * p

    @pl.when(i == ITERS - 1)
    def _():
        for h in range(HEADS):
            x_out[h] = x_s[h].astype(bf16)


def common_scratch(tokens):
    square = pltpu.VMEM((HEADS, HEAD_DIM, tokens), f32)
    return [
        pltpu.VMEM((HEADS, HEAD_DIM, HEAD_DIM + tokens), bf16),
        pltpu.VMEM((HEADS // 2, tokens, 2 * HEAD_DIM), bf16),
        pltpu.VMEM((HEADS, 8, tokens), f32),
        pltpu.VMEM((HEADS // 2, 2 * HEAD_DIM, 2 * tokens), bf16),
        square, square, square,
    ]


def solve(place, q, k, states, c, mask, ridge):
    tokens = q.shape[2]
    step = pl.BlockSpec((AT_ONCE, HEADS, HEAD_DIM, tokens), lambda i: (i, 0, 0, 0))
    steps = (ITERS, HEADS, HEAD_DIM, tokens)
    return pl.pallas_call(
        solve_kernel,
        grid=(ITERS // AT_ONCE,),
        in_specs=[smem(), whole(HEADS, HEAD_DIM, tokens), whole(HEADS, tokens, HEAD_DIM)] + [whole(*PAIR)] * FOUR
        + [whole(HEADS, tokens), whole(HEADS, tokens, tokens), whole(HEADS, HEAD_DIM, tokens)],
        out_specs=[whole(HEADS, HEAD_DIM, tokens), step, step, step, whole(HEADS, 3 * ITERS, tokens)],
        out_shape=[
            like((HEADS, HEAD_DIM, tokens), bf16), like(steps), like(steps), like(steps, bf16),
            like((HEADS, 3 * ITERS, tokens)),
        ],
        scratch_shapes=common_scratch(tokens),
        compiler_params=pltpu.CompilerParams(vmem_limit_bytes=VMEM_LIMIT),
        cost_estimate=pl.CostEstimate(flops=1, bytes_accessed=1, transcendentals=0),
        name="solve",
    )(place, q, k, *states, c, mask, ridge)


def attend_back_kernel(place, ga_ref, k_ref, v_ref, x_ref, s0, s1, s2, s3, c_ref, mask_ref, gx_o, dk_o, dv_o, state_o):
    quarter = pl.program_id(0)
    tokens = k_ref.shape[1]
    for m in range(SHARE):
        head = quarter * SHARE + m
        c = c_ref[pl.ds(head, 1), :]
        mask = mask_ref[m]
        e = jnp.exp(c)
        state = s0[SHARE + m]
        for i, other in ((1, s1), (2, s2), (3, s3)):
            state = jnp.where((place[0] ^ i) == quarter, other[SHARE + m], state)
        ga = ga_ref[:, cut(m)].T
        low = ga.astype(bf16)
        x = x_ref[m]
        k = k_ref[m]
        scores = (nn(k, x) * mask).astype(bf16)
        dscores = (nn(v_ref[m], low) * mask).astype(bf16)
        ega = (e * ga).astype(bf16)
        gx_o[m] = tn(state, ega) + tn(k, dscores)
        dv_o[m] = nt(scores, low)
        dk_o[m] = nt(dscores, x)
        state_o[m] = nt(ega, x).astype(bf16)


def attend_back(place, ga, k, v, x, states, c, mask):
    tokens = k.shape[1]
    square = like((HEADS, HEAD_DIM, tokens))
    return pl.pallas_call(
        attend_back_kernel,
        grid=(QUARTERS,),
        in_specs=[smem(), quarter_columns(tokens, 0)] + [per_quarter(tokens, HEAD_DIM)] * 2
        + [per_quarter(HEAD_DIM, tokens)] + [whole(*PAIR)] * FOUR + [whole(HEADS, tokens), per_quarter(tokens, tokens)],
        out_specs=[per_quarter(HEAD_DIM, tokens)] * 4,
        out_shape=[square] * 3 + [like((HEADS, HEAD_DIM, HEAD_DIM), bf16)],
        cost_estimate=pl.CostEstimate(flops=1, bytes_accessed=1, transcendentals=0),
        name="attend_back",
    )(place, ga, k, v, x, *states, c, mask)


def adjoint_kernel(
    spot, place, gx_ref, k_ref, s0, s1, s2, s3, c_ref, mask, ridge, p_ref, m_ref, score_ref, scal_ref, values_ref,
    dq_ref, dk_ref, dridge_ref, o0, o1, o2, o3,
    left, wide, decay, pair, gr_s, gp_s, acc_s, next_s, gnorm_s, low_s, steps_p, steps_g, steps_s, stack,
):
    s = pl.program_id(0)
    tokens = k_ref.shape[1]

    @pl.when(s == 0)
    def _():
        prepare(k_ref, c_ref, (s0, s1, s2, s3), place[0], left, wide, decay, pair)
        gr_s[...] = jnp.zeros_like(gr_s)
        gp_s[...] = jnp.zeros_like(gp_s)
        acc_s[...] = jnp.zeros_like(acc_s)
        next_s[...] = jnp.zeros_like(next_s)
        gnorm_s[...] = jnp.zeros_like(gnorm_s)

    for t in reversed(range(AT_ONCE)):
        i = ITERS - AT_ONCE * (s + 1) + t
        at = pl.ds(pl.multiple_of(i * tokens, tokens), tokens)
        for h in range(HEADS):
            p, m, gx = p_ref[t, h], m_ref[t, h], gx_ref[h]
            norm = scal_ref[h, pl.ds(i, 1)]
            dot = scal_ref[h, pl.ds(2 * ITERS + i, 1)]
            size = norm / dot
            ratio = jnp.where(i == ITERS - 1, 0.0, scal_ref[h, pl.ds(i + 1, 1)] / norm)
            gp = gp_s[h]
            gratio = jnp.sum(gp * p, axis=0, keepdims=True)
            gnext = gnorm_s[h, 0:1] + gratio / norm
            gr = gr_s[h] + gp + (2.0 * gnext) * (next_s[h] - ratio * p)
            gsize = jnp.sum(gx * p - gr * m, axis=0, keepdims=True)
            gdot = -gsize * size / dot
            gm = gdot * p - size * gr
            gr_s[h] = gr
            gp_s[h] = ratio * gp + size * gx + gdot * m + ridge[h] * gm
            acc_s[h] = acc_s[h] + gm * p
            next_s[h] = p
            gnorm_s[h, 0:1] = gsize / dot - gratio * ratio / norm
            low = gm.astype(bf16)
            low_s[h] = low
            egm = (decay[h, 0:1] * gm).astype(bf16)
            steps_g[h, :, at] = low
            steps_p[h, :, at] = p.astype(bf16)
            steps_s[h, :, at] = score_ref[t, h]
            stack[h, HEAD_DIM:, at] = egm
        products = key_products(lambda h: low_s[h], wide, pair)
        for h in range(HEADS):
            dscores = (products[h] * mask[h]).astype(bf16)
            stack[h, :HEAD_DIM, at] = dscores
            stacked = jnp.concatenate([stack[h, HEAD_DIM:, at], dscores], axis=0)
            gp_s[h] = gp_s[h] + nn(left[h], stacked)

    @pl.when(s == ITERS // AT_ONCE - 1)
    def _():
        for h in range(HEADS):
            dq_ref[h] = gr_s[h] + gp_s[h] + 2.0 * gnorm_s[h, 0:1] * p_ref[0, h]
            both = nt(steps_p[h], stack[h])
            dk_ref[h] = (nt(steps_g[h], steps_s[h]) + both[:, :HEAD_DIM]).T
            left[h, :, :HEAD_DIM] = both[:, HEAD_DIM:].T.astype(bf16)
            dridge_ref[h] = jnp.sum(acc_s[h].T, axis=0, keepdims=True)
        for j, out in enumerate((o0, o1, o2, o3)):
            for m in range(SHARE):
                head = (position(spot) ^ j) * SHARE + m
                decay = decay_rows(block_decay(c_ref, head))
                out[m, :HEAD_DIM] = left[head, :, :HEAD_DIM]
                out[m, HEAD_DIM:] = decay
                out[SHARE + m, :HEAD_DIM] = values_ref[head]
                out[SHARE + m, HEAD_DIM:] = decay


def adjoint(spot, place, gx, k, states, c, mask, ridge, p_all, m_all, scores, scal, value_states):
    tokens = k.shape[1]
    step = pl.BlockSpec((AT_ONCE, HEADS, HEAD_DIM, tokens), lambda s: (ITERS // AT_ONCE - 1 - s, 0, 0, 0))
    square = pltpu.VMEM((HEADS, HEAD_DIM, tokens), f32)
    line = pltpu.VMEM((HEADS, HEAD_DIM, ITERS * tokens), bf16)
    return pl.pallas_call(
        adjoint_kernel,
        grid=(ITERS // AT_ONCE,),
        in_specs=[smem(), smem(), whole(HEADS, HEAD_DIM, tokens), whole(HEADS, tokens, HEAD_DIM)] + [whole(*PAIR)] * FOUR
        + [whole(HEADS, tokens), whole(HEADS, tokens, tokens), whole(HEADS, HEAD_DIM, tokens), step, step, step, whole(HEADS, 3 * ITERS, tokens), whole(HEADS, HEAD_DIM, HEAD_DIM)],
        out_specs=[whole(HEADS, HEAD_DIM, tokens), whole(HEADS, tokens, HEAD_DIM), whole(HEADS, 1, HEAD_DIM)]
        + [whole(*MESSAGE)] * FOUR,
        out_shape=[like((HEADS, HEAD_DIM, tokens)), like((HEADS, tokens, HEAD_DIM)), like((HEADS, 1, HEAD_DIM))]
        + [like(MESSAGE, bf16)] * FOUR,
        scratch_shapes=common_scratch(tokens) + [
            square,
            pltpu.VMEM((HEADS, 8, tokens), f32),
            pltpu.VMEM((HEADS, HEAD_DIM, tokens), bf16),
            line, line, line,
            pltpu.VMEM((HEADS, 2 * HEAD_DIM, ITERS * tokens), bf16),
        ],
        compiler_params=pltpu.CompilerParams(vmem_limit_bytes=VMEM_LIMIT),
        cost_estimate=pl.CostEstimate(flops=1, bytes_accessed=1, transcendentals=0),
        name="adjoint",
    )(spot, place, gx, k, *states, c, mask, ridge, p_all, m_all, scores, scal, value_states)


def conv_forward(own, lent, halo, t):
    total, shifted = conv_parts(with_halo(own, lent, halo), t[...])
    sig = jax.nn.sigmoid(total)
    return shifted, sig * (1.0 + total * (1.0 - sig)), total * sig


def unit_back(act, grad):
    scale = lax.rsqrt(jnp.sum(act * act, axis=-1, keepdims=True) + 1e-06)
    rows = act * scale
    return scale * (grad - rows * jnp.sum(rows * grad, axis=-1, keepdims=True))


def conv_back(dconv, shifted, t, g, dt):
    taps = t[...]
    tokens = dconv.shape[0]
    blank = jnp.zeros((HALO, dconv.shape[1]), f32)
    padded = jnp.concatenate([blank, dconv, blank], axis=0)
    rows = tokens + HALO
    total = taps[KW - 1 : KW] * padded[:rows]
    for j in range(KW - 1):
        total = total + taps[j : j + 1] * padded[KW - 1 - j : KW - 1 - j + rows]
    g[...] = total.astype(bf16)
    dt[...] = jnp.concatenate(
        [jnp.sum(dconv * shifted[j], axis=0, keepdims=True) for j in range(KW)], axis=0
    )


def queries_back_kernel(own, lent, halo, t, dq_ref, g, dt):
    shifted, slope, act = conv_forward(own, lent, halo, t)
    grads = [unit_back(act[:, cut(m)], dq_ref[m].T) for m in range(SHARE)]
    conv_back(jnp.concatenate(grads, axis=1) * slope, shifted, t, g, dt)


def returned(place, quarter, refs, m):
    state = refs[0][m]
    for i in range(1, FOUR):
        state = jnp.where((place ^ i) == quarter, refs[i][m], state)
    return state


def values_back_kernel(spot, own, lent, halo, t, dv_ref, k_ref, r0, r1, r2, r3, ending_ref, g, dt):
    quarter = pl.program_id(0)
    shifted, slope, _ = conv_forward(own, lent, halo, t)
    grads = []
    for m in range(SHARE):
        rv = returned(position(spot), quarter, (r0, r1, r2, r3), SHARE + m)
        grads.append(dv_ref[m] + ending_ref[m] * nt(k_ref[m], rv))
    conv_back(jnp.concatenate(grads, axis=1) * slope, shifted, t, g, dt)


def keys_back_kernel(
    spot, own, lent, halo, t, dk1, dk2, k_ref, v_ref, r0, r1, r2, r3, ending_ref, g, dt
):
    quarter = pl.program_id(0)
    shifted, slope, act = conv_forward(own, lent, halo, t)
    grads = []
    for m in range(SHARE):
        rv = returned(position(spot), quarter, (r0, r1, r2, r3), SHARE + m)
        rk = returned(position(spot), quarter, (r0, r1, r2, r3), m).astype(f32)
        rk = (rk + rk.T).astype(bf16)
        ending = ending_ref[m]
        dk = dk1[m] + dk2[m] + ending * (nn(k_ref[m], rk) + nn(v_ref[m], rv))
        grads.append(unit_back(act[:, cut(m)], dk))
    conv_back(jnp.concatenate(grads, axis=1) * slope, shifted, t, g, dt)


def third_back(kernel, name, which, taps_third, projected, taps, before, others, specs):
    own, lent, halo = projected
    tokens = own.shape[0]
    return pl.pallas_call(
        kernel,
        grid=(QUARTERS,),
        in_specs=[smem()] * len(before) + [quarter_columns(rows, which) for rows in (tokens, tokens, halo.shape[0])]
        + [quarter_columns(KW, taps_third)] + specs,
        out_specs=[quarter_columns(tokens + HALO, 0), quarter_columns(KW, 0)],
        out_shape=[like((tokens + HALO, D), bf16), like((KW, D))],
        cost_estimate=pl.CostEstimate(flops=1, bytes_accessed=1, transcendentals=0),
        name=name,
    )(*before, own, lent, halo, taps, *others)


def queries_back(projected, taps, dq):
    return third_back(queries_back_kernel, "queries_back", 0, 0, projected, taps, (), (dq,), [per_quarter(HEAD_DIM, HEAD_DIM)])


def values_back(spot, projected, taps, dv, k, states, ending):
    square = per_quarter(HEAD_DIM, HEAD_DIM)
    return third_back(
        values_back_kernel, "values_back", 2, 2, projected, taps, (spot,), (dv, k, *states, ending),
        [square] * 2 + [whole(*PAIR)] * FOUR + [square],
    )


def keys_back(spot, projected, taps, dk1, dk2, k, v, states, ending):
    square = per_quarter(HEAD_DIM, HEAD_DIM)
    return third_back(
        keys_back_kernel, "keys_back", 1, 1, projected, taps, (spot,), (dk1, dk2, k, v, *states, ending),
        [square] * 4 + [whole(*PAIR)] * FOUR + [square],
    )


def keys_values_back_kernel(
    spot, ok, lk, hk, tk, ov, lv, hv, tv, dk1, dk2, dv_ref, k_ref, v_ref, r0, r1, r2, r3, ending_ref, gk, dtk, gv, dtv
):
    values_back_kernel(spot, ov, lv, hv, tv, dv_ref, k_ref, r0, r1, r2, r3, ending_ref, gv, dtv)
    keys_back_kernel(spot, ok, lk, hk, tk, dk1, dk2, k_ref, v_ref, r0, r1, r2, r3, ending_ref, gk, dtk)


def keys_values_back(spot, projected, taps, dk1, dk2, dv, k, v, states, ending):
    own, lent, halo = projected
    tokens = own.shape[0]
    square = per_quarter(HEAD_DIM, HEAD_DIM)
    out = [quarter_columns(tokens + HALO, 0), quarter_columns(KW, 0)]
    return pl.pallas_call(
        keys_values_back_kernel,
        grid=(QUARTERS,),
        in_specs=[smem()]
        + [quarter_columns(rows, third) for third in (1, 2) for rows in (tokens, tokens, halo.shape[0], KW)]
        + [square] * 5 + [whole(*PAIR)] * FOUR + [square],
        out_specs=out * 2,
        out_shape=[like((tokens + HALO, D), bf16), like((KW, D))] * 2,
        cost_estimate=pl.CostEstimate(flops=1, bytes_accessed=1, transcendentals=0),
        name="keys_values_back",
    )(spot, own, lent, halo, taps, own, lent, halo, taps, dk1, dk2, dv, k, v, *states, ending)


def completed(ref, extra):
    more = extra[...].astype(f32)
    more = jnp.concatenate([jnp.zeros_like(more), more], axis=0)
    last = ref.shape[0] - 16
    return [ref[HALO:last], (ref[last:].astype(f32) + more).astype(bf16)]


def products_kernel(plan, joined, cuts, spot, *refs):
    count = len(plan)
    odd = spot[0] % 2 == 1
    outs, scratch = refs[-count - (1 if joined else 1 + len(cuts)) : -count], refs[-count:]

    @pl.when(pl.program_id(0) == 0)
    def _():
        for (lefts, _, _), both in zip(plan, scratch):
            both[...] = jnp.concatenate([refs[at][...] if rows is None else refs[at][rows] for at, rows in lefts], axis=1)

    start = 0
    def right(at, stacked):
        if not stacked:
            return refs[at][...]
        return jnp.concatenate([refs[at][i : i + stacked] for i in range(0, refs[at].shape[0], stacked)], axis=1)

    for (_, rights, size), both in zip(plan, scratch):
        if len(rights) == 4:
            rows = [part for i in (0, 1) for part in completed(refs[rights[i][0]], refs[rights[2 + i][0]])]
        else:
            rows = [right(*at) for at in rights]
        product = nn(both[...], jnp.concatenate(rows, axis=0))
        at = slice(start, start + size)
        start += size
        if joined:
            outs[0][:, at, :] = product.reshape(product.shape[0] // size, size, product.shape[1]).astype(bf16)
            continue
        blocks = product.reshape(product.shape[0] // (2 * size), 2, size, product.shape[1])
        outs[0][:, at, :] = jnp.where(odd, blocks[:, 1], blocks[:, 0]).astype(bf16)
        other = jnp.where(odd, blocks[:, 0], blocks[:, 1]).astype(bf16)
        for out, cut_at in zip(outs[1:], cuts):
            first, last = max(at.start, cut_at.start), min(at.stop, cut_at.stop)
            if first < last:
                out[:, first - cut_at.start : last - cut_at.start, :] = other[:, first - at.start : last - at.start]


def unstacked(array, index):
    row, tokens = index
    return jnp.concatenate([array[row + i * tokens : row + (i + 1) * tokens] for i in range(D // HEAD_DIM)], axis=1)


def products(spot, peers, lefts, rights, tile, joined=False, messages=1):
    sizes = [(part[0][1].stop - part[0][1].start) // peers for part in lefts]
    width = rights[0][0][0].shape[1] if rights[0][0][1] is None else D
    count, number = (peers, 1) if joined else (peers // 2, 2)
    shape = (count, sum(sizes), width)
    cuts = [slice(i * shape[1] // messages, (i + 1) * shape[1] // messages) for i in range(messages)]
    if any(size % 8 for size in sizes):
        odd = spot[0] % 2
        sides = []
        for side in range(number):
            parts = []
            for left, right in zip(lefts, rights):
                if len(right) == 4:
                    rows = []
                    for i in (0, 1):
                        (array, third), (extra, _) = right[i], right[2 + i]
                        size = array.shape[0] // 3
                        rows += completed(array[third * size : (third + 1) * size], extra[:, third * D : (third + 1) * D])
                else:
                    rows = [unstacked(array, index) if index else array for array, index in right]
                blocks = nn(jnp.concatenate([array[at] for array, at in left], axis=1), jnp.concatenate(rows, axis=0))
                blocks = blocks.astype(bf16).reshape(count, number, -1, width)
                parts.append(lax.dynamic_index_in_dim(blocks, 0 if joined else odd ^ side, 1, keepdims=False))
            sides.append(jnp.concatenate(parts, axis=1))
        return sides if joined else sides[:1] + [sides[1][:, at] for at in cuts]
    arrays, specs, plan = [], [], []

    def place_of(array, spec):
        for at, other in enumerate(arrays):
            if other is array and specs[at] is None and spec is None:
                return at
        arrays.append(array)
        specs.append(spec)
        return len(arrays) - 1

    def columns(array, index):
        if index is None:
            return pl.BlockSpec((array.shape[0], tile), lambda j: (0, j))
        if isinstance(index, int) and array.shape[1] == D:
            return pl.BlockSpec((array.shape[0] // 3, tile), lambda j: (index, j))
        if isinstance(index, int):
            return pl.BlockSpec((array.shape[0], tile), lambda j: (0, index * (D // tile) + j))
        size = index[1] * tile // HEAD_DIM
        return pl.BlockSpec((size, HEAD_DIM), lambda j: (index[0] // size + j, 0))

    def left_part(array, rows):
        size = rows.stop - rows.start
        if rows.start % size:
            return place_of(array, None), rows
        at = rows.start // size
        return place_of(array, pl.BlockSpec((size, array.shape[1]), lambda j: (at, 0))), None

    for left, right, size in zip(lefts, rights, sizes):
        plan.append((
            [left_part(array, rows) for array, rows in left],
            [(place_of(array, columns(array, index)), index[1] if isinstance(index, tuple) else None) for array, index in right],
            size,
        ))
    heights = [shape[1]] + ([] if joined else [at.stop - at.start for at in cuts])
    return pl.pallas_call(
        functools.partial(products_kernel, plan, joined, cuts),
        grid=(width // tile,),
        in_specs=[smem()] + [spec or whole(*array.shape) for array, spec in zip(arrays, specs)],
        out_specs=[pl.BlockSpec((count, height, tile), lambda j: (0, 0, j)) for height in heights],
        out_shape=[like((count, height, width), bf16) for height in heights],
        scratch_shapes=[
            pltpu.VMEM((left[0][1].stop - left[0][1].start, sum(array.shape[1] for array, _ in left)), bf16) for left in lefts
        ],
        compiler_params=pltpu.CompilerParams(vmem_limit_bytes=VMEM_LIMIT),
        cost_estimate=pl.CostEstimate(flops=1, bytes_accessed=1, transcendentals=0),
        name="products",
    )(spot, *arrays)


def lent_kernel(own, peer, extra1, extra2, logit1, logit2, qkv_ref, gate_ref, own_o, theirs_o):
    rows = own_o.shape[0]
    logits = [unstacked(ref, (D // HEAD_DIM * rows, rows)) for ref in (logit1, logit2)]
    total = nt(jnp.concatenate(logits, axis=0), gate_ref[...])
    size = rows + HALO
    for third in range(3):
        at, columns = slice(third * size, (third + 1) * size), slice(third * D, (third + 1) * D)
        both = completed(own.at[at], extra1[:, columns]) + completed(peer.at[at], extra2[:, columns])
        total = total + nt(jnp.concatenate(both, axis=0), qkv_ref[:, columns])
    own_o[...] = total[:rows]
    theirs_o[...] = total[rows:].astype(bf16)


def lent_rows(own, peer, extras, logits, qkv_weight, gate_weight):
    rows = own.shape[0] // 3 - HALO
    half = qkv_weight.shape[0]
    vmem = pl.BlockSpec(memory_space=pltpu.VMEM)
    return pl.pallas_call(
        lent_kernel,
        in_specs=[vmem] * 8,
        out_specs=[vmem] * 2,
        out_shape=[like((rows, half)), like((rows, half), bf16)],
        compiler_params=pltpu.CompilerParams(vmem_limit_bytes=VMEM_LIMIT),
        cost_estimate=pl.CostEstimate(flops=1, bytes_accessed=1, transcendentals=0),
        name="lent_rows",
    )(own, peer, *extras, *logits, qkv_weight, gate_weight)


def norm_back_kernel(place, own, back, tok_ref, gain_ref, hid_ref, tq, tk, tv, second_ref, ridge_ref, tok_o, vec_o):
    mine, other = own[...], back[...].astype(f32)
    grad = jnp.where(
        place[0] == 0, jnp.concatenate([mine, other], axis=1), jnp.concatenate([other, mine], axis=1)
    )
    tokens = tok_ref[...]
    scale = lax.rsqrt(jnp.mean(tokens * tokens, axis=-1, keepdims=True) + 1e-05)
    rows = tokens * scale
    grows = grad * gain_ref[...]
    tok_o[...] = hid_ref[...] + scale * (grows - rows * jnp.mean(grows * rows, axis=-1, keepdims=True))
    vec_o[:KW] = jnp.concatenate([tq[...], tk[...], tv[...]], axis=1)
    ridge = jnp.concatenate([ridge_ref[h] for h in range(HEADS)], axis=1)
    first = jnp.sum(grad * rows, axis=0, keepdims=True)
    vec_o[KW : KW + 1] = jnp.concatenate([first, second_ref[...], ridge], axis=1)
    vec_o[KW + 1 :] = jnp.zeros((8 - KW - 1, 3 * D), f32)


def norm_back(place, own, back, tokens, gain, hidden, taps, second, ridge):
    vmem = pl.BlockSpec(memory_space=pltpu.VMEM)
    return pl.pallas_call(
        norm_back_kernel,
        in_specs=[smem()] + [vmem] * 10,
        out_specs=[vmem] * 2,
        out_shape=[like(tokens.shape), like((8, 3 * D))],
        cost_estimate=pl.CostEstimate(flops=1, bytes_accessed=1, transcendentals=0),
        name="norm_back",
    )(place, own, back, tokens, gain, hidden, *taps, second, ridge)


def step_kernel(bit, kept_mine, kept_other, *refs):
    mine_o, other_o = refs[-2:]
    start = 0
    for mine, other in zip(refs[0:-2:2], refs[1:-2:2]):
        at = slice(start, start + mine.shape[1])
        start += mine.shape[1]
        mine_o[0, at] = (kept_mine[0, at].astype(f32) + mine[0].astype(f32)).astype(bf16)
        other_o[0, at] = (kept_other[0, at].astype(f32) + other[0].astype(f32)).astype(bf16)


def halving_step(bit, below, kept, got):
    count, size, width = kept.shape

    def half(side, rows):
        def index(i, s):
            return ((i // below) * 2 * below + (s[0] if side == 0 else 1 - s[0]) * below + i % below, 0, 0)

        return pl.BlockSpec((1, rows, width), index)

    out = pl.BlockSpec((1, size, width), lambda i, s: (i, 0, 0))
    arrays = [kept] + list(got)
    return pl.pallas_call(
        step_kernel,
        grid_spec=pltpu.PrefetchScalarGridSpec(
            num_scalar_prefetch=1,
            grid=(count // 2,),
            in_specs=[half(side, x.shape[1]) for x in arrays for side in (0, 1)],
            out_specs=[out, out],
        ),
        out_shape=[like((count // 2, size, width), bf16)] * 2,
        cost_estimate=pl.CostEstimate(flops=1, bytes_accessed=1, transcendentals=0),
        name="halving",
    )(bit, *[x for x in arrays for _ in (0, 1)])


BLOCKS = D // HEAD_DIM


def middle_kernel(
    owners, place, x_ref, s0, s1, s2, s3, k_ref, v_ref, c_ref, mask_ref, own_logit, lent_logit, tok_ref, cot_ref, gain_ref, first_ref,
    own_out, out_a, out_b, out_c, out_d, *refs,
):
    own_up = refs[:4]
    up_parts = (refs[4:8], refs[8:12])
    own_down = refs[12]
    down_parts = refs[13:17]
    (out_o, hid_o, gatt_o, own_o, sent_o, ggu_o, dgain_o) = refs[17:24]
    out_s, up_s, down_s, nf_s, gb_s, att_s, sig_s, hid_s, acc_s, gnf_s, inner_s = refs[24:]
    j = pl.program_id(0)
    y = place[0]
    half = D // 2

    def aligned(at, by):
        return pl.multiple_of(at, by)

    mine = pl.ds(aligned(y * half, half), half)
    theirs = pl.ds(aligned((1 - y) * half, half), half)

    def order(q):
        return [q, q ^ 2, q ^ 1, q ^ 3]

    tile = own_up[0].shape[1]
    tokens = tok_ref.shape[0]

    def spread_rows(rows, start):
        total = rows.shape[0]
        size = total // owners
        own_at = slice(start, start + total // 2)
        sent_at = slice(3 * BLOCKS * tokens + start, 3 * BLOCKS * tokens + start + total // 2)
        if size % 8:
            own_o[own_at], sent_o[sent_at] = rows[: total // 2].astype(bf16), rows[total // 2 :].astype(bf16)
            return
        blocks = rows.reshape(owners // 2, 2, size, rows.shape[1])
        for out, at, odd in ((own_o, own_at, y == 1), (sent_o, sent_at, y == 0)):
            out[at] = jnp.where(odd, blocks[:, 1], blocks[:, 0]).reshape(total // 2, rows.shape[1]).astype(bf16)

    def stack_right(value, index):
        for i in range(BLOCKS):
            sent_o[(index * BLOCKS + i) * tokens : (index * BLOCKS + i + 1) * tokens] = value[:, cut(i)]

    def scale_of(hidden):
        return lax.rsqrt(jnp.mean(hidden * hidden, axis=-1, keepdims=True) + 1e-05)

    @pl.when(j == 0)
    def _():
        for i, state in enumerate((s0, s1, s2, s3)):
            for m in range(SHARE):
                head = (place[1] ^ i) * SHARE + m
                c = c_ref[pl.ds(head, 1), :]
                x = x_ref[head]
                scores = (nn(k_ref[head], x) * mask_ref[head]).astype(bf16)
                part = jnp.exp(c) * nn(state[SHARE + m], x) + tn(v_ref[head], scores)
                att_s[:, pl.ds(aligned(head * HEAD_DIM, HEAD_DIM), HEAD_DIM)] = part.T
        out_s[mine, :] = own_out[...]
        wide = out_a.shape[1]
        for part, q in zip((out_a, out_b, out_c, out_d), order(place[1])):
            out_s[theirs, pl.ds(aligned(q * wide, wide), wide)] = part[...]
        sig = jax.nn.sigmoid(own_logit[...] + lent_logit[...].astype(f32))
        sig_s[...] = sig
        mix = (att_s[...] * sig).astype(bf16)
        spread_rows(mix.astype(f32).T, half)
        normed = tok_ref[...] * scale_of(tok_ref[...]) * first_ref[...]
        spread_rows(normed.astype(bf16).astype(f32).T, 2 * half)
        hidden = tok_ref[...] + nn(mix, out_s[...])
        hid_s[...] = hidden
        normed = (hidden * scale_of(hidden) * gain_ref[...]).astype(bf16)
        nf_s[...] = normed
        spread_rows(normed.astype(f32).T, 0)
        gb_s[...] = cot_ref[...].astype(bf16)
        stack_right(gb_s[...], 2)
        acc_s[...] = jnp.zeros_like(acc_s)
        gnf_s[...] = jnp.zeros_like(gnf_s)

    for i in range(4):
        up_s[mine, i * tile : (i + 1) * tile] = own_up[i][...]
    count = up_parts[0][0].shape[0]
    at = pl.ds(aligned((1 - y) * half, 16), count)
    for part, q in zip(up_parts[0], order(place[2])):
        slot = (q >> 1) * 2 + ((q & 1) ^ y)
        up_s[at, pl.ds(aligned(slot * tile, tile), tile)] = part[...]
    at = pl.ds(aligned((1 - y) * half + count, 16), half - count)
    for i, part in enumerate(up_parts[1]):
        slot = ((place[1] ^ (i // 2)) & 1) * 2 + i % 2
        up_s[at, pl.ds(aligned(slot * tile, tile), tile)] = part[...]
    down_s[:tile, :] = own_down[...]
    wide = down_parts[0].shape[1]
    for part, q in zip(down_parts, order(place[1])):
        down_s[tile:, pl.ds(aligned(q * wide, wide), wide)] = part[...]
    product = nn(nf_s[...], up_s[...])
    gate, up = product[:, : 2 * tile], product[:, 2 * tile :]
    ginner = nt(gb_s[...], down_s[...])
    sig = jax.nn.sigmoid(gate)
    silu = gate * sig
    inner = (silu * up).astype(bf16)
    ggate = (ginner * up * (sig * (1.0 + gate * (1.0 - sig)))).astype(bf16)
    gup = (ginner * silu).astype(bf16)
    ggu = jnp.concatenate([ggate, gup], axis=1)
    acc_s[...] += nn(inner, down_s[...])
    gnf_s[...] += nt(ggu, up_s[...])
    inner_t = inner.astype(f32).T
    for slot, value in ((y, inner_t[:tile]), (1 - y, inner_t[tile:])):
        inner_s[pl.ds(aligned(slot * (FF // 2) + j * tile, tile), tile), :] = value
    share = FF // 2
    for i, (slot, value) in enumerate(((y, ggate), (1 - y, ggate), (2 + y, gup), (3 - y, gup))):
        at = pl.ds(aligned(slot * share + j * tile, tile), tile)
        ggu_o[:, at] = value[:, (i % 2) * tile : (i % 2 + 1) * tile]

    @pl.when(j == pl.num_programs(0) - 1)
    def _():
        spread_rows(inner_s[...], 3 * half)
        hidden = hid_s[...]
        out_o[...] = hidden + acc_s[...]
        scale = scale_of(hidden)
        rows = hidden * scale
        gnf = gnf_s[...]
        dgain_o[...] = jnp.sum(gnf * rows, axis=0, keepdims=True)
        grows = gnf * gain_ref[...]
        ghid = cot_ref[...] + scale * (grows - rows * jnp.mean(grows * rows, axis=-1, keepdims=True))
        hid_o[...] = ghid
        low = ghid.astype(bf16)
        stack_right(low, 0)
        gmix = nt(low, out_s[...])
        sig = sig_s[...]
        gatt = gmix * sig
        gatt_o[...] = gatt
        stack_right((gatt * att_s[...] * (1.0 - sig)).astype(bf16), 1)


def middle(owners, place, attention, own_logit, lent_logit, tok, cot, gain, gain_first, out_weight, up_weight, down_weight, up_parts, rest_parts):
    tokens = tok.shape[0]
    tile = 128
    share = FF // 2 // tile
    half = D // 2
    left_rows = 3 * half + FF // 2

    def full(*shape):
        return pl.BlockSpec(shape, lambda j, s: (0,) * len(shape))

    rows = full(tokens, D)
    own_up = [
        pl.BlockSpec((half, tile), lambda j, s: (0, s[0] * share + j)),
        pl.BlockSpec((half, tile), lambda j, s: (0, (1 - s[0]) * share + j)),
        pl.BlockSpec((half, tile), lambda j, s: (0, (2 + s[0]) * share + j)),
        pl.BlockSpec((half, tile), lambda j, s: (0, (3 - s[0]) * share + j)),
    ]
    up_specs = [pl.BlockSpec((p.shape[0], tile), lambda j, s: (0, j)) for p in up_parts[:4]]
    rest_rows = up_parts[4].shape[0]
    up_specs += [
        pl.BlockSpec((rest_rows, tile), lambda j, s: (0, s[0] * share + j)),
        pl.BlockSpec((rest_rows, tile), lambda j, s: (0, (1 - s[0]) * share + j)),
    ] * 2
    up_parts = up_parts[:4] + (up_parts[4],) * 2 + (up_parts[5],) * 2
    own_down = pl.BlockSpec((tile, D), lambda j, s: (j, 0))
    down_specs = [pl.BlockSpec((tile, D // 4), lambda j, s: (half // tile + j, 0))] * 4
    square = (HEAD_DIM, HEAD_DIM)
    return pl.pallas_call(
        functools.partial(middle_kernel, owners),
        grid_spec=pltpu.PrefetchScalarGridSpec(
            num_scalar_prefetch=1,
            grid=(share,),
            in_specs=[full(HEADS, HEAD_DIM, tokens)] + [full(*PAIR)] * FOUR + [full(HEADS, tokens, HEAD_DIM)] * 2
            + [full(HEADS, tokens), full(HEADS, tokens, tokens)]
            + [pl.BlockSpec((tokens, D), lambda j, s: (0, 3))] * 2
            + [rows] * 2 + [full(1, D), full(1, D), full(half, D)] + [full(half, D // 4)] * 4
            + own_up + up_specs + [own_down] + down_specs,
            out_specs=[
                rows, rows, rows, full(left_rows, tokens), full(3 * BLOCKS * tokens + left_rows, tokens),
                full(tokens, 2 * FF),
                full(1, D),
            ],
            scratch_shapes=[
                pltpu.VMEM((D, D), bf16),
                pltpu.VMEM((D, 4 * tile), bf16),
                pltpu.VMEM((2 * tile, D), bf16),
                pltpu.VMEM((tokens, D), bf16),
                pltpu.VMEM((tokens, D), bf16),
                pltpu.VMEM((tokens, D), f32),
                pltpu.VMEM((tokens, D), f32),
                pltpu.VMEM((tokens, D), f32),
                pltpu.VMEM((tokens, D), f32),
                pltpu.VMEM((tokens, D), f32),
                pltpu.VMEM((FF, tokens), f32),
            ],
        ),
        out_shape=[
            like((tokens, D)), like((tokens, D)), like((tokens, D)),
            like((left_rows, tokens), bf16), like((3 * BLOCKS * tokens + left_rows, tokens), bf16),
            like((tokens, 2 * FF), bf16),
            like((1, D)),
        ],
        compiler_params=pltpu.CompilerParams(vmem_limit_bytes=VMEM_LIMIT),
        cost_estimate=pl.CostEstimate(flops=1, bytes_accessed=1, transcendentals=0),
        name="middle",
    )(
        place, *attention, own_logit, lent_logit, tok, cot, gain, gain_first, out_weight, *rest_parts,
        *[up_weight] * 4, *up_parts, down_weight, *rest_parts,
    )


def shifted(x, axis, by):
    peers = lax.axis_size(axis)
    return lax.ppermute(x, axis, [(i, i + by) for i in range(peers) if 0 <= i + by < peers])


def crossed(x, by):
    peers, pair = lax.axis_size("ctx"), 2
    return lax.ppermute(
        x,
        ("ctx", "fsdp"),
        [(i * pair + s, (i + by) * pair + 1 - s) for i in range(peers) if 0 <= i + by < peers for s in range(pair)],
    )


def pick(x, index, axis=0):
    return lax.dynamic_index_in_dim(x, index, axis, keepdims=False)


def part(x, index, axis):
    size = x.shape[axis] // 2
    return lax.dynamic_slice_in_dim(x, index * size, size, axis)


def quarter(shard, q, start=0, count=None):
    wide = shard.shape[1] // 4
    return lax.dynamic_slice(shard, (start, q * wide), (count or shard.shape[0], wide))


class Reduction:
    def __init__(self, order, blocks):
        self.here = lax.axis_index("ctx")
        levels = lax.axis_size("ctx").bit_length() - 1
        self.order = list(order) + [level for level in range(levels) if level not in order]
        self.left = list(range(levels))
        self.kept, *sent = blocks
        self.send(sent)

    def bit(self):
        return (self.here >> self.order[0]) & 1

    def send(self, arrays):
        level = self.order.pop(0)
        self.left.remove(level)
        self.got = [partner(array, "ctx", 1 << level) for array in arrays]

    def step(self):
        below = 1 << self.left.index(self.order[0])
        self.kept, sent = halving_step(self.bit().astype(jnp.int32)[None], below, self.kept, self.got)
        self.send([sent])
        return sent

    def result(self, sizes):
        while self.order:
            self.step()
        total = (self.kept.astype(f32) + self.got[0].astype(f32))[0]
        ends = [sum(sizes[: i + 1]) for i in range(len(sizes))]
        return [total[end - size : end] for end, size in zip(ends, sizes)]


class Sequence:
    def __init__(self):
        self.last = ()

    def gate(self, *values):
        return lax.optimization_barrier(values + self.last)[: len(values)]

    def mark(self, *values):
        self.last = values


def added(value, axis):
    for level in range(lax.axis_size(axis).bit_length() - 1):
        value = value + partner(value, axis, 1 << level)
    return value


def rms_scale(values, gain):
    return values * lax.rsqrt(jnp.mean(values * values, axis=-1, keepdims=True) + 1e-05) * gain


def sided(mine, theirs, y, axis):
    return jnp.where(
        y == 0, jnp.concatenate([mine, theirs], axis=axis), jnp.concatenate([theirs, mine], axis=axis)
    )


UP_ROWS = 400


def local(
    inputs,
    qkv_weight,
    gate_weight,
    out_weight,
    up_weight,
    down_weight,
    conv_taps,
    gain_attn,
    gain_ffn,
    ridge_terms,
    forget,
    cotangent,
):
    tokens = inputs[0]
    rows = tokens.shape[0]
    y = lax.axis_index("fsdp")
    here = lax.axis_index("ctx")
    peers = lax.axis_size("ctx")
    owners = peers * 2
    near_x = here % 4
    near_z = here % 2 + 2 * ((here // 4) % 2)
    place = jnp.stack([y, near_x, near_z]).astype(jnp.int32)
    spot = here.astype(jnp.int32)[None]
    spot_back = (peers - 1 - here).astype(jnp.int32)[None]
    ring = near_x.astype(jnp.int32)[None]
    seq = Sequence()

    lines = jnp.stack([gain_attn, gain_ffn, ridge_terms, ridge_terms])
    mine, theirs = norm(place, tokens, conv_taps, lines)
    theirs = partner(theirs, "fsdp")
    lent = weigh(theirs, rows, gain_attn[None], qkv_weight, gate_weight, bf16)
    seq.mark(lent)
    lent = partner(lent, "fsdp")
    peer_extra = theirs[rows:].astype(f32)
    (peer_extra,) = seq.gate(peer_extra)
    taps_rows = KW * 3
    vectors = sided(lines[:3].astype(f32), peer_extra[taps_rows : taps_rows + 3], y, 1)
    taps = sided(conv_taps.astype(f32), peer_extra[:taps_rows].reshape(conv_taps.shape), y, 1)
    gain_first, gain_second = vectors[0], vectors[1:2]
    ridge = vectors[2].reshape(HEADS, HEAD_DIM)
    cumulative = jnp.cumsum(jnp.log(forget[0]).T, axis=-1)
    strength = (1.0 - forget[0]).T
    out_here, up_here, down_here = seq.gate(out_weight, up_weight, down_weight)
    rest_quarter = jnp.concatenate([quarter(out_here, near_x), quarter(down_here, near_x)], axis=0)
    seq.mark(rest_quarter)
    rest_direct = partner(rest_quarter, "fsdp")
    (up_here,) = seq.gate(up_here)
    up_quarters = [
        quarter(up_here, near_z, 0, UP_ROWS),
        lax.dynamic_slice(up_here, (UP_ROWS, (here % 2) * FF), (D // 2 - UP_ROWS, FF)),
    ]
    seq.mark(*up_quarters)
    cumulative, strength, ridge, taps, mine = seq.gate(cumulative, strength, ridge, taps, mine)
    own = weigh(mine, rows, gain_attn[None], qkv_weight, gate_weight, f32)
    mask, ending, ridge = tables(cumulative, strength, ridge)
    seq.mark(mask, own)

    own, lent, up_first = seq.gate(own, lent, up_quarters[0])
    halo = shifted((own[rows - 8 :, : 3 * D] + lent[rows - 8 :, : 3 * D].astype(f32)).astype(bf16), "ctx", 1)
    projected = own, lent, halo
    queries, keys_low, values_low, *near = features(spot, projected, taps, ending, cumulative)
    seq.mark(*near)
    scan = Scan(spot, swapped(near, "ctx"), "ctx")
    up_first = partner(up_first, "fsdp")

    def split(left):
        flat = left.reshape(peers, 2, left.shape[0] // owners, left.shape[1])
        return [pick(flat, side, 1).reshape(-1, left.shape[1]) for side in (y, 1 - y)]

    scan.near = list(seq.gate(*scan.near))
    scan.group()
    seq.mark(scan.total)
    (rest_direct,) = seq.gate(rest_direct)
    rest_across = partner(rest_direct, "ctx", 2)
    scan.far = list(seq.gate(*scan.far))
    states = scan.spread()
    seq.mark(scan.parts[0])
    up_first, up_second = seq.gate(up_first, up_quarters[1])
    up_second = partner(up_second, "fsdp")
    first_across = partner(up_first, "ctx", 4)
    *states, queries = seq.gate(*states, queries)
    seq.mark(states[1], states[2], states[3])
    rest_direct, rest_across, up_first = seq.gate(rest_direct, rest_across, up_first)
    rest_core, rest_far, first_core = partner(rest_direct, "ctx", 1), partner(rest_across, "ctx", 1), partner(up_first, "ctx", 1)
    (queries,) = seq.gate(queries)
    x, p_all, m_all, scores, scal = solve(ring, queries, keys_low, states, cumulative, mask, ridge)
    seq.mark(x)

    def split(left):
        flat = left.reshape(peers, 2, left.shape[0] // owners, left.shape[1])
        return [pick(flat, side, 1).reshape(-1, left.shape[1]) for side in (y, 1 - y)]

    def share(right):
        return right, partner(right, "fsdp")

    up_second, rest_core, rest_far = seq.gate(up_second, rest_core, rest_far)
    second_core = partner(up_second, "ctx", 1)
    (first_across,) = seq.gate(first_across)
    rest_parts = (rest_direct, rest_across, rest_core, rest_far)
    up_parts = (up_first, first_across, first_core, partner(first_across, "ctx", 1))
    up_parts += (up_second, second_core)

    output, grad_hidden, grad_attended, lefts, message, grad_gate_up, grad_second_gain = middle(
        owners, place, (x, *states, keys_low, values_low, cumulative, mask), own, lent,
        tokens, cotangent[0], gain_second, gain_first[None], out_weight, up_weight, down_weight, up_parts, rest_parts
    )
    size = D // 2
    parts = [slice(0, size), slice(size, 2 * size), slice(2 * size, 3 * size), slice(3 * size, 3 * size + FF // 2)]
    start = 3 * BLOCKS * rows
    peer_parts = [slice(start + at.start, start + at.stop) for at in parts]
    if (D // owners) % 8 or (FF // owners) % 8:
        pairs = [split(jnp.concatenate([lefts[at], message[there]], axis=0)) for at, there in zip(parts, peer_parts)]
        lefts = jnp.concatenate([own for own, _ in pairs], axis=0)
        message = jnp.concatenate([message[:start]] + [sent for _, sent in pairs], axis=0)
    seq.mark(grad_second_gain)
    message_peer = partner(message, "fsdp")
    (grad_attended,) = seq.gate(grad_attended)
    gx, dk_attend, dv, value_states = attend_back(
        ring, grad_attended, keys_low, values_low, x, states, cumulative, mask
    )
    dq, dk_solve, grad_ridge, *own = adjoint(
        spot_back, ring, gx, keys_low, states, cumulative, mask, ridge, p_all, m_all, scores, scal, value_states
    )
    seq.mark(*own)
    back = Scan(spot_back, swapped(own, "ctx"), "ctx")
    (up_here,) = seq.gate(grad_gate_up)
    both_up = share(up_here)
    dq, back.near[1] = seq.gate(dq, back.near[1])
    low_q, taps_q = queries_back(projected, taps, dq)
    seq.mark(low_q)
    back.near = list(seq.gate(*back.near))
    back.group()
    seq.mark(back.total)
    lefts_here, message_peer, back.far[1] = seq.gate(lefts, message_peer, back.far[1])
    rights = [(i * BLOCKS * rows, rows) for i in range(3)]
    (early,) = products(
        spot, peers, [[(lefts_here, parts[i]), (message_peer, peer_parts[i])] for i in (1, 2, 3)],
        [[(message, at), (message_peer, at)] for at in rights], 1024, joined=True
    )
    seq.mark(early)
    early = lax.psum_scatter(early.reshape(-1, D), "ctx", scatter_dimension=0, tiled=True)
    back.far = list(seq.gate(*back.far))
    states_back = back.spread()
    seq.mark(back.parts[0])
    dv, *states_back = seq.gate(dv, *states_back)
    low_k, taps_k, low_v, taps_v = keys_values_back(
        spot_back, projected, taps, dk_attend, dk_solve, dv, keys_low, values_low, states_back, ending
    )
    seq.mark(low_k)
    (up_peer,) = seq.gate(both_up[1])
    blocks = products(
        spot, peers, [[(lefts, parts[0]), (message_peer, peer_parts[0])]], [[(both_up[0], None), (up_peer, None)]], 2816
    )
    seq.mark(blocks[0])
    ups = Reduction((0, 1, 2), blocks)
    low_q, low_k, low_v = seq.gate(low_q, low_k, low_v)
    ahead = jnp.concatenate([low[HALO - 8 : HALO] for low in (low_q, low_k, low_v)], axis=1)
    extra = shifted(ahead, "ctx", -1), crossed(ahead, -1)
    thirds = jnp.concatenate([low_q, low_k, low_v], axis=0)
    thirds, *extra = lax.optimization_barrier((thirds, *extra))
    thirds_peer = partner(thirds, "fsdp")
    *ups.got, extra1, extra2 = seq.gate(*ups.got, *extra)
    extra = extra1, extra2
    seq.mark(ups.step())
    lefts_here, thirds_peer = seq.gate(lefts, thirds_peer)
    left = [(lefts_here, parts[2]), (message_peer, peer_parts[2])]
    rights = [[(thirds, i), (thirds_peer, i), (extra[0], i), (extra[1], i)] for i in range(3)]
    blocks = products(spot, peers, [left] * 3, rights, 1024, messages=2)
    seq.mark(blocks[0])
    late = Reduction((0, 1, 2), blocks)
    late.got = seq.gate(*late.got)
    seq.mark(late.step())
    (thirds_here,) = seq.gate(thirds)
    kept, lent = lent_rows(thirds_here, thirds_peer, extra, (message, message_peer), qkv_weight, gate_weight)
    seq.mark(lent)
    arriving = partner(lent, "fsdp")
    ups.got = seq.gate(*ups.got)
    seq.mark(ups.step())
    (arriving,) = seq.gate(arriving)
    grad_tokens, vector = norm_back(
        place, kept, arriving, tokens, gain_first[None], grad_hidden, (taps_q, taps_k, taps_v), grad_second_gain, grad_ridge
    )
    seq.mark(vector)
    size, width = D // owners, 3 * D // owners
    vector = jnp.concatenate(
        [vector[:KW].reshape(KW, owners, width).transpose(1, 0, 2).reshape(owners, KW * width),
         vector[KW].reshape(3, owners, size).transpose(1, 0, 2).reshape(owners, 3 * size)], axis=1
    ).reshape(peers, 2, KW * width + 3 * size)
    vector_kept, vector_sent = pick(vector, y, 1), pick(vector, 1 - y, 1)
    seq.mark(vector_sent)
    arriving = partner(vector_sent, "fsdp")
    late.got = seq.gate(*late.got)
    seq.mark(late.step())
    *ups.got, early = seq.gate(*ups.got, early)
    seq.mark(ups.step())
    vector_kept, arriving = seq.gate(vector_kept, arriving)
    vector = vector_kept + arriving
    seq.mark(vector)
    vector = lax.all_to_all(vector, "ctx", 0, 0, tiled=True)
    late.got = seq.gate(*late.got)
    seq.mark(late.step())
    vector = jnp.sum(seq.gate(vector)[0], axis=0)
    size = D // owners
    grad_up = ups.result([size])[0]
    grad_q, grad_k, grad_v = late.result([size] * 3)
    grad_qkv = jnp.concatenate([grad_q, grad_k, grad_v], axis=1)
    early = early.astype(f32)
    grad_out, grad_gate, grad_down = early[:size], early[size : 2 * size], early[2 * size :]
    return (
        output[None],
        grad_tokens[None],
        grad_qkv,
        grad_gate,
        grad_out,
        grad_up,
        grad_down,
        vector[: KW * width].reshape(KW, width),
        vector[KW * width : KW * width + size],
        vector[KW * width + size : KW * width + 2 * size],
        vector[KW * width + 2 * size :],
    )


def solution(mesh):
    tokens = P("fsdp", "ctx", None)
    rows = P("fsdp", None)
    vector = P("fsdp")
    owned = P(("ctx", "fsdp"), None)
    owned_vector = P(("ctx", "fsdp"))
    return jax.shard_map(
        local,
        mesh=mesh,
        in_specs=(
            tokens, rows, rows, rows, rows, rows, P(None, "fsdp"), vector, vector, vector, tokens, tokens,
        ),
        out_specs=(
            tokens, tokens, owned, owned, owned, owned, owned, P(None, ("ctx", "fsdp")),
            owned_vector, owned_vector, owned_vector,
        ),
        check_vma=False,
    )
```
